32 devices in a mesh: dp: 16 (over z, y, x), mod: 2 (over core).
Axes of the slice: x: 2, y: 2, z: 4, core: 2. Of those that a mesh axis runs over, the one named last changes fastest.
Arguments:
- latents: float32 [128, 256, 16], P(('dp', 'mod')), may hold values from -6 to 6
- noise: float32 [128, 256, 16], P(('dp', 'mod')), may hold values from -6 to 6
- timesteps: int32 [128], P(('dp', 'mod')), may hold values from 0 to 999
- labels: int32 [128], P(('dp', 'mod')), may hold values from 0 to 999
- drops: int32 [128], P(('dp', 'mod')), may hold values 0 or 1
- block_weights: float32 [1152, 13824], P('dp'), may hold values from -0.1875 to 0.1875
- block_first: float32 [1152, 13824], P('dp'), may hold values from -5.722046e-06 to 5.722046e-06
- block_second: float32 [1152, 13824], P('dp'), may hold values from 8.512235e-14 to 3.404894e-13
- mod_weights: float32 [1152, 9216], P('dp', 'mod'), may hold values from -0.1875 to 0.1875
- mod_first: float32 [1152, 9216], P('dp', 'mod'), may hold values from -5.722046e-06 to 5.722046e-06
- mod_second: float32 [1152, 9216], P('dp', 'mod'), may hold values from 8.512235e-14 to 3.404894e-13
- embed_weights: float32 [2441, 1152], P(None, 'dp'), may hold values from -0.375 to 0.375
- embed_first: float32 [2441, 1152], P(None, 'dp'), may hold values from -5.722046e-06 to 5.722046e-06
- embed_second: float32 [2441, 1152], P(None, 'dp'), may hold values from 8.512235e-14 to 3.404894e-13
- rel_bias: float32 [16, 961], replicated, may hold values from -3 to 3
- rel_first: float32 [16, 961], replicated, may hold values from -3.545532e-08 to 3.545532e-08
- rel_second: float32 [16, 961], replicated, may hold values from 1.2681992e-20 to 1.298636e-17
Outputs:
- loss_sum: float32 [], replicated
- grad_norm: float32 [], replicated
- matrix_norms: float32 [2, 12], replicated
- block_new: float32 [1152, 13824], P('dp')
- block_first_new: float32 [1152, 13824], P('dp')
- block_second_new: float32 [1152, 13824], P('dp')
- block_copy: bfloat16 [1152, 13824], P('dp')
- mod_new: float32 [1152, 9216], P('dp', 'mod')
- mod_first_new: float32 [1152, 9216], P('dp', 'mod')
- mod_second_new: float32 [1152, 9216], P('dp', 'mod')
- mod_copy: bfloat16 [1152, 9216], P('dp', 'mod')
- embed_new: float32 [2441, 1152], P(None, 'dp')
- embed_first_new: float32 [2441, 1152], P(None, 'dp')
- embed_second_new: float32 [2441, 1152], P(None, 'dp')
- embed_copy: bfloat16 [2441, 1152], P(None, 'dp')
- rel_new: float32 [16, 961], replicated
- rel_first_new: float32 [16, 961], replicated
- rel_second_new: float32 [16, 961], replicated
- rel_copy: bfloat16 [16, 961], replicated
- rel_clipped: float32 [16, 961], replicated
The draws below stay inside these ranges and needn't reach their ends.
All inputs are finite; a program needn't handle non-finite values. No bound on the sum of `drops` on one device may be relied on, other than what follows from the above.
Results may differ from the reference program's by a relative error of at most 0.023.
Values may be sent and summed in bfloat16 or wider, within the bound.
No kernel may reach another device: no remote copies, remote signals or barrier semaphores. Data moves between devices by JAX's collectives and lax.ppermute only.
A program may use at most 280 MiB of HBM per device.

```python
import math
import jax
import jax.numpy as jnp
import numpy as np
from jax import lax

D = 1152
HEADS = 16
HD = 72
MLPW = 4608
NCLASS = 1000
FREQ = 256
GRID = 16
PDIM = 16
NSTEPS = 1000
STEP = 10
SEQ = 256
REL = 961
EROWS = 2441
NPARAM = 29369488
IMAGES = 128


def bias_spread():
    places = jnp.arange(REL, dtype=jnp.int32)
    row_stride = 2 * GRID - 1
    row_gap = jnp.abs(places // row_stride - (GRID - 1))
    col_gap = jnp.abs(places % row_stride - (GRID - 1))
    pair_count = ((GRID - row_gap) * (GRID - col_gap)).astype(jnp.float32)
    base_level = 0.0068 * HD ** 0.5 / (SEQ * NPARAM ** 0.5)
    return base_level * jnp.sqrt(pair_count * (REL / GRID ** 4))


def draw_rel_first(key, part):
    key = jax.random.fold_in(key, 11)
    normal_values = jnp.clip(jax.random.normal(key, (HEADS, REL), jnp.float32), -4.0, 4.0)
    return normal_values * 0.11 * bias_spread()[None, :]


def draw_rel_second(key, part):
    key = jax.random.fold_in(key, 12)
    factor = jnp.exp(jax.random.uniform(key, (HEADS, REL), jnp.float32, math.log(0.5), math.log(2.0)))
    spread = bias_spread()
    return factor * 0.001 * (spread * spread)[None, :]


def place_ends(drawn, stream_key, low, high):
    place = [jax.random.randint(jax.random.fold_in(stream_key, axis), (), 0, length) for axis, length in enumerate(drawn.shape)]
    longest = drawn.shape.index(max(drawn.shape))
    neighbour = place[:longest] + [(place[longest] + 1) % drawn.shape[longest]] + place[longest + 1:]
    return drawn.at[tuple(place)].set(low).at[tuple(neighbour)].set(high)


def level_of(rng, shape, split, smallest, top_value):
    level = 1.0
    for dim, blocks in split:
        steps = jax.random.uniform(jax.random.fold_in(jax.random.fold_in(rng, 6), dim), (blocks,), jnp.float32, smallest / len(split), top_value / len(split))
        level = level * jnp.repeat(jnp.exp(steps), shape[dim] // blocks).reshape((-1,) + (1,) * (len(shape) - 1 - dim))
    return level


def scatter_about(own_key, extent, scale, limit, shards=(), kind=jnp.bfloat16):
    drawn = jax.random.normal(own_key, extent, jnp.float32) * scale
    if len(shards) > 0:
        drawn = level_of(own_key, extent, shards, -0.22, 0.18) * drawn
    return jnp.clip(drawn, min=-limit, max=limit).astype(kind)


def setup_inputs(seed: int = 0) -> dict:
    key_list = jax.random.split(jax.random.key(seed), 18)
    return {
        "latents": scatter_about(key_list[0], (IMAGES, SEQ, PDIM), 1.0, 6.0, ((0, 32),), jnp.float32),
        "noise": scatter_about(key_list[1], (IMAGES, SEQ, PDIM), 1.0, 6.0, ((0, 32),), jnp.float32),
        "timesteps": place_ends(jax.random.randint(key_list[2], (IMAGES,), 0, NSTEPS), jax.random.fold_in(key_list[2], 1), 0, NSTEPS - 1).astype(jnp.int32),
        "labels": place_ends(jax.random.randint(key_list[3], (IMAGES,), 0, NCLASS), jax.random.fold_in(key_list[3], 1), 0, NCLASS - 1).astype(jnp.int32),
        "drops": place_ends((jax.random.randint(key_list[4], (IMAGES,), 0, 10) < 1).astype(jnp.int32), jax.random.fold_in(key_list[4], 1), 0, 1),
        "block_weights": scatter_about(key_list[5], (D, 4 * D + 2 * MLPW), D ** -0.5, 0.1875, ((0, 16),), jnp.float32),
        "block_first": scatter_about(key_list[6], (D, 4 * D + 2 * MLPW), (0.0055 / NPARAM ** 0.5), 5.7220458984375e-06, ((0, 16),), jnp.float32),
        "block_second": jnp.clip(jnp.exp(math.log(3.4048940967049135e-13) - 1.3862944 * jax.random.uniform(key_list[7], (D, 4 * D + 2 * MLPW), jnp.float32) ** level_of(key_list[7], (D, 4 * D + 2 * MLPW), ((0, 16),), -0.2, 0.2)), 8.512235241762284e-14, 3.4048940967049135e-13),
        "mod_weights": scatter_about(key_list[8], (D, 8 * D), D ** -0.5, 0.1875, ((0, 16), (1, 2)), jnp.float32),
        "mod_first": scatter_about(key_list[9], (D, 8 * D), (0.0055 / NPARAM ** 0.5), 5.7220458984375e-06, ((0, 16), (1, 2)), jnp.float32),
        "mod_second": jnp.clip(jnp.exp(math.log(3.4048940967049135e-13) - 1.3862944 * jax.random.uniform(key_list[10], (D, 8 * D), jnp.float32) ** level_of(key_list[10], (D, 8 * D), ((0, 16), (1, 2)), -0.2, 0.2)), 8.512235241762284e-14, 3.4048940967049135e-13),
        "embed_weights": scatter_about(key_list[11], (EROWS, D), FREQ ** -0.5, 0.375, ((1, 16),), jnp.float32),
        "embed_first": scatter_about(key_list[12], (EROWS, D), (0.0055 / NPARAM ** 0.5), 5.7220458984375e-06, ((1, 16),), jnp.float32),
        "embed_second": jnp.clip(jnp.exp(math.log(3.4048940967049135e-13) - 1.3862944 * jax.random.uniform(key_list[13], (EROWS, D), jnp.float32) ** level_of(key_list[13], (EROWS, D), ((1, 16),), -0.2, 0.2)), 8.512235241762284e-14, 3.4048940967049135e-13),
        "rel_bias": scatter_about(key_list[14], (HEADS, REL), 0.5, 3.0, (), jnp.float32),
        "rel_first": draw_rel_first(jax.random.fold_in(key_list[17], 71), 0),
        "rel_second": draw_rel_second(jax.random.fold_in(key_list[17], 71), 0),
    }


@jax.custom_vjp
def low(v):
    return lax.optimization_barrier(v.astype(jnp.bfloat16)).astype(jnp.float32)

@jax.custom_vjp
def low_back(v):
    return v

def low_keep(v):
    return (low(v), None)

def low_pass(kept, grad):
    return (grad,)

def back_keep(v):
    return (v, None)

def back_low(kept, grad):
    return (low(grad),)
low.defvjp(low_keep, low_pass)
low_back.defvjp(back_keep, back_low)
FIRST_DECAY = 0.9
SECOND_DECAY = 0.999
ADAM_EPSILON = 1e-08
WEIGHT_DECAY = 0.01
LEARN_RATE = 0.25
CLIP_NORM = 0.05
HIGH = lax.Precision.HIGHEST

def matmul_high(left, right):
    return jnp.dot(left, right, precision=HIGH, preferred_element_type=jnp.float32)

def layer_norm(values):
    center = values - lax.optimization_barrier(jnp.mean(values, -1, keepdims=True))
    return center * lax.rsqrt(lax.optimization_barrier(jnp.mean(center * center, -1, keepdims=True)) + 1e-06)

def plan_table():
    betas = jnp.linspace(0.0001, 0.02, NSTEPS, dtype=jnp.float32)
    return jnp.exp(jnp.cumsum(jnp.log(1.0 - betas)))

def sinusoid(steps):
    half_width = FREQ // 2
    freqs = jnp.exp(-math.log(10000.0) * jnp.arange(half_width, dtype=jnp.float32) / half_width)
    angles = steps.astype(jnp.float32)[:, None] * freqs[None, :]
    return jnp.concatenate([jnp.cos(angles), jnp.sin(angles)], 1)

def relative_index():
    places = jnp.arange(GRID * GRID, dtype=jnp.int32)
    rows_of = places // GRID
    cols_of = places % GRID
    offset = (rows_of[:, None] - rows_of[None, :] + GRID - 1) * (2 * GRID - 1)
    return (offset + cols_of[:, None] - cols_of[None, :] + GRID - 1).astype(jnp.int32)

def image_loss(weights, sample):
    block, modw, embed, relative = weights
    latent, noisy, tstep, label, dropped = sample
    start = NCLASS + 1
    table = embed[:start]
    time_in = embed[start:start + FREQ]
    time_out = embed[start + FREQ:start + FREQ + D]
    patch = embed[start + FREQ + D:start + FREQ + D + PDIM]
    head = embed[start + FREQ + D + PDIM:]
    chosen = jnp.where(dropped == 1, NCLASS, label).astype(jnp.int32)
    sinus = sinusoid(tstep[None])
    cond = matmul_high(jax.nn.silu(matmul_high(sinus, time_in)), time_out) + table[chosen][None, :]
    scaled = low(jax.nn.silu(cond))
    modulation = low_back(matmul_high(scaled, modw)).reshape(8, D)
    alpha_bar = plan_table()[tstep]
    mixed = low(jnp.sqrt(alpha_bar) * latent + jnp.sqrt(1.0 - alpha_bar) * noisy)
    hidden0 = low_back(matmul_high(mixed, patch))
    attn_in = low(layer_norm(hidden0) * (1.0 + modulation[1]) + modulation[0])
    qkv = low_back(low(matmul_high(attn_in, block[:, :3 * D]))).reshape(SEQ, 3, HEADS, HD)
    scores = jnp.einsum('qhd,khd->hqk', qkv[:, 0], qkv[:, 1], precision=HIGH) * HD ** (-0.5)
    scores = low_back(scores + relative[:, relative_index()])
    probs = low(jax.nn.softmax(scores, -1))
    attn_out = jnp.einsum('hqk,khd->qhd', probs, qkv[:, 2], precision=HIGH).reshape(SEQ, D)
    attn_out = low_back(low(attn_out))
    branch_one = low_back(matmul_high(attn_out, block[:, 3 * D:4 * D]))
    hidden1 = hidden0 + modulation[2] * branch_one
    mlp_in = low(layer_norm(hidden1) * (1.0 + modulation[4]) + modulation[3])
    pre_act = low_back(matmul_high(mlp_in, block[:, 4 * D:4 * D + MLPW]))
    act = low(jax.nn.gelu(pre_act, approximate=True))
    branch_two = low_back(matmul_high(act, block[:, 4 * D + MLPW:].T))
    hidden2 = hidden1 + modulation[5] * branch_two
    final_in = low(layer_norm(hidden2) * (1.0 + modulation[7]) + modulation[6])
    predicted = low_back(matmul_high(final_in, head.T))
    return jnp.sum((predicted - noisy) ** 2)

def total_loss(weights, latents, noise, timesteps, labels, drops):
    rounded = (low(weights[0]), low(weights[1]), low(weights[2]), weights[3])
    single = jax.checkpoint(lambda sample: image_loss(rounded, sample))

    def accumulate(carry, sample):
        return (carry + single(sample), None)
    total, unused = lax.scan(accumulate, jnp.zeros((), jnp.float32), (latents, noise, timesteps, labels, drops))
    return total

def segment_ids():
    block_ids = np.concatenate([np.full(3 * D, 0), np.full(D, 1), np.full(MLPW, 2), np.full(MLPW, 3)])
    mod_ids = np.concatenate([np.full(6 * D, 4), np.full(2 * D, 5)])
    embed_ids = np.concatenate([np.full(NCLASS + 1, 6), np.full(FREQ, 7), np.full(D, 8), np.full(PDIM, 9), np.full(PDIM, 10)])
    return (jnp.asarray(block_ids.astype(np.int32)), jnp.asarray(mod_ids.astype(np.int32)), jnp.asarray(embed_ids.astype(np.int32)))

def squares(parts, ids):
    block, modw, embed, relative = parts
    total = jax.ops.segment_sum(lax.optimization_barrier(jnp.sum(block * block, 0)), ids[0], 12)
    total = total + jax.ops.segment_sum(lax.optimization_barrier(jnp.sum(modw * modw, 0)), ids[1], 12)
    total = total + jax.ops.segment_sum(lax.optimization_barrier(jnp.sum(embed * embed, 1)), ids[2], 12)
    return total + jnp.zeros((12,), jnp.float32).at[11].set(jnp.sum(relative * relative))

def reference(latents, noise, timesteps, labels, drops, block_weights, block_first, block_second, mod_weights, mod_first, mod_second, embed_weights, embed_first, embed_second, rel_bias, rel_first, rel_second):
    weights = (block_weights, mod_weights, embed_weights, rel_bias)
    loss_sum, pull = jax.vjp(lambda params: total_loss(params, latents, noise, timesteps, labels, drops), weights)
    count = latents.shape[0] * latents.shape[1] * latents.shape[2]
    grads = pull(jnp.asarray(1.0 / count, dtype=jnp.float32))[0]
    ids = segment_ids()
    grad_norm = jnp.sqrt(jnp.sum(squares(grads, ids)))
    clip = jnp.minimum(1.0, CLIP_NORM / grad_norm)
    firsts = (block_first, mod_first, embed_first, rel_first)
    seconds = (block_second, mod_second, embed_second, rel_second)
    new_first = tuple((FIRST_DECAY * m + (1.0 - FIRST_DECAY) * (g * clip) for m, g in zip(firsts, grads)))
    new_second = tuple((SECOND_DECAY * s + (1.0 - SECOND_DECAY) * (g * clip) ** 2 for s, g in zip(seconds, grads)))
    updates = tuple((m / (1.0 - FIRST_DECAY ** STEP) / (jnp.sqrt(s / (1.0 - SECOND_DECAY ** STEP)) + ADAM_EPSILON) + WEIGHT_DECAY * w for m, s, w in zip(new_first, new_second, weights)))
    weight_norm = jnp.sqrt(squares(weights, ids))
    update_norm = jnp.sqrt(squares(updates, ids))
    ratio = weight_norm / update_norm
    block_new = block_weights - LEARN_RATE * ratio[ids[0]][None, :] * updates[0]
    mod_new = mod_weights - LEARN_RATE * ratio[ids[1]][None, :] * updates[1]
    embed_new = embed_weights - LEARN_RATE * ratio[ids[2]][:, None] * updates[2]
    rel_new = rel_bias - LEARN_RATE * ratio[11] * updates[3]
    matrix_norms = jnp.stack([weight_norm, update_norm])
    return (loss_sum, grad_norm, matrix_norms, block_new, new_first[0], new_second[0], block_new.astype(jnp.bfloat16), mod_new, new_first[1], new_second[1], mod_new.astype(jnp.bfloat16), embed_new, new_first[2], new_second[2], embed_new.astype(jnp.bfloat16), rel_new, new_first[3], new_second[3], rel_new.astype(jnp.bfloat16), grads[3] * clip)
```

```python
import functools
import math

import jax
import jax.numpy as jnp
from jax import lax
from jax.experimental import pallas as pl
from jax.experimental.pallas import tpu as pltpu
from jax.sharding import PartitionSpec as P

D = 1152
HEADS = 16
HD = 72
MLPW = 4608
NCLASS = 1000
FREQ = 256
GRID = 16
PDIM = 16
NSTEPS = 1000
STEP = 10
SIDE = 2 * GRID - 1
QKV_HALF = 3 * D // 2
QKV_PAD = -(-QKV_HALF // 128) * 128
SPREAD = 2 * GRID * GRID


FIRST_DECAY = 0.9
SECOND_DECAY = 0.999
ADAM_EPSILON = 1e-08
WEIGHT_DECAY = 0.01
LEARN_RATE = 0.25
CLIP_NORM = 0.05
HIGH = lax.Precision.HIGHEST


def dense(left, right):
    return jnp.dot(left, right, preferred_element_type=jnp.float32)


def dense_trans(left, right):
    return lax.dot_general(
        left, right, (((left.ndim - 1,), (1,)), ((), ())), preferred_element_type=jnp.float32
    )


def outer_sum(left, right):
    flat_left = left.reshape(-1, left.shape[-1])
    flat_right = right.reshape(-1, right.shape[-1])
    return lax.dot_general(
        flat_left, flat_right, (((0,), (0,)), ((), ())), preferred_element_type=jnp.float32
    )


def first_contract(left, right):
    return lax.dot_general(
        left, right, (((0,), (0,)), ((), ())), precision=HIGH, preferred_element_type=jnp.float32
    )


def layer_norm(values):
    center = values - jnp.mean(values, -1, keepdims=True)
    inverse = lax.rsqrt(jnp.mean(center * center, -1, keepdims=True) + 1e-06)
    return (center * inverse, inverse)


def norm_back(upstream, normed, inverse):
    return inverse * (
        upstream
        - jnp.mean(upstream, -1, keepdims=True)
        - normed * jnp.mean(upstream * normed, -1, keepdims=True)
    )


def silu_slope(values):
    sigma = jax.nn.sigmoid(values)
    return sigma * (1.0 + values * (1.0 - sigma))


def plan_table():
    betas = jnp.linspace(0.0001, 0.02, NSTEPS, dtype=jnp.float32)
    return jnp.exp(jnp.cumsum(jnp.log(1.0 - betas)))


def sinusoid(steps):
    half_width = FREQ // 2
    freqs = jnp.exp(-math.log(10000.0) * jnp.arange(half_width, dtype=jnp.float32) / half_width)
    angles = steps.astype(jnp.float32)[:, None] * freqs[None, :]
    return jnp.concatenate([jnp.cos(angles), jnp.sin(angles)], 1)


def dp_peers(mask):
    spread, pair = lax.axis_size("dp"), lax.axis_size("mod")
    return [(i * pair + c, (i ^ mask) * pair + c) for i in range(spread) for c in range(pair)]


def plane_peers(masks):
    spread, pair = lax.axis_size("dp"), lax.axis_size("mod")
    return [(i * pair + c, (i ^ masks[c]) * pair + c) for i in range(spread) for c in range(pair)]


def send(values, peers):
    return lax.ppermute(values, ("dp", "mod"), peers)


def swap_cores(values):
    return lax.ppermute(values, "mod", [(0, 1), (1, 0)])


def far_groups():
    spread = lax.axis_size("dp")
    bits = [1 << k for k in range(2, spread.bit_length() - 1)]
    if len(bits) == 2:
        return [[bits[0], bits[1], bits[0] | bits[1]]]
    return [[bit] for bit in bits]


def far_masks():
    masks = [0]
    for group in far_groups():
        masks = masks + [mask | have for mask in group for have in masks]
    return masks


def block_places():
    me, core = lax.axis_index("dp"), lax.axis_index("mod")
    second = jnp.where(core == 0, 1, 2)
    third = jnp.where(core == 0, 2, 1)
    far = jnp.array(far_masks(), jnp.int32)
    near = jnp.stack([jnp.zeros_like(second), second, third, second | third])
    return (me ^ (near[:, None] | far[None, :])).reshape(-1).astype(jnp.int32)


def place_kernel(counts, places, *refs):
    ins, out, sems = (refs[: len(counts)], refs[len(counts)], refs[len(counts) + 1])
    copies = []
    for part, count in enumerate(counts):
        for row in range(count):
            at = len(copies)
            copies.append(
                pltpu.make_async_copy(ins[part].at[row], out.at[places[at]], sems.at[at])
            )
            copies[-1].start()
    for copy in copies:
        copy.wait()


def pick_kernel(counts, places, source, *refs):
    outs, sems = (refs[: len(counts)], refs[len(counts)])
    copies = []
    for part, count in enumerate(counts):
        for row in range(count):
            at = len(copies)
            copies.append(
                pltpu.make_async_copy(source.at[places[at]], outs[part].at[row], sems.at[at])
            )
            copies[-1].start()
    for copy in copies:
        copy.wait()


def place_blocks(parts, places):
    counts = [part.shape[0] for part in parts]
    total = sum(counts)
    return pl.pallas_call(
        functools.partial(place_kernel, counts),
        grid_spec=pltpu.PrefetchScalarGridSpec(
            num_scalar_prefetch=1,
            grid=(1,),
            in_specs=[pl.BlockSpec(memory_space=pl.ANY)] * len(parts),
            out_specs=pl.BlockSpec(memory_space=pl.ANY),
            scratch_shapes=[pltpu.SemaphoreType.DMA((total,))],
        ),
        out_shape=jax.ShapeDtypeStruct((total,) + parts[0].shape[1:], parts[0].dtype),
        name="place_blocks",
    )(places, *parts)


def pick_blocks(values, places):
    total = values.shape[0]
    counts = [total // 4] * 4
    return pl.pallas_call(
        functools.partial(pick_kernel, counts),
        grid_spec=pltpu.PrefetchScalarGridSpec(
            num_scalar_prefetch=1,
            grid=(1,),
            in_specs=[pl.BlockSpec(memory_space=pl.ANY)],
            out_specs=[pl.BlockSpec(memory_space=pl.ANY)] * 4,
            scratch_shapes=[pltpu.SemaphoreType.DMA((total,))],
        ),
        out_shape=[
            jax.ShapeDtypeStruct((count,) + values.shape[1:], values.dtype) for count in counts
        ],
        name="pick_blocks",
    )(places, values)


def gather_blocks(block, places):
    stack = block[None]
    for group in far_groups():
        stack = jnp.concatenate([stack] + [send(stack, dp_peers(mask)) for mask in group], 0)
    second = send(stack, plane_peers((1, 2)))
    third = send(stack, plane_peers((2, 1)))
    both = send(second, plane_peers((2, 1)))
    return place_blocks([stack, second, third, both], places)


def scatter_blocks(values, places):
    kind = values.dtype
    wide = jnp.float32
    own, second, third, both = pick_blocks(values, places)
    from_both = send(both, plane_peers((2, 1)))
    from_third = send(third, plane_peers((2, 1)))
    second = (second.astype(wide) + from_both.astype(wide)).astype(kind)
    from_second = send(second, plane_peers((1, 2)))
    own = (own.astype(wide) + from_third.astype(wide) + from_second.astype(wide)).astype(kind)
    for group in reversed(far_groups()):
        count = own.shape[0] // (len(group) + 1)
        total = own[:count].astype(wide)
        for pos, mask in enumerate(group):
            total = total + send(
                own[(pos + 1) * count : (pos + 2) * count], dp_peers(mask)
            ).astype(wide)
        own = total if count == 1 else total.astype(kind)
    return own[0].astype(wide)


def all_sum(values):
    values = values + swap_cores(values)
    return dp_sum(values)


def dp_sum(values):
    for bit in range(lax.axis_size("dp").bit_length() - 1):
        values = values + send(values, dp_peers(1 << bit))
    return values


def product(left, right, dims):
    return lax.dot_general(left, right, (dims, ((), ())), preferred_element_type=jnp.float32)


def fill_bias(spread_ref, bias):
    tokens = GRID * GRID
    for head in range(bias.shape[0]):
        spread = spread_ref[head]
        for row in range(GRID):
            off = (GRID - 1 - row) * GRID
            moved = spread if off == 0 else pltpu.roll(spread, SPREAD - off, 1)
            bias[head, row * GRID : (row + 1) * GRID, :] = moved[:, :tokens]


def head_slices(values, head, heads):
    width = heads * HD
    return [
        values[:, part * width + head * HD : part * width + (head + 1) * HD] for part in range(3)
    ]


def attention_kernel(heads, qkv_ref, spread_ref, out_ref, log_ref, bias):
    @pl.when(pl.program_id(0) == 0)
    def _():
        fill_bias(spread_ref, bias)

    values = qkv_ref[...]
    outs, logs = ([], [])
    for head in range(heads):
        query, key, value = head_slices(values, head, heads)
        scores = product(query, key, ((1,), (1,))) * HD ** (-0.5) + bias[head]
        top = jnp.max(scores, -1, keepdims=True)
        powers = jnp.exp(scores - top)
        total = jnp.sum(powers, -1, keepdims=True)
        probs = (powers * (1.0 / total)).astype(jnp.bfloat16)
        outs.append(product(probs, value, ((1,), (0,))).astype(jnp.bfloat16))
        logs.append(top + jnp.log(total))
    out_ref[...] = jnp.concatenate(outs, 1)
    log_ref[...] = jnp.concatenate(logs, 1)


def attention(qkv, spread):
    rows, columns = qkv.shape
    heads = spread.shape[0]
    tokens = GRID * GRID
    return pl.pallas_call(
        functools.partial(attention_kernel, heads),
        grid=(rows // tokens,),
        in_specs=[
            pl.BlockSpec((tokens, columns), lambda step: (step, 0)),
            pl.BlockSpec(spread.shape, lambda step: (0, 0, 0)),
        ],
        out_specs=[
            pl.BlockSpec((tokens, heads * HD), lambda step: (step, 0)),
            pl.BlockSpec((tokens, heads), lambda step: (step, 0)),
        ],
        out_shape=[
            jax.ShapeDtypeStruct((rows, heads * HD), jnp.bfloat16),
            jax.ShapeDtypeStruct((rows, heads), jnp.float32),
        ],
        scratch_shapes=[pltpu.VMEM((heads, tokens, tokens), jnp.float32)],
        compiler_params=pltpu.CompilerParams(vmem_limit_bytes=48 << 20),
        cost_estimate=pl.CostEstimate(
            flops=4 * rows * tokens * heads * 256,
            bytes_accessed=rows * columns * 4,
            transcendentals=rows * tokens * heads,
        ),
        name="attention",
    )(qkv, spread)


def attention_back_kernel(
    heads, qkv_ref, upstream_ref, log_ref, spread_ref, d_qkv_ref, d_spread_ref, bias, d_bias
):
    tokens = GRID * GRID

    @pl.when(pl.program_id(0) == 0)
    def _():
        fill_bias(spread_ref, bias)
        d_bias[...] = jnp.zeros_like(d_bias)

    values, upstream, logs = (qkv_ref[...], upstream_ref[...], log_ref[...])
    d_query, d_key, d_value = ([], [], [])
    for head in range(heads):
        query, key, value = head_slices(values, head, heads)
        d_out = upstream[:, head * HD : (head + 1) * HD]
        scores = product(query, key, ((1,), (1,))) * HD ** (-0.5) + bias[head]
        probs = jnp.exp(scores - logs[:, head : head + 1])
        d_probs = product(d_out, value, ((1,), (1,)))
        d_scores = probs * (d_probs - jnp.sum(probs * d_probs, -1, keepdims=True))
        d_scores = d_scores.astype(jnp.bfloat16)
        d_bias[head] += d_scores.astype(jnp.float32)
        d_query.append((product(d_scores, key, ((1,), (0,))) * HD ** (-0.5)).astype(jnp.bfloat16))
        d_key.append((product(d_scores, query, ((0,), (0,))) * HD ** (-0.5)).astype(jnp.bfloat16))
        d_value.append(
            product(probs.astype(jnp.bfloat16), d_out, ((0,), (0,))).astype(jnp.bfloat16)
        )
    pieces = d_query + d_key + d_value
    spare = d_qkv_ref.shape[1] - 3 * heads * HD
    if spare:
        pieces = pieces + [jnp.zeros((tokens, spare), jnp.bfloat16)]
    d_qkv_ref[...] = jnp.concatenate(pieces, 1)

    @pl.when(pl.program_id(0) == pl.num_programs(0) - 1)
    def _():
        for head in range(heads):
            total = jnp.zeros((GRID, SPREAD), jnp.float32)
            for row in range(GRID):
                off = (GRID - 1 - row) * GRID
                rows = d_bias[head, row * GRID : (row + 1) * GRID, :]
                wide = jnp.concatenate([rows, jnp.zeros((GRID, SPREAD - tokens), jnp.float32)], 1)
                total += wide if off == 0 else pltpu.roll(wide, off, 1)
            d_spread_ref[head] = total


def attention_back(qkv, upstream, logs, spread):
    rows, columns = qkv.shape
    heads = spread.shape[0]
    tokens = GRID * GRID
    return pl.pallas_call(
        functools.partial(attention_back_kernel, heads),
        grid=(rows // tokens,),
        in_specs=[
            pl.BlockSpec((tokens, columns), lambda step: (step, 0)),
            pl.BlockSpec((tokens, heads * HD), lambda step: (step, 0)),
            pl.BlockSpec((tokens, heads), lambda step: (step, 0)),
            pl.BlockSpec(spread.shape, lambda step: (0, 0, 0)),
        ],
        out_specs=[
            pl.BlockSpec((tokens, columns), lambda step: (step, 0)),
            pl.BlockSpec(spread.shape, lambda step: (0, 0, 0)),
        ],
        out_shape=[
            jax.ShapeDtypeStruct((rows, columns), jnp.bfloat16),
            jax.ShapeDtypeStruct(spread.shape, jnp.float32),
        ],
        scratch_shapes=[pltpu.VMEM((heads, tokens, tokens), jnp.float32)] * 2,
        compiler_params=pltpu.CompilerParams(vmem_limit_bytes=48 << 20),
        cost_estimate=pl.CostEstimate(
            flops=10 * rows * tokens * heads * 256,
            bytes_accessed=rows * columns * 6,
            transcendentals=rows * tokens * heads,
        ),
        name="attention_back",
    )(qkv, upstream, logs, spread)


def spread_bias(relative):
    turned = relative.reshape(-1, SIDE, SIDE)[:, ::-1, ::-1]
    rows = [turned[:, :, GRID - 1 - row : SIDE - row] for row in range(GRID)]
    spread = jnp.stack(rows, 1).reshape(-1, GRID, SIDE * GRID)
    return jnp.pad(spread, ((0, 0), (0, 0), (0, SPREAD - SIDE * GRID)))


def gather_bias(d_spread):
    parts = d_spread[:, :, : SIDE * GRID].reshape(-1, GRID, SIDE, GRID)
    total = sum(
        jnp.pad(parts[:, row], ((0, 0), (0, 0), (GRID - 1 - row, row))) for row in range(GRID)
    )
    return total[:, ::-1, ::-1].reshape(-1, SIDE * SIDE)


def core_half(values, core, starts, width):
    return [
        jnp.where(
            core == 0,
            values[:, start : start + width],
            values[:, start + width : start + 2 * width],
        )
        for start in starts
    ]


def both_cores(mine, other, core, axis):
    return jnp.where(
        core == 0,
        jnp.concatenate([mine, other], axis),
        jnp.concatenate([other, mine], axis),
    )


def part_squares(block_part, mod_part, embed_part, first_core, core_index):
    column_sq = jnp.sum(block_part * block_part, 0)
    block_terms = [
        jnp.sum(column_sq[: 3 * D]),
        jnp.sum(column_sq[3 * D : 4 * D]),
        jnp.sum(column_sq[4 * D : 4 * D + MLPW]),
        jnp.sum(column_sq[4 * D + MLPW :]),
    ]
    mod_sq = jnp.sum(mod_part * mod_part, 0)
    global_cols = core_index * mod_part.shape[1] + jnp.arange(mod_part.shape[1], dtype=jnp.int32)
    first_mod = jnp.sum(jnp.where(global_cols < 6 * D, mod_sq, 0.0))
    second_mod = jnp.sum(jnp.where(global_cols < 6 * D, 0.0, mod_sq))
    row_sq = jnp.sum(embed_part * embed_part, 1)
    bounds = [
        0,
        NCLASS + 1,
        NCLASS + 1 + FREQ,
        NCLASS + 1 + FREQ + D,
        NCLASS + 1 + FREQ + D + PDIM,
        NCLASS + 1 + FREQ + D + 2 * PDIM,
    ]
    embed_terms = [jnp.sum(row_sq[bounds[pos] : bounds[pos + 1]]) for pos in range(5)]
    replicated = jnp.stack(block_terms + embed_terms) * first_core
    return jnp.concatenate([replicated[:4], jnp.stack([first_mod, second_mod]), replicated[4:]])


def adam_update(grad, first, second, weight, clip):
    first_new = FIRST_DECAY * first + (1.0 - FIRST_DECAY) * (grad * clip)
    second_new = SECOND_DECAY * second + (1.0 - SECOND_DECAY) * (grad * clip) ** 2
    update = (
        first_new
        / (1.0 - FIRST_DECAY**STEP)
        / (jnp.sqrt(second_new / (1.0 - SECOND_DECAY**STEP)) + ADAM_EPSILON)
        + WEIGHT_DECAY * weight
    )
    return (first_new, second_new, update)


def on_device(
    latents,
    noise,
    timesteps,
    labels,
    drops,
    block_weights,
    block_first,
    block_second,
    mod_weights,
    mod_first,
    mod_second,
    embed_weights,
    embed_first,
    embed_second,
    rel_bias,
    rel_first,
    rel_second,
):
    low = jnp.bfloat16
    wide = jnp.float32
    core = lax.axis_index("mod")
    spread = lax.axis_size("dp")
    images = latents.shape[0]
    length = latents.shape[1]
    rows = images * length
    share = embed_weights.shape[1]
    count = float(images * spread * lax.axis_size("mod") * length * latents.shape[2])
    places = block_places()

    half = D // 2
    wide_half = MLPW // 2
    block_low = block_weights.astype(low)
    q_part, k_part, v_part, p_part = core_half(
        block_low, core, [0, D, 2 * D, 3 * D], half
    )
    in_part, out_part = core_half(block_low, core, [4 * D, 4 * D + MLPW], wide_half)
    pad_part = jnp.zeros((block_low.shape[0], QKV_PAD - QKV_HALF), low)
    attn_part = jnp.concatenate([q_part, k_part, v_part, pad_part, p_part], 1)

    start = NCLASS + 1
    chosen = jnp.where(drops == 1, NCLASS, labels)
    codes = jnp.stack([timesteps // 32, timesteps % 32, chosen // 32, chosen % 32], 1)
    codes = codes.astype(low)
    codes = both_cores(codes, swap_cores(codes), core, 0)
    code_rows = -(-codes.size // share)
    codes = jnp.pad(codes.reshape(-1), (0, code_rows * share - codes.size))
    embed_low = embed_weights.astype(low)
    table = embed_low[:start]
    time_out = embed_low[start + FREQ : start + FREQ + D].astype(wide)
    small = jnp.concatenate(
        [
            embed_low[start : start + FREQ],
            embed_low[start + FREQ + D :],
            codes.reshape(code_rows, share),
        ],
        0,
    )
    small = gather_blocks(small, places)
    everyone = small[:, FREQ + 2 * PDIM :].reshape(spread, -1)[:, : 2 * images * 4]
    everyone = everyone.reshape(spread * 2 * images, 4).astype(wide)
    all_steps = 32.0 * everyone[:, 0] + everyone[:, 1]
    all_chosen = (32.0 * everyone[:, 2] + everyone[:, 3]).astype(jnp.int32)
    small = small[:, : FREQ + 2 * PDIM].transpose(1, 0, 2).reshape(FREQ + 2 * PDIM, D)
    time_in = small[:FREQ].astype(wide)
    patch = small[FREQ : FREQ + PDIM]
    head = small[FREQ + PDIM :]

    attn_low = gather_blocks(attn_part, places).reshape(D, -1)
    in_low = gather_blocks(in_part, places).reshape(D, -1)
    out_low = gather_blocks(out_part, places).reshape(D, -1)
    qkv_low = attn_low[:, :QKV_PAD]
    proj_half = attn_low[:, QKV_PAD:]
    proj_low = both_cores(proj_half, swap_cores(proj_half), core, 1)

    sinus = sinusoid(all_steps)
    pre_time = jnp.dot(sinus, time_in, precision=HIGH, preferred_element_type=wide)
    time_act = jax.nn.silu(pre_time)
    onehot = all_chosen[:, None] == jnp.arange(start, dtype=jnp.int32)[None, :]
    cond = jnp.dot(time_act, time_out, precision=HIGH, preferred_element_type=wide) + dense(
        onehot.astype(low), table
    )
    scaled = jax.nn.silu(cond).astype(low)
    mod_low = mod_weights.astype(low)
    mod_partial = dense(scaled, mod_low).astype(low)
    half_mod = scatter_blocks(mod_partial.reshape(spread, 2 * images, -1), places)
    mine = jnp.where(core == 0, half_mod[:images], half_mod[images:])
    theirs = jnp.where(core == 0, half_mod[images:], half_mod[:images])
    modulation = both_cores(mine, swap_cores(theirs), core, 1).reshape(images, 8, D)

    def moved(normed, shift):
        return (
            normed * (1.0 + modulation[:, shift + 1 : shift + 2]) + modulation[:, shift : shift + 1]
        ).astype(low)

    def with_sibling(values):
        flat = values.reshape(rows, -1)
        return jnp.concatenate([flat, swap_cores(flat)], 0)

    def sum_cores(partial):
        return (partial[:rows] + swap_cores(partial[rows:].astype(low)).astype(wide)).reshape(
            images, length, -1
        )

    alpha_bar = jnp.sum(
        jnp.where(
            timesteps[:, None] == jnp.arange(NSTEPS, dtype=jnp.int32)[None, :],
            plan_table()[None, :],
            0.0,
        ),
        1,
    )
    mixed = (
        jnp.sqrt(alpha_bar)[:, None, None] * latents
        + jnp.sqrt(1.0 - alpha_bar)[:, None, None] * noise
    ).astype(low)
    hidden0 = dense(mixed, patch)
    normed1, inverse1 = layer_norm(hidden0)
    attn_in = with_sibling(moved(normed1, 0))
    qkv = dense(attn_in, qkv_low).astype(low)
    heads = HEADS // 2
    bias_rows = spread_bias(jnp.where(core == 0, rel_bias[:heads], rel_bias[heads:]))
    heads_out, logs = attention(qkv, bias_rows)
    attn_out = both_cores(heads_out[:rows], swap_cores(heads_out[rows:]), core, 1)
    branch_one = dense(attn_out, proj_low).reshape(images, length, D)
    hidden1 = hidden0 + modulation[:, 2:3] * branch_one
    normed2, inverse2 = layer_norm(hidden1)
    mlp_in = with_sibling(moved(normed2, 3))
    pre_act = dense(mlp_in, in_low)
    act = jax.nn.gelu(pre_act, approximate=True).astype(low)
    branch_two = sum_cores(dense_trans(act, out_low))
    hidden2 = hidden1 + modulation[:, 5:6] * branch_two

    normed3, inverse3 = layer_norm(hidden2)
    final_in = moved(normed3, 6)
    predicted = dense_trans(final_in, head)
    error = predicted - noise
    loss_here = jnp.sum(error * error)
    d_predicted = (error * (2.0 / count)).astype(low)
    d_final = dense(d_predicted, head)
    g_head = outer_sum(d_predicted, final_in)
    d_scale3 = jnp.sum(d_final * normed3, 1)
    d_shift3 = jnp.sum(d_final, 1)
    d_hidden2 = norm_back(d_final * (1.0 + modulation[:, 7:8]), normed3, inverse3)

    d_branch_two = with_sibling((modulation[:, 5:6] * d_hidden2).astype(low))
    d_gate2 = jnp.sum(d_hidden2 * branch_two, 1)
    d_act = dense(d_branch_two, out_low)
    gelu_pull = jax.vjp(lambda entries: jax.nn.gelu(entries, approximate=True), pre_act)[1]
    d_pre = gelu_pull(d_act)[0].astype(low)
    g_out = scatter_blocks(
        outer_sum(d_branch_two, act).astype(low).reshape(spread, -1, wide_half), places
    )
    d_mlp_in = sum_cores(dense_trans(d_pre, in_low))
    g_in = scatter_blocks(
        outer_sum(mlp_in, d_pre).astype(low).reshape(spread, -1, wide_half), places
    )
    d_scale2 = jnp.sum(d_mlp_in * normed2, 1)
    d_shift2 = jnp.sum(d_mlp_in, 1)
    d_hidden1 = d_hidden2 + norm_back(d_mlp_in * (1.0 + modulation[:, 4:5]), normed2, inverse2)
    d_branch_one = (modulation[:, 2:3] * d_hidden1).astype(low).reshape(rows, D)
    d_gate1 = jnp.sum(d_hidden1 * branch_one, 1)
    d_attn_out = dense_trans(d_branch_one, proj_low).astype(low)
    d_mine = jnp.where(core == 0, d_attn_out[:, :half], d_attn_out[:, half:])
    d_theirs = jnp.where(core == 0, d_attn_out[:, half:], d_attn_out[:, :half])
    d_heads = jnp.concatenate([d_mine, swap_cores(d_theirs)], 0)
    g_proj = outer_sum(attn_out, d_branch_one)
    g_proj_mine = jnp.where(core == 0, g_proj[:, :half], g_proj[:, half:])
    g_proj_theirs = jnp.where(core == 0, g_proj[:, half:], g_proj[:, :half]).astype(low)
    g_proj = (g_proj_mine + swap_cores(g_proj_theirs).astype(wide)).astype(low)
    d_qkv, d_spread = attention_back(qkv, d_heads, logs, bias_rows)
    d_attn_in = sum_cores(dense_trans(d_qkv, qkv_low))
    g_qkv = outer_sum(attn_in, d_qkv).astype(low)
    g_attn = scatter_blocks(
        jnp.concatenate([g_qkv, g_proj], 1).reshape(spread, -1, QKV_PAD + half), places
    )
    d_scale1 = jnp.sum(d_attn_in * normed1, 1)
    d_shift1 = jnp.sum(d_attn_in, 1)
    d_hidden0 = d_hidden1 + norm_back(d_attn_in * (1.0 + modulation[:, 1:2]), normed1, inverse1)
    g_patch = outer_sum(mixed, d_hidden0.astype(low))

    d_modulation = jnp.stack(
        [d_shift1, d_scale1, d_gate1, d_shift2, d_scale2, d_gate2, d_shift3, d_scale3], 1
    )
    d_modulation = d_modulation.reshape(images, 8 * D).astype(low)
    mod_half = 4 * D
    d_keep = jnp.where(core == 0, d_modulation[:, :mod_half], d_modulation[:, mod_half:])
    d_give = jnp.where(core == 0, d_modulation[:, mod_half:], d_modulation[:, :mod_half])
    d_pair = both_cores(d_keep, swap_cores(d_give), core, 0)
    d_all = gather_blocks(d_pair, places).reshape(spread * 2 * images, mod_half)
    mod_grad = outer_sum(scaled, d_all)
    d_scaled = dense_trans(d_all, mod_low)
    d_scaled = d_scaled + swap_cores(d_scaled)
    d_cond = d_scaled * silu_slope(cond)
    g_table = first_contract(onehot.astype(wide), d_cond)
    g_time_out = first_contract(time_act, d_cond)
    d_time = lax.dot_general(
        d_cond, time_out, (((1,), (1,)), ((), ())), precision=HIGH, preferred_element_type=wide
    )
    g_ends = jnp.concatenate([g_patch, g_head], 0)
    g_ends = g_ends + swap_cores(g_ends)
    tail = jnp.concatenate([d_time, g_ends], 0)
    tail = scatter_blocks(tail.reshape(-1, spread, share).transpose(1, 0, 2), places)
    d_time_here, g_ends = (tail[: -2 * PDIM], tail[-2 * PDIM :])
    first_column = lax.axis_index("dp") * share
    pre_time_here = lax.dynamic_slice_in_dim(pre_time, first_column, share, 1)
    g_time_in = first_contract(sinus, d_time_here * silu_slope(pre_time_here))
    embed_grad = jnp.concatenate([g_table, g_time_in, g_time_out, g_ends], 0)

    g_here = jnp.concatenate([g_attn, g_in, g_out], 1).astype(low)
    g_there = swap_cores(g_here)
    zero_part = jnp.where(core == 0, g_here, g_there).astype(wide)
    one_part = jnp.where(core == 0, g_there, g_here).astype(wide)
    bounds = [0, half, 2 * half, 3 * half, QKV_PAD, QKV_PAD + half]
    bounds = bounds + [bounds[-1] + wide_half, bounds[-1] + 2 * wide_half]
    pieces = []
    for low_end, high_end in zip(bounds[:-1], bounds[1:]):
        if (low_end, high_end) != (3 * half, QKV_PAD):
            pieces = pieces + [zero_part[:, low_end:high_end], one_part[:, low_end:high_end]]
    block_grad = jnp.concatenate(pieces, 1)

    rel_half = gather_bias(d_spread)
    packed = jnp.concatenate([rel_half.reshape(-1), (loss_here * jnp.ones(1, wide))])
    packed = dp_sum(packed)
    packed_other = swap_cores(packed)
    rel_grad = both_cores(
        packed[:-1].reshape(heads, -1), packed_other[:-1].reshape(heads, -1), core, 0
    )
    loss_sum = packed[-1] + packed_other[-1]

    first_core = (core == 0).astype(wide)
    grad_parts, weight_parts = jnp.split(
        all_sum(
            jnp.concatenate(
                [
                    part_squares(block_grad, mod_grad, embed_grad, first_core, core),
                    part_squares(block_weights, mod_weights, embed_weights, first_core, core),
                ]
            )
        ),
        2,
    )
    grad_sq = jnp.concatenate([grad_parts, jnp.sum(rel_grad * rel_grad)[None]])
    weight_sq = jnp.concatenate([weight_parts, jnp.sum(rel_bias * rel_bias)[None]])
    grad_norm = jnp.sqrt(jnp.sum(grad_sq))
    clip = jnp.minimum(1.0, CLIP_NORM / grad_norm)
    block_m, block_s, block_step = adam_update(
        block_grad, block_first, block_second, block_weights, clip
    )
    mod_m, mod_s, mod_step = adam_update(mod_grad, mod_first, mod_second, mod_weights, clip)
    embed_m, embed_s, embed_step = adam_update(
        embed_grad, embed_first, embed_second, embed_weights, clip
    )
    rel_m, rel_s, rel_step = adam_update(rel_grad, rel_first, rel_second, rel_bias, clip)
    update_parts = all_sum(part_squares(block_step, mod_step, embed_step, first_core, core))
    update_sq = jnp.concatenate([update_parts, jnp.sum(rel_step * rel_step)[None]])
    weight_norm = jnp.sqrt(weight_sq)
    update_norm = jnp.sqrt(update_sq)
    ratio = weight_norm / update_norm
    block_ratio = jnp.concatenate(
        [
            jnp.broadcast_to(ratio[0], (3 * D,)),
            jnp.broadcast_to(ratio[1], (D,)),
            jnp.broadcast_to(ratio[2], (MLPW,)),
            jnp.broadcast_to(ratio[3], (MLPW,)),
        ]
    )
    global_cols = core * mod_weights.shape[1] + jnp.arange(
        mod_weights.shape[1], dtype=jnp.int32
    )
    mod_ratio = jnp.where(global_cols < 6 * D, ratio[4], ratio[5])
    embed_ratio = jnp.concatenate(
        [
            jnp.broadcast_to(ratio[6], (NCLASS + 1,)),
            jnp.broadcast_to(ratio[7], (FREQ,)),
            jnp.broadcast_to(ratio[8], (D,)),
            jnp.broadcast_to(ratio[9], (PDIM,)),
            jnp.broadcast_to(ratio[10], (PDIM,)),
        ]
    )
    block_new = block_weights - LEARN_RATE * block_ratio[None, :] * block_step
    mod_new = mod_weights - LEARN_RATE * mod_ratio[None, :] * mod_step
    embed_new = embed_weights - LEARN_RATE * embed_ratio[:, None] * embed_step
    rel_new = rel_bias - LEARN_RATE * ratio[11] * rel_step
    matrix_norms = jnp.stack([weight_norm, update_norm])
    return (
        loss_sum,
        grad_norm,
        matrix_norms,
        block_new,
        block_m,
        block_s,
        block_new.astype(jnp.bfloat16),
        mod_new,
        mod_m,
        mod_s,
        mod_new.astype(jnp.bfloat16),
        embed_new,
        embed_m,
        embed_s,
        embed_new.astype(jnp.bfloat16),
        rel_new,
        rel_m,
        rel_s,
        rel_new.astype(jnp.bfloat16),
        rel_grad * clip,
    )


def solution(mesh):
    placed = (
        P(("dp", "mod"), None, None),
        P(("dp", "mod"), None, None),
        P(("dp", "mod")),
        P(("dp", "mod")),
        P(("dp", "mod")),
        P("dp", None),
        P("dp", None),
        P("dp", None),
        P("dp", "mod"),
        P("dp", "mod"),
        P("dp", "mod"),
        P(None, "dp"),
        P(None, "dp"),
        P(None, "dp"),
        P(),
        P(),
        P(),
    )
    return jax.shard_map(
        on_device,
        mesh=mesh,
        in_specs=placed,
        out_specs=(
            P(),
            P(),
            P(),
            P("dp", None),
            P("dp", None),
            P("dp", None),
            P("dp", None),
            P("dp", "mod"),
            P("dp", "mod"),
            P("dp", "mod"),
            P("dp", "mod"),
            P(None, "dp"),
            P(None, "dp"),
            P(None, "dp"),
            P(None, "dp"),
            P(),
            P(),
            P(),
            P(),
            P(),
        ),
        check_vma=False,
    )
```

```python
import functools
import math

import jax
import jax.numpy as jnp
from jax import lax
from jax.experimental import pallas as pl
from jax.experimental.pallas import tpu as pltpu
from jax.sharding import PartitionSpec as P

D = 1152
HEADS = 16
HD = 72
MLPW = 4608
NCLASS = 1000
FREQ = 256
GRID = 16
PDIM = 16
NSTEPS = 1000
STEP = 10
SIDE = 2 * GRID - 1
QKV_HALF = 3 * D // 2
QKV_PAD = -(-QKV_HALF // 128) * 128
SPREAD = 2 * GRID * GRID


FIRST_DECAY = 0.9
SECOND_DECAY = 0.999
ADAM_EPSILON = 1e-08
WEIGHT_DECAY = 0.01
LEARN_RATE = 0.25
CLIP_NORM = 0.05
HIGH = lax.Precision.HIGHEST


def dense(left, right):
    return jnp.dot(left, right, preferred_element_type=jnp.float32)


def dense_trans(left, right):
    return lax.dot_general(
        left, right, (((left.ndim - 1,), (1,)), ((), ())), preferred_element_type=jnp.float32
    )


def outer_sum(left, right):
    flat_left = left.reshape(-1, left.shape[-1])
    flat_right = right.reshape(-1, right.shape[-1])
    return lax.dot_general(
        flat_left, flat_right, (((0,), (0,)), ((), ())), preferred_element_type=jnp.float32
    )


def first_contract(left, right):
    return lax.dot_general(
        left, right, (((0,), (0,)), ((), ())), precision=HIGH, preferred_element_type=jnp.float32
    )


def layer_norm(values):
    center = values - jnp.mean(values, -1, keepdims=True)
    inverse = lax.rsqrt(jnp.mean(center * center, -1, keepdims=True) + 1e-06)
    return (center * inverse, inverse)


def norm_back(upstream, normed, inverse):
    return inverse * (
        upstream
        - jnp.mean(upstream, -1, keepdims=True)
        - normed * jnp.mean(upstream * normed, -1, keepdims=True)
    )


def silu_slope(values):
    sigma = jax.nn.sigmoid(values)
    return sigma * (1.0 + values * (1.0 - sigma))


def plan_table():
    betas = jnp.linspace(0.0001, 0.02, NSTEPS, dtype=jnp.float32)
    return jnp.exp(jnp.cumsum(jnp.log(1.0 - betas)))


def sinusoid(steps):
    half_width = FREQ // 2
    freqs = jnp.exp(-math.log(10000.0) * jnp.arange(half_width, dtype=jnp.float32) / half_width)
    angles = steps.astype(jnp.float32)[:, None] * freqs[None, :]
    return jnp.concatenate([jnp.cos(angles), jnp.sin(angles)], 1)


def dp_peers(mask):
    spread, pair = lax.axis_size("dp"), lax.axis_size("mod")
    return [(i * pair + c, (i ^ mask) * pair + c) for i in range(spread) for c in range(pair)]


def plane_peers(masks):
    spread, pair = lax.axis_size("dp"), lax.axis_size("mod")
    return [(i * pair + c, (i ^ masks[c]) * pair + c) for i in range(spread) for c in range(pair)]


def send(values, peers):
    return lax.ppermute(values, ("dp", "mod"), peers)


def swap_cores(values):
    return lax.ppermute(values, "mod", [(0, 1), (1, 0)])


def far_groups():
    spread = lax.axis_size("dp")
    bits = [1 << k for k in range(2, spread.bit_length() - 1)]
    if len(bits) == 2:
        return [[bits[0], bits[1], bits[0] | bits[1]]]
    return [[bit] for bit in bits]


def far_masks():
    masks = [0]
    for group in far_groups():
        masks = masks + [mask | have for mask in group for have in masks]
    return masks


def block_places():
    me, core = lax.axis_index("dp"), lax.axis_index("mod")
    second = jnp.where(core == 0, 1, 2)
    third = jnp.where(core == 0, 2, 1)
    far = jnp.array(far_masks(), jnp.int32)
    near = jnp.stack([jnp.zeros_like(second), second, third, second | third])
    return (me ^ (near[:, None] | far[None, :])).reshape(-1).astype(jnp.int32)


def move_kernel(slots, sources, targets, hold, in_sems, out_sems):
    total = len(sources)
    for first in range(0, total, slots):
        wave = range(first, min(first + slots, total))
        arriving = [
            pltpu.make_async_copy(sources[at], hold.at[at - first], in_sems.at[at]) for at in wave
        ]
        for copy in arriving:
            copy.start()
        leaving = []
        for at, copy in zip(wave, arriving):
            copy.wait()
            leaving.append(
                pltpu.make_async_copy(hold.at[at - first], targets[at], out_sems.at[at])
            )
            leaving[-1].start()
        for copy in leaving:
            copy.wait()


def place_kernel(counts, slots, places, *refs):
    ins, out = (refs[: len(counts)], refs[len(counts)])
    sources = [ins[part].at[row] for part, count in enumerate(counts) for row in range(count)]
    targets = [out.at[places[at]] for at in range(len(sources))]
    move_kernel(slots, sources, targets, *refs[len(counts) + 1 :])


def pick_kernel(counts, slots, places, source, *refs):
    outs = refs[: len(counts)]
    targets = [outs[part].at[row] for part, count in enumerate(counts) for row in range(count)]
    sources = [source.at[places[at]] for at in range(len(targets))]
    move_kernel(slots, sources, targets, *refs[len(counts) :])


def plane_slots(total, plane, kind):
    rows, columns = plane
    padded = -(-rows // 16) * 16 * -(-columns // 128) * 128 * jnp.dtype(kind).itemsize
    return max(1, min(total, (24 << 20) // padded))


def move_call(kernel, counts, places, operands, out_shape, out_count, plane, kind):
    total = sum(counts)
    slots = plane_slots(total, plane, kind)
    any_space = pl.BlockSpec(memory_space=pl.ANY)
    return pl.pallas_call(
        functools.partial(kernel, counts, slots),
        grid_spec=pltpu.PrefetchScalarGridSpec(
            num_scalar_prefetch=1,
            grid=(1,),
            in_specs=[any_space] * len(operands),
            out_specs=any_space if out_count is None else [any_space] * out_count,
            scratch_shapes=[
                pltpu.VMEM((slots,) + plane, kind),
                pltpu.SemaphoreType.DMA((total,)),
                pltpu.SemaphoreType.DMA((total,)),
            ],
        ),
        out_shape=out_shape,
        compiler_params=pltpu.CompilerParams(vmem_limit_bytes=40 << 20),
        cost_estimate=pl.CostEstimate(
            flops=0,
            bytes_accessed=2 * total * plane[0] * plane[1] * jnp.dtype(kind).itemsize,
            transcendentals=0,
        ),
        name="move_blocks",
    )(places, *operands)


def place_blocks(parts, places):
    counts = [part.shape[0] for part in parts]
    plane, kind = (parts[0].shape[1:], parts[0].dtype)
    shape = jax.ShapeDtypeStruct((sum(counts),) + plane, kind)
    return move_call(place_kernel, counts, places, parts, shape, None, plane, kind)


def pick_blocks(values, places):
    counts = [values.shape[0] // 4] * 4
    plane, kind = (values.shape[1:], values.dtype)
    shape = [jax.ShapeDtypeStruct((count,) + plane, kind) for count in counts]
    return move_call(pick_kernel, counts, places, [values], shape, 4, plane, kind)


def gather_blocks(block, places):
    stack = block[None]
    for group in far_groups():
        stack = jnp.concatenate([stack] + [send(stack, dp_peers(mask)) for mask in group], 0)
    second = send(stack, plane_peers((1, 2)))
    third = send(stack, plane_peers((2, 1)))
    both = send(second, plane_peers((2, 1)))
    return place_blocks([stack, second, third, both], places)


def scatter_blocks(values, places):
    kind = values.dtype
    wide = jnp.float32
    own, second, third, both = pick_blocks(values, places)
    from_both = send(both, plane_peers((2, 1)))
    from_third = send(third, plane_peers((2, 1)))
    second = (second.astype(wide) + from_both.astype(wide)).astype(kind)
    from_second = send(second, plane_peers((1, 2)))
    own = (own.astype(wide) + from_third.astype(wide) + from_second.astype(wide)).astype(kind)
    for group in reversed(far_groups()):
        count = own.shape[0] // (len(group) + 1)
        total = own[:count].astype(wide)
        for pos, mask in enumerate(group):
            total = total + send(
                own[(pos + 1) * count : (pos + 2) * count], dp_peers(mask)
            ).astype(wide)
        own = total if count == 1 else total.astype(kind)
    return own[0].astype(wide)


def all_sum(values):
    values = values + swap_cores(values)
    return dp_sum(values)


def dp_sum(values):
    for bit in range(lax.axis_size("dp").bit_length() - 1):
        values = values + send(values, dp_peers(1 << bit))
    return values


def product(left, right, dims):
    return lax.dot_general(left, right, (dims, ((), ())), preferred_element_type=jnp.float32)


def fill_bias(spread_ref, bias):
    tokens = GRID * GRID
    for head in range(bias.shape[0]):
        spread = spread_ref[head]
        for row in range(GRID):
            off = (GRID - 1 - row) * GRID
            moved = spread if off == 0 else pltpu.roll(spread, SPREAD - off, 1)
            bias[head, row * GRID : (row + 1) * GRID, :] = moved[:, :tokens]


def head_slices(values, head, heads):
    width = heads * HD
    return [
        values[:, part * width + head * HD : part * width + (head + 1) * HD] for part in range(3)
    ]


def attention_kernel(heads, qkv_ref, spread_ref, out_ref, log_ref, bias):
    @pl.when(pl.program_id(0) == 0)
    def _():
        fill_bias(spread_ref, bias)

    values = qkv_ref[...]
    outs, logs = ([], [])
    for head in range(heads):
        query, key, value = head_slices(values, head, heads)
        scores = product(query, key, ((1,), (1,))) * HD ** (-0.5) + bias[head]
        top = jnp.max(scores, -1, keepdims=True)
        powers = jnp.exp(scores - top)
        total = jnp.sum(powers, -1, keepdims=True)
        probs = (powers * (1.0 / total)).astype(jnp.bfloat16)
        outs.append(product(probs, value, ((1,), (0,))).astype(jnp.bfloat16))
        logs.append(top + jnp.log(total))
    out_ref[...] = jnp.concatenate(outs, 1)
    log_ref[...] = jnp.concatenate(logs, 1)


def attention(qkv, spread):
    rows, columns = qkv.shape
    heads = spread.shape[0]
    tokens = GRID * GRID
    return pl.pallas_call(
        functools.partial(attention_kernel, heads),
        grid=(rows // tokens,),
        in_specs=[
            pl.BlockSpec((tokens, columns), lambda step: (step, 0)),
            pl.BlockSpec(spread.shape, lambda step: (0, 0, 0)),
        ],
        out_specs=[
            pl.BlockSpec((tokens, heads * HD), lambda step: (step, 0)),
            pl.BlockSpec((tokens, heads), lambda step: (step, 0)),
        ],
        out_shape=[
            jax.ShapeDtypeStruct((rows, heads * HD), jnp.bfloat16),
            jax.ShapeDtypeStruct((rows, heads), jnp.float32),
        ],
        scratch_shapes=[pltpu.VMEM((heads, tokens, tokens), jnp.float32)],
        compiler_params=pltpu.CompilerParams(vmem_limit_bytes=48 << 20),
        cost_estimate=pl.CostEstimate(
            flops=4 * rows * tokens * heads * 256,
            bytes_accessed=rows * columns * 4,
            transcendentals=rows * tokens * heads,
        ),
        name="attention",
    )(qkv, spread)


def attention_back_kernel(
    heads, qkv_ref, upstream_ref, log_ref, spread_ref, d_qkv_ref, d_spread_ref, bias, d_bias
):
    tokens = GRID * GRID

    @pl.when(pl.program_id(0) == 0)
    def _():
        fill_bias(spread_ref, bias)
        d_bias[...] = jnp.zeros_like(d_bias)

    values, upstream, logs = (qkv_ref[...], upstream_ref[...], log_ref[...])
    d_query, d_key, d_value = ([], [], [])
    for head in range(heads):
        query, key, value = head_slices(values, head, heads)
        d_out = upstream[:, head * HD : (head + 1) * HD]
        scores = product(query, key, ((1,), (1,))) * HD ** (-0.5) + bias[head]
        probs = jnp.exp(scores - logs[:, head : head + 1])
        d_probs = product(d_out, value, ((1,), (1,)))
        d_scores = probs * (d_probs - jnp.sum(probs * d_probs, -1, keepdims=True))
        d_scores = d_scores.astype(jnp.bfloat16)
        d_bias[head] += d_scores.astype(jnp.float32)
        d_query.append((product(d_scores, key, ((1,), (0,))) * HD ** (-0.5)).astype(jnp.bfloat16))
        d_key.append((product(d_scores, query, ((0,), (0,))) * HD ** (-0.5)).astype(jnp.bfloat16))
        d_value.append(
            product(probs.astype(jnp.bfloat16), d_out, ((0,), (0,))).astype(jnp.bfloat16)
        )
    pieces = d_query + d_key + d_value
    spare = d_qkv_ref.shape[1] - 3 * heads * HD
    if spare:
        pieces = pieces + [jnp.zeros((tokens, spare), jnp.bfloat16)]
    d_qkv_ref[...] = jnp.concatenate(pieces, 1)

    @pl.when(pl.program_id(0) == pl.num_programs(0) - 1)
    def _():
        for head in range(heads):
            total = jnp.zeros((GRID, SPREAD), jnp.float32)
            for row in range(GRID):
                off = (GRID - 1 - row) * GRID
                rows = d_bias[head, row * GRID : (row + 1) * GRID, :]
                wide = jnp.concatenate([rows, jnp.zeros((GRID, SPREAD - tokens), jnp.float32)], 1)
                total += wide if off == 0 else pltpu.roll(wide, off, 1)
            d_spread_ref[head] = total


def attention_back(qkv, upstream, logs, spread):
    rows, columns = qkv.shape
    heads = spread.shape[0]
    tokens = GRID * GRID
    return pl.pallas_call(
        functools.partial(attention_back_kernel, heads),
        grid=(rows // tokens,),
        in_specs=[
            pl.BlockSpec((tokens, columns), lambda step: (step, 0)),
            pl.BlockSpec((tokens, heads * HD), lambda step: (step, 0)),
            pl.BlockSpec((tokens, heads), lambda step: (step, 0)),
            pl.BlockSpec(spread.shape, lambda step: (0, 0, 0)),
        ],
        out_specs=[
            pl.BlockSpec((tokens, columns), lambda step: (step, 0)),
            pl.BlockSpec(spread.shape, lambda step: (0, 0, 0)),
        ],
        out_shape=[
            jax.ShapeDtypeStruct((rows, columns), jnp.bfloat16),
            jax.ShapeDtypeStruct(spread.shape, jnp.float32),
        ],
        scratch_shapes=[pltpu.VMEM((heads, tokens, tokens), jnp.float32)] * 2,
        compiler_params=pltpu.CompilerParams(vmem_limit_bytes=48 << 20),
        cost_estimate=pl.CostEstimate(
            flops=10 * rows * tokens * heads * 256,
            bytes_accessed=rows * columns * 6,
            transcendentals=rows * tokens * heads,
        ),
        name="attention_back",
    )(qkv, upstream, logs, spread)


def spread_bias(relative):
    turned = relative.reshape(-1, SIDE, SIDE)[:, ::-1, ::-1]
    rows = [turned[:, :, GRID - 1 - row : SIDE - row] for row in range(GRID)]
    spread = jnp.stack(rows, 1).reshape(-1, GRID, SIDE * GRID)
    return jnp.pad(spread, ((0, 0), (0, 0), (0, SPREAD - SIDE * GRID)))


def gather_bias(d_spread):
    parts = d_spread[:, :, : SIDE * GRID].reshape(-1, GRID, SIDE, GRID)
    total = sum(
        jnp.pad(parts[:, row], ((0, 0), (0, 0), (GRID - 1 - row, row))) for row in range(GRID)
    )
    return total[:, ::-1, ::-1].reshape(-1, SIDE * SIDE)


def core_half(values, core, starts, width):
    return [
        jnp.where(
            core == 0,
            values[:, start : start + width],
            values[:, start + width : start + 2 * width],
        )
        for start in starts
    ]


def both_cores(mine, other, core, axis):
    return jnp.where(
        core == 0,
        jnp.concatenate([mine, other], axis),
        jnp.concatenate([other, mine], axis),
    )


def part_squares(block_part, mod_part, embed_part, first_core, core_index):
    column_sq = jnp.sum(block_part * block_part, 0)
    block_terms = [
        jnp.sum(column_sq[: 3 * D]),
        jnp.sum(column_sq[3 * D : 4 * D]),
        jnp.sum(column_sq[4 * D : 4 * D + MLPW]),
        jnp.sum(column_sq[4 * D + MLPW :]),
    ]
    mod_sq = jnp.sum(mod_part * mod_part, 0)
    global_cols = core_index * mod_part.shape[1] + jnp.arange(mod_part.shape[1], dtype=jnp.int32)
    first_mod = jnp.sum(jnp.where(global_cols < 6 * D, mod_sq, 0.0))
    second_mod = jnp.sum(jnp.where(global_cols < 6 * D, 0.0, mod_sq))
    row_sq = jnp.sum(embed_part * embed_part, 1)
    bounds = [
        0,
        NCLASS + 1,
        NCLASS + 1 + FREQ,
        NCLASS + 1 + FREQ + D,
        NCLASS + 1 + FREQ + D + PDIM,
        NCLASS + 1 + FREQ + D + 2 * PDIM,
    ]
    embed_terms = [jnp.sum(row_sq[bounds[pos] : bounds[pos + 1]]) for pos in range(5)]
    replicated = jnp.stack(block_terms + embed_terms) * first_core
    return jnp.concatenate([replicated[:4], jnp.stack([first_mod, second_mod]), replicated[4:]])


def adam_update(grad, first, second, weight, clip):
    first_new = FIRST_DECAY * first + (1.0 - FIRST_DECAY) * (grad * clip)
    second_new = SECOND_DECAY * second + (1.0 - SECOND_DECAY) * (grad * clip) ** 2
    update = (
        first_new
        / (1.0 - FIRST_DECAY**STEP)
        / (jnp.sqrt(second_new / (1.0 - SECOND_DECAY**STEP)) + ADAM_EPSILON)
        + WEIGHT_DECAY * weight
    )
    return (first_new, second_new, update)


def on_device(
    latents,
    noise,
    timesteps,
    labels,
    drops,
    block_weights,
    block_first,
    block_second,
    mod_weights,
    mod_first,
    mod_second,
    embed_weights,
    embed_first,
    embed_second,
    rel_bias,
    rel_first,
    rel_second,
):
    low = jnp.bfloat16
    wide = jnp.float32
    core = lax.axis_index("mod")
    spread = lax.axis_size("dp")
    images = latents.shape[0]
    length = latents.shape[1]
    rows = images * length
    share = embed_weights.shape[1]
    count = float(images * spread * lax.axis_size("mod") * length * latents.shape[2])
    places = block_places()

    half = D // 2
    wide_half = MLPW // 2
    block_low = block_weights.astype(low)
    q_part, k_part, v_part, p_part = core_half(
        block_low, core, [0, D, 2 * D, 3 * D], half
    )
    in_part, out_part = core_half(block_low, core, [4 * D, 4 * D + MLPW], wide_half)
    pad_part = jnp.zeros((block_low.shape[0], QKV_PAD - QKV_HALF), low)
    attn_part = jnp.concatenate([q_part, k_part, v_part, pad_part, p_part], 1)

    start = NCLASS + 1
    chosen = jnp.where(drops == 1, NCLASS, labels)
    codes = jnp.stack([timesteps // 32, timesteps % 32, chosen // 32, chosen % 32], 1)
    codes = codes.astype(low)
    codes = both_cores(codes, swap_cores(codes), core, 0)
    code_rows = -(-codes.size // share)
    codes = jnp.pad(codes.reshape(-1), (0, code_rows * share - codes.size))
    embed_low = embed_weights.astype(low)
    table = embed_low[:start]
    time_out = embed_low[start + FREQ : start + FREQ + D].astype(wide)
    small = jnp.concatenate(
        [
            embed_low[start : start + FREQ],
            embed_low[start + FREQ + D :],
            codes.reshape(code_rows, share),
        ],
        0,
    )
    small = gather_blocks(small, places)
    everyone = small[:, FREQ + 2 * PDIM :].reshape(spread, -1)[:, : 2 * images * 4]
    everyone = everyone.reshape(spread * 2 * images, 4).astype(wide)
    all_steps = 32.0 * everyone[:, 0] + everyone[:, 1]
    all_chosen = (32.0 * everyone[:, 2] + everyone[:, 3]).astype(jnp.int32)
    small = small[:, : FREQ + 2 * PDIM].transpose(1, 0, 2).reshape(FREQ + 2 * PDIM, D)
    time_in = small[:FREQ].astype(wide)
    patch = small[FREQ : FREQ + PDIM]
    head = small[FREQ + PDIM :]

    attn_low = gather_blocks(attn_part, places).reshape(D, -1)
    in_low = gather_blocks(in_part, places).reshape(D, -1)
    out_low = gather_blocks(out_part, places).reshape(D, -1)
    qkv_low = attn_low[:, :QKV_PAD]
    proj_half = attn_low[:, QKV_PAD:]
    proj_low = both_cores(proj_half, swap_cores(proj_half), core, 1)

    sinus = sinusoid(all_steps)
    pre_time = jnp.dot(sinus, time_in, precision=HIGH, preferred_element_type=wide)
    time_act = jax.nn.silu(pre_time)
    onehot = all_chosen[:, None] == jnp.arange(start, dtype=jnp.int32)[None, :]
    cond = jnp.dot(time_act, time_out, precision=HIGH, preferred_element_type=wide) + dense(
        onehot.astype(low), table
    )
    scaled = jax.nn.silu(cond).astype(low)
    mod_low = mod_weights.astype(low)
    mod_partial = dense(scaled, mod_low).astype(low)
    half_mod = scatter_blocks(mod_partial.reshape(spread, 2 * images, -1), places)
    mine = jnp.where(core == 0, half_mod[:images], half_mod[images:])
    theirs = jnp.where(core == 0, half_mod[images:], half_mod[:images])
    modulation = both_cores(mine, swap_cores(theirs), core, 1).reshape(images, 8, D)

    def moved(normed, shift):
        return (
            normed * (1.0 + modulation[:, shift + 1 : shift + 2]) + modulation[:, shift : shift + 1]
        ).astype(low)

    def with_sibling(values):
        flat = values.reshape(rows, -1)
        return jnp.concatenate([flat, swap_cores(flat)], 0)

    def sum_cores(partial):
        return (partial[:rows] + swap_cores(partial[rows:].astype(low)).astype(wide)).reshape(
            images, length, -1
        )

    alpha_bar = jnp.sum(
        jnp.where(
            timesteps[:, None] == jnp.arange(NSTEPS, dtype=jnp.int32)[None, :],
            plan_table()[None, :],
            0.0,
        ),
        1,
    )
    mixed = (
        jnp.sqrt(alpha_bar)[:, None, None] * latents
        + jnp.sqrt(1.0 - alpha_bar)[:, None, None] * noise
    ).astype(low)
    hidden0 = dense(mixed, patch)
    normed1, inverse1 = layer_norm(hidden0)
    attn_in = with_sibling(moved(normed1, 0))
    qkv = dense(attn_in, qkv_low).astype(low)
    heads = HEADS // 2
    bias_rows = spread_bias(jnp.where(core == 0, rel_bias[:heads], rel_bias[heads:]))
    heads_out, logs = attention(qkv, bias_rows)
    attn_out = both_cores(heads_out[:rows], swap_cores(heads_out[rows:]), core, 1)
    branch_one = dense(attn_out, proj_low).reshape(images, length, D)
    hidden1 = hidden0 + modulation[:, 2:3] * branch_one
    normed2, inverse2 = layer_norm(hidden1)
    mlp_in = with_sibling(moved(normed2, 3))
    pre_act = dense(mlp_in, in_low)
    act = jax.nn.gelu(pre_act, approximate=True).astype(low)
    branch_two = sum_cores(dense_trans(act, out_low))
    hidden2 = hidden1 + modulation[:, 5:6] * branch_two

    normed3, inverse3 = layer_norm(hidden2)
    final_in = moved(normed3, 6)
    predicted = dense_trans(final_in, head)
    error = predicted - noise
    loss_here = jnp.sum(error * error)
    d_predicted = (error * (2.0 / count)).astype(low)
    d_final = dense(d_predicted, head)
    g_head = outer_sum(d_predicted, final_in)
    d_scale3 = jnp.sum(d_final * normed3, 1)
    d_shift3 = jnp.sum(d_final, 1)
    d_hidden2 = norm_back(d_final * (1.0 + modulation[:, 7:8]), normed3, inverse3)

    d_branch_two = with_sibling((modulation[:, 5:6] * d_hidden2).astype(low))
    d_gate2 = jnp.sum(d_hidden2 * branch_two, 1)
    d_act = dense(d_branch_two, out_low)
    gelu_pull = jax.vjp(lambda entries: jax.nn.gelu(entries, approximate=True), pre_act)[1]
    d_pre = gelu_pull(d_act)[0].astype(low)
    g_out = scatter_blocks(
        outer_sum(d_branch_two, act).astype(low).reshape(spread, -1, wide_half), places
    )
    d_mlp_in = sum_cores(dense_trans(d_pre, in_low))
    g_in = scatter_blocks(
        outer_sum(mlp_in, d_pre).astype(low).reshape(spread, -1, wide_half), places
    )
    d_scale2 = jnp.sum(d_mlp_in * normed2, 1)
    d_shift2 = jnp.sum(d_mlp_in, 1)
    d_hidden1 = d_hidden2 + norm_back(d_mlp_in * (1.0 + modulation[:, 4:5]), normed2, inverse2)
    d_branch_one = (modulation[:, 2:3] * d_hidden1).astype(low).reshape(rows, D)
    d_gate1 = jnp.sum(d_hidden1 * branch_one, 1)
    d_attn_out = dense_trans(d_branch_one, proj_low).astype(low)
    d_mine = jnp.where(core == 0, d_attn_out[:, :half], d_attn_out[:, half:])
    d_theirs = jnp.where(core == 0, d_attn_out[:, half:], d_attn_out[:, :half])
    d_heads = jnp.concatenate([d_mine, swap_cores(d_theirs)], 0)
    g_proj = outer_sum(attn_out, d_branch_one)
    g_proj_mine = jnp.where(core == 0, g_proj[:, :half], g_proj[:, half:])
    g_proj_theirs = jnp.where(core == 0, g_proj[:, half:], g_proj[:, :half]).astype(low)
    g_proj = (g_proj_mine + swap_cores(g_proj_theirs).astype(wide)).astype(low)
    d_qkv, d_spread = attention_back(qkv, d_heads, logs, bias_rows)
    d_attn_in = sum_cores(dense_trans(d_qkv, qkv_low))
    g_qkv = outer_sum(attn_in, d_qkv).astype(low)
    g_attn = scatter_blocks(
        jnp.concatenate([g_qkv, g_proj], 1).reshape(spread, -1, QKV_PAD + half), places
    )
    d_scale1 = jnp.sum(d_attn_in * normed1, 1)
    d_shift1 = jnp.sum(d_attn_in, 1)
    d_hidden0 = d_hidden1 + norm_back(d_attn_in * (1.0 + modulation[:, 1:2]), normed1, inverse1)
    g_patch = outer_sum(mixed, d_hidden0.astype(low))

    d_modulation = jnp.stack(
        [d_shift1, d_scale1, d_gate1, d_shift2, d_scale2, d_gate2, d_shift3, d_scale3], 1
    )
    d_modulation = d_modulation.reshape(images, 8 * D).astype(low)
    mod_half = 4 * D
    d_keep = jnp.where(core == 0, d_modulation[:, :mod_half], d_modulation[:, mod_half:])
    d_give = jnp.where(core == 0, d_modulation[:, mod_half:], d_modulation[:, :mod_half])
    d_pair = both_cores(d_keep, swap_cores(d_give), core, 0)
    d_all = gather_blocks(d_pair, places).reshape(spread * 2 * images, mod_half)
    mod_grad = outer_sum(scaled, d_all)
    d_scaled = dense_trans(d_all, mod_low)
    d_scaled = d_scaled + swap_cores(d_scaled)
    d_cond = d_scaled * silu_slope(cond)
    g_table = first_contract(onehot.astype(wide), d_cond)
    g_time_out = first_contract(time_act, d_cond)
    d_time = lax.dot_general(
        d_cond, time_out, (((1,), (1,)), ((), ())), precision=HIGH, preferred_element_type=wide
    )
    g_ends = jnp.concatenate([g_patch, g_head], 0)
    g_ends = g_ends + swap_cores(g_ends)
    tail = jnp.concatenate([d_time, g_ends], 0)
    tail = scatter_blocks(tail.reshape(-1, spread, share).transpose(1, 0, 2), places)
    d_time_here, g_ends = (tail[: -2 * PDIM], tail[-2 * PDIM :])
    first_column = lax.axis_index("dp") * share
    pre_time_here = lax.dynamic_slice_in_dim(pre_time, first_column, share, 1)
    g_time_in = first_contract(sinus, d_time_here * silu_slope(pre_time_here))
    embed_grad = jnp.concatenate([g_table, g_time_in, g_time_out, g_ends], 0)

    g_here = jnp.concatenate([g_attn, g_in, g_out], 1).astype(low)
    g_there = swap_cores(g_here)
    zero_part = jnp.where(core == 0, g_here, g_there).astype(wide)
    one_part = jnp.where(core == 0, g_there, g_here).astype(wide)
    bounds = [0, half, 2 * half, 3 * half, QKV_PAD, QKV_PAD + half]
    bounds = bounds + [bounds[-1] + wide_half, bounds[-1] + 2 * wide_half]
    pieces = []
    for low_end, high_end in zip(bounds[:-1], bounds[1:]):
        if (low_end, high_end) != (3 * half, QKV_PAD):
            pieces = pieces + [zero_part[:, low_end:high_end], one_part[:, low_end:high_end]]
    block_grad = jnp.concatenate(pieces, 1)

    rel_half = gather_bias(d_spread)
    packed = jnp.concatenate([rel_half.reshape(-1), (loss_here * jnp.ones(1, wide))])
    packed = dp_sum(packed)
    packed_other = swap_cores(packed)
    rel_grad = both_cores(
        packed[:-1].reshape(heads, -1), packed_other[:-1].reshape(heads, -1), core, 0
    )
    loss_sum = packed[-1] + packed_other[-1]

    first_core = (core == 0).astype(wide)
    grad_parts, weight_parts = jnp.split(
        all_sum(
            jnp.concatenate(
                [
                    part_squares(block_grad, mod_grad, embed_grad, first_core, core),
                    part_squares(block_weights, mod_weights, embed_weights, first_core, core),
                ]
            )
        ),
        2,
    )
    grad_sq = jnp.concatenate([grad_parts, jnp.sum(rel_grad * rel_grad)[None]])
    weight_sq = jnp.concatenate([weight_parts, jnp.sum(rel_bias * rel_bias)[None]])
    grad_norm = jnp.sqrt(jnp.sum(grad_sq))
    clip = jnp.minimum(1.0, CLIP_NORM / grad_norm)
    block_m, block_s, block_step = adam_update(
        block_grad, block_first, block_second, block_weights, clip
    )
    mod_m, mod_s, mod_step = adam_update(mod_grad, mod_first, mod_second, mod_weights, clip)
    embed_m, embed_s, embed_step = adam_update(
        embed_grad, embed_first, embed_second, embed_weights, clip
    )
    rel_m, rel_s, rel_step = adam_update(rel_grad, rel_first, rel_second, rel_bias, clip)
    update_parts = all_sum(part_squares(block_step, mod_step, embed_step, first_core, core))
    update_sq = jnp.concatenate([update_parts, jnp.sum(rel_step * rel_step)[None]])
    weight_norm = jnp.sqrt(weight_sq)
    update_norm = jnp.sqrt(update_sq)
    ratio = weight_norm / update_norm
    block_ratio = jnp.concatenate(
        [
            jnp.broadcast_to(ratio[0], (3 * D,)),
            jnp.broadcast_to(ratio[1], (D,)),
            jnp.broadcast_to(ratio[2], (MLPW,)),
            jnp.broadcast_to(ratio[3], (MLPW,)),
        ]
    )
    global_cols = core * mod_weights.shape[1] + jnp.arange(
        mod_weights.shape[1], dtype=jnp.int32
    )
    mod_ratio = jnp.where(global_cols < 6 * D, ratio[4], ratio[5])
    embed_ratio = jnp.concatenate(
        [
            jnp.broadcast_to(ratio[6], (NCLASS + 1,)),
            jnp.broadcast_to(ratio[7], (FREQ,)),
            jnp.broadcast_to(ratio[8], (D,)),
            jnp.broadcast_to(ratio[9], (PDIM,)),
            jnp.broadcast_to(ratio[10], (PDIM,)),
        ]
    )
    block_new = block_weights - LEARN_RATE * block_ratio[None, :] * block_step
    mod_new = mod_weights - LEARN_RATE * mod_ratio[None, :] * mod_step
    embed_new = embed_weights - LEARN_RATE * embed_ratio[:, None] * embed_step
    rel_new = rel_bias - LEARN_RATE * ratio[11] * rel_step
    matrix_norms = jnp.stack([weight_norm, update_norm])
    return (
        loss_sum,
        grad_norm,
        matrix_norms,
        block_new,
        block_m,
        block_s,
        block_new.astype(jnp.bfloat16),
        mod_new,
        mod_m,
        mod_s,
        mod_new.astype(jnp.bfloat16),
        embed_new,
        embed_m,
        embed_s,
        embed_new.astype(jnp.bfloat16),
        rel_new,
        rel_m,
        rel_s,
        rel_new.astype(jnp.bfloat16),
        rel_grad * clip,
    )


def solution(mesh):
    placed = (
        P(("dp", "mod"), None, None),
        P(("dp", "mod"), None, None),
        P(("dp", "mod")),
        P(("dp", "mod")),
        P(("dp", "mod")),
        P("dp", None),
        P("dp", None),
        P("dp", None),
        P("dp", "mod"),
        P("dp", "mod"),
        P("dp", "mod"),
        P(None, "dp"),
        P(None, "dp"),
        P(None, "dp"),
        P(),
        P(),
        P(),
    )
    return jax.shard_map(
        on_device,
        mesh=mesh,
        in_specs=placed,
        out_specs=(
            P(),
            P(),
            P(),
            P("dp", None),
            P("dp", None),
            P("dp", None),
            P("dp", None),
            P("dp", "mod"),
            P("dp", "mod"),
            P("dp", "mod"),
            P("dp", "mod"),
            P(None, "dp"),
            P(None, "dp"),
            P(None, "dp"),
            P(None, "dp"),
            P(),
            P(),
            P(),
            P(),
            P(),
        ),
        check_vma=False,
    )
```

```python
import functools
import math

import jax
import jax.numpy as jnp
from jax import lax
from jax.experimental import pallas as pl
from jax.experimental.pallas import tpu as pltpu
from jax.sharding import PartitionSpec as P

D = 1152
HEADS = 16
HD = 72
MLPW = 4608
NCLASS = 1000
FREQ = 256
GRID = 16
PDIM = 16
NSTEPS = 1000
STEP = 10
SIDE = 2 * GRID - 1
QKV_HALF = 3 * D // 2
QKV_PAD = -(-QKV_HALF // 128) * 128
SPREAD = 2 * GRID * GRID
DP = ("far", "near")
VMEM = 60 << 20


FIRST_DECAY = 0.9
SECOND_DECAY = 0.999
ADAM_EPSILON = 1e-08
WEIGHT_DECAY = 0.01
LEARN_RATE = 0.25
CLIP_NORM = 0.05
HIGH = lax.Precision.HIGHEST


def dense(left, right):
    return jnp.dot(left, right, preferred_element_type=jnp.float32)


def dense_trans(left, right):
    return lax.dot_general(
        left, right, (((left.ndim - 1,), (1,)), ((), ())), preferred_element_type=jnp.float32
    )


def outer_sum(left, right):
    flat_left = left.reshape(-1, left.shape[-1])
    flat_right = right.reshape(-1, right.shape[-1])
    return lax.dot_general(
        flat_left, flat_right, (((0,), (0,)), ((), ())), preferred_element_type=jnp.float32
    )


def first_contract(left, right):
    return lax.dot_general(
        left, right, (((0,), (0,)), ((), ())), precision=HIGH, preferred_element_type=jnp.float32
    )


def layer_norm(values):
    center = values - jnp.mean(values, -1, keepdims=True)
    inverse = lax.rsqrt(jnp.mean(center * center, -1, keepdims=True) + 1e-06)
    return (center * inverse, inverse)


def norm_back(upstream, normed, inverse):
    return inverse * (
        upstream
        - jnp.mean(upstream, -1, keepdims=True)
        - normed * jnp.mean(upstream * normed, -1, keepdims=True)
    )


def silu_slope(values):
    sigma = jax.nn.sigmoid(values)
    return sigma * (1.0 + values * (1.0 - sigma))


def plan_table():
    betas = jnp.linspace(0.0001, 0.02, NSTEPS, dtype=jnp.float32)
    return jnp.exp(jnp.cumsum(jnp.log(1.0 - betas)))


def sinusoid(steps):
    half_width = FREQ // 2
    freqs = jnp.exp(-math.log(10000.0) * jnp.arange(half_width, dtype=jnp.float32) / half_width)
    angles = steps.astype(jnp.float32)[:, None] * freqs[None, :]
    return jnp.concatenate([jnp.cos(angles), jnp.sin(angles)], 1)


def dp_peers(mask):
    spread, pair = lax.axis_size(DP), lax.axis_size("mod")
    return [(i * pair + c, (i ^ mask) * pair + c) for i in range(spread) for c in range(pair)]


def plane_peers(masks):
    spread, pair = lax.axis_size(DP), lax.axis_size("mod")
    return [(i * pair + c, (i ^ masks[c]) * pair + c) for i in range(spread) for c in range(pair)]


def send(values, peers):
    return lax.ppermute(values, DP + ("mod",), peers)


def swap_cores(values):
    return lax.ppermute(values, "mod", [(0, 1), (1, 0)])


def far_groups():
    spread = lax.axis_size(DP)
    bits = [1 << k for k in range(2, spread.bit_length() - 1)]
    if len(bits) == 2:
        return [[bits[0], bits[1], bits[0] | bits[1]]]
    return [[bit] for bit in bits]


def far_masks():
    masks = [0]
    for group in far_groups():
        masks = masks + [mask | have for mask in group for have in masks]
    return masks


def block_places(far):
    me, core = lax.axis_index(DP), lax.axis_index("mod")
    second = jnp.where(core == 0, 1, 2)
    third = jnp.where(core == 0, 2, 1)
    near = jnp.stack([jnp.zeros_like(second), second, third, second | third])
    return ((me ^ near)[:, None] ^ far[None, :]).reshape(-1).astype(jnp.int32)


def relative_places():
    return block_places(jnp.array(far_masks(), jnp.int32))


def stacked_places():
    far = jnp.arange(lax.axis_size("far"), dtype=jnp.int32)
    return block_places(4 * (far ^ lax.axis_index("far")))


def move_kernel(slots, sources, targets, hold, in_sems, out_sems):
    total = len(sources)
    for first in range(0, total, slots):
        wave = range(first, min(first + slots, total))
        arriving = [
            pltpu.make_async_copy(sources[at], hold.at[at - first], in_sems.at[at]) for at in wave
        ]
        for copy in arriving:
            copy.start()
        leaving = []
        for at, copy in zip(wave, arriving):
            copy.wait()
            leaving.append(
                pltpu.make_async_copy(hold.at[at - first], targets[at], out_sems.at[at])
            )
            leaving[-1].start()
        for copy in leaving:
            copy.wait()


def place_kernel(counts, slots, places, *refs):
    ins, out = (refs[: len(counts)], refs[len(counts)])
    sources = [ins[part].at[row] for part, count in enumerate(counts) for row in range(count)]
    targets = [out.at[places[at]] for at in range(len(sources))]
    move_kernel(slots, sources, targets, *refs[len(counts) + 1 :])


def pick_kernel(counts, slots, places, source, *refs):
    outs = refs[: len(counts)]
    targets = [outs[part].at[row] for part, count in enumerate(counts) for row in range(count)]
    sources = [source.at[places[at]] for at in range(len(targets))]
    move_kernel(slots, sources, targets, *refs[len(counts) :])


def plane_slots(total, plane, kind):
    rows, columns = plane
    padded = -(-rows // 16) * 16 * -(-columns // 128) * 128 * jnp.dtype(kind).itemsize
    return max(1, min(total, (24 << 20) // padded))


def move_call(kernel, counts, places, operands, out_shape, out_count, plane, kind):
    total = sum(counts)
    slots = plane_slots(total, plane, kind)
    any_space = pl.BlockSpec(memory_space=pl.ANY)
    return pl.pallas_call(
        functools.partial(kernel, counts, slots),
        grid_spec=pltpu.PrefetchScalarGridSpec(
            num_scalar_prefetch=1,
            grid=(1,),
            in_specs=[any_space] * len(operands),
            out_specs=any_space if out_count is None else [any_space] * out_count,
            scratch_shapes=[
                pltpu.VMEM((slots,) + plane, kind),
                pltpu.SemaphoreType.DMA((total,)),
                pltpu.SemaphoreType.DMA((total,)),
            ],
        ),
        out_shape=out_shape,
        compiler_params=pltpu.CompilerParams(vmem_limit_bytes=VMEM),
        cost_estimate=pl.CostEstimate(
            flops=0,
            bytes_accessed=2 * total * plane[0] * plane[1] * jnp.dtype(kind).itemsize,
            transcendentals=0,
        ),
        name="move_blocks",
    )(places, *operands)


def place_blocks(parts, places):
    counts = [part.shape[0] for part in parts]
    plane, kind = (parts[0].shape[1:], parts[0].dtype)
    shape = jax.ShapeDtypeStruct((sum(counts),) + plane, kind)
    return move_call(place_kernel, counts, places, parts, shape, None, plane, kind)


def pick_blocks(values, places):
    counts = [values.shape[0] // 4] * 4
    plane, kind = (values.shape[1:], values.dtype)
    shape = [jax.ShapeDtypeStruct((count,) + plane, kind) for count in counts]
    return move_call(pick_kernel, counts, places, [values], shape, 4, plane, kind)


def tie(*values):
    return lax.optimization_barrier(values)


def gather_far(block):
    stack = block[None]
    for group in far_groups():
        stack = jnp.concatenate([stack] + [send(stack, dp_peers(mask)) for mask in group], 0)
    return stack


def gather_near(stack):
    return send(stack, plane_peers((1, 2))), send(stack, plane_peers((2, 1)))


def gather_last(second):
    return send(second, plane_peers((2, 1)))


def gather_parts(block):
    stack = gather_far(block)
    second, third = gather_near(stack)
    return [stack, second, third, gather_last(second)]


def far_stack(block):
    return lax.all_gather(block, "far", axis=0)


def far_share(stack):
    return lax.psum_scatter(stack, "far", scatter_dimension=0)


def add_low(left, right):
    return (left.astype(jnp.float32) + right.astype(jnp.float32)).astype(left.dtype)


def scatter_far(own):
    wide = jnp.float32
    for group in reversed(far_groups()):
        count = own.shape[0] // (len(group) + 1)
        total = own[:count].astype(wide)
        for pos, mask in enumerate(group):
            total = total + send(
                own[(pos + 1) * count : (pos + 2) * count], dp_peers(mask)
            ).astype(wide)
        own = total if count == 1 else total.astype(own.dtype)
    return own[0].astype(wide)


def scatter_parts(own, second, third, both):
    second = add_low(second, send(both, plane_peers((2, 1))))
    from_third = send(third, plane_peers((2, 1)))
    from_second = send(second, plane_peers((1, 2)))
    return scatter_far(add_low(add_low(own, from_third), from_second))


def all_sum(values):
    values = values + swap_cores(values)
    return dp_sum(values)


def dp_sum(values):
    for bit in range(lax.axis_size(DP).bit_length() - 1):
        values = values + send(values, dp_peers(1 << bit))
    return values


def product(left, right, dims):
    return lax.dot_general(left, right, (dims, ((), ())), preferred_element_type=jnp.float32)


def fill_bias(spread_ref, bias):
    tokens = GRID * GRID
    for head in range(bias.shape[0]):
        spread = spread_ref[head]
        for row in range(GRID):
            off = (GRID - 1 - row) * GRID
            moved = spread if off == 0 else pltpu.roll(spread, SPREAD - off, 1)
            bias[head, row * GRID : (row + 1) * GRID, :] = moved[:, :tokens]


def head_slices(values, head, heads):
    width = heads * HD
    return [
        values[:, part * width + head * HD : part * width + (head + 1) * HD] for part in range(3)
    ]


def attention_kernel(heads, qkv_ref, spread_ref, out_ref, log_ref, bias):
    @pl.when(pl.program_id(0) == 0)
    def _():
        fill_bias(spread_ref, bias)

    values = qkv_ref[...]
    outs, logs = ([], [])
    for head in range(heads):
        query, key, value = head_slices(values, head, heads)
        scores = product(query, key, ((1,), (1,))) * HD ** (-0.5) + bias[head]
        top = jnp.max(scores, -1, keepdims=True)
        powers = jnp.exp(scores - top)
        total = jnp.sum(powers, -1, keepdims=True)
        probs = (powers * (1.0 / total)).astype(jnp.bfloat16)
        outs.append(product(probs, value, ((1,), (0,))).astype(jnp.bfloat16))
        logs.append(top + jnp.log(total))
    out_ref[...] = jnp.concatenate(outs, 1)
    log_ref[...] = jnp.concatenate(logs, 1)


def attention(qkv, spread):
    rows, columns = qkv.shape
    heads = spread.shape[0]
    tokens = GRID * GRID
    return pl.pallas_call(
        functools.partial(attention_kernel, heads),
        grid=(rows // tokens,),
        in_specs=[
            pl.BlockSpec((tokens, columns), lambda step: (step, 0)),
            pl.BlockSpec(spread.shape, lambda step: (0, 0, 0)),
        ],
        out_specs=[
            pl.BlockSpec((tokens, heads * HD), lambda step: (step, 0)),
            pl.BlockSpec((tokens, heads), lambda step: (step, 0)),
        ],
        out_shape=[
            jax.ShapeDtypeStruct((rows, heads * HD), jnp.bfloat16),
            jax.ShapeDtypeStruct((rows, heads), jnp.float32),
        ],
        scratch_shapes=[pltpu.VMEM((heads, tokens, tokens), jnp.float32)],
        compiler_params=pltpu.CompilerParams(vmem_limit_bytes=VMEM),
        cost_estimate=pl.CostEstimate(
            flops=4 * rows * tokens * heads * 256,
            bytes_accessed=rows * columns * 4,
            transcendentals=rows * tokens * heads,
        ),
        name="attention",
    )(qkv, spread)


def attention_back_kernel(
    heads, qkv_ref, upstream_ref, log_ref, spread_ref, d_qkv_ref, d_spread_ref, bias, d_bias
):
    tokens = GRID * GRID

    @pl.when(pl.program_id(0) == 0)
    def _():
        fill_bias(spread_ref, bias)
        d_bias[...] = jnp.zeros_like(d_bias)

    values, upstream, logs = (qkv_ref[...], upstream_ref[...], log_ref[...])
    d_query, d_key, d_value = ([], [], [])
    for head in range(heads):
        query, key, value = head_slices(values, head, heads)
        d_out = upstream[:, head * HD : (head + 1) * HD]
        scores = product(query, key, ((1,), (1,))) * HD ** (-0.5) + bias[head]
        probs = jnp.exp(scores - logs[:, head : head + 1])
        d_probs = product(d_out, value, ((1,), (1,)))
        d_scores = probs * (d_probs - jnp.sum(probs * d_probs, -1, keepdims=True))
        d_scores = d_scores.astype(jnp.bfloat16)
        d_bias[head] += d_scores.astype(jnp.float32)
        d_query.append((product(d_scores, key, ((1,), (0,))) * HD ** (-0.5)).astype(jnp.bfloat16))
        d_key.append((product(d_scores, query, ((0,), (0,))) * HD ** (-0.5)).astype(jnp.bfloat16))
        d_value.append(
            product(probs.astype(jnp.bfloat16), d_out, ((0,), (0,))).astype(jnp.bfloat16)
        )
    pieces = d_query + d_key + d_value
    spare = d_qkv_ref.shape[1] - 3 * heads * HD
    if spare:
        pieces = pieces + [jnp.zeros((tokens, spare), jnp.bfloat16)]
    d_qkv_ref[...] = jnp.concatenate(pieces, 1)

    @pl.when(pl.program_id(0) == pl.num_programs(0) - 1)
    def _():
        for head in range(heads):
            total = jnp.zeros((GRID, SPREAD), jnp.float32)
            for row in range(GRID):
                off = (GRID - 1 - row) * GRID
                rows = d_bias[head, row * GRID : (row + 1) * GRID, :]
                wide = jnp.concatenate([rows, jnp.zeros((GRID, SPREAD - tokens), jnp.float32)], 1)
                total += wide if off == 0 else pltpu.roll(wide, off, 1)
            d_spread_ref[head] = total


def attention_back(qkv, upstream, logs, spread):
    rows, columns = qkv.shape
    heads = spread.shape[0]
    tokens = GRID * GRID
    return pl.pallas_call(
        functools.partial(attention_back_kernel, heads),
        grid=(rows // tokens,),
        in_specs=[
            pl.BlockSpec((tokens, columns), lambda step: (step, 0)),
            pl.BlockSpec((tokens, heads * HD), lambda step: (step, 0)),
            pl.BlockSpec((tokens, heads), lambda step: (step, 0)),
            pl.BlockSpec(spread.shape, lambda step: (0, 0, 0)),
        ],
        out_specs=[
            pl.BlockSpec((tokens, columns), lambda step: (step, 0)),
            pl.BlockSpec(spread.shape, lambda step: (0, 0, 0)),
        ],
        out_shape=[
            jax.ShapeDtypeStruct((rows, columns), jnp.bfloat16),
            jax.ShapeDtypeStruct(spread.shape, jnp.float32),
        ],
        scratch_shapes=[pltpu.VMEM((heads, tokens, tokens), jnp.float32)] * 2,
        compiler_params=pltpu.CompilerParams(vmem_limit_bytes=VMEM),
        cost_estimate=pl.CostEstimate(
            flops=10 * rows * tokens * heads * 256,
            bytes_accessed=rows * columns * 6,
            transcendentals=rows * tokens * heads,
        ),
        name="attention_back",
    )(qkv, upstream, logs, spread)


def whole_block(shape):
    return pl.BlockSpec(shape, lambda step: (0,) * len(shape), pipeline_mode=pl.Buffered(1))


def column_tile(columns):
    return 256 if columns % 256 == 0 else 128


def feed_in_kernel(values_ref, weights_ref, act_ref, slope_ref):
    weights = weights_ref[...]
    rate = math.sqrt(2.0 / math.pi)
    cubic = 0.044715 * rate
    for row in range(0, values_ref.shape[0], 256):
        pre = product(values_ref[row : row + 256, :], weights, ((1,), (0,)))
        square = pre * pre
        gate = 0.5 + 0.5 * jnp.tanh(pre * (rate + cubic * square))
        act = pre * gate
        slope = gate + (act - act * gate) * (2.0 * rate + 6.0 * cubic * square)
        act_ref[row : row + 256, :] = act.astype(jnp.bfloat16)
        slope_ref[row : row + 256, :] = slope.astype(jnp.bfloat16)


def feed_in(values, weights):
    rows, depth = values.shape
    columns = weights.shape[1]
    tile = column_tile(columns)
    return pl.pallas_call(
        feed_in_kernel,
        grid=(columns // tile,),
        in_specs=[whole_block((rows, depth)), pl.BlockSpec((depth, tile), lambda step: (0, step))],
        out_specs=[pl.BlockSpec((rows, tile), lambda step: (0, step))] * 2,
        out_shape=[jax.ShapeDtypeStruct((rows, columns), jnp.bfloat16)] * 2,
        compiler_params=pltpu.CompilerParams(vmem_limit_bytes=VMEM),
        cost_estimate=pl.CostEstimate(
            flops=2 * rows * depth * columns,
            bytes_accessed=4 * rows * columns,
            transcendentals=rows * columns,
        ),
        name="feed_in",
    )(values, weights)


def feed_back_kernel(values_ref, weights_ref, slope_ref, out_ref):
    weights = weights_ref[...]
    for row in range(0, values_ref.shape[0], 256):
        d_act = product(values_ref[row : row + 256, :], weights, ((1,), (0,)))
        d_pre = d_act * slope_ref[row : row + 256, :].astype(jnp.float32)
        out_ref[row : row + 256, :] = d_pre.astype(jnp.bfloat16)


def feed_back(values, weights, slope):
    rows, depth = values.shape
    columns = weights.shape[1]
    tile = column_tile(columns)
    return pl.pallas_call(
        feed_back_kernel,
        grid=(columns // tile,),
        in_specs=[
            whole_block((rows, depth)),
            pl.BlockSpec((depth, tile), lambda step: (0, step)),
            pl.BlockSpec((rows, tile), lambda step: (0, step)),
        ],
        out_specs=pl.BlockSpec((rows, tile), lambda step: (0, step)),
        out_shape=jax.ShapeDtypeStruct((rows, columns), jnp.bfloat16),
        compiler_params=pltpu.CompilerParams(vmem_limit_bytes=VMEM),
        cost_estimate=pl.CostEstimate(
            flops=2 * rows * depth * columns,
            bytes_accessed=4 * rows * columns,
            transcendentals=0,
        ),
        name="feed_back",
    )(values, weights, slope)


def into_heads_kernel(values_ref, weights_ref, out_ref):
    weights = weights_ref[...]
    for row in range(0, values_ref.shape[0], 256):
        out_ref[row : row + 256, :] = product(
            values_ref[row : row + 256, :], weights, ((1,), (0,))
        ).astype(jnp.bfloat16)


def into_heads(values, weights):
    rows, depth = values.shape
    columns = weights.shape[1]
    tile = column_tile(columns)
    return pl.pallas_call(
        into_heads_kernel,
        grid=(columns // tile,),
        in_specs=[whole_block((rows, depth)), pl.BlockSpec((depth, tile), lambda step: (0, step))],
        out_specs=pl.BlockSpec((rows, tile), lambda step: (0, step)),
        out_shape=jax.ShapeDtypeStruct((rows, columns), jnp.bfloat16),
        compiler_params=pltpu.CompilerParams(vmem_limit_bytes=VMEM),
        cost_estimate=pl.CostEstimate(
            flops=2 * rows * depth * columns, bytes_accessed=2 * rows * columns, transcendentals=0
        ),
        name="into_heads",
    )(values, weights)


def out_of_kernel(values_ref, weights_ref, out_ref):
    out_ref[...] = product(values_ref[...], weights_ref[...], ((1,), (1,))).astype(out_ref.dtype)


def out_of(values, weights, kind):
    rows, depth = values.shape
    columns = weights.shape[0]
    tile = min(rows, 256)
    return pl.pallas_call(
        out_of_kernel,
        grid=(rows // tile,),
        in_specs=[pl.BlockSpec((tile, depth), lambda step: (step, 0)), whole_block(weights.shape)],
        out_specs=pl.BlockSpec((tile, columns), lambda step: (step, 0)),
        out_shape=jax.ShapeDtypeStruct((rows, columns), kind),
        compiler_params=pltpu.CompilerParams(vmem_limit_bytes=VMEM),
        cost_estimate=pl.CostEstimate(
            flops=2 * rows * depth * columns, bytes_accessed=4 * rows * columns, transcendentals=0
        ),
        name="out_of",
    )(values, weights)


def weight_grad_kernel(places, left_one, left_two, right_one, right_two, *refs):
    outs, total = (refs[:4], refs[4])
    total[...] = product(left_one[...], right_one[...], ((0,), (0,))) + product(
        left_two[...], right_two[...], ((0,), (0,))
    )
    count, rows = outs[0].shape[:2]
    for part in range(4):
        for row in range(count):
            first = pl.multiple_of(places[part * count + row] * rows, 8)
            outs[part][row] = total[pl.ds(first, rows), :].astype(jnp.bfloat16)


def weight_grad(left, right, places):
    rows, depth = left[0].shape
    columns = right[0].shape[1]
    total = places.shape[0]
    block = depth // total
    if block % 8:
        whole = outer_sum(left[0], right[0]) + outer_sum(left[1], right[1])
        return pick_blocks(whole.astype(jnp.bfloat16).reshape(total, block, columns), places)
    tile = column_tile(columns)

    def whole_left(shape):
        return pl.BlockSpec(shape, lambda step, _: (0, 0), pipeline_mode=pl.Buffered(1))

    return pl.pallas_call(
        weight_grad_kernel,
        grid_spec=pltpu.PrefetchScalarGridSpec(
            num_scalar_prefetch=1,
            grid=(columns // tile,),
            in_specs=[whole_left((rows, depth))] * 2
            + [pl.BlockSpec((rows, tile), lambda step, _: (0, step))] * 2,
            out_specs=[pl.BlockSpec((total // 4, block, tile), lambda step, _: (0, 0, step))] * 4,
            scratch_shapes=[pltpu.VMEM((depth, tile), jnp.float32)],
        ),
        out_shape=[jax.ShapeDtypeStruct((total // 4, block, columns), jnp.bfloat16)] * 4,
        compiler_params=pltpu.CompilerParams(vmem_limit_bytes=VMEM),
        cost_estimate=pl.CostEstimate(
            flops=4 * rows * depth * columns, bytes_accessed=4 * depth * columns, transcendentals=0
        ),
        name="weight_grad",
    )(places, *left, *right)


def shifts():
    offset = jnp.arange(SIDE, dtype=jnp.int32)[:, None, None]
    column = jnp.arange(GRID, dtype=jnp.int32)
    return (offset == GRID - 1 - column[:, None] + column[None, :]).astype(jnp.float32)


def spread_bias(relative):
    turned = relative.reshape(-1, SIDE, SIDE)[:, ::-1, ::-1]
    spread = jnp.einsum("hed,dxy->hxey", turned, shifts(), precision=HIGH)
    spread = spread.reshape(-1, GRID, SIDE * GRID)
    return jnp.pad(spread, ((0, 0), (0, 0), (0, SPREAD - SIDE * GRID)))


def gather_bias(d_spread):
    parts = d_spread[:, :, : SIDE * GRID].reshape(-1, GRID, SIDE, GRID)
    total = jnp.einsum("hxey,dxy->hed", parts, shifts(), precision=HIGH)
    return total[:, ::-1, ::-1].reshape(-1, SIDE * SIDE)


def core_half(values, core, starts, width):
    return [
        jnp.where(
            core == 0,
            values[:, start : start + width],
            values[:, start + width : start + 2 * width],
        )
        for start in starts
    ]


def both_cores(mine, other, core, axis):
    return jnp.where(
        core == 0,
        jnp.concatenate([mine, other], axis),
        jnp.concatenate([other, mine], axis),
    )


def segment_sums(values, bounds, first):
    place = jnp.arange(values.shape[0], dtype=jnp.int32)
    segment = first + sum((place >= bound).astype(jnp.int32) for bound in bounds)
    wanted = segment[None, :] == jnp.arange(11, dtype=jnp.int32)[:, None]
    return jnp.sum(jnp.where(wanted, values[None, :], 0.0), 1)


def mod_squares(values, core):
    columns = jnp.sum(values * values, 0)
    bound = 6 * D - core * values.shape[1]
    return segment_sums(columns, [bound], 4)


def embed_squares(values):
    bounds = [NCLASS + 1, NCLASS + 1 + FREQ, NCLASS + 1 + FREQ + D, NCLASS + 1 + FREQ + D + PDIM]
    return segment_sums(jnp.sum(values * values, 1), bounds, 6)


def block_squares(values):
    return segment_sums(jnp.sum(values * values, 0), [3 * D, 4 * D, 4 * D + MLPW], 0)


def adam_update(grad, first, second, weight, clip):
    first_new = FIRST_DECAY * first + (1.0 - FIRST_DECAY) * (grad * clip)
    second_new = SECOND_DECAY * second + (1.0 - SECOND_DECAY) * (grad * clip) ** 2
    update = (
        first_new
        / (1.0 - FIRST_DECAY**STEP)
        / (jnp.sqrt(second_new / (1.0 - SECOND_DECAY**STEP)) + ADAM_EPSILON)
        + WEIGHT_DECAY * weight
    )
    return (first_new, second_new, update)


def on_device(
    latents,
    noise,
    timesteps,
    labels,
    drops,
    block_weights,
    block_first,
    block_second,
    mod_weights,
    mod_first,
    mod_second,
    embed_weights,
    embed_first,
    embed_second,
    rel_bias,
    rel_first,
    rel_second,
):
    low = jnp.bfloat16
    wide = jnp.float32
    core = lax.axis_index("mod")
    spread = lax.axis_size(DP)
    images = latents.shape[0]
    length = latents.shape[1]
    rows = images * length
    share = embed_weights.shape[1]
    count = float(images * spread * lax.axis_size("mod") * length * latents.shape[2])
    relative, stacked = (relative_places(), stacked_places())

    half = D // 2
    wide_half = MLPW // 2
    block_low = block_weights.astype(low)
    q_part, k_part, v_part, p_part = core_half(
        block_low, core, [0, D, 2 * D, 3 * D], half
    )
    in_part, out_part = core_half(block_low, core, [4 * D, 4 * D + MLPW], wide_half)
    pad_part = jnp.zeros((block_low.shape[0], QKV_PAD - QKV_HALF), low)
    attn_part = jnp.concatenate([q_part, k_part, v_part, pad_part], 1)
    in_part = jnp.concatenate([in_part, p_part], 1)

    start = NCLASS + 1
    chosen = jnp.where(drops == 1, NCLASS, labels)
    codes = jnp.stack([timesteps // 32, timesteps % 32, chosen // 32, chosen % 32], 1)
    codes = codes.astype(low)
    codes = both_cores(codes, swap_cores(codes), core, 0)
    code_rows = -(-codes.size // share)
    codes = jnp.pad(codes.reshape(-1), (0, code_rows * share - codes.size))
    embed_low = embed_weights.astype(low)
    table = embed_low[:start]
    time_out = embed_low[start + FREQ : start + FREQ + D].astype(wide)
    small = jnp.concatenate(
        [
            embed_low[start : start + FREQ],
            embed_low[start + FREQ + D :],
            codes.reshape(code_rows, share),
        ],
        0,
    )
    small_far = gather_far(small)
    attn_part, small_far = tie(attn_part, small_far)
    attn_far = far_stack(attn_part)
    small_second, small_third = gather_near(small_far)
    small_second, attn_far = tie(small_second, attn_far)
    small = [small_far, small_second, small_third, gather_last(small_second)]
    everyone = jnp.concatenate([part[:, FREQ + 2 * PDIM :] for part in small], 0)
    everyone = everyone.reshape(spread, -1)[:, : 2 * images * 4]
    everyone = everyone.reshape(spread * 2 * images, 4).astype(wide)
    all_steps = 32.0 * everyone[:, 0] + everyone[:, 1]
    all_chosen = (32.0 * everyone[:, 2] + everyone[:, 3]).astype(jnp.int32)
    small = place_blocks(small, relative)[:, : FREQ + 2 * PDIM]
    small = small.transpose(1, 0, 2).reshape(FREQ + 2 * PDIM, D)
    time_in = small[:FREQ].astype(wide)
    patch = small[FREQ : FREQ + PDIM]
    head = small[FREQ + PDIM :]

    attn_second, attn_third = gather_near(attn_far)
    in_part, attn_far = tie(in_part, attn_far)
    in_far = far_stack(in_part)

    sinus = sinusoid(all_steps)
    pre_time = jnp.dot(sinus, time_in, precision=HIGH, preferred_element_type=wide)
    time_act = jax.nn.silu(pre_time)
    image_of = relative[:, None] * 2 * images + jnp.arange(2 * images, dtype=jnp.int32)[None, :]
    sorting = image_of.reshape(1, -1) == jnp.arange(image_of.size, dtype=jnp.int32)[:, None]

    def sort_images(values):
        return jnp.dot(sorting.astype(wide), values, precision=HIGH, preferred_element_type=wide)

    sorted_sinus = sort_images(sinus)
    sorted_act = sort_images(time_act)
    classes = jnp.arange(start, dtype=jnp.int32)[None, :]
    sorted_onehot = sort_images(all_chosen[:, None].astype(wide)).astype(jnp.int32) == classes
    first_column = lax.axis_index(DP) * share
    sorted_slope = sort_images(
        silu_slope(lax.dynamic_slice_in_dim(pre_time, first_column, share, 1))
    )
    onehot = all_chosen[:, None] == classes
    cond = jnp.dot(time_act, time_out, precision=HIGH, preferred_element_type=wide) + dense(
        onehot.astype(low), table
    )
    scaled = jax.nn.silu(cond).astype(low)
    scaled, attn_second, attn_third = tie(scaled, attn_second, attn_third)
    attn_both = gather_last(attn_second)
    mod_low = mod_weights.astype(low)
    mod_partial = dense(scaled, mod_low).astype(low)
    half_mod = scatter_parts(*jnp.split(mod_partial.reshape(spread, 2 * images, -1), 4))
    heads = HEADS // 2
    bias_rows = spread_bias(jnp.where(core == 0, rel_bias[:heads], rel_bias[heads:]))
    half_mod, attn_both, in_far, bias_rows = tie(half_mod, attn_both, in_far, bias_rows)
    qkv_low = place_blocks([attn_far, attn_second, attn_third, attn_both], stacked).reshape(D, -1)
    in_second, in_third = gather_near(in_far)
    out_part, in_far = tie(out_part, in_far)
    out_far = far_stack(out_part)
    mine = jnp.where(core == 0, half_mod[:images], half_mod[images:])
    theirs = jnp.where(core == 0, half_mod[images:], half_mod[:images])
    modulation = both_cores(mine, swap_cores(theirs), core, 1).reshape(images, 8, D)

    def moved(normed, shift):
        return (
            normed * (1.0 + modulation[:, shift + 1 : shift + 2]) + modulation[:, shift : shift + 1]
        ).astype(low)

    def flat(values):
        return values.reshape(rows, -1)

    def sum_cores(mine, theirs):
        return (mine + swap_cores(theirs).astype(wide)).reshape(images, length, -1)

    alpha_bar = jnp.sum(
        jnp.where(
            timesteps[:, None] == jnp.arange(NSTEPS, dtype=jnp.int32)[None, :],
            plan_table()[None, :],
            0.0,
        ),
        1,
    )
    mixed = (
        jnp.sqrt(alpha_bar)[:, None, None] * latents
        + jnp.sqrt(1.0 - alpha_bar)[:, None, None] * noise
    ).astype(low)
    hidden0 = dense(mixed, patch)
    normed1, inverse1 = layer_norm(hidden0)
    attn_in = flat(moved(normed1, 0))
    attn_in_two = swap_cores(attn_in)
    qkv = into_heads(attn_in, qkv_low)
    qkv_two = into_heads(attn_in_two, qkv_low)
    heads_two, logs_two = attention(qkv_two, bias_rows)
    qkv, logs_two, in_second, in_third, out_far = tie(qkv, logs_two, in_second, in_third, out_far)
    heads_two = swap_cores(heads_two)
    in_both = gather_last(in_second)
    out_second, out_third = gather_near(out_far)
    heads_one, logs = attention(qkv, bias_rows)
    heads_one, in_both = tie(heads_one, in_both)
    in_low = place_blocks([in_far, in_second, in_third, in_both], stacked).reshape(D, -1)
    proj_half = in_low[:, wide_half:]
    in_low = in_low[:, :wide_half]
    proj_low = both_cores(proj_half, swap_cores(proj_half), core, 1)
    attn_out = both_cores(heads_one, heads_two, core, 1)
    branch_one = dense(attn_out, proj_low).reshape(images, length, D)
    hidden1 = hidden0 + modulation[:, 2:3] * branch_one
    normed2, inverse2 = layer_norm(hidden1)
    mlp_in = flat(moved(normed2, 3))
    mlp_in_two = swap_cores(mlp_in)
    act, slope = feed_in(mlp_in, in_low)
    act, out_second, out_third, mlp_in_two = tie(act, out_second, out_third, mlp_in_two)
    out_both = gather_last(out_second)
    act_two, slope_two = feed_in(mlp_in_two, in_low)
    act_two, out_both = tie(act_two, out_both)
    out_low = place_blocks([out_far, out_second, out_third, out_both], stacked).reshape(D, -1)
    branch_theirs = out_of(act_two, out_low, low)
    branch_two = sum_cores(out_of(act, out_low, wide), branch_theirs)
    hidden2 = hidden1 + modulation[:, 5:6] * branch_two

    normed3, inverse3 = layer_norm(hidden2)
    final_in = moved(normed3, 6)
    predicted = dense_trans(final_in, head)
    error = predicted - noise
    loss_here = jnp.sum(error * error)
    d_predicted = (error * (2.0 / count)).astype(low)
    d_final = dense(d_predicted, head)
    g_head = outer_sum(d_predicted, final_in)
    d_scale3 = jnp.sum(d_final * normed3, 1)
    d_shift3 = jnp.sum(d_final, 1)
    d_hidden2 = norm_back(d_final * (1.0 + modulation[:, 7:8]), normed3, inverse3)

    d_branch_two = flat((modulation[:, 5:6] * d_hidden2).astype(low))
    d_branch_two_two = swap_cores(d_branch_two)
    d_gate2 = jnp.sum(d_hidden2 * branch_two, 1)
    d_pre = feed_back(d_branch_two, out_low, slope)
    d_pre, d_branch_two_two = tie(d_pre, d_branch_two_two)
    d_pre_two = feed_back(d_branch_two_two, out_low, slope_two)
    out_own, out_second, out_third, out_both = weight_grad(
        (d_branch_two, d_branch_two_two), (act, act_two), stacked
    )
    out_back = send(out_both, plane_peers((2, 1)))
    d_pre, out_third = tie(d_pre, out_third)
    d_mlp_theirs = swap_cores(out_of(d_pre_two, in_low, low))
    d_mlp_mine = out_of(d_pre, in_low, wide)
    d_pre, d_mlp_mine, out_back = tie(d_pre, d_mlp_mine, out_back)
    out_second = send(add_low(out_second, out_back), plane_peers((1, 2)))
    out_third = send(out_third, plane_peers((2, 1)))
    in_own, in_second, in_third, in_both = weight_grad(
        (mlp_in, mlp_in_two), (d_pre, d_pre_two), stacked
    )
    in_both, d_mlp_theirs, d_mlp_mine = tie(in_both, d_mlp_theirs, d_mlp_mine)
    d_mlp_in = (d_mlp_mine + d_mlp_theirs.astype(wide)).reshape(images, length, D)
    d_scale2 = jnp.sum(d_mlp_in * normed2, 1)
    d_shift2 = jnp.sum(d_mlp_in, 1)
    d_hidden1 = d_hidden2 + norm_back(d_mlp_in * (1.0 + modulation[:, 4:5]), normed2, inverse2)
    d_branch_one = (modulation[:, 2:3] * d_hidden1).astype(low).reshape(rows, D)
    d_branch_one, out_second, out_third, in_both = tie(
        d_branch_one, out_second, out_third, in_both
    )
    in_back = send(in_both, plane_peers((2, 1)))
    g_out = far_share(add_low(add_low(out_own, out_third), out_second))
    d_gate1 = jnp.sum(d_hidden1 * branch_one, 1)
    d_attn_out = dense_trans(d_branch_one, proj_low).astype(low)
    d_mine = jnp.where(core == 0, d_attn_out[:, :half], d_attn_out[:, half:])
    d_theirs = jnp.where(core == 0, d_attn_out[:, half:], d_attn_out[:, :half])
    d_theirs = swap_cores(d_theirs)
    g_proj = outer_sum(attn_out, d_branch_one)
    g_proj_mine = jnp.where(core == 0, g_proj[:, :half], g_proj[:, half:])
    g_proj_theirs = jnp.where(core == 0, g_proj[:, half:], g_proj[:, :half]).astype(low)
    g_proj = (g_proj_mine + swap_cores(g_proj_theirs).astype(wide)).astype(low)
    d_mine, in_back, in_third, g_proj = tie(d_mine, in_back, in_third, g_proj)
    in_second = send(add_low(in_second, in_back), plane_peers((1, 2)))
    in_third = send(in_third, plane_peers((2, 1)))
    d_qkv, d_spread = attention_back(qkv, d_mine, logs, bias_rows)
    proj_own, proj_second, proj_third, proj_both = pick_blocks(
        g_proj.reshape(spread, -1, half), stacked
    )
    d_qkv, proj_both, d_theirs, g_out, in_second, in_third = tie(
        d_qkv, proj_both, d_theirs, g_out, in_second, in_third
    )
    g_in = far_share(add_low(add_low(in_own, in_third), in_second))
    proj_back = send(proj_both, plane_peers((2, 1)))
    d_qkv_two, d_spread_two = attention_back(qkv_two, d_theirs, logs_two, bias_rows)
    d_spread = d_spread + d_spread_two
    d_qkv_two, proj_back, proj_third = tie(d_qkv_two, proj_back, proj_third)
    proj_second = send(add_low(proj_second, proj_back), plane_peers((1, 2)))
    proj_third = send(proj_third, plane_peers((2, 1)))
    rel_half = gather_bias(d_spread)
    packed = jnp.concatenate([rel_half.reshape(-1), (loss_here * jnp.ones(1, wide))])
    packed = dp_sum(packed)
    d_attn_theirs = swap_cores(out_of(d_qkv_two, qkv_low, low))
    d_attn_mine = out_of(d_qkv, qkv_low, wide)
    d_qkv_two, d_attn_mine, proj_second, proj_third = tie(
        d_qkv_two, d_attn_mine, proj_second, proj_third
    )
    g_proj = far_share(add_low(add_low(proj_own, proj_third), proj_second))
    attn_own, attn_second, attn_third, attn_both = weight_grad(
        (attn_in, attn_in_two), (d_qkv, d_qkv_two), stacked
    )
    attn_both, attn_third, packed, d_attn_mine, d_attn_theirs, g_in = tie(
        attn_both, attn_third, packed, d_attn_mine, d_attn_theirs, g_in
    )
    attn_back = send(attn_both, plane_peers((2, 1)))
    d_attn_in = (d_attn_mine + d_attn_theirs.astype(wide)).reshape(images, length, D)
    d_scale1 = jnp.sum(d_attn_in * normed1, 1)
    d_shift1 = jnp.sum(d_attn_in, 1)
    d_hidden0 = d_hidden1 + norm_back(d_attn_in * (1.0 + modulation[:, 1:2]), normed1, inverse1)
    g_patch = outer_sum(mixed, d_hidden0.astype(low))

    d_modulation = jnp.stack(
        [d_shift1, d_scale1, d_gate1, d_shift2, d_scale2, d_gate2, d_shift3, d_scale3], 1
    )
    d_modulation = d_modulation.reshape(images, 8 * D).astype(low)
    mod_half = 4 * D
    d_keep = jnp.where(core == 0, d_modulation[:, :mod_half], d_modulation[:, mod_half:])
    d_give = jnp.where(core == 0, d_modulation[:, mod_half:], d_modulation[:, :mod_half])
    d_pair = both_cores(d_keep, swap_cores(d_give), core, 0)
    d_pair, attn_back = tie(d_pair, attn_back)
    attn_second = send(add_low(attn_second, attn_back), plane_peers((1, 2)))
    attn_third = send(attn_third, plane_peers((2, 1)))
    d_parts = gather_parts(d_pair)
    d_parts[0], attn_second, attn_third = tie(d_parts[0], attn_second, attn_third)
    g_qkv = far_share(add_low(add_low(attn_own, attn_third), attn_second))
    d_all = jnp.concatenate(d_parts, 0).reshape(spread * 2 * images, mod_half)
    mod_grad = outer_sum(scaled, d_all)
    d_scaled = dense_trans(d_all, mod_low)
    theirs = jnp.split(swap_cores(d_scaled), 4)
    d_scaled = d_scaled + jnp.concatenate([theirs[0], theirs[2], theirs[1], theirs[3]], 0)
    d_cond = sort_images(d_scaled * silu_slope(cond))
    g_table = first_contract(sorted_onehot.astype(wide), d_cond)
    g_time_out = first_contract(sorted_act, d_cond)
    d_time = lax.dot_general(
        d_cond, time_out, (((1,), (1,)), ((), ())), precision=HIGH, preferred_element_type=wide
    )
    g_ends = jnp.concatenate([g_patch, g_head], 0)
    g_ends = g_ends + swap_cores(g_ends)
    tail = jnp.concatenate([d_time, g_ends], 0)
    tail = tail.reshape(-1, spread, share).transpose(1, 0, 2)
    tail = scatter_parts(*pick_blocks(tail, relative))
    tail, g_qkv, g_proj = tie(tail, g_qkv, g_proj)
    d_time_here, g_ends = (tail[: -2 * PDIM], tail[-2 * PDIM :])
    g_time_in = first_contract(sorted_sinus, d_time_here * sorted_slope)
    embed_grad = jnp.concatenate([g_table, g_time_in, g_time_out, g_ends], 0)

    g_here = jnp.concatenate([g_qkv, g_in, g_proj, g_out], 1)
    g_there = swap_cores(g_here)
    g_mine = g_here.astype(wide)
    g_squares = segment_sums(
        jnp.sum(g_mine * g_mine, 0), [QKV_PAD, QKV_PAD + wide_half, QKV_PAD + wide_half + half], 0
    )
    g_squares = g_squares[jnp.array([0, 2, 1, 3] + list(range(4, 11)))]
    zero_part = jnp.where(core == 0, g_here, g_there)
    one_part = jnp.where(core == 0, g_there, g_here)
    after = QKV_PAD + wide_half
    spans = [(part * half, half) for part in range(3)] + [(after, half)]
    spans = spans + [(QKV_PAD, wide_half), (after + half, wide_half)]
    pieces = []
    for low_end, width in spans:
        pieces.append(zero_part[:, low_end : low_end + width])
        pieces.append(one_part[:, low_end : low_end + width])
    block_grad = jnp.concatenate(pieces, 1).astype(wide)

    packed_other = swap_cores(packed)
    rel_grad = both_cores(
        packed[:-1].reshape(heads, -1), packed_other[:-1].reshape(heads, -1), core, 0
    )
    loss_sum = packed[-1] + packed_other[-1]

    first_core = (core == 0).astype(wide)

    def replica_squares(block, mod, embed):
        copied = block_squares(block) + embed_squares(embed)
        return first_core * copied + mod_squares(mod, core)

    grad_parts, weight_parts = jnp.split(
        all_sum(
            jnp.concatenate(
                [
                    g_squares + mod_squares(mod_grad, core) + first_core * embed_squares(embed_grad),
                    replica_squares(block_weights, mod_weights, embed_weights),
                ]
            )
        ),
        2,
    )
    grad_sq = jnp.concatenate([grad_parts, jnp.sum(rel_grad * rel_grad)[None]])
    weight_sq = jnp.concatenate([weight_parts, jnp.sum(rel_bias * rel_bias)[None]])
    grad_norm = jnp.sqrt(jnp.sum(grad_sq))
    clip = jnp.minimum(1.0, CLIP_NORM / grad_norm)
    block_m, block_s, block_step = adam_update(
        block_grad, block_first, block_second, block_weights, clip
    )
    mod_m, mod_s, mod_step = adam_update(mod_grad, mod_first, mod_second, mod_weights, clip)
    embed_m, embed_s, embed_step = adam_update(
        embed_grad, embed_first, embed_second, embed_weights, clip
    )
    rel_m, rel_s, rel_step = adam_update(rel_grad, rel_first, rel_second, rel_bias, clip)
    update_parts = all_sum(replica_squares(block_step, mod_step, embed_step))
    update_sq = jnp.concatenate([update_parts, jnp.sum(rel_step * rel_step)[None]])
    weight_norm = jnp.sqrt(weight_sq)
    update_norm = jnp.sqrt(update_sq)
    ratio = weight_norm / update_norm
    block_ratio = jnp.concatenate(
        [
            jnp.broadcast_to(ratio[0], (3 * D,)),
            jnp.broadcast_to(ratio[1], (D,)),
            jnp.broadcast_to(ratio[2], (MLPW,)),
            jnp.broadcast_to(ratio[3], (MLPW,)),
        ]
    )
    global_cols = core * mod_weights.shape[1] + jnp.arange(
        mod_weights.shape[1], dtype=jnp.int32
    )
    mod_ratio = jnp.where(global_cols < 6 * D, ratio[4], ratio[5])
    embed_ratio = jnp.concatenate(
        [
            jnp.broadcast_to(ratio[6], (NCLASS + 1,)),
            jnp.broadcast_to(ratio[7], (FREQ,)),
            jnp.broadcast_to(ratio[8], (D,)),
            jnp.broadcast_to(ratio[9], (PDIM,)),
            jnp.broadcast_to(ratio[10], (PDIM,)),
        ]
    )
    block_new = block_weights - LEARN_RATE * block_ratio[None, :] * block_step
    mod_new = mod_weights - LEARN_RATE * mod_ratio[None, :] * mod_step
    embed_new = embed_weights - LEARN_RATE * embed_ratio[:, None] * embed_step
    rel_new = rel_bias - LEARN_RATE * ratio[11] * rel_step
    matrix_norms = jnp.stack([weight_norm, update_norm])
    return (
        loss_sum,
        grad_norm,
        matrix_norms,
        block_new,
        block_m,
        block_s,
        block_new.astype(jnp.bfloat16),
        mod_new,
        mod_m,
        mod_s,
        mod_new.astype(jnp.bfloat16),
        embed_new,
        embed_m,
        embed_s,
        embed_new.astype(jnp.bfloat16),
        rel_new,
        rel_m,
        rel_s,
        rel_new.astype(jnp.bfloat16),
        rel_grad * clip,
    )


def solution(mesh):
    spread, pair = mesh.devices.shape
    grid = jax.sharding.Mesh(mesh.devices.reshape(spread // 4, 4, pair), DP + ("mod",))
    placed = (
        P(DP + ("mod",), None, None),
        P(DP + ("mod",), None, None),
        P(DP + ("mod",)),
        P(DP + ("mod",)),
        P(DP + ("mod",)),
        P(DP, None),
        P(DP, None),
        P(DP, None),
        P(DP, "mod"),
        P(DP, "mod"),
        P(DP, "mod"),
        P(None, DP),
        P(None, DP),
        P(None, DP),
        P(),
        P(),
        P(),
    )
    return jax.shard_map(
        on_device,
        mesh=grid,
        in_specs=placed,
        out_specs=(
            P(),
            P(),
            P(),
            P(DP, None),
            P(DP, None),
            P(DP, None),
            P(DP, None),
            P(DP, "mod"),
            P(DP, "mod"),
            P(DP, "mod"),
            P(DP, "mod"),
            P(None, DP),
            P(None, DP),
            P(None, DP),
            P(None, DP),
            P(),
            P(),
            P(),
            P(),
            P(),
        ),
        check_vma=False,
    )
```

```python
import functools
import math

import jax
import jax.numpy as jnp
from jax import lax
from jax.experimental import pallas as pl
from jax.experimental.pallas import tpu as pltpu
from jax.sharding import PartitionSpec as P

D = 1152
HEADS = 16
HD = 72
MLPW = 4608
NCLASS = 1000
FREQ = 256
GRID = 16
PDIM = 16
NSTEPS = 1000
STEP = 10
SIDE = 2 * GRID - 1
QKV_HALF = 3 * D // 2
QKV_PAD = -(-QKV_HALF // 128) * 128
SPREAD = 2 * GRID * GRID
DP = ("far", "near")
VMEM = 60 << 20
PACE = 1
LOG2E = math.log2(math.e)


FIRST_DECAY = 0.9
SECOND_DECAY = 0.999
ADAM_EPSILON = 1e-08
WEIGHT_DECAY = 0.01
LEARN_RATE = 0.25
CLIP_NORM = 0.05
HIGH = lax.Precision.HIGHEST


def dense(left, right):
    return jnp.dot(left, right, preferred_element_type=jnp.float32)


def dense_trans(left, right):
    return lax.dot_general(
        left, right, (((left.ndim - 1,), (1,)), ((), ())), preferred_element_type=jnp.float32
    )


def outer_sum(left, right):
    flat_left = left.reshape(-1, left.shape[-1])
    flat_right = right.reshape(-1, right.shape[-1])
    return lax.dot_general(
        flat_left, flat_right, (((0,), (0,)), ((), ())), preferred_element_type=jnp.float32
    )


def first_contract(left, right):
    return lax.dot_general(
        left, right, (((0,), (0,)), ((), ())), precision=HIGH, preferred_element_type=jnp.float32
    )


def layer_norm(values):
    center = values - jnp.mean(values, -1, keepdims=True)
    inverse = lax.rsqrt(jnp.mean(center * center, -1, keepdims=True) + 1e-06)
    return (center * inverse, inverse)


def norm_back(upstream, normed, inverse):
    return inverse * (
        upstream
        - jnp.mean(upstream, -1, keepdims=True)
        - normed * jnp.mean(upstream * normed, -1, keepdims=True)
    )


def silu_slope(values):
    sigma = jax.nn.sigmoid(values)
    return sigma * (1.0 + values * (1.0 - sigma))


def plan_table():
    betas = jnp.linspace(0.0001, 0.02, NSTEPS, dtype=jnp.float32)
    return jnp.exp(jnp.cumsum(jnp.log(1.0 - betas)))


def sinusoid(steps):
    half_width = FREQ // 2
    freqs = jnp.exp(-math.log(10000.0) * jnp.arange(half_width, dtype=jnp.float32) / half_width)
    angles = steps.astype(jnp.float32)[:, None] * freqs[None, :]
    return jnp.concatenate([jnp.cos(angles), jnp.sin(angles)], 1)


def dp_peers(mask):
    spread, pair = lax.axis_size(DP), lax.axis_size("mod")
    return [(i * pair + c, (i ^ mask) * pair + c) for i in range(spread) for c in range(pair)]


def plane_peers(masks):
    spread, pair = lax.axis_size(DP), lax.axis_size("mod")
    return [(i * pair + c, (i ^ masks[c]) * pair + c) for i in range(spread) for c in range(pair)]


def send(values, peers):
    return lax.ppermute(values, DP + ("mod",), peers)


def swap_cores(values):
    return lax.ppermute(values, "mod", [(0, 1), (1, 0)])


def far_groups():
    spread = lax.axis_size(DP)
    bits = [1 << k for k in range(2, spread.bit_length() - 1)]
    if len(bits) == 2:
        return [[bits[0], bits[1], bits[0] | bits[1]]]
    return [[bit] for bit in bits]


def far_masks():
    masks = [0]
    for group in far_groups():
        masks = masks + [mask | have for mask in group for have in masks]
    return masks


def block_places(far):
    me, core = lax.axis_index(DP), lax.axis_index("mod")
    second = jnp.where(core == 0, 1, 2)
    third = jnp.where(core == 0, 2, 1)
    near = jnp.stack([jnp.zeros_like(second), second, third, second | third])
    return ((me ^ near)[:, None] ^ far[None, :]).reshape(-1).astype(jnp.int32)


def relative_places():
    return block_places(jnp.array(far_masks(), jnp.int32))


def stacked_places():
    far = jnp.arange(lax.axis_size("far"), dtype=jnp.int32)
    return block_places(4 * (far ^ lax.axis_index("far")))


def move_kernel(slots, sources, targets, hold, in_sems, out_sems):
    total = len(sources)
    for first in range(0, total, slots):
        wave = range(first, min(first + slots, total))
        arriving = [
            pltpu.make_async_copy(sources[at], hold.at[at - first], in_sems.at[at]) for at in wave
        ]
        for copy in arriving:
            copy.start()
        leaving = []
        for at, copy in zip(wave, arriving):
            copy.wait()
            leaving.append(
                pltpu.make_async_copy(hold.at[at - first], targets[at], out_sems.at[at])
            )
            leaving[-1].start()
        for copy in leaving:
            copy.wait()


def place_kernel(counts, slots, places, *refs):
    ins, out = (refs[: len(counts)], refs[len(counts)])
    sources = [ins[part].at[row] for part, count in enumerate(counts) for row in range(count)]
    targets = [out.at[places[at]] for at in range(len(sources))]
    move_kernel(slots, sources, targets, *refs[len(counts) + 1 :])


def pick_kernel(counts, slots, places, source, *refs):
    outs = refs[: len(counts)]
    targets = [outs[part].at[row] for part, count in enumerate(counts) for row in range(count)]
    sources = [source.at[places[at]] for at in range(len(targets))]
    move_kernel(slots, sources, targets, *refs[len(counts) :])


def plane_slots(total, plane, kind):
    rows, columns = plane
    padded = -(-rows // 16) * 16 * -(-columns // 128) * 128 * jnp.dtype(kind).itemsize
    return max(1, min(total, (24 << 20) // padded))


def move_call(kernel, counts, places, operands, out_shape, out_count, plane, kind):
    total = sum(counts)
    slots = plane_slots(total, plane, kind)
    any_space = pl.BlockSpec(memory_space=pl.ANY)
    return pl.pallas_call(
        functools.partial(kernel, counts, slots),
        grid_spec=pltpu.PrefetchScalarGridSpec(
            num_scalar_prefetch=1,
            grid=(1,),
            in_specs=[any_space] * len(operands),
            out_specs=any_space if out_count is None else [any_space] * out_count,
            scratch_shapes=[
                pltpu.VMEM((slots,) + plane, kind),
                pltpu.SemaphoreType.DMA((total,)),
                pltpu.SemaphoreType.DMA((total,)),
            ],
        ),
        out_shape=out_shape,
        compiler_params=pltpu.CompilerParams(vmem_limit_bytes=VMEM),
        cost_estimate=pl.CostEstimate(
            flops=0,
            bytes_accessed=2 * total * plane[0] * plane[1] * jnp.dtype(kind).itemsize,
            transcendentals=0,
        ),
        name="move_blocks",
    )(places, *operands)


def place_blocks(parts, places):
    counts = [part.shape[0] for part in parts]
    plane, kind = (parts[0].shape[1:], parts[0].dtype)
    shape = jax.ShapeDtypeStruct((sum(counts),) + plane, kind)
    return move_call(place_kernel, counts, places, parts, shape, None, plane, kind)


def pick_blocks(values, places):
    counts = [values.shape[0] // 4] * 4
    plane, kind = (values.shape[1:], values.dtype)
    shape = [jax.ShapeDtypeStruct((count,) + plane, kind) for count in counts]
    return move_call(pick_kernel, counts, places, [values], shape, 4, plane, kind)


def tie(*values):
    return lax.optimization_barrier(values)


def gather_far(block):
    stack = block[None]
    for group in far_groups():
        stack = jnp.concatenate([stack] + [send(stack, dp_peers(mask)) for mask in group], 0)
    return stack


def gather_near(stack):
    return send(stack, plane_peers((1, 2))), send(stack, plane_peers((2, 1)))


def gather_last(second):
    return send(second, plane_peers((2, 1)))


def gather_parts(block):
    stack = gather_far(block)
    second, third = gather_near(stack)
    return [stack, second, third, gather_last(second)]


def far_stack(block):
    return lax.all_gather(block, "far", axis=0)


def far_share(stack):
    return lax.psum_scatter(stack, "far", scatter_dimension=0)


def add_low(left, right):
    return (left.astype(jnp.float32) + right.astype(jnp.float32)).astype(left.dtype)


def scatter_far(own):
    wide = jnp.float32
    for group in reversed(far_groups()):
        count = own.shape[0] // (len(group) + 1)
        total = own[:count].astype(wide)
        for pos, mask in enumerate(group):
            total = total + send(
                own[(pos + 1) * count : (pos + 2) * count], dp_peers(mask)
            ).astype(wide)
        own = total if count == 1 else total.astype(own.dtype)
    return own[0].astype(wide)


def scatter_parts(own, second, third, both, meanwhile=()):
    second = add_low(second, send(both, plane_peers((2, 1))))
    second, *meanwhile = tie(second, *meanwhile)
    from_third = send(third, plane_peers((2, 1)))
    from_second = send(second, plane_peers((1, 2)))
    share = scatter_far(add_low(add_low(own, from_third), from_second))
    return (share, *meanwhile) if meanwhile else share


def all_sum(values, meanwhile=()):
    return dp_sum(values + swap_cores(values), meanwhile)


def dp_sum(values, meanwhile=()):
    for pos in range(lax.axis_size(DP).bit_length() - 1):
        values = values + send(values, dp_peers(1 << pos))
        if pos == 1:
            values, *meanwhile = tie(values, *meanwhile)
    return (values, *meanwhile) if meanwhile else values


def product(left, right, dims):
    return lax.dot_general(left, right, (dims, ((), ())), preferred_element_type=jnp.float32)


def fill_bias(spread_ref, bias):
    tokens = GRID * GRID
    for head in range(bias.shape[0]):
        spread = spread_ref[head] * LOG2E
        for row in range(GRID):
            off = (GRID - 1 - row) * GRID
            moved = spread if off == 0 else pltpu.roll(spread, SPREAD - off, 1)
            bias[head, row * GRID : (row + 1) * GRID, :] = moved[:, :tokens]


def head_slices(values, head, heads):
    width = heads * HD
    return [
        values[:, part * width + head * HD : part * width + (head + 1) * HD] for part in range(3)
    ]


def attention_kernel(heads, qkv_ref, spread_ref, out_ref, log_ref, bias):
    @pl.when(pl.program_id(0) == 0)
    def _():
        fill_bias(spread_ref, bias)

    values = qkv_ref[...]
    outs, logs = ([], [])
    for head in range(heads):
        query, key, value = head_slices(values, head, heads)
        scores = product(query, key, ((1,), (1,))) * (HD ** (-0.5) * LOG2E) + bias[head]
        top = jnp.max(scores, -1, keepdims=True)
        powers = jnp.exp2(scores - top)
        total = jnp.sum(powers, -1, keepdims=True)
        summed = product(powers.astype(jnp.bfloat16), value, ((1,), (0,)))
        outs.append((summed * (1.0 / total)).astype(jnp.bfloat16))
        logs.append(top + jnp.log2(total))
    out_ref[...] = jnp.concatenate(outs, 1)
    log_ref[...] = jnp.concatenate(logs, 1)


def attention(qkv, spread):
    rows, columns = qkv.shape
    heads = spread.shape[0]
    tokens = GRID * GRID
    return pl.pallas_call(
        functools.partial(attention_kernel, heads),
        grid=(rows // tokens,),
        in_specs=[
            pl.BlockSpec((tokens, columns), lambda step: (step, 0)),
            pl.BlockSpec(spread.shape, lambda step: (0, 0, 0)),
        ],
        out_specs=[
            pl.BlockSpec((tokens, heads * HD), lambda step: (step, 0)),
            pl.BlockSpec((tokens, heads), lambda step: (step, 0)),
        ],
        out_shape=[
            jax.ShapeDtypeStruct((rows, heads * HD), jnp.bfloat16),
            jax.ShapeDtypeStruct((rows, heads), jnp.float32),
        ],
        scratch_shapes=[pltpu.VMEM((heads, tokens, tokens), jnp.float32)],
        compiler_params=pltpu.CompilerParams(vmem_limit_bytes=VMEM),
        cost_estimate=pl.CostEstimate(
            flops=4 * rows * tokens * heads * 256,
            bytes_accessed=rows * columns * 4,
            transcendentals=rows * tokens * heads,
        ),
        name="attention",
    )(qkv, spread)


def attention_back_kernel(
    heads, qkv_ref, upstream_ref, log_ref, spread_ref, d_qkv_ref, d_spread_ref, bias, d_bias
):
    tokens = GRID * GRID

    @pl.when(pl.program_id(0) == 0)
    def _():
        fill_bias(spread_ref, bias)
        d_bias[...] = jnp.zeros_like(d_bias)

    values, upstream, logs = (qkv_ref[...], upstream_ref[...], log_ref[...])
    d_query, d_key, d_value = ([], [], [])
    for head in range(heads):
        query, key, value = head_slices(values, head, heads)
        d_out = upstream[:, head * HD : (head + 1) * HD]
        scores = product(query, key, ((1,), (1,))) * (HD ** (-0.5) * LOG2E) + bias[head]
        probs = jnp.exp2(scores - logs[:, head : head + 1])
        d_probs = product(d_out, value, ((1,), (1,)))
        d_scores = probs * (d_probs - jnp.sum(probs * d_probs, -1, keepdims=True))
        d_bias[head] += d_scores
        d_scores = d_scores.astype(jnp.bfloat16)
        d_query.append((product(d_scores, key, ((1,), (0,))) * HD ** (-0.5)).astype(jnp.bfloat16))
        d_key.append((product(d_scores, query, ((0,), (0,))) * HD ** (-0.5)).astype(jnp.bfloat16))
        d_value.append(
            product(probs.astype(jnp.bfloat16), d_out, ((0,), (0,))).astype(jnp.bfloat16)
        )
    pieces = d_query + d_key + d_value
    spare = d_qkv_ref.shape[1] - 3 * heads * HD
    if spare:
        pieces = pieces + [jnp.zeros((tokens, spare), jnp.bfloat16)]
    d_qkv_ref[...] = jnp.concatenate(pieces, 1)

    @pl.when(pl.program_id(0) == pl.num_programs(0) - 1)
    def _():
        for head in range(heads):
            total = jnp.zeros((GRID, SPREAD), jnp.float32)
            for row in range(GRID):
                off = (GRID - 1 - row) * GRID
                rows = d_bias[head, row * GRID : (row + 1) * GRID, :]
                wide = jnp.concatenate([rows, jnp.zeros((GRID, SPREAD - tokens), jnp.float32)], 1)
                total += wide if off == 0 else pltpu.roll(wide, off, 1)
            d_spread_ref[head] = total


def attention_back(qkv, upstream, logs, spread):
    rows, columns = qkv.shape
    heads = spread.shape[0]
    tokens = GRID * GRID
    return pl.pallas_call(
        functools.partial(attention_back_kernel, heads),
        grid=(rows // tokens,),
        in_specs=[
            pl.BlockSpec((tokens, columns), lambda step: (step, 0)),
            pl.BlockSpec((tokens, heads * HD), lambda step: (step, 0)),
            pl.BlockSpec((tokens, heads), lambda step: (step, 0)),
            pl.BlockSpec(spread.shape, lambda step: (0, 0, 0)),
        ],
        out_specs=[
            pl.BlockSpec((tokens, columns), lambda step: (step, 0)),
            pl.BlockSpec(spread.shape, lambda step: (0, 0, 0)),
        ],
        out_shape=[
            jax.ShapeDtypeStruct((rows, columns), jnp.bfloat16),
            jax.ShapeDtypeStruct(spread.shape, jnp.float32),
        ],
        scratch_shapes=[pltpu.VMEM((heads, tokens, tokens), jnp.float32)] * 2,
        compiler_params=pltpu.CompilerParams(vmem_limit_bytes=VMEM),
        cost_estimate=pl.CostEstimate(
            flops=10 * rows * tokens * heads * 256,
            bytes_accessed=rows * columns * 6,
            transcendentals=rows * tokens * heads,
        ),
        name="attention_back",
    )(qkv, upstream, logs, spread)


def whole_block(shape):
    return pl.BlockSpec(shape, lambda step: (0,) * len(shape), pipeline_mode=pl.Buffered(1))


def column_tile(columns, choices=(768, 896, 256)):
    return next((tile for tile in choices if columns % tile == 0), 128)


def feed_in_kernel(values_ref, weights_ref, act_ref, slope_ref):
    weights = weights_ref[...]
    rate = math.sqrt(2.0 / math.pi)
    cubic = 0.044715 * rate
    for row in range(0, values_ref.shape[0], 256):
        pre = product(values_ref[row : row + 256, :], weights, ((1,), (0,)))
        square = pre * pre
        gate = 0.5 + 0.5 * jnp.tanh(pre * (rate + cubic * square))
        act = pre * gate
        slope = gate + (act - act * gate) * (2.0 * rate + 6.0 * cubic * square)
        act_ref[row : row + 256, :] = act.astype(jnp.bfloat16)
        slope_ref[row : row + 256, :] = slope.astype(jnp.bfloat16)


def feed_in(values, weights, columns):
    rows, depth = values.shape
    tile = column_tile(columns)
    return pl.pallas_call(
        feed_in_kernel,
        grid=(columns // tile,),
        in_specs=[whole_block((rows, depth)), pl.BlockSpec((depth, tile), lambda step: (0, step))],
        out_specs=[pl.BlockSpec((rows, tile), lambda step: (0, step))] * 2,
        out_shape=[jax.ShapeDtypeStruct((rows, columns), jnp.bfloat16)] * 2,
        compiler_params=pltpu.CompilerParams(vmem_limit_bytes=VMEM),
        cost_estimate=pl.CostEstimate(
            flops=2 * rows * depth * columns,
            bytes_accessed=4 * rows * columns,
            transcendentals=rows * columns,
        ),
        name="feed_in",
    )(values, weights)


def feed_back_kernel(values_ref, weights_ref, slope_ref, out_ref):
    weights = weights_ref[...]
    for row in range(0, values_ref.shape[0], 256):
        d_act = product(values_ref[row : row + 256, :], weights, ((1,), (0,)))
        d_pre = d_act * slope_ref[row : row + 256, :].astype(jnp.float32)
        out_ref[row : row + 256, :] = d_pre.astype(jnp.bfloat16)


def feed_back(values, weights, slope):
    rows, depth = values.shape
    columns = weights.shape[1]
    tile = column_tile(columns)
    return pl.pallas_call(
        feed_back_kernel,
        grid=(columns // tile,),
        in_specs=[
            whole_block((rows, depth)),
            pl.BlockSpec((depth, tile), lambda step: (0, step)),
            pl.BlockSpec((rows, tile), lambda step: (0, step)),
        ],
        out_specs=pl.BlockSpec((rows, tile), lambda step: (0, step)),
        out_shape=jax.ShapeDtypeStruct((rows, columns), jnp.bfloat16),
        compiler_params=pltpu.CompilerParams(vmem_limit_bytes=VMEM),
        cost_estimate=pl.CostEstimate(
            flops=2 * rows * depth * columns,
            bytes_accessed=4 * rows * columns,
            transcendentals=0,
        ),
        name="feed_back",
    )(values, weights, slope)


def into_heads_kernel(values_ref, weights_ref, out_ref):
    weights = weights_ref[...]
    for row in range(0, values_ref.shape[0], 256):
        out_ref[row : row + 256, :] = product(
            values_ref[row : row + 256, :], weights, ((1,), (0,))
        ).astype(jnp.bfloat16)


def into_heads(values, weights):
    rows, depth = values.shape
    columns = weights.shape[1]
    tile = column_tile(columns)
    return pl.pallas_call(
        into_heads_kernel,
        grid=(columns // tile,),
        in_specs=[whole_block((rows, depth)), pl.BlockSpec((depth, tile), lambda step: (0, step))],
        out_specs=pl.BlockSpec((rows, tile), lambda step: (0, step)),
        out_shape=jax.ShapeDtypeStruct((rows, columns), jnp.bfloat16),
        compiler_params=pltpu.CompilerParams(vmem_limit_bytes=VMEM),
        cost_estimate=pl.CostEstimate(
            flops=2 * rows * depth * columns, bytes_accessed=2 * rows * columns, transcendentals=0
        ),
        name="into_heads",
    )(values, weights)


def out_of_kernel(values_ref, weights_ref, out_ref):
    out_ref[...] = product(values_ref[...], weights_ref[...], ((1,), (1,))).astype(out_ref.dtype)


def out_of(values, weights, kind):
    rows, depth = values.shape
    columns = weights.shape[0]
    tile = min(rows, 256)
    return pl.pallas_call(
        out_of_kernel,
        grid=(rows // tile,),
        in_specs=[pl.BlockSpec((tile, depth), lambda step: (step, 0)), whole_block((columns, depth))],
        out_specs=pl.BlockSpec((tile, columns), lambda step: (step, 0)),
        out_shape=jax.ShapeDtypeStruct((rows, columns), kind),
        compiler_params=pltpu.CompilerParams(vmem_limit_bytes=VMEM),
        cost_estimate=pl.CostEstimate(
            flops=2 * rows * depth * columns, bytes_accessed=4 * rows * columns, transcendentals=0
        ),
        name="out_of",
    )(values, weights)


def weight_grad_kernel(places, left_one, left_two, right_one, right_two, *refs):
    outs, total = (refs[:4], refs[4])
    total[...] = product(left_one[...], right_one[...], ((0,), (0,))) + product(
        left_two[...], right_two[...], ((0,), (0,))
    )
    count, rows = outs[0].shape[:2]
    for part in range(4):
        for row in range(count):
            first = pl.multiple_of(places[part * count + row] * rows, 8)
            outs[part][row] = total[pl.ds(first, rows), :].astype(jnp.bfloat16)


def weight_grad(left, right, places):
    rows, depth = left[0].shape
    columns = right[0].shape[1]
    total = places.shape[0]
    block = depth // total
    if block % 8:
        whole = outer_sum(left[0], right[0]) + outer_sum(left[1], right[1])
        return pick_blocks(whole.astype(jnp.bfloat16).reshape(total, block, columns), places)
    tile = column_tile(columns, (256,))

    def whole_left(shape):
        return pl.BlockSpec(shape, lambda step, _: (0, 0), pipeline_mode=pl.Buffered(1))

    return pl.pallas_call(
        weight_grad_kernel,
        grid_spec=pltpu.PrefetchScalarGridSpec(
            num_scalar_prefetch=1,
            grid=(columns // tile,),
            in_specs=[whole_left((rows, depth))] * 2
            + [pl.BlockSpec((rows, tile), lambda step, _: (0, step))] * 2,
            out_specs=[pl.BlockSpec((total // 4, block, tile), lambda step, _: (0, 0, step))] * 4,
            scratch_shapes=[pltpu.VMEM((depth, tile), jnp.float32)],
        ),
        out_shape=[jax.ShapeDtypeStruct((total // 4, block, columns), jnp.bfloat16)] * 4,
        compiler_params=pltpu.CompilerParams(vmem_limit_bytes=VMEM),
        cost_estimate=pl.CostEstimate(
            flops=4 * rows * depth * columns, bytes_accessed=4 * depth * columns, transcendentals=0
        ),
        name="weight_grad",
    )(places, *left, *right)


def shifts():
    offset = jnp.arange(SIDE, dtype=jnp.int32)[:, None, None]
    column = jnp.arange(GRID, dtype=jnp.int32)
    return (offset == GRID - 1 - column[:, None] + column[None, :]).astype(jnp.float32)


def spread_bias(relative):
    turned = relative.reshape(-1, SIDE, SIDE)[:, ::-1, ::-1]
    spread = jnp.einsum("hed,dxy->hxey", turned, shifts(), precision=HIGH)
    spread = spread.reshape(-1, GRID, SIDE * GRID)
    return jnp.pad(spread, ((0, 0), (0, 0), (0, SPREAD - SIDE * GRID)))


def gather_bias(d_spread):
    parts = d_spread[:, :, : SIDE * GRID].reshape(-1, GRID, SIDE, GRID)
    total = jnp.einsum("hxey,dxy->hed", parts, shifts(), precision=HIGH)
    return total[:, ::-1, ::-1].reshape(-1, SIDE * SIDE)


def core_half(values, core, starts, width):
    return [
        jnp.where(
            core == 0,
            values[:, start : start + width],
            values[:, start + width : start + 2 * width],
        )
        for start in starts
    ]


def both_cores(mine, other, core, axis):
    return jnp.where(
        core == 0,
        jnp.concatenate([mine, other], axis),
        jnp.concatenate([other, mine], axis),
    )


def segment_sums(values, bounds, first):
    place = jnp.arange(values.shape[0], dtype=jnp.int32)
    segment = first + sum((place >= bound).astype(jnp.int32) for bound in bounds)
    wanted = segment[None, :] == jnp.arange(11, dtype=jnp.int32)[:, None]
    return jnp.sum(jnp.where(wanted, values[None, :], 0.0), 1)


def mod_squares(values, core):
    columns = jnp.sum(values * values, 0)
    bound = 6 * D - core * values.shape[1]
    return segment_sums(columns, [bound], 4)


def embed_squares(values):
    bounds = [NCLASS + 1, NCLASS + 1 + FREQ, NCLASS + 1 + FREQ + D, NCLASS + 1 + FREQ + D + PDIM]
    return segment_sums(jnp.sum(values * values, 1), bounds, 6)


def block_squares(values):
    return segment_sums(jnp.sum(values * values, 0), [3 * D, 4 * D, 4 * D + MLPW], 0)


def adam_update(grad, first, second, weight, clip):
    first_new = FIRST_DECAY * first + (1.0 - FIRST_DECAY) * (grad * clip)
    second_new = SECOND_DECAY * second + (1.0 - SECOND_DECAY) * (grad * clip) ** 2
    update = (
        first_new
        / (1.0 - FIRST_DECAY**STEP)
        / (jnp.sqrt(second_new / (1.0 - SECOND_DECAY**STEP)) + ADAM_EPSILON)
        + WEIGHT_DECAY * weight
    )
    return (first_new, second_new, update)


def on_device(
    latents,
    noise,
    timesteps,
    labels,
    drops,
    block_weights,
    block_first,
    block_second,
    mod_weights,
    mod_first,
    mod_second,
    embed_weights,
    embed_first,
    embed_second,
    rel_bias,
    rel_first,
    rel_second,
):
    low = jnp.bfloat16
    wide = jnp.float32
    core = lax.axis_index("mod")
    spread = lax.axis_size(DP)
    images = latents.shape[0]
    length = latents.shape[1]
    rows = images * length
    share = embed_weights.shape[1]
    count = float(images * spread * lax.axis_size("mod") * length * latents.shape[2])
    relative, stacked = (relative_places(), stacked_places())

    start = NCLASS + 1
    chosen = jnp.where(drops == 1, NCLASS, labels)
    codes = jnp.stack([timesteps // 32, timesteps % 32, chosen // 32, chosen % 32], 1)
    codes = codes.astype(low)
    codes = both_cores(codes, swap_cores(codes), core, 0)
    code_rows = -(-codes.size // share)
    codes = jnp.pad(codes.reshape(-1), (0, code_rows * share - codes.size))
    small = jnp.concatenate(
        [
            embed_weights[start : start + FREQ].astype(low),
            embed_weights[start + FREQ + D :].astype(low),
            codes.reshape(code_rows, share),
        ],
        0,
    )
    half = D // 2
    wide_half = MLPW // 2
    small_far = gather_far(small)
    now_weights, small_far = tie(block_weights, small_far)
    block_low = now_weights.astype(low)
    q_part, k_part, v_part, p_part = core_half(
        block_low, core, [0, D, 2 * D, 3 * D], half
    )
    in_part, out_part = core_half(block_low, core, [4 * D, 4 * D + MLPW], wide_half)
    pad_part = jnp.zeros((block_low.shape[0], QKV_PAD - QKV_HALF), low)
    attn_part = jnp.concatenate([q_part, k_part, v_part, pad_part], 1)
    in_part = jnp.concatenate([in_part, p_part], 1)
    attn_far = gather_far(attn_part)
    small_second, small_third = gather_near(small_far)
    small = [small_far, small_second, small_third, gather_last(small_second)]
    later_weights, later_bias, later_embed, small[0] = tie(
        block_weights, rel_bias, embed_weights, small[0]
    )
    table = later_embed[:start].astype(low)
    time_out = later_embed[start + FREQ : start + FREQ + D].astype(low).astype(wide)
    everyone = jnp.concatenate([part[:, FREQ + 2 * PDIM :] for part in small], 0)
    everyone = everyone.reshape(spread, -1)[:, : 2 * images * 4]
    everyone = everyone.reshape(spread * 2 * images, 4).astype(wide)
    all_steps = 32.0 * everyone[:, 0] + everyone[:, 1]
    all_chosen = (32.0 * everyone[:, 2] + everyone[:, 3]).astype(jnp.int32)
    small = place_blocks(small, relative)[:, : FREQ + 2 * PDIM]
    small = small.transpose(1, 0, 2).reshape(FREQ + 2 * PDIM, D)
    time_in = small[:FREQ].astype(wide)
    patch = small[FREQ : FREQ + PDIM]
    head = small[FREQ + PDIM :]

    attn_second, attn_third = gather_near(attn_far)
    in_part, attn_far = tie(in_part, attn_far)
    in_far = far_stack(in_part)

    sinus = sinusoid(all_steps)
    pre_time = jnp.dot(sinus, time_in, precision=HIGH, preferred_element_type=wide)
    time_act = jax.nn.silu(pre_time)
    image_of = relative[:, None] * 2 * images + jnp.arange(2 * images, dtype=jnp.int32)[None, :]
    sorting = image_of.reshape(1, -1) == jnp.arange(image_of.size, dtype=jnp.int32)[:, None]

    def sort_images(values):
        return jnp.dot(sorting.astype(wide), values, precision=HIGH, preferred_element_type=wide)

    sorted_sinus = sort_images(sinus)
    sorted_act = sort_images(time_act)
    classes = jnp.arange(start, dtype=jnp.int32)[None, :]
    sorted_onehot = sort_images(all_chosen[:, None].astype(wide)).astype(jnp.int32) == classes
    first_column = lax.axis_index(DP) * share
    sorted_slope = sort_images(
        silu_slope(lax.dynamic_slice_in_dim(pre_time, first_column, share, 1))
    )
    onehot = all_chosen[:, None] == classes
    cond = jnp.dot(time_act, time_out, precision=HIGH, preferred_element_type=wide) + dense(
        onehot.astype(low), table
    )
    scaled = jax.nn.silu(cond).astype(low)
    scaled, attn_second, attn_third = tie(scaled, attn_second, attn_third)
    attn_both = gather_last(attn_second)
    mod_low = mod_weights.astype(low)
    mod_partial = dense(scaled, mod_low).astype(low)
    mod_parts = jnp.split(mod_partial.reshape(spread, 2 * images, -1), 4)
    heads = HEADS // 2
    bias_rows = spread_bias(jnp.where(core == 0, later_bias[:heads], later_bias[heads:]))
    block_weight_squares = block_squares(later_weights)
    half_mod, in_far, attn_both, bias_rows, block_weight_squares = scatter_parts(
        *mod_parts, meanwhile=(in_far, attn_both, bias_rows, block_weight_squares)
    )
    qkv_low = place_blocks([attn_far, attn_second, attn_third, attn_both], relative).reshape(D, -1)
    in_second, in_third = gather_near(in_far)
    out_part, in_far = tie(out_part, in_far)
    out_far = far_stack(out_part)
    mine = jnp.where(core == 0, half_mod[:images], half_mod[images:])
    theirs = jnp.where(core == 0, half_mod[images:], half_mod[:images])
    modulation = both_cores(mine, swap_cores(theirs), core, 1).reshape(images, 8, D)

    def moved(normed, shift):
        return (
            normed * (1.0 + modulation[:, shift + 1 : shift + 2]) + modulation[:, shift : shift + 1]
        ).astype(low)

    def flat(values):
        return values.reshape(rows, -1)

    def sum_cores(mine, theirs):
        return (mine + swap_cores(theirs).astype(wide)).reshape(images, length, -1)

    alpha_bar = jnp.sum(
        jnp.where(
            timesteps[:, None] == jnp.arange(NSTEPS, dtype=jnp.int32)[None, :],
            plan_table()[None, :],
            0.0,
        ),
        1,
    )
    mixed = (
        jnp.sqrt(alpha_bar)[:, None, None] * latents
        + jnp.sqrt(1.0 - alpha_bar)[:, None, None] * noise
    ).astype(low)
    hidden0 = dense(mixed, patch)
    normed1, inverse1 = layer_norm(hidden0)
    attn_in = flat(moved(normed1, 0))
    attn_in_two = swap_cores(attn_in)
    qkv = into_heads(attn_in, qkv_low)
    qkv_two = into_heads(attn_in_two, qkv_low)
    heads_two, logs_two = attention(qkv_two, bias_rows)
    qkv, logs_two, in_second, in_third, out_far = tie(qkv, logs_two, in_second, in_third, out_far)
    heads_two = swap_cores(heads_two)
    in_both = gather_last(in_second)
    out_second, out_third = gather_near(out_far)
    heads_one, logs = attention(qkv, bias_rows)
    heads_one, in_both, out_second = tie(heads_one, in_both, out_second)
    out_both = gather_last(out_second)
    in_low = place_blocks([in_far, in_second, in_third, in_both], stacked).reshape(D, -1)
    proj_half = in_low[:, wide_half:]
    proj_low = both_cores(proj_half, swap_cores(proj_half), core, 1)
    attn_out = both_cores(heads_one, heads_two, core, 1)
    branch_one = dense(attn_out, proj_low).reshape(images, length, D)
    hidden1 = hidden0 + modulation[:, 2:3] * branch_one
    normed2, inverse2 = layer_norm(hidden1)
    mlp_in = flat(moved(normed2, 3))
    mlp_in_two = swap_cores(mlp_in)
    mlp_in, out_third = tie(mlp_in, out_third)
    act, slope = feed_in(mlp_in, in_low, wide_half)
    act, mlp_in_two = tie(act, mlp_in_two)
    act_two, slope_two = feed_in(mlp_in_two, in_low, wide_half)
    act_two, out_both = tie(act_two, out_both)
    out_low = place_blocks([out_far, out_second, out_third, out_both], stacked).reshape(D, -1)
    branch_theirs = out_of(act_two, out_low, low)
    branch_two = sum_cores(out_of(act, out_low, wide), branch_theirs)
    hidden2 = hidden1 + modulation[:, 5:6] * branch_two

    normed3, inverse3 = layer_norm(hidden2)
    final_in = moved(normed3, 6)
    predicted = dense_trans(final_in, head)
    error = predicted - noise
    loss_here = jnp.sum(error * error)
    d_predicted = (error * (2.0 / count)).astype(low)
    d_final = dense(d_predicted, head)
    g_head = outer_sum(d_predicted, final_in)
    d_scale3 = jnp.sum(d_final * normed3, 1)
    d_shift3 = jnp.sum(d_final, 1)
    d_hidden2 = norm_back(d_final * (1.0 + modulation[:, 7:8]), normed3, inverse3)

    d_branch_two = flat((modulation[:, 5:6] * d_hidden2).astype(low))
    d_branch_two_two = swap_cores(d_branch_two)
    d_gate2 = jnp.sum(d_hidden2 * branch_two, 1)
    d_pre = feed_back(d_branch_two, out_low, slope)
    d_pre, d_branch_two_two = tie(d_pre, d_branch_two_two)
    d_pre_two = feed_back(d_branch_two_two, out_low, slope_two)
    out_own, out_second, out_third, out_both = weight_grad(
        (d_branch_two, d_branch_two_two), (act, act_two), stacked
    )
    out_back = send(out_both, plane_peers((2, 1)))
    d_pre, out_third = tie(d_pre, out_third)
    d_mlp_theirs = swap_cores(out_of(d_pre_two, in_low, low))
    d_mlp_mine = out_of(d_pre, in_low, wide)
    d_pre, d_mlp_mine, out_back = tie(d_pre, d_mlp_mine, out_back)
    out_second = send(add_low(out_second, out_back), plane_peers((1, 2)))
    out_third = send(out_third, plane_peers((2, 1)))
    in_own, in_second, in_third, in_both = weight_grad(
        (mlp_in, mlp_in_two), (d_pre, d_pre_two), stacked
    )
    in_both, d_mlp_theirs, d_mlp_mine = tie(in_both, d_mlp_theirs, d_mlp_mine)
    d_mlp_in = (d_mlp_mine + d_mlp_theirs.astype(wide)).reshape(images, length, D)
    d_scale2 = jnp.sum(d_mlp_in * normed2, 1)
    d_shift2 = jnp.sum(d_mlp_in, 1)
    d_hidden1 = d_hidden2 + norm_back(d_mlp_in * (1.0 + modulation[:, 4:5]), normed2, inverse2)
    d_branch_one = (modulation[:, 2:3] * d_hidden1).astype(low).reshape(rows, D)
    d_branch_one, out_second, out_third, in_both = tie(
        d_branch_one, out_second, out_third, in_both
    )
    in_back = send(in_both, plane_peers((2, 1)))
    g_out = far_share(add_low(add_low(out_own, out_third), out_second))
    d_gate1 = jnp.sum(d_hidden1 * branch_one, 1)
    d_attn_out = dense_trans(d_branch_one, proj_low).astype(low)
    d_mine = jnp.where(core == 0, d_attn_out[:, :half], d_attn_out[:, half:])
    d_theirs = jnp.where(core == 0, d_attn_out[:, half:], d_attn_out[:, :half])
    d_theirs = swap_cores(d_theirs)
    g_proj = outer_sum(attn_out, d_branch_one)
    g_proj_mine = jnp.where(core == 0, g_proj[:, :half], g_proj[:, half:])
    g_proj_theirs = jnp.where(core == 0, g_proj[:, half:], g_proj[:, :half]).astype(low)
    g_proj = (g_proj_mine + swap_cores(g_proj_theirs).astype(wide)).astype(low)
    d_mine, in_back, in_third, g_proj = tie(d_mine, in_back, in_third, g_proj)
    in_second = send(add_low(in_second, in_back), plane_peers((1, 2)))
    in_third = send(in_third, plane_peers((2, 1)))
    d_qkv, d_spread = attention_back(qkv, d_mine, logs, bias_rows)
    proj_own, proj_second, proj_third, proj_both = pick_blocks(
        g_proj.reshape(spread, -1, half), stacked
    )
    d_qkv, proj_both, d_theirs, g_out, in_second, in_third = tie(
        d_qkv, proj_both, d_theirs, g_out, in_second, in_third
    )
    g_in = far_share(add_low(add_low(in_own, in_third), in_second))
    proj_back = send(proj_both, plane_peers((2, 1)))
    d_qkv_two, d_spread_two = attention_back(qkv_two, d_theirs, logs_two, bias_rows)
    d_spread = d_spread + d_spread_two
    d_qkv_two, proj_back, proj_third = tie(d_qkv_two, proj_back, proj_third)
    proj_second = send(add_low(proj_second, proj_back), plane_peers((1, 2)))
    proj_third = send(proj_third, plane_peers((2, 1)))
    rel_half = gather_bias(d_spread)
    packed = jnp.concatenate([rel_half.reshape(-1), (loss_here * jnp.ones(1, wide))])
    bits = [1 << pos for pos in range(2, spread.bit_length() - 1)] + [1, 2]
    for bit in bits[:-3]:
        packed = packed + send(packed, dp_peers(bit))
    attn_own, attn_second, attn_third, attn_both = weight_grad(
        (attn_in, attn_in_two), (d_qkv, d_qkv_two), stacked
    )
    attn_both, proj_second, proj_third, packed = tie(attn_both, proj_second, proj_third, packed)
    packed = packed + send(packed, dp_peers(bits[-3]))
    g_proj = far_share(add_low(add_low(proj_own, proj_third), proj_second))
    attn_back = send(attn_both, plane_peers((2, 1)))
    d_qkv_two, attn_both, attn_third = tie(d_qkv_two, attn_both, attn_third)
    d_attn_theirs = out_of(d_qkv_two, qkv_low, low)
    d_qkv, d_attn_theirs, attn_back, packed = tie(d_qkv, d_attn_theirs, attn_back, packed)
    packed = packed + send(packed, dp_peers(bits[-2]))
    d_attn_theirs = swap_cores(d_attn_theirs)
    attn_second = send(add_low(attn_second, attn_back), plane_peers((1, 2)))
    attn_third = send(attn_third, plane_peers((2, 1)))
    d_attn_mine = out_of(d_qkv, qkv_low, wide)
    d_attn_mine, g_in, packed = tie(d_attn_mine, g_in, packed)
    packed = packed + send(packed, dp_peers(bits[-1]))
    d_attn_in = (d_attn_mine + d_attn_theirs.astype(wide)).reshape(images, length, D)
    d_scale1 = jnp.sum(d_attn_in * normed1, 1)
    d_shift1 = jnp.sum(d_attn_in, 1)
    d_hidden0 = d_hidden1 + norm_back(d_attn_in * (1.0 + modulation[:, 1:2]), normed1, inverse1)
    g_patch = outer_sum(mixed, d_hidden0.astype(low))

    d_modulation = jnp.stack(
        [d_shift1, d_scale1, d_gate1, d_shift2, d_scale2, d_gate2, d_shift3, d_scale3], 1
    )
    d_modulation = d_modulation.reshape(images, 8 * D).astype(low)
    mod_half = 4 * D
    d_keep = jnp.where(core == 0, d_modulation[:, :mod_half], d_modulation[:, mod_half:])
    d_give = jnp.where(core == 0, d_modulation[:, mod_half:], d_modulation[:, :mod_half])
    d_pair = both_cores(d_keep, swap_cores(d_give), core, 0)
    d_pair, attn_second, attn_third, packed = tie(d_pair, attn_second, attn_third, packed)
    d_far = gather_far(d_pair)
    attn_own, d_far, g_patch = tie(attn_own, d_far, g_patch)
    g_qkv = far_share(add_low(add_low(attn_own, attn_third), attn_second))
    d_second, d_third = gather_near(d_far)
    d_parts = [d_far, d_second, d_third, gather_last(d_second)]
    d_all = jnp.concatenate(d_parts, 0).reshape(spread * 2 * images, mod_half)
    mod_grad = outer_sum(scaled, d_all)
    d_scaled = dense_trans(d_all, mod_low)
    theirs = jnp.split(swap_cores(d_scaled), 4)
    d_scaled = d_scaled + jnp.concatenate([theirs[0], theirs[2], theirs[1], theirs[3]], 0)
    d_cond = sort_images(d_scaled * silu_slope(cond))
    g_table = first_contract(sorted_onehot.astype(wide), d_cond)
    g_time_out = first_contract(sorted_act, d_cond)
    d_time = lax.dot_general(
        d_cond, time_out, (((1,), (1,)), ((), ())), precision=HIGH, preferred_element_type=wide
    )
    g_ends = jnp.concatenate([g_patch, g_head], 0)
    g_ends = g_ends + swap_cores(g_ends)
    tail = jnp.concatenate([d_time, g_ends], 0)
    tail = tail.reshape(-1, spread, share).transpose(1, 0, 2)
    tail = scatter_parts(*pick_blocks(tail, relative))
    tail, g_qkv, g_proj = tie(tail, g_qkv, g_proj)
    d_time_here, g_ends = (tail[: -2 * PDIM], tail[-2 * PDIM :])
    g_time_in = first_contract(sorted_sinus, d_time_here * sorted_slope)
    embed_grad = jnp.concatenate([g_table, g_time_in, g_time_out, g_ends], 0)

    g_here = jnp.concatenate([g_qkv, g_in, g_proj, g_out], 1)
    g_there = swap_cores(g_here)
    g_mine = g_here.astype(wide)
    g_squares = segment_sums(
        jnp.sum(g_mine * g_mine, 0), [QKV_PAD, QKV_PAD + wide_half, QKV_PAD + wide_half + half], 0
    )
    g_squares = g_squares[jnp.array([0, 2, 1, 3] + list(range(4, 11)))]
    zero_part = jnp.where(core == 0, g_here, g_there)
    one_part = jnp.where(core == 0, g_there, g_here)
    after = QKV_PAD + wide_half
    spans = [(part * half, half) for part in range(3)] + [(after, half)]
    spans = spans + [(QKV_PAD, wide_half), (after + half, wide_half)]
    pieces = []
    for low_end, width in spans:
        pieces.append(zero_part[:, low_end : low_end + width])
        pieces.append(one_part[:, low_end : low_end + width])
    block_grad = jnp.concatenate(pieces, 1)

    packed_other = swap_cores(packed)
    rel_grad = both_cores(
        packed[:-1].reshape(heads, -1), packed_other[:-1].reshape(heads, -1), core, 0
    )
    loss_sum = packed[-1] + packed_other[-1]

    first_core = (core == 0).astype(wide)

    def replica_squares(block, mod, embed):
        return first_core * (block + embed_squares(embed)) + mod_squares(mod, core)

    squares = jnp.concatenate(
        [
            g_squares + mod_squares(mod_grad, core) + first_core * embed_squares(embed_grad),
            replica_squares(block_weight_squares, mod_weights, embed_weights),
        ]
    )
    squares, block_grad, rel_grad = all_sum(squares, (block_grad, rel_grad))
    block_grad = block_grad.astype(wide)
    grad_parts, weight_parts = jnp.split(squares, 2)
    grad_sq = jnp.concatenate([grad_parts, jnp.sum(rel_grad * rel_grad)[None]])
    weight_sq = jnp.concatenate([weight_parts, jnp.sum(rel_bias * rel_bias)[None]])
    grad_norm = jnp.sqrt(jnp.sum(grad_sq))
    clip = jnp.minimum(1.0, CLIP_NORM / grad_norm)
    block_m, block_s, block_step = adam_update(
        block_grad, block_first, block_second, block_weights, clip
    )
    mod_m, mod_s, mod_step = adam_update(mod_grad, mod_first, mod_second, mod_weights, clip)
    embed_m, embed_s, embed_step = adam_update(
        embed_grad, embed_first, embed_second, embed_weights, clip
    )
    rel_m, rel_s, rel_step = adam_update(rel_grad, rel_first, rel_second, rel_bias, clip)
    update_parts = all_sum(replica_squares(block_squares(block_step), mod_step, embed_step))
    update_sq = jnp.concatenate([update_parts, jnp.sum(rel_step * rel_step)[None]])
    weight_norm = jnp.sqrt(weight_sq)
    update_norm = jnp.sqrt(update_sq)
    ratio = weight_norm / update_norm
    def spread_ratio(length, bounds, first, shift=0):
        place = shift + jnp.arange(length, dtype=jnp.int32)
        chosen = ratio[first]
        for step, bound in enumerate(bounds):
            chosen = jnp.where(place >= bound, ratio[first + step + 1], chosen)
        return chosen

    block_ratio = spread_ratio(block_weights.shape[1], [3 * D, 4 * D, 4 * D + MLPW], 0)
    mod_columns = mod_weights.shape[1]
    mod_ratio = spread_ratio(mod_columns, [6 * D], 4, core * mod_columns)
    ends = start + FREQ + D
    embed_bounds = [start, start + FREQ, ends, ends + PDIM]
    embed_ratio = spread_ratio(embed_weights.shape[0], embed_bounds, 6)
    block_new = block_weights - LEARN_RATE * block_ratio[None, :] * block_step
    mod_new = mod_weights - LEARN_RATE * mod_ratio[None, :] * mod_step
    embed_new = embed_weights - LEARN_RATE * embed_ratio[:, None] * embed_step
    rel_new = rel_bias - LEARN_RATE * ratio[11] * rel_step
    matrix_norms = jnp.stack([weight_norm, update_norm])
    return (
        loss_sum,
        grad_norm,
        matrix_norms,
        block_new,
        block_m,
        block_s,
        block_new.astype(jnp.bfloat16),
        mod_new,
        mod_m,
        mod_s,
        mod_new.astype(jnp.bfloat16),
        embed_new,
        embed_m,
        embed_s,
        embed_new.astype(jnp.bfloat16),
        rel_new,
        rel_m,
        rel_s,
        rel_new.astype(jnp.bfloat16),
        rel_grad * clip,
    )


def solution(mesh):
    spread, pair = mesh.devices.shape
    grid = jax.sharding.Mesh(mesh.devices.reshape(spread // 4, 4, pair), DP + ("mod",))
    placed = (
        P(DP + ("mod",), None, None),
        P(DP + ("mod",), None, None),
        P(DP + ("mod",)),
        P(DP + ("mod",)),
        P(DP + ("mod",)),
        P(DP, None),
        P(DP, None),
        P(DP, None),
        P(DP, "mod"),
        P(DP, "mod"),
        P(DP, "mod"),
        P(None, DP),
        P(None, DP),
        P(None, DP),
        P(),
        P(),
        P(),
    )
    return jax.shard_map(
        on_device,
        mesh=grid,
        in_specs=placed,
        out_specs=(
            P(),
            P(),
            P(),
            P(DP, None),
            P(DP, None),
            P(DP, None),
            P(DP, None),
            P(DP, "mod"),
            P(DP, "mod"),
            P(DP, "mod"),
            P(DP, "mod"),
            P(None, DP),
            P(None, DP),
            P(None, DP),
            P(None, DP),
            P(),
            P(),
            P(),
            P(),
            P(),
        ),
        check_vma=False,
    )
```

```python
import functools
import math

import jax
import jax.numpy as jnp
from jax import lax
from jax.experimental import pallas as pl
from jax.experimental.pallas import tpu as pltpu
from jax.sharding import PartitionSpec as P

D = 1152
HEADS = 16
HD = 72
MLPW = 4608
NCLASS = 1000
FREQ = 256
GRID = 16
PDIM = 16
NSTEPS = 1000
STEP = 10
SIDE = 2 * GRID - 1
QKV_HALF = 3 * D // 2
QKV_PAD = -(-QKV_HALF // 128) * 128
SPREAD = 2 * GRID * GRID
DP = ("far", "near")
VMEM = 60 << 20
PACE = 1
LOG2E = math.log2(math.e)


FIRST_DECAY = 0.9
SECOND_DECAY = 0.999
ADAM_EPSILON = 1e-08
WEIGHT_DECAY = 0.01
LEARN_RATE = 0.25
CLIP_NORM = 0.05
HIGH = lax.Precision.HIGHEST


def dense(left, right):
    return jnp.dot(left, right, preferred_element_type=jnp.float32)


def dense_trans(left, right):
    return lax.dot_general(
        left, right, (((left.ndim - 1,), (1,)), ((), ())), preferred_element_type=jnp.float32
    )


def outer_sum(left, right):
    flat_left = left.reshape(-1, left.shape[-1])
    flat_right = right.reshape(-1, right.shape[-1])
    return lax.dot_general(
        flat_left, flat_right, (((0,), (0,)), ((), ())), preferred_element_type=jnp.float32
    )


def first_contract(left, right):
    return lax.dot_general(
        left, right, (((0,), (0,)), ((), ())), precision=HIGH, preferred_element_type=jnp.float32
    )


def layer_norm(values):
    center = values - jnp.mean(values, -1, keepdims=True)
    inverse = lax.rsqrt(jnp.mean(center * center, -1, keepdims=True) + 1e-06)
    return (center * inverse, inverse)


def norm_back(upstream, normed, inverse):
    return inverse * (
        upstream
        - jnp.mean(upstream, -1, keepdims=True)
        - normed * jnp.mean(upstream * normed, -1, keepdims=True)
    )


def silu_slope(values):
    sigma = jax.nn.sigmoid(values)
    return sigma * (1.0 + values * (1.0 - sigma))


def plan_table():
    betas = jnp.linspace(0.0001, 0.02, NSTEPS, dtype=jnp.float32)
    return jnp.exp(jnp.cumsum(jnp.log(1.0 - betas)))


def sinusoid(steps):
    half_width = FREQ // 2
    freqs = jnp.exp(-math.log(10000.0) * jnp.arange(half_width, dtype=jnp.float32) / half_width)
    angles = steps.astype(jnp.float32)[:, None] * freqs[None, :]
    return jnp.concatenate([jnp.cos(angles), jnp.sin(angles)], 1)


def dp_peers(mask):
    spread, pair = lax.axis_size(DP), lax.axis_size("mod")
    return [(i * pair + c, (i ^ mask) * pair + c) for i in range(spread) for c in range(pair)]


def plane_peers(masks):
    spread, pair = lax.axis_size(DP), lax.axis_size("mod")
    return [(i * pair + c, (i ^ masks[c]) * pair + c) for i in range(spread) for c in range(pair)]


def send(values, peers):
    return lax.ppermute(values, DP + ("mod",), peers)


def swap_cores(values):
    return lax.ppermute(values, "mod", [(0, 1), (1, 0)])


def far_groups():
    spread = lax.axis_size(DP)
    bits = [1 << k for k in range(2, spread.bit_length() - 1)]
    if len(bits) == 2:
        return [[bits[0], bits[1], bits[0] | bits[1]]]
    return [[bit] for bit in bits]


def far_masks():
    masks = [0]
    for group in far_groups():
        masks = masks + [mask | have for mask in group for have in masks]
    return masks


def block_places(far):
    me, core = lax.axis_index(DP), lax.axis_index("mod")
    second = jnp.where(core == 0, 1, 2)
    third = jnp.where(core == 0, 2, 1)
    near = jnp.stack([jnp.zeros_like(second), second, third, second | third])
    return ((me ^ near)[:, None] ^ far[None, :]).reshape(-1).astype(jnp.int32)


def relative_places():
    return block_places(jnp.array(far_masks(), jnp.int32))


def stacked_places():
    far = jnp.arange(lax.axis_size("far"), dtype=jnp.int32)
    return block_places(4 * (far ^ lax.axis_index("far")))


def move_kernel(slots, sources, targets, hold, in_sems, out_sems):
    total = len(sources)
    for first in range(0, total, slots):
        wave = range(first, min(first + slots, total))
        arriving = [
            pltpu.make_async_copy(sources[at], hold.at[at - first], in_sems.at[at]) for at in wave
        ]
        for copy in arriving:
            copy.start()
        leaving = []
        for at, copy in zip(wave, arriving):
            copy.wait()
            leaving.append(
                pltpu.make_async_copy(hold.at[at - first], targets[at], out_sems.at[at])
            )
            leaving[-1].start()
        for copy in leaving:
            copy.wait()


def place_kernel(counts, slots, places, *refs):
    ins, out = (refs[: len(counts)], refs[len(counts)])
    sources = [ins[part].at[row] for part, count in enumerate(counts) for row in range(count)]
    targets = [out.at[places[at]] for at in range(len(sources))]
    move_kernel(slots, sources, targets, *refs[len(counts) + 1 :])


def pick_kernel(counts, slots, places, source, *refs):
    outs = refs[: len(counts)]
    targets = [outs[part].at[row] for part, count in enumerate(counts) for row in range(count)]
    sources = [source.at[places[at]] for at in range(len(targets))]
    move_kernel(slots, sources, targets, *refs[len(counts) :])


def plane_slots(total, plane, kind):
    rows, columns = plane
    padded = -(-rows // 16) * 16 * -(-columns // 128) * 128 * jnp.dtype(kind).itemsize
    return max(1, min(total, (24 << 20) // padded))


def move_call(kernel, counts, places, operands, out_shape, out_count, plane, kind):
    total = sum(counts)
    slots = plane_slots(total, plane, kind)
    any_space = pl.BlockSpec(memory_space=pl.ANY)
    return pl.pallas_call(
        functools.partial(kernel, counts, slots),
        grid_spec=pltpu.PrefetchScalarGridSpec(
            num_scalar_prefetch=1,
            grid=(1,),
            in_specs=[any_space] * len(operands),
            out_specs=any_space if out_count is None else [any_space] * out_count,
            scratch_shapes=[
                pltpu.VMEM((slots,) + plane, kind),
                pltpu.SemaphoreType.DMA((total,)),
                pltpu.SemaphoreType.DMA((total,)),
            ],
        ),
        out_shape=out_shape,
        compiler_params=pltpu.CompilerParams(vmem_limit_bytes=VMEM),
        cost_estimate=pl.CostEstimate(
            flops=0,
            bytes_accessed=2 * total * plane[0] * plane[1] * jnp.dtype(kind).itemsize,
            transcendentals=0,
        ),
        name="move_blocks",
    )(places, *operands)


def place_blocks(parts, places):
    counts = [part.shape[0] for part in parts]
    plane, kind = (parts[0].shape[1:], parts[0].dtype)
    shape = jax.ShapeDtypeStruct((sum(counts),) + plane, kind)
    return move_call(place_kernel, counts, places, parts, shape, None, plane, kind)


def pick_blocks(values, places):
    counts = [values.shape[0] // 4] * 4
    plane, kind = (values.shape[1:], values.dtype)
    shape = [jax.ShapeDtypeStruct((count,) + plane, kind) for count in counts]
    return move_call(pick_kernel, counts, places, [values], shape, 4, plane, kind)


def tie(*values):
    return lax.optimization_barrier(values)


def gather_far(block):
    stack = block[None]
    for group in far_groups():
        stack = jnp.concatenate([stack] + [send(stack, dp_peers(mask)) for mask in group], 0)
    return stack


def gather_near(stack):
    return send(stack, plane_peers((1, 2))), send(stack, plane_peers((2, 1)))


def gather_last(second):
    return send(second, plane_peers((2, 1)))


def gather_parts(block):
    stack = gather_far(block)
    second, third = gather_near(stack)
    return [stack, second, third, gather_last(second)]


def far_stack(block):
    return lax.all_gather(block, "far", axis=0)


def far_share(stack):
    return lax.psum_scatter(stack, "far", scatter_dimension=0)


def add_low(left, right):
    return (left.astype(jnp.float32) + right.astype(jnp.float32)).astype(left.dtype)


def scatter_far(own):
    wide = jnp.float32
    for group in reversed(far_groups()):
        count = own.shape[0] // (len(group) + 1)
        total = own[:count].astype(wide)
        for pos, mask in enumerate(group):
            total = total + send(
                own[(pos + 1) * count : (pos + 2) * count], dp_peers(mask)
            ).astype(wide)
        own = total if count == 1 else total.astype(own.dtype)
    return own[0].astype(wide)


def scatter_parts(own, second, third, both, meanwhile=()):
    second = add_low(second, send(both, plane_peers((2, 1))))
    second, *meanwhile = tie(second, *meanwhile)
    from_third = send(third, plane_peers((2, 1)))
    from_second = send(second, plane_peers((1, 2)))
    share = scatter_far(add_low(add_low(own, from_third), from_second))
    return (share, *meanwhile) if meanwhile else share


def all_sum(values, meanwhile=()):
    return dp_sum(values + swap_cores(values), meanwhile)


def dp_sum(values, meanwhile=()):
    for pos in range(lax.axis_size(DP).bit_length() - 1):
        values = values + send(values, dp_peers(1 << pos))
        if pos == 1:
            values, *meanwhile = tie(values, *meanwhile)
    return (values, *meanwhile) if meanwhile else values


def product(left, right, dims):
    return lax.dot_general(left, right, (dims, ((), ())), preferred_element_type=jnp.float32)


def fill_bias(spread_ref, bias):
    tokens = GRID * GRID
    for head in range(bias.shape[0]):
        spread = spread_ref[head] * LOG2E
        for row in range(GRID):
            off = (GRID - 1 - row) * GRID
            moved = spread if off == 0 else pltpu.roll(spread, SPREAD - off, 1)
            bias[head, row * GRID : (row + 1) * GRID, :] = moved[:, :tokens]


def head_slices(values, head, heads):
    width = heads * HD
    return [
        values[:, part * width + head * HD : part * width + (head + 1) * HD] for part in range(3)
    ]


def attention_kernel(heads, qkv_ref, spread_ref, out_ref, log_ref, bias):
    @pl.when(pl.program_id(0) == 0)
    def _():
        fill_bias(spread_ref, bias)

    values = qkv_ref[...]
    outs, logs = ([], [])
    for head in range(heads):
        query, key, value = head_slices(values, head, heads)
        scores = product(query, key, ((1,), (1,))) * (HD ** (-0.5) * LOG2E) + bias[head]
        top = jnp.max(scores, -1, keepdims=True)
        powers = jnp.exp2(scores - top)
        total = jnp.sum(powers, -1, keepdims=True)
        summed = product(powers.astype(jnp.bfloat16), value, ((1,), (0,)))
        outs.append((summed * (1.0 / total)).astype(jnp.bfloat16))
        logs.append(top + jnp.log2(total))
    out_ref[...] = jnp.concatenate(outs, 1)
    log_ref[...] = jnp.concatenate(logs, 1)


def attention(qkv, spread):
    rows, columns = qkv.shape
    heads = spread.shape[0]
    tokens = GRID * GRID
    return pl.pallas_call(
        functools.partial(attention_kernel, heads),
        grid=(rows // tokens,),
        in_specs=[
            pl.BlockSpec((tokens, columns), lambda step: (step, 0)),
            pl.BlockSpec(spread.shape, lambda step: (0, 0, 0)),
        ],
        out_specs=[
            pl.BlockSpec((tokens, heads * HD), lambda step: (step, 0)),
            pl.BlockSpec((tokens, heads), lambda step: (step, 0)),
        ],
        out_shape=[
            jax.ShapeDtypeStruct((rows, heads * HD), jnp.bfloat16),
            jax.ShapeDtypeStruct((rows, heads), jnp.float32),
        ],
        scratch_shapes=[pltpu.VMEM((heads, tokens, tokens), jnp.float32)],
        compiler_params=pltpu.CompilerParams(vmem_limit_bytes=VMEM),
        cost_estimate=pl.CostEstimate(
            flops=4 * rows * tokens * heads * 256,
            bytes_accessed=rows * columns * 4,
            transcendentals=rows * tokens * heads,
        ),
        name="attention",
    )(qkv, spread)


def attention_back_kernel(
    heads, qkv_ref, upstream_ref, log_ref, spread_ref, d_qkv_ref, d_spread_ref, bias, d_bias
):
    tokens = GRID * GRID

    @pl.when(pl.program_id(0) == 0)
    def _():
        fill_bias(spread_ref, bias)
        d_bias[...] = jnp.zeros_like(d_bias)

    values, upstream, logs = (qkv_ref[...], upstream_ref[...], log_ref[...])
    d_query, d_key, d_value = ([], [], [])
    for head in range(heads):
        query, key, value = head_slices(values, head, heads)
        d_out = upstream[:, head * HD : (head + 1) * HD]
        scores = product(query, key, ((1,), (1,))) * (HD ** (-0.5) * LOG2E) + bias[head]
        probs = jnp.exp2(scores - logs[:, head : head + 1])
        d_probs = product(d_out, value, ((1,), (1,)))
        d_scores = probs * (d_probs - jnp.sum(probs * d_probs, -1, keepdims=True))
        d_bias[head] += d_scores
        d_scores = d_scores.astype(jnp.bfloat16)
        d_query.append((product(d_scores, key, ((1,), (0,))) * HD ** (-0.5)).astype(jnp.bfloat16))
        d_key.append((product(d_scores, query, ((0,), (0,))) * HD ** (-0.5)).astype(jnp.bfloat16))
        d_value.append(
            product(probs.astype(jnp.bfloat16), d_out, ((0,), (0,))).astype(jnp.bfloat16)
        )
    pieces = d_query + d_key + d_value
    spare = d_qkv_ref.shape[1] - 3 * heads * HD
    if spare:
        pieces = pieces + [jnp.zeros((tokens, spare), jnp.bfloat16)]
    d_qkv_ref[...] = jnp.concatenate(pieces, 1)

    @pl.when(pl.program_id(0) == pl.num_programs(0) - 1)
    def _():
        for head in range(heads):
            total = jnp.zeros((GRID, SPREAD), jnp.float32)
            for row in range(GRID):
                off = (GRID - 1 - row) * GRID
                rows = d_bias[head, row * GRID : (row + 1) * GRID, :]
                wide = jnp.concatenate([rows, jnp.zeros((GRID, SPREAD - tokens), jnp.float32)], 1)
                total += wide if off == 0 else pltpu.roll(wide, off, 1)
            d_spread_ref[head] = total


def attention_back(qkv, upstream, logs, spread):
    rows, columns = qkv.shape
    heads = spread.shape[0]
    tokens = GRID * GRID
    return pl.pallas_call(
        functools.partial(attention_back_kernel, heads),
        grid=(rows // tokens,),
        in_specs=[
            pl.BlockSpec((tokens, columns), lambda step: (step, 0)),
            pl.BlockSpec((tokens, heads * HD), lambda step: (step, 0)),
            pl.BlockSpec((tokens, heads), lambda step: (step, 0)),
            pl.BlockSpec(spread.shape, lambda step: (0, 0, 0)),
        ],
        out_specs=[
            pl.BlockSpec((tokens, columns), lambda step: (step, 0)),
            pl.BlockSpec(spread.shape, lambda step: (0, 0, 0)),
        ],
        out_shape=[
            jax.ShapeDtypeStruct((rows, columns), jnp.bfloat16),
            jax.ShapeDtypeStruct(spread.shape, jnp.float32),
        ],
        scratch_shapes=[pltpu.VMEM((heads, tokens, tokens), jnp.float32)] * 2,
        compiler_params=pltpu.CompilerParams(vmem_limit_bytes=VMEM),
        cost_estimate=pl.CostEstimate(
            flops=10 * rows * tokens * heads * 256,
            bytes_accessed=rows * columns * 6,
            transcendentals=rows * tokens * heads,
        ),
        name="attention_back",
    )(qkv, upstream, logs, spread)


def whole_block(shape):
    return pl.BlockSpec(shape, lambda step: (0,) * len(shape), pipeline_mode=pl.Buffered(1))


def column_tile(columns, choices=(768, 896, 256)):
    return next((tile for tile in choices if columns % tile == 0), 128)


def feed_in_kernel(values_ref, weights_ref, act_ref, slope_ref):
    weights = weights_ref[...]
    rate = math.sqrt(2.0 / math.pi)
    cubic = 0.044715 * rate
    for row in range(0, values_ref.shape[0], 256):
        pre = product(values_ref[row : row + 256, :], weights, ((1,), (0,)))
        square = pre * pre
        gate = 0.5 + 0.5 * jnp.tanh(pre * (rate + cubic * square))
        act = pre * gate
        slope = gate + (act - act * gate) * (2.0 * rate + 6.0 * cubic * square)
        act_ref[row : row + 256, :] = act.astype(jnp.bfloat16)
        slope_ref[row : row + 256, :] = slope.astype(jnp.bfloat16)


def feed_in(values, weights, columns):
    rows, depth = values.shape
    tile = column_tile(columns)
    return pl.pallas_call(
        feed_in_kernel,
        grid=(columns // tile,),
        in_specs=[whole_block((rows, depth)), pl.BlockSpec((depth, tile), lambda step: (0, step))],
        out_specs=[pl.BlockSpec((rows, tile), lambda step: (0, step))] * 2,
        out_shape=[jax.ShapeDtypeStruct((rows, columns), jnp.bfloat16)] * 2,
        compiler_params=pltpu.CompilerParams(vmem_limit_bytes=VMEM),
        cost_estimate=pl.CostEstimate(
            flops=2 * rows * depth * columns,
            bytes_accessed=4 * rows * columns,
            transcendentals=rows * columns,
        ),
        name="feed_in",
    )(values, weights)


def feed_back_kernel(values_ref, weights_ref, slope_ref, out_ref):
    weights = weights_ref[...]
    for row in range(0, values_ref.shape[0], 256):
        d_act = product(values_ref[row : row + 256, :], weights, ((1,), (0,)))
        d_pre = d_act * slope_ref[row : row + 256, :].astype(jnp.float32)
        out_ref[row : row + 256, :] = d_pre.astype(jnp.bfloat16)


def feed_back(values, weights, slope):
    rows, depth = values.shape
    columns = weights.shape[1]
    tile = column_tile(columns)
    return pl.pallas_call(
        feed_back_kernel,
        grid=(columns // tile,),
        in_specs=[
            whole_block((rows, depth)),
            pl.BlockSpec((depth, tile), lambda step: (0, step)),
            pl.BlockSpec((rows, tile), lambda step: (0, step)),
        ],
        out_specs=pl.BlockSpec((rows, tile), lambda step: (0, step)),
        out_shape=jax.ShapeDtypeStruct((rows, columns), jnp.bfloat16),
        compiler_params=pltpu.CompilerParams(vmem_limit_bytes=VMEM),
        cost_estimate=pl.CostEstimate(
            flops=2 * rows * depth * columns,
            bytes_accessed=4 * rows * columns,
            transcendentals=0,
        ),
        name="feed_back",
    )(values, weights, slope)


def into_heads_kernel(values_ref, weights_ref, out_ref):
    weights = weights_ref[...]
    for row in range(0, values_ref.shape[0], 256):
        out_ref[row : row + 256, :] = product(
            values_ref[row : row + 256, :], weights, ((1,), (0,))
        ).astype(jnp.bfloat16)


def into_heads(values, weights):
    rows, depth = values.shape
    columns = weights.shape[1]
    tile = column_tile(columns)
    return pl.pallas_call(
        into_heads_kernel,
        grid=(columns // tile,),
        in_specs=[whole_block((rows, depth)), pl.BlockSpec((depth, tile), lambda step: (0, step))],
        out_specs=pl.BlockSpec((rows, tile), lambda step: (0, step)),
        out_shape=jax.ShapeDtypeStruct((rows, columns), jnp.bfloat16),
        compiler_params=pltpu.CompilerParams(vmem_limit_bytes=VMEM),
        cost_estimate=pl.CostEstimate(
            flops=2 * rows * depth * columns, bytes_accessed=2 * rows * columns, transcendentals=0
        ),
        name="into_heads",
    )(values, weights)


def out_of_kernel(values_ref, weights_ref, out_ref):
    out_ref[...] = product(values_ref[...], weights_ref[...], ((1,), (1,))).astype(out_ref.dtype)


def out_of(values, weights, kind):
    rows, depth = values.shape
    columns = weights.shape[0]
    tile = min(rows, 256)
    return pl.pallas_call(
        out_of_kernel,
        grid=(rows // tile,),
        in_specs=[pl.BlockSpec((tile, depth), lambda step: (step, 0)), whole_block((columns, depth))],
        out_specs=pl.BlockSpec((tile, columns), lambda step: (step, 0)),
        out_shape=jax.ShapeDtypeStruct((rows, columns), kind),
        compiler_params=pltpu.CompilerParams(vmem_limit_bytes=VMEM),
        cost_estimate=pl.CostEstimate(
            flops=2 * rows * depth * columns, bytes_accessed=4 * rows * columns, transcendentals=0
        ),
        name="out_of",
    )(values, weights)


def weight_grad_kernel(places, left_one, left_two, right_one, right_two, *refs):
    outs, total = (refs[:4], refs[4])
    total[...] = product(left_one[...], right_one[...], ((0,), (0,))) + product(
        left_two[...], right_two[...], ((0,), (0,))
    )
    count, rows = outs[0].shape[:2]
    for part in range(4):
        for row in range(count):
            first = pl.multiple_of(places[part * count + row] * rows, 8)
            outs[part][row] = total[pl.ds(first, rows), :].astype(jnp.bfloat16)


def weight_grad(left, right, places):
    rows, depth = left[0].shape
    columns = right[0].shape[1]
    total = places.shape[0]
    block = depth // total
    if block % 8:
        whole = outer_sum(left[0], right[0]) + outer_sum(left[1], right[1])
        return pick_blocks(whole.astype(jnp.bfloat16).reshape(total, block, columns), places)
    tile = column_tile(columns, (256,))

    def whole_left(shape):
        return pl.BlockSpec(shape, lambda step, _: (0, 0), pipeline_mode=pl.Buffered(1))

    return pl.pallas_call(
        weight_grad_kernel,
        grid_spec=pltpu.PrefetchScalarGridSpec(
            num_scalar_prefetch=1,
            grid=(columns // tile,),
            in_specs=[whole_left((rows, depth))] * 2
            + [pl.BlockSpec((rows, tile), lambda step, _: (0, step))] * 2,
            out_specs=[pl.BlockSpec((total // 4, block, tile), lambda step, _: (0, 0, step))] * 4,
            scratch_shapes=[pltpu.VMEM((depth, tile), jnp.float32)],
        ),
        out_shape=[jax.ShapeDtypeStruct((total // 4, block, columns), jnp.bfloat16)] * 4,
        compiler_params=pltpu.CompilerParams(vmem_limit_bytes=VMEM),
        cost_estimate=pl.CostEstimate(
            flops=4 * rows * depth * columns, bytes_accessed=4 * depth * columns, transcendentals=0
        ),
        name="weight_grad",
    )(places, *left, *right)


def norm_rows(values):
    center = values - jnp.mean(values, -1, keepdims=True)
    inverse = lax.rsqrt(jnp.mean(center * center, -1, keepdims=True) + 1e-06)
    return center * inverse, inverse


def row_sum(values):
    return jnp.sum(values, 0, keepdims=True)


def image_call(kernel, name, operands, outs, images, sums=(), core=None):
    tokens = GRID * GRID
    lead = () if core is None else (core,)

    def spec(shape, whole):
        if whole:
            return pl.BlockSpec(
                shape, lambda step, *_: (0,) * len(shape), pipeline_mode=pl.Buffered(1)
            )
        if len(shape) == 3:
            return pl.BlockSpec((1,) + shape[1:], lambda step, *_: (step, 0, 0))
        return pl.BlockSpec((tokens, shape[1]), lambda step, *_: (step, 0))

    rows = images * tokens

    def is_whole(shape):
        return len(shape) == 2 and shape[0] != rows

    summed = [pl.BlockSpec(item.shape, lambda step, *_: (0, 0)) for item in sums]
    return pl.pallas_call(
        kernel,
        grid_spec=pltpu.PrefetchScalarGridSpec(
            num_scalar_prefetch=len(lead),
            grid=(images,),
            in_specs=[spec(item.shape, is_whole(item.shape)) for item in operands],
            out_specs=[spec(item.shape, False) for item in outs] + summed,
        ),
        out_shape=list(outs) + list(sums),
        compiler_params=pltpu.CompilerParams(vmem_limit_bytes=VMEM),
        cost_estimate=pl.CostEstimate(
            flops=4 * rows * D * D if lead else 64 * rows * D,
            bytes_accessed=16 * rows * D,
            transcendentals=0,
        ),
        name=name,
    )(*lead, *operands)


def core_rows(ref, core, mine):
    half = D // 2
    first = core * half if mine else (1 - core) * half
    return ref[pl.ds(pl.multiple_of(first, 16), half), :]


def merge_kernel(
    core_ref, one_ref, two_ref, mine_ref, other_ref, hidden_ref, mod_ref, branch_ref, out_ref, in_ref
):
    core = core_ref[0]
    one, two, mod = (one_ref[...], two_ref[...], mod_ref[0])

    def columns(ref):
        return product(one, core_rows(ref, core, True), ((1,), (0,))) + product(
            two, core_rows(ref, core, False), ((1,), (0,))
        )

    mine, other = (columns(mine_ref), columns(other_ref))
    first = jnp.where(core == 0, mine, other)
    branch = jnp.concatenate([first, jnp.where(core == 0, other, mine)], 1)
    hidden = hidden_ref[...] + mod[2:3] * branch
    normed, _ = norm_rows(hidden)
    branch_ref[...] = branch.astype(jnp.bfloat16)
    out_ref[...] = hidden
    in_ref[...] = (normed * (1.0 + mod[4:5]) + mod[3:4]).astype(jnp.bfloat16)


def ends_kernel(
    count, mine_ref, theirs_ref, hidden_ref, noise_ref, head_ref, mod_ref, *refs
):
    d_hidden_ref, d_branch_ref, d_mod_ref, g_head_ref, loss_ref = refs
    wide, low = (jnp.float32, jnp.bfloat16)

    @pl.when(pl.program_id(0) == 0)
    def _():
        g_head_ref[...] = jnp.zeros_like(g_head_ref)
        loss_ref[...] = jnp.zeros_like(loss_ref)

    mod, head = (mod_ref[0], head_ref[...])
    branch = mine_ref[...] + theirs_ref[...].astype(wide)
    normed, inverse = norm_rows(hidden_ref[...] + mod[5:6] * branch)
    final_in = (normed * (1.0 + mod[7:8]) + mod[6:7]).astype(low)
    error = product(final_in, head, ((1,), (1,))) - noise_ref[...]
    loss_ref[...] += jnp.sum(error * error)
    d_predicted = (error * (2.0 / count)).astype(low)
    d_final = product(d_predicted, head, ((1,), (0,)))
    g_head_ref[...] += product(d_predicted, final_in, ((0,), (0,)))
    d_hidden = norm_back(d_final * (1.0 + mod[7:8]), normed, inverse)
    d_hidden_ref[...] = d_hidden
    d_branch_ref[...] = (mod[5:6] * d_hidden).astype(low)
    blank = jnp.zeros((5, D), wide)
    gate, shift, scale = (row_sum(d_hidden * branch), row_sum(d_final), row_sum(d_final * normed))
    d_mod_ref[0] = jnp.concatenate([blank, gate, shift, scale], 0)


def merge_back_kernel(
    core_ref, mine_ref, theirs_ref, hidden_ref, branch_ref, d_hidden_ref, p_mine, p_other, mod_ref,
    d_mod_ref, *refs
):
    d_out_ref, d_branch_ref, d_one_ref, d_two_ref, d_mod_out_ref = refs
    core = core_ref[0]
    wide, low = (jnp.float32, jnp.bfloat16)
    mod, half = (mod_ref[0], D // 2)
    d_in = mine_ref[...] + theirs_ref[...].astype(wide)
    normed, inverse = norm_rows(hidden_ref[...])
    d_hidden = d_hidden_ref[...] + norm_back(d_in * (1.0 + mod[4:5]), normed, inverse)
    d_out_ref[...] = d_hidden
    gate = row_sum(d_hidden * branch_ref[...].astype(wide))
    d_branch = mod[2:3] * d_hidden
    d_branch_ref[...] = d_branch.astype(low)
    low_half, high_half = (d_branch[:, :half], d_branch[:, half:])
    d_mine = jnp.where(core == 0, low_half, high_half).astype(low)
    d_other = jnp.where(core == 0, high_half, low_half).astype(low)

    def heads(mine):
        return product(d_mine, core_rows(p_mine, core, mine), ((1,), (1,))) + product(
            d_other, core_rows(p_other, core, mine), ((1,), (1,))
        )

    d_one_ref[...] = heads(True).astype(low)
    d_two_ref[...] = heads(False).astype(low)
    blank = jnp.zeros((2, D), wide)
    sums = [blank, gate, row_sum(d_in), row_sum(d_in * normed), d_mod_ref[0][5:8]]
    d_mod_out_ref[0] = jnp.concatenate(sums, 0)


def start_back_kernel(
    mine_ref, theirs_ref, hidden_ref, d_hidden_ref, mixed_ref, mod_ref, d_mod_ref, *refs
):
    d_mod_out_ref, g_patch_ref = refs
    wide = jnp.float32

    @pl.when(pl.program_id(0) == 0)
    def _():
        g_patch_ref[...] = jnp.zeros_like(g_patch_ref)

    mod = mod_ref[0]
    d_in = mine_ref[...] + theirs_ref[...].astype(wide)
    normed, inverse = norm_rows(hidden_ref[...])
    d_hidden = d_hidden_ref[...] + norm_back(d_in * (1.0 + mod[1:2]), normed, inverse)
    g_patch_ref[...] += product(mixed_ref[...], d_hidden.astype(jnp.bfloat16), ((0,), (0,)))
    d_mod_out_ref[0] = jnp.concatenate(
        [row_sum(d_in), row_sum(d_in * normed), d_mod_ref[0][2:8]], 0
    )


def shifts():
    offset = jnp.arange(SIDE, dtype=jnp.int32)[:, None, None]
    column = jnp.arange(GRID, dtype=jnp.int32)
    return (offset == GRID - 1 - column[:, None] + column[None, :]).astype(jnp.float32)


def spread_bias(relative):
    turned = relative.reshape(-1, SIDE, SIDE)[:, ::-1, ::-1]
    spread = jnp.einsum("hed,dxy->hxey", turned, shifts(), precision=HIGH)
    spread = spread.reshape(-1, GRID, SIDE * GRID)
    return jnp.pad(spread, ((0, 0), (0, 0), (0, SPREAD - SIDE * GRID)))


def gather_bias(d_spread):
    parts = d_spread[:, :, : SIDE * GRID].reshape(-1, GRID, SIDE, GRID)
    total = jnp.einsum("hxey,dxy->hed", parts, shifts(), precision=HIGH)
    return total[:, ::-1, ::-1].reshape(-1, SIDE * SIDE)


def core_half(values, core, starts, width):
    return [
        jnp.where(
            core == 0,
            values[:, start : start + width],
            values[:, start + width : start + 2 * width],
        )
        for start in starts
    ]


def both_cores(mine, other, core, axis):
    return jnp.where(
        core == 0,
        jnp.concatenate([mine, other], axis),
        jnp.concatenate([other, mine], axis),
    )


def segment_sums(values, bounds, first):
    place = jnp.arange(values.shape[0], dtype=jnp.int32)
    segment = first + sum((place >= bound).astype(jnp.int32) for bound in bounds)
    wanted = segment[None, :] == jnp.arange(11, dtype=jnp.int32)[:, None]
    return jnp.sum(jnp.where(wanted, values[None, :], 0.0), 1)


def mod_squares(values, core):
    columns = jnp.sum(values * values, 0)
    bound = 6 * D - core * values.shape[1]
    return segment_sums(columns, [bound], 4)


def embed_squares(values):
    bounds = [NCLASS + 1, NCLASS + 1 + FREQ, NCLASS + 1 + FREQ + D, NCLASS + 1 + FREQ + D + PDIM]
    return segment_sums(jnp.sum(values * values, 1), bounds, 6)


def block_squares(values):
    return segment_sums(jnp.sum(values * values, 0), [3 * D, 4 * D, 4 * D + MLPW], 0)


def adam_update(grad, first, second, weight, clip):
    first_new = FIRST_DECAY * first + (1.0 - FIRST_DECAY) * (grad * clip)
    second_new = SECOND_DECAY * second + (1.0 - SECOND_DECAY) * (grad * clip) ** 2
    update = (
        first_new
        / (1.0 - FIRST_DECAY**STEP)
        / (jnp.sqrt(second_new / (1.0 - SECOND_DECAY**STEP)) + ADAM_EPSILON)
        + WEIGHT_DECAY * weight
    )
    return (first_new, second_new, update)


def on_device(
    latents,
    noise,
    timesteps,
    labels,
    drops,
    block_weights,
    block_first,
    block_second,
    mod_weights,
    mod_first,
    mod_second,
    embed_weights,
    embed_first,
    embed_second,
    rel_bias,
    rel_first,
    rel_second,
):
    low = jnp.bfloat16
    wide = jnp.float32
    core = lax.axis_index("mod")
    spread = lax.axis_size(DP)
    images = latents.shape[0]
    length = latents.shape[1]
    rows = images * length
    share = embed_weights.shape[1]
    count = float(images * spread * lax.axis_size("mod") * length * latents.shape[2])
    relative, stacked = (relative_places(), stacked_places())

    start = NCLASS + 1
    chosen = jnp.where(drops == 1, NCLASS, labels)
    codes = jnp.stack([timesteps // 32, timesteps % 32, chosen // 32, chosen % 32], 1)
    codes = codes.astype(low)
    codes = both_cores(codes, swap_cores(codes), core, 0)
    code_rows = -(-codes.size // share)
    codes = jnp.pad(codes.reshape(-1), (0, code_rows * share - codes.size))
    small = jnp.concatenate(
        [
            embed_weights[start : start + FREQ].astype(low),
            embed_weights[start + FREQ + D :].astype(low),
            codes.reshape(code_rows, share),
        ],
        0,
    )
    half = D // 2
    wide_half = MLPW // 2
    small_far = gather_far(small)
    now_weights, small_far = tie(block_weights, small_far)
    block_low = now_weights.astype(low)
    q_part, k_part, v_part, p_part = core_half(
        block_low, core, [0, D, 2 * D, 3 * D], half
    )
    in_part, out_part = core_half(block_low, core, [4 * D, 4 * D + MLPW], wide_half)
    pad_part = jnp.zeros((block_low.shape[0], QKV_PAD - QKV_HALF), low)
    attn_part = jnp.concatenate([q_part, k_part, v_part, pad_part], 1)
    in_part = jnp.concatenate([in_part, p_part], 1)
    attn_far = gather_far(attn_part)
    small_second, small_third = gather_near(small_far)
    small = [small_far, small_second, small_third, gather_last(small_second)]
    later_weights, later_bias, later_embed, small[0] = tie(
        block_weights, rel_bias, embed_weights, small[0]
    )
    table = later_embed[:start].astype(low)
    time_out = later_embed[start + FREQ : start + FREQ + D].astype(low).astype(wide)
    everyone = jnp.concatenate([part[:, FREQ + 2 * PDIM :] for part in small], 0)
    everyone = everyone.reshape(spread, -1)[:, : 2 * images * 4]
    everyone = everyone.reshape(spread * 2 * images, 4).astype(wide)
    all_steps = 32.0 * everyone[:, 0] + everyone[:, 1]
    all_chosen = (32.0 * everyone[:, 2] + everyone[:, 3]).astype(jnp.int32)
    small = place_blocks(small, relative)[:, : FREQ + 2 * PDIM]
    small = small.transpose(1, 0, 2).reshape(FREQ + 2 * PDIM, D)
    time_in = small[:FREQ].astype(wide)
    patch = small[FREQ : FREQ + PDIM]
    head = small[FREQ + PDIM :]

    attn_second, attn_third = gather_near(attn_far)
    in_part, attn_far = tie(in_part, attn_far)
    in_far = far_stack(in_part)

    sinus = sinusoid(all_steps)
    pre_time = jnp.dot(sinus, time_in, precision=HIGH, preferred_element_type=wide)
    time_act = jax.nn.silu(pre_time)
    image_of = relative[:, None] * 2 * images + jnp.arange(2 * images, dtype=jnp.int32)[None, :]
    sorting = image_of.reshape(1, -1) == jnp.arange(image_of.size, dtype=jnp.int32)[:, None]

    def sort_images(values):
        return jnp.dot(sorting.astype(wide), values, precision=HIGH, preferred_element_type=wide)

    sorted_sinus = sort_images(sinus)
    sorted_act = sort_images(time_act)
    classes = jnp.arange(start, dtype=jnp.int32)[None, :]
    sorted_onehot = sort_images(all_chosen[:, None].astype(wide)).astype(jnp.int32) == classes
    first_column = lax.axis_index(DP) * share
    sorted_slope = sort_images(
        silu_slope(lax.dynamic_slice_in_dim(pre_time, first_column, share, 1))
    )
    onehot = all_chosen[:, None] == classes
    cond = jnp.dot(time_act, time_out, precision=HIGH, preferred_element_type=wide) + dense(
        onehot.astype(low), table
    )
    scaled = jax.nn.silu(cond).astype(low)
    scaled, attn_second, attn_third = tie(scaled, attn_second, attn_third)
    attn_both = gather_last(attn_second)
    mod_low = mod_weights.astype(low)
    mod_partial = dense(scaled, mod_low).astype(low)
    mod_parts = jnp.split(mod_partial.reshape(spread, 2 * images, -1), 4)
    heads = HEADS // 2
    bias_rows = spread_bias(jnp.where(core == 0, later_bias[:heads], later_bias[heads:]))
    block_weight_squares = block_squares(later_weights)
    half_mod, in_far, attn_both, bias_rows, block_weight_squares = scatter_parts(
        *mod_parts, meanwhile=(in_far, attn_both, bias_rows, block_weight_squares)
    )
    qkv_low = place_blocks([attn_far, attn_second, attn_third, attn_both], relative).reshape(D, -1)
    in_second, in_third = gather_near(in_far)
    out_part, in_far = tie(out_part, in_far)
    out_far = far_stack(out_part)
    mine = jnp.where(core == 0, half_mod[:images], half_mod[images:])
    theirs = jnp.where(core == 0, half_mod[images:], half_mod[:images])
    modulation = both_cores(mine, swap_cores(theirs), core, 1).reshape(images, 8, D)

    def moved(normed, shift):
        return (
            normed * (1.0 + modulation[:, shift + 1 : shift + 2]) + modulation[:, shift : shift + 1]
        ).astype(low)

    def flat(values):
        return values.reshape(rows, -1)

    def sum_cores(mine, theirs):
        return (mine + swap_cores(theirs).astype(wide)).reshape(images, length, -1)

    alpha_bar = jnp.sum(
        jnp.where(
            timesteps[:, None] == jnp.arange(NSTEPS, dtype=jnp.int32)[None, :],
            plan_table()[None, :],
            0.0,
        ),
        1,
    )
    mixed = (
        jnp.sqrt(alpha_bar)[:, None, None] * latents
        + jnp.sqrt(1.0 - alpha_bar)[:, None, None] * noise
    ).astype(low)
    hidden0 = dense(mixed, patch)
    normed1, inverse1 = layer_norm(hidden0)
    attn_in = flat(moved(normed1, 0))
    attn_in_two = swap_cores(attn_in)
    qkv = into_heads(attn_in, qkv_low)
    qkv_two = into_heads(attn_in_two, qkv_low)
    heads_two, logs_two = attention(qkv_two, bias_rows)
    qkv, logs_two, in_second, in_third, out_far = tie(qkv, logs_two, in_second, in_third, out_far)
    heads_two = swap_cores(heads_two)
    in_both = gather_last(in_second)
    heads_one, logs = attention(qkv, bias_rows)
    heads_one, in_both, out_far = tie(heads_one, in_both, out_far)
    out_second, out_third = gather_near(out_far)
    in_low = place_blocks([in_far, in_second, in_third, in_both], stacked).reshape(D, -1)
    in_low, out_second = tie(in_low, out_second)
    proj_half = in_low[:, wide_half:]
    proj_other = swap_cores(proj_half)
    core_place = core.astype(jnp.int32).reshape(1)
    rows_wide = jax.ShapeDtypeStruct((rows, D), wide)
    rows_low = jax.ShapeDtypeStruct((rows, D), low)
    rows_heads = jax.ShapeDtypeStruct((rows, half), low)
    mod_shape = jax.ShapeDtypeStruct((images, 8, D), wide)
    patch_shape = jax.ShapeDtypeStruct((PDIM, D), wide)
    branch_one, hidden1, mlp_in = image_call(
        merge_kernel,
        "merge_heads",
        [heads_one, heads_two, proj_half, proj_other, flat(hidden0), modulation],
        [rows_low, rows_wide, rows_low],
        images,
        core=core_place,
    )
    mlp_in, out_third = tie(mlp_in, out_third)
    mlp_in_two = swap_cores(mlp_in)
    out_both = gather_last(out_second)
    act, slope = feed_in(mlp_in, in_low, wide_half)
    act, mlp_in_two, out_both = tie(act, mlp_in_two, out_both)
    act_two, slope_two = feed_in(mlp_in_two, in_low, wide_half)
    out_low = place_blocks([out_far, out_second, out_third, out_both], stacked).reshape(D, -1)
    branch_theirs = out_of(act_two, out_low, low)
    branch_theirs = swap_cores(branch_theirs)
    branch_mine = out_of(act, out_low, wide)
    d_hidden2, d_branch_two, d_mod, g_head, loss_tile = image_call(
        functools.partial(ends_kernel, count),
        "ends",
        [
            branch_mine,
            branch_theirs,
            hidden1,
            noise.reshape(rows, -1),
            head,
            modulation,
        ],
        [rows_wide, rows_low, mod_shape],
        images,
        sums=[patch_shape, jax.ShapeDtypeStruct((8, 128), wide)],
    )
    loss_here = loss_tile[0, 0]
    d_branch_two_two = swap_cores(d_branch_two)
    d_pre = feed_back(d_branch_two, out_low, slope)
    d_pre, d_branch_two_two = tie(d_pre, d_branch_two_two)
    d_pre_two = feed_back(d_branch_two_two, out_low, slope_two)
    out_own, out_second, out_third, out_both = weight_grad(
        (d_branch_two, d_branch_two_two), (act, act_two), stacked
    )
    out_back = send(out_both, plane_peers((2, 1)))
    d_pre, out_third = tie(d_pre, out_third)
    d_mlp_theirs = swap_cores(out_of(d_pre_two, in_low, low))
    d_mlp_mine = out_of(d_pre, in_low, wide)
    d_pre, d_mlp_mine, out_back = tie(d_pre, d_mlp_mine, out_back)
    out_second = send(add_low(out_second, out_back), plane_peers((1, 2)))
    out_third = send(out_third, plane_peers((2, 1)))
    in_own, in_second, in_third, in_both = weight_grad(
        (mlp_in, mlp_in_two), (d_pre, d_pre_two), stacked
    )
    in_both, d_mlp_theirs, d_mlp_mine = tie(in_both, d_mlp_theirs, d_mlp_mine)
    d_hidden1, d_branch_one, d_mine, d_theirs, d_mod = image_call(
        merge_back_kernel,
        "merge_heads_back",
        [
            d_mlp_mine,
            d_mlp_theirs,
            hidden1,
            branch_one,
            d_hidden2,
            proj_half,
            proj_other,
            modulation,
            d_mod,
        ],
        [rows_wide, rows_low, rows_heads, rows_heads, mod_shape],
        images,
        core=core_place,
    )
    d_branch_one, d_mine, out_second, out_third, in_both = tie(
        d_branch_one, d_mine, out_second, out_third, in_both
    )
    in_back = send(in_both, plane_peers((2, 1)))
    g_out = far_share(add_low(add_low(out_own, out_third), out_second))
    d_theirs = swap_cores(d_theirs)
    d_qkv, d_spread = attention_back(qkv, d_mine, logs, bias_rows)
    d_qkv, d_branch_one, d_theirs, in_back, in_third = tie(
        d_qkv, d_branch_one, d_theirs, in_back, in_third
    )
    in_second = send(add_low(in_second, in_back), plane_peers((1, 2)))
    in_third = send(in_third, plane_peers((2, 1)))
    g_proj = both_cores(
        outer_sum(heads_one, d_branch_one), outer_sum(heads_two, d_branch_one), core, 0
    )
    g_proj_mine = jnp.where(core == 0, g_proj[:, :half], g_proj[:, half:])
    g_proj_theirs = jnp.where(core == 0, g_proj[:, half:], g_proj[:, :half]).astype(low)
    g_proj = (g_proj_mine + swap_cores(g_proj_theirs).astype(wide)).astype(low)
    proj_own, proj_second, proj_third, proj_both = pick_blocks(
        g_proj.reshape(spread, -1, half), stacked
    )
    proj_both, d_theirs = tie(proj_both, d_theirs)
    proj_back = send(proj_both, plane_peers((2, 1)))
    d_qkv_two, d_spread_two = attention_back(qkv_two, d_theirs, logs_two, bias_rows)
    d_qkv_two, in_second, in_third, proj_back, proj_third, g_out = tie(
        d_qkv_two, in_second, in_third, proj_back, proj_third, g_out
    )
    g_in = far_share(add_low(add_low(in_own, in_third), in_second))
    d_spread = d_spread + d_spread_two
    proj_second = send(add_low(proj_second, proj_back), plane_peers((1, 2)))
    proj_third = send(proj_third, plane_peers((2, 1)))
    rel_half = gather_bias(d_spread)
    packed = jnp.concatenate([rel_half.reshape(-1), (loss_here * jnp.ones(1, wide))])
    bits = [1 << pos for pos in range(2, spread.bit_length() - 1)] + [1, 2]
    for bit in bits[:-3]:
        packed = packed + send(packed, dp_peers(bit))
    attn_own, attn_second, attn_third, attn_both = weight_grad(
        (attn_in, attn_in_two), (d_qkv, d_qkv_two), stacked
    )
    attn_both, proj_second, proj_third, packed = tie(attn_both, proj_second, proj_third, packed)
    packed = packed + send(packed, dp_peers(bits[-3]))
    g_proj = far_share(add_low(add_low(proj_own, proj_third), proj_second))
    attn_back = send(attn_both, plane_peers((2, 1)))
    d_qkv_two, attn_both, attn_third = tie(d_qkv_two, attn_both, attn_third)
    d_attn_theirs = out_of(d_qkv_two, qkv_low, low)
    d_qkv, d_attn_theirs, attn_back, packed = tie(d_qkv, d_attn_theirs, attn_back, packed)
    packed = packed + send(packed, dp_peers(bits[-2]))
    d_attn_theirs = swap_cores(d_attn_theirs)
    attn_second = send(add_low(attn_second, attn_back), plane_peers((1, 2)))
    attn_third = send(attn_third, plane_peers((2, 1)))
    d_attn_mine = out_of(d_qkv, qkv_low, wide)
    d_attn_mine, g_in, packed = tie(d_attn_mine, g_in, packed)
    packed = packed + send(packed, dp_peers(bits[-1]))
    d_mod, g_patch = image_call(
        start_back_kernel,
        "start_back",
        [
            d_attn_mine,
            d_attn_theirs,
            flat(hidden0),
            d_hidden1,
            flat(mixed),
            modulation,
            d_mod,
        ],
        [mod_shape],
        images,
        sums=[patch_shape],
    )

    d_modulation = d_mod.reshape(images, 8 * D).astype(low)
    mod_half = 4 * D
    d_keep = jnp.where(core == 0, d_modulation[:, :mod_half], d_modulation[:, mod_half:])
    d_give = jnp.where(core == 0, d_modulation[:, mod_half:], d_modulation[:, :mod_half])
    d_pair = both_cores(d_keep, swap_cores(d_give), core, 0)
    d_pair, attn_second, attn_third, packed = tie(d_pair, attn_second, attn_third, packed)
    d_far = gather_far(d_pair)
    attn_own, d_far = tie(attn_own, d_far)
    g_qkv = far_share(add_low(add_low(attn_own, attn_third), attn_second))
    d_second, d_third = gather_near(d_far)
    d_parts = [d_far, d_second, d_third, gather_last(d_second)]
    d_all = jnp.concatenate(d_parts, 0).reshape(spread * 2 * images, mod_half)
    mod_grad = outer_sum(scaled, d_all)
    d_scaled = dense_trans(d_all, mod_low)
    theirs = jnp.split(swap_cores(d_scaled), 4)
    d_scaled = d_scaled + jnp.concatenate([theirs[0], theirs[2], theirs[1], theirs[3]], 0)
    d_cond = sort_images(d_scaled * silu_slope(cond))
    g_table = first_contract(sorted_onehot.astype(wide), d_cond)
    g_time_out = first_contract(sorted_act, d_cond)
    d_time = lax.dot_general(
        d_cond, time_out, (((1,), (1,)), ((), ())), precision=HIGH, preferred_element_type=wide
    )
    g_ends = jnp.concatenate([g_patch, g_head], 0)
    g_ends = g_ends + swap_cores(g_ends)
    tail = jnp.concatenate([d_time, g_ends], 0)
    tail = tail.reshape(-1, spread, share).transpose(1, 0, 2)
    tail = scatter_parts(*pick_blocks(tail, relative))
    tail, g_qkv, g_proj = tie(tail, g_qkv, g_proj)
    d_time_here, g_ends = (tail[: -2 * PDIM], tail[-2 * PDIM :])
    g_time_in = first_contract(sorted_sinus, d_time_here * sorted_slope)
    embed_grad = jnp.concatenate([g_table, g_time_in, g_time_out, g_ends], 0)

    g_here = jnp.concatenate([g_qkv, g_in, g_proj, g_out], 1)
    g_there = swap_cores(g_here)
    g_mine = g_here.astype(wide)
    g_squares = segment_sums(
        jnp.sum(g_mine * g_mine, 0), [QKV_PAD, QKV_PAD + wide_half, QKV_PAD + wide_half + half], 0
    )
    g_squares = g_squares[jnp.array([0, 2, 1, 3] + list(range(4, 11)))]
    zero_part = jnp.where(core == 0, g_here, g_there)
    one_part = jnp.where(core == 0, g_there, g_here)
    after = QKV_PAD + wide_half
    spans = [(part * half, half) for part in range(3)] + [(after, half)]
    spans = spans + [(QKV_PAD, wide_half), (after + half, wide_half)]
    pieces = []
    for low_end, width in spans:
        pieces.append(zero_part[:, low_end : low_end + width])
        pieces.append(one_part[:, low_end : low_end + width])
    block_grad = jnp.concatenate(pieces, 1)

    packed_other = swap_cores(packed)
    rel_grad = both_cores(
        packed[:-1].reshape(heads, -1), packed_other[:-1].reshape(heads, -1), core, 0
    )
    loss_sum = packed[-1] + packed_other[-1]

    first_core = (core == 0).astype(wide)

    def replica_squares(block, mod, embed):
        return first_core * (block + embed_squares(embed)) + mod_squares(mod, core)

    squares = jnp.concatenate(
        [
            g_squares + mod_squares(mod_grad, core) + first_core * embed_squares(embed_grad),
            replica_squares(block_weight_squares, mod_weights, embed_weights),
        ]
    )
    squares, block_grad, rel_grad = all_sum(squares, (block_grad, rel_grad))
    block_grad = block_grad.astype(wide)
    grad_parts, weight_parts = jnp.split(squares, 2)
    grad_sq = jnp.concatenate([grad_parts, jnp.sum(rel_grad * rel_grad)[None]])
    weight_sq = jnp.concatenate([weight_parts, jnp.sum(rel_bias * rel_bias)[None]])
    grad_norm = jnp.sqrt(jnp.sum(grad_sq))
    clip = jnp.minimum(1.0, CLIP_NORM / grad_norm)
    block_m, block_s, block_step = adam_update(
        block_grad, block_first, block_second, block_weights, clip
    )
    mod_m, mod_s, mod_step = adam_update(mod_grad, mod_first, mod_second, mod_weights, clip)
    embed_m, embed_s, embed_step = adam_update(
        embed_grad, embed_first, embed_second, embed_weights, clip
    )
    rel_m, rel_s, rel_step = adam_update(rel_grad, rel_first, rel_second, rel_bias, clip)
    update_parts = all_sum(replica_squares(block_squares(block_step), mod_step, embed_step))
    update_sq = jnp.concatenate([update_parts, jnp.sum(rel_step * rel_step)[None]])
    weight_norm = jnp.sqrt(weight_sq)
    update_norm = jnp.sqrt(update_sq)
    ratio = weight_norm / update_norm
    def spread_ratio(length, bounds, first, shift=0):
        place = shift + jnp.arange(length, dtype=jnp.int32)
        chosen = ratio[first]
        for step, bound in enumerate(bounds):
            chosen = jnp.where(place >= bound, ratio[first + step + 1], chosen)
        return chosen

    block_ratio = spread_ratio(block_weights.shape[1], [3 * D, 4 * D, 4 * D + MLPW], 0)
    mod_columns = mod_weights.shape[1]
    mod_ratio = spread_ratio(mod_columns, [6 * D], 4, core * mod_columns)
    ends = start + FREQ + D
    embed_bounds = [start, start + FREQ, ends, ends + PDIM]
    embed_ratio = spread_ratio(embed_weights.shape[0], embed_bounds, 6)
    block_new = block_weights - LEARN_RATE * block_ratio[None, :] * block_step
    mod_new = mod_weights - LEARN_RATE * mod_ratio[None, :] * mod_step
    embed_new = embed_weights - LEARN_RATE * embed_ratio[:, None] * embed_step
    rel_new = rel_bias - LEARN_RATE * ratio[11] * rel_step
    matrix_norms = jnp.stack([weight_norm, update_norm])
    return (
        loss_sum,
        grad_norm,
        matrix_norms,
        block_new,
        block_m,
        block_s,
        block_new.astype(jnp.bfloat16),
        mod_new,
        mod_m,
        mod_s,
        mod_new.astype(jnp.bfloat16),
        embed_new,
        embed_m,
        embed_s,
        embed_new.astype(jnp.bfloat16),
        rel_new,
        rel_m,
        rel_s,
        rel_new.astype(jnp.bfloat16),
        rel_grad * clip,
    )


def solution(mesh):
    spread, pair = mesh.devices.shape
    grid = jax.sharding.Mesh(mesh.devices.reshape(spread // 4, 4, pair), DP + ("mod",))
    placed = (
        P(DP + ("mod",), None, None),
        P(DP + ("mod",), None, None),
        P(DP + ("mod",)),
        P(DP + ("mod",)),
        P(DP + ("mod",)),
        P(DP, None),
        P(DP, None),
        P(DP, None),
        P(DP, "mod"),
        P(DP, "mod"),
        P(DP, "mod"),
        P(None, DP),
        P(None, DP),
        P(None, DP),
        P(),
        P(),
        P(),
    )
    return jax.shard_map(
        on_device,
        mesh=grid,
        in_specs=placed,
        out_specs=(
            P(),
            P(),
            P(),
            P(DP, None),
            P(DP, None),
            P(DP, None),
            P(DP, None),
            P(DP, "mod"),
            P(DP, "mod"),
            P(DP, "mod"),
            P(DP, "mod"),
            P(None, DP),
            P(None, DP),
            P(None, DP),
            P(None, DP),
            P(),
            P(),
            P(),
            P(),
            P(),
        ),
        check_vma=False,
    )
```

```python
import functools
import math

import jax
import jax.numpy as jnp
from jax import lax
from jax.experimental import pallas as pl
from jax.experimental.pallas import tpu as pltpu
from jax.sharding import PartitionSpec as P

D = 1152
HEADS = 16
HD = 72
MLPW = 4608
NCLASS = 1000
FREQ = 256
GRID = 16
PDIM = 16
NSTEPS = 1000
STEP = 10
SIDE = 2 * GRID - 1
QKV_HALF = 3 * D // 2
QKV_PAD = -(-QKV_HALF // 128) * 128
SPREAD = 2 * GRID * GRID
DP = ("far", "near")
VMEM = 60 << 20
LOG2E = math.log2(math.e)
HALF_PAD = -(-D // 256) * 128


FIRST_DECAY = 0.9
SECOND_DECAY = 0.999
ADAM_EPSILON = 1e-08
WEIGHT_DECAY = 0.01
LEARN_RATE = 0.25
CLIP_NORM = 0.05
HIGH = lax.Precision.HIGHEST


def dense(left, right):
    return jnp.dot(left, right, preferred_element_type=jnp.float32)


def dense_trans(left, right):
    return lax.dot_general(
        left, right, (((left.ndim - 1,), (1,)), ((), ())), preferred_element_type=jnp.float32
    )


def outer_sum(left, right):
    flat_left = left.reshape(-1, left.shape[-1])
    flat_right = right.reshape(-1, right.shape[-1])
    return lax.dot_general(
        flat_left, flat_right, (((0,), (0,)), ((), ())), preferred_element_type=jnp.float32
    )


def first_contract(left, right):
    return lax.dot_general(
        left, right, (((0,), (0,)), ((), ())), precision=HIGH, preferred_element_type=jnp.float32
    )


def layer_norm(values):
    center = values - jnp.mean(values, -1, keepdims=True)
    inverse = lax.rsqrt(jnp.mean(center * center, -1, keepdims=True) + 1e-06)
    return (center * inverse, inverse)


def norm_back(upstream, normed, inverse):
    return inverse * (
        upstream
        - jnp.mean(upstream, -1, keepdims=True)
        - normed * jnp.mean(upstream * normed, -1, keepdims=True)
    )


def silu_slope(values):
    sigma = jax.nn.sigmoid(values)
    return sigma * (1.0 + values * (1.0 - sigma))


def plan_table():
    betas = jnp.linspace(0.0001, 0.02, NSTEPS, dtype=jnp.float32)
    return jnp.exp(jnp.cumsum(jnp.log(1.0 - betas)))


def sinusoid(steps):
    half_width = FREQ // 2
    freqs = jnp.exp(-math.log(10000.0) * jnp.arange(half_width, dtype=jnp.float32) / half_width)
    angles = steps.astype(jnp.float32)[:, None] * freqs[None, :]
    return jnp.concatenate([jnp.cos(angles), jnp.sin(angles)], 1)


def dp_peers(mask):
    spread, pair = lax.axis_size(DP), lax.axis_size("mod")
    return [(i * pair + c, (i ^ mask) * pair + c) for i in range(spread) for c in range(pair)]


def plane_peers(masks):
    spread, pair = lax.axis_size(DP), lax.axis_size("mod")
    return [(i * pair + c, (i ^ masks[c]) * pair + c) for i in range(spread) for c in range(pair)]


def send(values, peers):
    return lax.ppermute(values, DP + ("mod",), peers)


def swap_cores(values):
    return lax.ppermute(values, "mod", [(0, 1), (1, 0)])


def far_groups():
    spread = lax.axis_size(DP)
    bits = [1 << k for k in range(2, spread.bit_length() - 1)]
    if len(bits) == 2:
        return [[bits[0], bits[1], bits[0] | bits[1]]]
    return [[bit] for bit in bits]


def far_masks():
    masks = [0]
    for group in far_groups():
        masks = masks + [mask | have for mask in group for have in masks]
    return masks


def block_places(far):
    me, core = lax.axis_index(DP), lax.axis_index("mod")
    second = jnp.where(core == 0, 1, 2)
    third = jnp.where(core == 0, 2, 1)
    near = jnp.stack([jnp.zeros_like(second), second, third, second | third])
    return ((me ^ near)[:, None] ^ far[None, :]).reshape(-1).astype(jnp.int32)


def relative_places():
    return block_places(jnp.array(far_masks(), jnp.int32))


def stacked_places():
    far = jnp.arange(lax.axis_size("far"), dtype=jnp.int32)
    return block_places(4 * (far ^ lax.axis_index("far")))


def move_kernel(slots, sources, targets, hold, in_sems, out_sems):
    total = len(sources)
    for first in range(0, total, slots):
        wave = range(first, min(first + slots, total))
        arriving = [
            pltpu.make_async_copy(sources[at], hold.at[at - first], in_sems.at[at]) for at in wave
        ]
        for copy in arriving:
            copy.start()
        leaving = []
        for at, copy in zip(wave, arriving):
            copy.wait()
            leaving.append(
                pltpu.make_async_copy(hold.at[at - first], targets[at], out_sems.at[at])
            )
            leaving[-1].start()
        for copy in leaving:
            copy.wait()


def place_kernel(counts, slots, places, *refs):
    ins, out = (refs[: len(counts)], refs[len(counts)])
    sources = [ins[part].at[row] for part, count in enumerate(counts) for row in range(count)]
    targets = [out.at[places[at]] for at in range(len(sources))]
    move_kernel(slots, sources, targets, *refs[len(counts) + 1 :])


def pick_kernel(counts, slots, places, source, *refs):
    outs = refs[: len(counts)]
    targets = [outs[part].at[row] for part, count in enumerate(counts) for row in range(count)]
    sources = [source.at[places[at]] for at in range(len(targets))]
    move_kernel(slots, sources, targets, *refs[len(counts) :])


def plane_slots(total, plane, kind):
    rows, columns = plane
    padded = -(-rows // 16) * 16 * -(-columns // 128) * 128 * jnp.dtype(kind).itemsize
    return max(1, min(total, (24 << 20) // padded))


def move_call(kernel, counts, places, operands, out_shape, out_count, plane, kind):
    total = sum(counts)
    slots = plane_slots(total, plane, kind)
    any_space = pl.BlockSpec(memory_space=pl.ANY)
    return pl.pallas_call(
        functools.partial(kernel, counts, slots),
        grid_spec=pltpu.PrefetchScalarGridSpec(
            num_scalar_prefetch=1,
            grid=(1,),
            in_specs=[any_space] * len(operands),
            out_specs=any_space if out_count is None else [any_space] * out_count,
            scratch_shapes=[
                pltpu.VMEM((slots,) + plane, kind),
                pltpu.SemaphoreType.DMA((total,)),
                pltpu.SemaphoreType.DMA((total,)),
            ],
        ),
        out_shape=out_shape,
        compiler_params=pltpu.CompilerParams(vmem_limit_bytes=VMEM),
        cost_estimate=pl.CostEstimate(
            flops=0,
            bytes_accessed=2 * total * plane[0] * plane[1] * jnp.dtype(kind).itemsize,
            transcendentals=0,
        ),
        name="move_blocks",
    )(places, *operands)


def place_blocks(parts, places):
    counts = [part.shape[0] for part in parts]
    plane, kind = (parts[0].shape[1:], parts[0].dtype)
    shape = jax.ShapeDtypeStruct((sum(counts),) + plane, kind)
    return move_call(place_kernel, counts, places, parts, shape, None, plane, kind)


def pick_blocks(values, places):
    counts = [values.shape[0] // 4] * 4
    plane, kind = (values.shape[1:], values.dtype)
    shape = [jax.ShapeDtypeStruct((count,) + plane, kind) for count in counts]
    return move_call(pick_kernel, counts, places, [values], shape, 4, plane, kind)


def tie(*values):
    return lax.optimization_barrier(values)


def gather_far(block):
    stack = block[None]
    for group in far_groups():
        stack = jnp.concatenate([stack] + [send(stack, dp_peers(mask)) for mask in group], 0)
    return stack


def gather_near(stack):
    return send(stack, plane_peers((1, 2))), send(stack, plane_peers((2, 1)))


def gather_last(second):
    return send(second, plane_peers((2, 1)))


def gather_parts(block):
    stack = gather_far(block)
    second, third = gather_near(stack)
    return [stack, second, third, gather_last(second)]


def far_stack(block):
    return lax.all_gather(block, "far", axis=0)


def far_share(stack):
    return lax.psum_scatter(stack, "far", scatter_dimension=0)


def add_low(left, right):
    return (left.astype(jnp.float32) + right.astype(jnp.float32)).astype(left.dtype)


def scatter_far(own):
    wide = jnp.float32
    for group in reversed(far_groups()):
        count = own.shape[0] // (len(group) + 1)
        total = own[:count].astype(wide)
        for pos, mask in enumerate(group):
            total = total + send(
                own[(pos + 1) * count : (pos + 2) * count], dp_peers(mask)
            ).astype(wide)
        own = total if count == 1 else total.astype(own.dtype)
    return own[0].astype(wide)


def scatter_parts(own, second, third, both, meanwhile=()):
    second = add_low(second, send(both, plane_peers((2, 1))))
    second, *meanwhile = tie(second, *meanwhile)
    from_third = send(third, plane_peers((2, 1)))
    from_second = send(second, plane_peers((1, 2)))
    share = scatter_far(add_low(add_low(own, from_third), from_second))
    return (share, *meanwhile) if meanwhile else share


def all_sum(values, meanwhile=()):
    return dp_sum(values + swap_cores(values), meanwhile)


def dp_sum(values, meanwhile=()):
    for pos in range(lax.axis_size(DP).bit_length() - 1):
        values = values + send(values, dp_peers(1 << pos))
        if pos == 1:
            values, *meanwhile = tie(values, *meanwhile)
    return (values, *meanwhile) if meanwhile else values


def product(left, right, dims):
    return lax.dot_general(left, right, (dims, ((), ())), preferred_element_type=jnp.float32)


def fill_bias(spread_ref, bias):
    tokens = GRID * GRID
    for head in range(bias.shape[0]):
        spread = spread_ref[head] * LOG2E
        for row in range(GRID):
            off = (GRID - 1 - row) * GRID
            moved = spread if off == 0 else pltpu.roll(spread, SPREAD - off, 1)
            bias[head, row * GRID : (row + 1) * GRID, :] = moved[:, :tokens]


def head_slices(values, head, heads):
    width = heads * HD
    return [
        values[:, part * width + head * HD : part * width + (head + 1) * HD] for part in range(3)
    ]


def attention_kernel(heads, qkv_ref, spread_ref, out_ref, log_ref, bias):
    @pl.when(pl.program_id(0) == 0)
    def _():
        fill_bias(spread_ref, bias)

    values = qkv_ref[...]
    outs, logs = ([], [])
    for head in range(heads):
        query, key, value = head_slices(values, head, heads)
        scores = product(query, key, ((1,), (1,))) * (HD ** (-0.5) * LOG2E) + bias[head]
        top = jnp.max(scores, -1, keepdims=True)
        powers = jnp.exp2(scores - top)
        total = jnp.sum(powers, -1, keepdims=True)
        summed = product(powers.astype(jnp.bfloat16), value, ((1,), (0,)))
        outs.append((summed * (1.0 / total)).astype(jnp.bfloat16))
        logs.append(top + jnp.log2(total))
    spare = out_ref.shape[1] - heads * HD
    if spare:
        outs.append(jnp.zeros((values.shape[0], spare), jnp.bfloat16))
    out_ref[...] = jnp.concatenate(outs, 1)
    log_ref[...] = jnp.concatenate(logs, 1)


def attention(qkv, spread):
    rows, columns = qkv.shape
    heads = spread.shape[0]
    tokens = GRID * GRID
    return pl.pallas_call(
        functools.partial(attention_kernel, heads),
        grid=(rows // tokens,),
        in_specs=[
            pl.BlockSpec((tokens, columns), lambda step: (step, 0)),
            pl.BlockSpec(spread.shape, lambda step: (0, 0, 0)),
        ],
        out_specs=[
            pl.BlockSpec((tokens, HALF_PAD), lambda step: (step, 0)),
            pl.BlockSpec((tokens, heads), lambda step: (step, 0)),
        ],
        out_shape=[
            jax.ShapeDtypeStruct((rows, HALF_PAD), jnp.bfloat16),
            jax.ShapeDtypeStruct((rows, heads), jnp.float32),
        ],
        scratch_shapes=[pltpu.VMEM((heads, tokens, tokens), jnp.float32)],
        compiler_params=pltpu.CompilerParams(vmem_limit_bytes=VMEM),
        cost_estimate=pl.CostEstimate(
            flops=4 * rows * tokens * heads * 256,
            bytes_accessed=rows * columns * 4,
            transcendentals=rows * tokens * heads,
        ),
        name="attention",
    )(qkv, spread)


def attention_back_kernel(
    heads, qkv_ref, upstream_ref, log_ref, spread_ref, d_qkv_ref, d_spread_ref, bias, d_bias
):
    tokens = GRID * GRID

    @pl.when(pl.program_id(0) == 0)
    def _():
        fill_bias(spread_ref, bias)
        d_bias[...] = jnp.zeros_like(d_bias)

    values, upstream, logs = (qkv_ref[...], upstream_ref[...], log_ref[...])
    d_query, d_key, d_value = ([], [], [])
    for head in range(heads):
        query, key, value = head_slices(values, head, heads)
        d_out = upstream[:, head * HD : (head + 1) * HD]
        scores = product(query, key, ((1,), (1,))) * (HD ** (-0.5) * LOG2E) + bias[head]
        probs = jnp.exp2(scores - logs[:, head : head + 1])
        d_probs = product(d_out, value, ((1,), (1,)))
        d_scores = probs * (d_probs - jnp.sum(probs * d_probs, -1, keepdims=True))
        d_bias[head] += d_scores
        d_scores = d_scores.astype(jnp.bfloat16)
        d_query.append((product(d_scores, key, ((1,), (0,))) * HD ** (-0.5)).astype(jnp.bfloat16))
        d_key.append((product(d_scores, query, ((0,), (0,))) * HD ** (-0.5)).astype(jnp.bfloat16))
        d_value.append(
            product(probs.astype(jnp.bfloat16), d_out, ((0,), (0,))).astype(jnp.bfloat16)
        )
    pieces = d_query + d_key + d_value
    spare = d_qkv_ref.shape[1] - 3 * heads * HD
    if spare:
        pieces = pieces + [jnp.zeros((tokens, spare), jnp.bfloat16)]
    d_qkv_ref[...] = jnp.concatenate(pieces, 1)

    @pl.when(pl.program_id(0) == pl.num_programs(0) - 1)
    def _():
        for head in range(heads):
            total = jnp.zeros((GRID, SPREAD), jnp.float32)
            for row in range(GRID):
                off = (GRID - 1 - row) * GRID
                rows = d_bias[head, row * GRID : (row + 1) * GRID, :]
                wide = jnp.concatenate([rows, jnp.zeros((GRID, SPREAD - tokens), jnp.float32)], 1)
                total += wide if off == 0 else pltpu.roll(wide, off, 1)
            d_spread_ref[head] = total


def attention_back(qkv, upstream, logs, spread):
    rows, columns = qkv.shape
    heads = spread.shape[0]
    tokens = GRID * GRID
    return pl.pallas_call(
        functools.partial(attention_back_kernel, heads),
        grid=(rows // tokens,),
        in_specs=[
            pl.BlockSpec((tokens, columns), lambda step: (step, 0)),
            pl.BlockSpec((tokens, upstream.shape[1]), lambda step: (step, 0)),
            pl.BlockSpec((tokens, heads), lambda step: (step, 0)),
            pl.BlockSpec(spread.shape, lambda step: (0, 0, 0)),
        ],
        out_specs=[
            pl.BlockSpec((tokens, columns), lambda step: (step, 0)),
            pl.BlockSpec(spread.shape, lambda step: (0, 0, 0)),
        ],
        out_shape=[
            jax.ShapeDtypeStruct((rows, columns), jnp.bfloat16),
            jax.ShapeDtypeStruct(spread.shape, jnp.float32),
        ],
        scratch_shapes=[pltpu.VMEM((heads, tokens, tokens), jnp.float32)] * 2,
        compiler_params=pltpu.CompilerParams(vmem_limit_bytes=VMEM),
        cost_estimate=pl.CostEstimate(
            flops=10 * rows * tokens * heads * 256,
            bytes_accessed=rows * columns * 6,
            transcendentals=rows * tokens * heads,
        ),
        name="attention_back",
    )(qkv, upstream, logs, spread)


def whole_block(shape):
    return pl.BlockSpec(shape, lambda step: (0,) * len(shape), pipeline_mode=pl.Buffered(1))


def column_tile(columns, choices=(768, 896, 256)):
    return next((tile for tile in choices if columns % tile == 0), 128)


def feed_in_kernel(values_ref, weights_ref, act_ref, slope_ref):
    weights = weights_ref[...]
    rate = math.sqrt(2.0 / math.pi)
    cubic = 0.044715 * rate
    for row in range(0, values_ref.shape[0], 256):
        pre = product(values_ref[row : row + 256, :], weights, ((1,), (0,)))
        square = pre * pre
        gate = 0.5 + 0.5 * jnp.tanh(pre * (rate + cubic * square))
        act = pre * gate
        slope = gate + (act - act * gate) * (2.0 * rate + 6.0 * cubic * square)
        act_ref[row : row + 256, :] = act.astype(jnp.bfloat16)
        slope_ref[row : row + 256, :] = slope.astype(jnp.bfloat16)


def feed_in(values, weights, columns):
    rows, depth = values.shape
    tile = column_tile(columns)
    return pl.pallas_call(
        feed_in_kernel,
        grid=(columns // tile,),
        in_specs=[whole_block((rows, depth)), pl.BlockSpec((depth, tile), lambda step: (0, step))],
        out_specs=[pl.BlockSpec((rows, tile), lambda step: (0, step))] * 2,
        out_shape=[jax.ShapeDtypeStruct((rows, columns), jnp.bfloat16)] * 2,
        compiler_params=pltpu.CompilerParams(vmem_limit_bytes=VMEM),
        cost_estimate=pl.CostEstimate(
            flops=2 * rows * depth * columns,
            bytes_accessed=4 * rows * columns,
            transcendentals=rows * columns,
        ),
        name="feed_in",
    )(values, weights)


def feed_back_kernel(values_ref, weights_ref, slope_ref, out_ref):
    weights = weights_ref[...]
    for row in range(0, values_ref.shape[0], 256):
        d_act = product(values_ref[row : row + 256, :], weights, ((1,), (0,)))
        d_pre = d_act * slope_ref[row : row + 256, :].astype(jnp.float32)
        out_ref[row : row + 256, :] = d_pre.astype(jnp.bfloat16)


def feed_back(values, weights, slope):
    rows, depth = values.shape
    columns = weights.shape[1]
    tile = column_tile(columns)
    return pl.pallas_call(
        feed_back_kernel,
        grid=(columns // tile,),
        in_specs=[
            whole_block((rows, depth)),
            pl.BlockSpec((depth, tile), lambda step: (0, step)),
            pl.BlockSpec((rows, tile), lambda step: (0, step)),
        ],
        out_specs=pl.BlockSpec((rows, tile), lambda step: (0, step)),
        out_shape=jax.ShapeDtypeStruct((rows, columns), jnp.bfloat16),
        compiler_params=pltpu.CompilerParams(vmem_limit_bytes=VMEM),
        cost_estimate=pl.CostEstimate(
            flops=2 * rows * depth * columns,
            bytes_accessed=4 * rows * columns,
            transcendentals=0,
        ),
        name="feed_back",
    )(values, weights, slope)


def into_heads_kernel(values_ref, weights_ref, out_ref):
    weights = weights_ref[...]
    for row in range(0, values_ref.shape[0], 256):
        out_ref[row : row + 256, :] = product(
            values_ref[row : row + 256, :], weights, ((1,), (0,))
        ).astype(jnp.bfloat16)


def into_heads(values, weights):
    rows, depth = values.shape
    columns = weights.shape[1]
    tile = column_tile(columns)
    return pl.pallas_call(
        into_heads_kernel,
        grid=(columns // tile,),
        in_specs=[whole_block((rows, depth)), pl.BlockSpec((depth, tile), lambda step: (0, step))],
        out_specs=pl.BlockSpec((rows, tile), lambda step: (0, step)),
        out_shape=jax.ShapeDtypeStruct((rows, columns), jnp.bfloat16),
        compiler_params=pltpu.CompilerParams(vmem_limit_bytes=VMEM),
        cost_estimate=pl.CostEstimate(
            flops=2 * rows * depth * columns, bytes_accessed=2 * rows * columns, transcendentals=0
        ),
        name="into_heads",
    )(values, weights)


def out_of_kernel(values_ref, weights_ref, out_ref):
    out_ref[...] = product(values_ref[...], weights_ref[...], ((1,), (1,))).astype(out_ref.dtype)


def out_of(values, weights, kind):
    rows, depth = values.shape
    columns = weights.shape[0]
    tile = min(rows, 256)
    return pl.pallas_call(
        out_of_kernel,
        grid=(rows // tile,),
        in_specs=[pl.BlockSpec((tile, depth), lambda step: (step, 0)), whole_block((columns, depth))],
        out_specs=pl.BlockSpec((tile, columns), lambda step: (step, 0)),
        out_shape=jax.ShapeDtypeStruct((rows, columns), kind),
        compiler_params=pltpu.CompilerParams(vmem_limit_bytes=VMEM),
        cost_estimate=pl.CostEstimate(
            flops=2 * rows * depth * columns, bytes_accessed=4 * rows * columns, transcendentals=0
        ),
        name="out_of",
    )(values, weights)


def weight_grad_kernel(places, left_one, left_two, right_one, right_two, *refs):
    outs, total = (refs[:4], refs[4])
    total[...] = product(left_one[...], right_one[...], ((0,), (0,))) + product(
        left_two[...], right_two[...], ((0,), (0,))
    )
    count, rows = outs[0].shape[:2]
    for part in range(4):
        for row in range(count):
            first = pl.multiple_of(places[part * count + row] * rows, 8)
            outs[part][row] = total[pl.ds(first, rows), :].astype(jnp.bfloat16)


def weight_grad(left, right, places):
    rows, depth = left[0].shape
    columns = right[0].shape[1]
    total = places.shape[0]
    block = depth // total
    if block % 8:
        whole = outer_sum(left[0], right[0]) + outer_sum(left[1], right[1])
        return pick_blocks(whole.astype(jnp.bfloat16).reshape(total, block, columns), places)
    tile = column_tile(columns, (256,))

    def whole_left(shape):
        return pl.BlockSpec(shape, lambda step, _: (0, 0), pipeline_mode=pl.Buffered(1))

    return pl.pallas_call(
        weight_grad_kernel,
        grid_spec=pltpu.PrefetchScalarGridSpec(
            num_scalar_prefetch=1,
            grid=(columns // tile,),
            in_specs=[whole_left((rows, depth))] * 2
            + [pl.BlockSpec((rows, tile), lambda step, _: (0, step))] * 2,
            out_specs=[pl.BlockSpec((total // 4, block, tile), lambda step, _: (0, 0, step))] * 4,
            scratch_shapes=[pltpu.VMEM((depth, tile), jnp.float32)],
        ),
        out_shape=[jax.ShapeDtypeStruct((total // 4, block, columns), jnp.bfloat16)] * 4,
        compiler_params=pltpu.CompilerParams(vmem_limit_bytes=VMEM),
        cost_estimate=pl.CostEstimate(
            flops=4 * rows * depth * columns, bytes_accessed=4 * depth * columns, transcendentals=0
        ),
        name="weight_grad",
    )(places, *left, *right)


def norm_rows(values):
    center = values - jnp.mean(values, -1, keepdims=True)
    inverse = lax.rsqrt(jnp.mean(center * center, -1, keepdims=True) + 1e-06)
    return center * inverse, inverse


def row_sum(values):
    return jnp.sum(values, 0, keepdims=True)


def image_call(kernel, name, operands, outs, images, sums=(), core=None):
    tokens = GRID * GRID
    lead = () if core is None else (core,)

    def spec(shape, whole):
        if whole:
            return pl.BlockSpec(
                shape, lambda step, *_: (0,) * len(shape), pipeline_mode=pl.Buffered(1)
            )
        if len(shape) == 3:
            return pl.BlockSpec((1,) + shape[1:], lambda step, *_: (step, 0, 0))
        return pl.BlockSpec((tokens, shape[1]), lambda step, *_: (step, 0))

    rows = images * tokens

    def is_whole(shape):
        return len(shape) == 2 and shape[0] != rows

    summed = [pl.BlockSpec(item.shape, lambda step, *_: (0, 0)) for item in sums]
    return pl.pallas_call(
        kernel,
        grid_spec=pltpu.PrefetchScalarGridSpec(
            num_scalar_prefetch=len(lead),
            grid=(images,),
            in_specs=[spec(item.shape, is_whole(item.shape)) for item in operands],
            out_specs=[spec(item.shape, False) for item in outs] + summed,
        ),
        out_shape=list(outs) + list(sums),
        compiler_params=pltpu.CompilerParams(vmem_limit_bytes=VMEM),
        cost_estimate=pl.CostEstimate(
            flops=4 * rows * D * D if lead else 64 * rows * D,
            bytes_accessed=16 * rows * D,
            transcendentals=0,
        ),
        name=name,
    )(*lead, *operands)


def core_rows(ref, core, mine):
    half = D // 2
    first = core * half if mine else (1 - core) * half
    return ref[pl.ds(pl.multiple_of(first, 16), half), :]


def merge_kernel(
    core_ref, one_ref, two_ref, mine_ref, other_ref, hidden_ref, mod_ref, branch_ref, out_ref, in_ref
):
    core = core_ref[0]
    half = D // 2
    one, two, mod = (one_ref[...][:, :half], two_ref[...][:, :half], mod_ref[0])

    def columns(ref):
        total = product(one, core_rows(ref, core, True), ((1,), (0,))) + product(
            two, core_rows(ref, core, False), ((1,), (0,))
        )
        return total[:, :half]

    mine, other = (columns(mine_ref), columns(other_ref))
    first = jnp.where(core == 0, mine, other)
    branch = jnp.concatenate([first, jnp.where(core == 0, other, mine)], 1)
    hidden = hidden_ref[...] + mod[2:3] * branch
    normed, _ = norm_rows(hidden)
    branch_ref[...] = branch.astype(jnp.bfloat16)
    out_ref[...] = hidden
    in_ref[...] = (normed * (1.0 + mod[4:5]) + mod[3:4]).astype(jnp.bfloat16)


def ends_kernel(
    count, mine_ref, theirs_ref, hidden_ref, noise_ref, head_ref, mod_ref, *refs
):
    d_hidden_ref, d_branch_ref, d_mod_ref, g_head_ref, loss_ref = refs
    wide, low = (jnp.float32, jnp.bfloat16)

    @pl.when(pl.program_id(0) == 0)
    def _():
        g_head_ref[...] = jnp.zeros_like(g_head_ref)
        loss_ref[...] = jnp.zeros_like(loss_ref)

    mod, head = (mod_ref[0], head_ref[...])
    branch = mine_ref[...] + theirs_ref[...].astype(wide)
    normed, inverse = norm_rows(hidden_ref[...] + mod[5:6] * branch)
    final_in = (normed * (1.0 + mod[7:8]) + mod[6:7]).astype(low)
    error = product(final_in, head, ((1,), (1,))) - noise_ref[...]
    loss_ref[...] += jnp.sum(error * error)
    d_predicted = (error * (2.0 / count)).astype(low)
    d_final = product(d_predicted, head, ((1,), (0,)))
    g_head_ref[...] += product(d_predicted, final_in, ((0,), (0,)))
    d_hidden = norm_back(d_final * (1.0 + mod[7:8]), normed, inverse)
    d_hidden_ref[...] = d_hidden
    d_branch_ref[...] = (mod[5:6] * d_hidden).astype(low)
    blank = jnp.zeros((5, D), wide)
    gate, shift, scale = (row_sum(d_hidden * branch), row_sum(d_final), row_sum(d_final * normed))
    d_mod_ref[0] = jnp.concatenate([blank, gate, shift, scale], 0)


def merge_back_kernel(
    core_ref, mine_ref, theirs_ref, hidden_ref, branch_ref, d_hidden_ref, p_mine, p_other, mod_ref,
    d_mod_ref, *refs
):
    d_out_ref, d_branch_ref, d_one_ref, d_two_ref, d_mod_out_ref = refs
    core = core_ref[0]
    wide, low = (jnp.float32, jnp.bfloat16)
    mod, half = (mod_ref[0], D // 2)
    d_in = mine_ref[...] + theirs_ref[...].astype(wide)
    normed, inverse = norm_rows(hidden_ref[...])
    d_hidden = d_hidden_ref[...] + norm_back(d_in * (1.0 + mod[4:5]), normed, inverse)
    d_out_ref[...] = d_hidden
    gate = row_sum(d_hidden * branch_ref[...].astype(wide))
    d_branch = mod[2:3] * d_hidden
    d_branch_ref[...] = d_branch.astype(low)
    low_half, high_half = (d_branch[:, :half], d_branch[:, half:])
    d_mine = jnp.where(core == 0, low_half, high_half).astype(low)
    d_other = jnp.where(core == 0, high_half, low_half).astype(low)

    def heads(mine):
        total = product(d_mine, core_rows(p_mine, core, mine)[:, :half], ((1,), (1,))) + product(
            d_other, core_rows(p_other, core, mine)[:, :half], ((1,), (1,))
        )
        spare = jnp.zeros((total.shape[0], HALF_PAD - half), low)
        return jnp.concatenate([total.astype(low), spare], 1)

    d_one_ref[...] = heads(True)
    d_two_ref[...] = heads(False)
    blank = jnp.zeros((2, D), wide)
    sums = [blank, gate, row_sum(d_in), row_sum(d_in * normed), d_mod_ref[0][5:8]]
    d_mod_out_ref[0] = jnp.concatenate(sums, 0)


def start_back_kernel(
    mine_ref, theirs_ref, hidden_ref, d_hidden_ref, mixed_ref, mod_ref, d_mod_ref, *refs
):
    d_mod_out_ref, g_patch_ref = refs
    wide = jnp.float32

    @pl.when(pl.program_id(0) == 0)
    def _():
        g_patch_ref[...] = jnp.zeros_like(g_patch_ref)

    mod = mod_ref[0]
    d_in = mine_ref[...] + theirs_ref[...].astype(wide)
    normed, inverse = norm_rows(hidden_ref[...])
    d_hidden = d_hidden_ref[...] + norm_back(d_in * (1.0 + mod[1:2]), normed, inverse)
    g_patch_ref[...] += product(mixed_ref[...], d_hidden.astype(jnp.bfloat16), ((0,), (0,)))
    d_mod_out_ref[0] = jnp.concatenate(
        [row_sum(d_in), row_sum(d_in * normed), d_mod_ref[0][2:8]], 0
    )


def shifts():
    offset = jnp.arange(SIDE, dtype=jnp.int32)[:, None, None]
    column = jnp.arange(GRID, dtype=jnp.int32)
    return (offset == GRID - 1 - column[:, None] + column[None, :]).astype(jnp.float32)


def spread_bias(relative):
    turned = relative.reshape(-1, SIDE, SIDE)[:, ::-1, ::-1]
    spread = jnp.einsum("hed,dxy->hxey", turned, shifts(), precision=HIGH)
    spread = spread.reshape(-1, GRID, SIDE * GRID)
    return jnp.pad(spread, ((0, 0), (0, 0), (0, SPREAD - SIDE * GRID)))


def gather_bias(d_spread):
    parts = d_spread[:, :, : SIDE * GRID].reshape(-1, GRID, SIDE, GRID)
    total = jnp.einsum("hxey,dxy->hed", parts, shifts(), precision=HIGH)
    return total[:, ::-1, ::-1].reshape(-1, SIDE * SIDE)


def both_columns_kernel(core_ref, here_ref, there_ref, out_ref):
    half, wide_half = (D // 2, MLPW // 2)
    after = QKV_PAD + wide_half
    spans = [(part * half, half) for part in range(3)] + [(after, half)]
    spans = spans + [(QKV_PAD, wide_half), (after + HALF_PAD, wide_half)]
    place = 0
    for start, width in spans:
        here = here_ref[:, start : start + width]
        there = there_ref[:, start : start + width]
        first = jnp.where(core_ref[0] == 0, here, there)
        second = jnp.where(core_ref[0] == 0, there, here)
        out_ref[:, place : place + 2 * width] = jnp.concatenate([first, second], 1)
        place += 2 * width


def both_columns(here, there, core):
    rows = here.shape[0]
    columns = 4 * D + 2 * MLPW
    whole = pl.BlockSpec(here.shape, lambda step, _: (0, 0))
    return pl.pallas_call(
        both_columns_kernel,
        grid_spec=pltpu.PrefetchScalarGridSpec(
            num_scalar_prefetch=1,
            grid=(1,),
            in_specs=[whole, whole],
            out_specs=pl.BlockSpec((rows, columns), lambda step, _: (0, 0)),
        ),
        out_shape=jax.ShapeDtypeStruct((rows, columns), here.dtype),
        compiler_params=pltpu.CompilerParams(vmem_limit_bytes=VMEM),
        name="both_columns",
    )(core, here, there)


def core_half(values, core, starts, width):
    return [
        jnp.where(
            core == 0,
            values[:, start : start + width],
            values[:, start + width : start + 2 * width],
        )
        for start in starts
    ]


def both_cores(mine, other, core, axis):
    return jnp.where(
        core == 0,
        jnp.concatenate([mine, other], axis),
        jnp.concatenate([other, mine], axis),
    )


def segment_sums(values, bounds, first):
    place = jnp.arange(values.shape[0], dtype=jnp.int32)
    segment = first + sum((place >= bound).astype(jnp.int32) for bound in bounds)
    wanted = segment[None, :] == jnp.arange(11, dtype=jnp.int32)[:, None]
    return jnp.sum(jnp.where(wanted, values[None, :], 0.0), 1)


def mod_squares(values, core):
    columns = jnp.sum(values * values, 0)
    bound = 6 * D - core * values.shape[1]
    return segment_sums(columns, [bound], 4)


def embed_squares(values):
    bounds = [NCLASS + 1, NCLASS + 1 + FREQ, NCLASS + 1 + FREQ + D, NCLASS + 1 + FREQ + D + PDIM]
    return segment_sums(jnp.sum(values * values, 1), bounds, 6)


def block_squares(values):
    return segment_sums(jnp.sum(values * values, 0), [3 * D, 4 * D, 4 * D + MLPW], 0)


def adam_update(grad, first, second, weight, clip):
    first_new = FIRST_DECAY * first + (1.0 - FIRST_DECAY) * (grad * clip)
    second_new = SECOND_DECAY * second + (1.0 - SECOND_DECAY) * (grad * clip) ** 2
    update = (
        first_new
        / (1.0 - FIRST_DECAY**STEP)
        / (jnp.sqrt(second_new / (1.0 - SECOND_DECAY**STEP)) + ADAM_EPSILON)
        + WEIGHT_DECAY * weight
    )
    return (first_new, second_new, update)


def on_device(
    latents,
    noise,
    timesteps,
    labels,
    drops,
    block_weights,
    block_first,
    block_second,
    mod_weights,
    mod_first,
    mod_second,
    embed_weights,
    embed_first,
    embed_second,
    rel_bias,
    rel_first,
    rel_second,
):
    low = jnp.bfloat16
    wide = jnp.float32
    core = lax.axis_index("mod")
    spread = lax.axis_size(DP)
    images = latents.shape[0]
    length = latents.shape[1]
    rows = images * length
    share = embed_weights.shape[1]
    count = float(images * spread * lax.axis_size("mod") * length * latents.shape[2])
    relative, stacked = (relative_places(), stacked_places())

    start = NCLASS + 1
    chosen = jnp.where(drops == 1, NCLASS, labels)
    codes = jnp.stack([timesteps // 32, timesteps % 32, chosen // 32, chosen % 32], 1)
    codes = codes.astype(low)
    codes = both_cores(codes, swap_cores(codes), core, 0)
    code_rows = -(-codes.size // share)
    codes = jnp.pad(codes.reshape(-1), (0, code_rows * share - codes.size))
    small = jnp.concatenate(
        [
            embed_weights[start : start + FREQ].astype(low),
            embed_weights[start + FREQ + D :].astype(low),
            codes.reshape(code_rows, share),
        ],
        0,
    )
    half = D // 2
    wide_half = MLPW // 2
    small_far = gather_far(small)
    now_weights, small_far = tie(block_weights, small_far)
    block_low = now_weights.astype(low)
    q_part, k_part, v_part, p_part = core_half(
        block_low, core, [0, D, 2 * D, 3 * D], half
    )
    in_part, out_part = core_half(block_low, core, [4 * D, 4 * D + MLPW], wide_half)
    pad_part = jnp.zeros((block_low.shape[0], QKV_PAD - QKV_HALF), low)
    attn_part = jnp.concatenate([q_part, k_part, v_part, pad_part], 1)
    proj_spare = jnp.zeros((block_low.shape[0], HALF_PAD - half), low)
    in_part = jnp.concatenate([in_part, p_part, proj_spare], 1)
    attn_far = gather_far(attn_part)
    small_second, small_third = gather_near(small_far)
    small = [small_far, small_second, small_third, gather_last(small_second)]
    later_weights, later_bias, later_embed, small[0] = tie(
        block_weights, rel_bias, embed_weights, small[0]
    )
    table = later_embed[:start].astype(low)
    time_out = later_embed[start + FREQ : start + FREQ + D].astype(low).astype(wide)
    everyone = jnp.concatenate([part[:, FREQ + 2 * PDIM :] for part in small], 0)
    everyone = everyone.reshape(spread, -1)[:, : 2 * images * 4]
    everyone = everyone.reshape(spread * 2 * images, 4).astype(wide)
    all_steps = 32.0 * everyone[:, 0] + everyone[:, 1]
    all_chosen = (32.0 * everyone[:, 2] + everyone[:, 3]).astype(jnp.int32)
    small = place_blocks(small, relative)[:, : FREQ + 2 * PDIM]
    small = small.transpose(1, 0, 2).reshape(FREQ + 2 * PDIM, D)
    time_in = small[:FREQ].astype(wide)
    patch = small[FREQ : FREQ + PDIM]
    head = small[FREQ + PDIM :]

    attn_second, attn_third = gather_near(attn_far)
    in_part, attn_far = tie(in_part, attn_far)
    in_far = far_stack(in_part)

    sinus = sinusoid(all_steps)
    pre_time = jnp.dot(sinus, time_in, precision=HIGH, preferred_element_type=wide)
    time_act = jax.nn.silu(pre_time)
    image_of = relative[:, None] * 2 * images + jnp.arange(2 * images, dtype=jnp.int32)[None, :]
    sorting = image_of.reshape(1, -1) == jnp.arange(image_of.size, dtype=jnp.int32)[:, None]

    def sort_images(values):
        return jnp.dot(sorting.astype(wide), values, precision=HIGH, preferred_element_type=wide)

    sorted_sinus = sort_images(sinus)
    sorted_act = sort_images(time_act)
    classes = jnp.arange(start, dtype=jnp.int32)[None, :]
    sorted_onehot = sort_images(all_chosen[:, None].astype(wide)).astype(jnp.int32) == classes
    first_column = lax.axis_index(DP) * share
    sorted_slope = sort_images(
        silu_slope(lax.dynamic_slice_in_dim(pre_time, first_column, share, 1))
    )
    onehot = all_chosen[:, None] == classes
    cond = jnp.dot(time_act, time_out, precision=HIGH, preferred_element_type=wide) + dense(
        onehot.astype(low), table
    )
    scaled = jax.nn.silu(cond).astype(low)
    scaled, attn_second, attn_third = tie(scaled, attn_second, attn_third)
    attn_both = gather_last(attn_second)
    mod_low = mod_weights.astype(low)
    mod_partial = dense(scaled, mod_low).astype(low)
    mod_parts = jnp.split(mod_partial.reshape(spread, 2 * images, -1), 4)
    heads = HEADS // 2
    bias_rows = spread_bias(jnp.where(core == 0, later_bias[:heads], later_bias[heads:]))
    block_weight_squares = block_squares(later_weights)
    half_mod, in_far, attn_both, bias_rows, block_weight_squares = scatter_parts(
        *mod_parts, meanwhile=(in_far, attn_both, bias_rows, block_weight_squares)
    )
    qkv_low = place_blocks([attn_far, attn_second, attn_third, attn_both], relative).reshape(D, -1)
    in_second, in_third = gather_near(in_far)
    out_part, in_far = tie(out_part, in_far)
    out_far = far_stack(out_part)
    mine = jnp.where(core == 0, half_mod[:images], half_mod[images:])
    theirs = jnp.where(core == 0, half_mod[images:], half_mod[:images])
    modulation = both_cores(mine, swap_cores(theirs), core, 1).reshape(images, 8, D)

    def moved(normed, shift):
        return (
            normed * (1.0 + modulation[:, shift + 1 : shift + 2]) + modulation[:, shift : shift + 1]
        ).astype(low)

    def flat(values):
        return values.reshape(rows, -1)

    def sum_cores(mine, theirs):
        return (mine + swap_cores(theirs).astype(wide)).reshape(images, length, -1)

    alpha_bar = jnp.sum(
        jnp.where(
            timesteps[:, None] == jnp.arange(NSTEPS, dtype=jnp.int32)[None, :],
            plan_table()[None, :],
            0.0,
        ),
        1,
    )
    mixed = (
        jnp.sqrt(alpha_bar)[:, None, None] * latents
        + jnp.sqrt(1.0 - alpha_bar)[:, None, None] * noise
    ).astype(low)
    hidden0 = dense(mixed, patch)
    normed1, inverse1 = layer_norm(hidden0)
    attn_in = flat(moved(normed1, 0))
    attn_in_two = swap_cores(attn_in)
    qkv = into_heads(attn_in, qkv_low)
    qkv_two = into_heads(attn_in_two, qkv_low)
    heads_two, logs_two = attention(qkv_two, bias_rows)
    qkv, logs_two, in_second, in_third, out_far = tie(qkv, logs_two, in_second, in_third, out_far)
    heads_two = swap_cores(heads_two)
    in_both = gather_last(in_second)
    heads_one, logs = attention(qkv, bias_rows)
    heads_one, heads_two, in_both, out_far = tie(heads_one, heads_two, in_both, out_far)
    out_second, out_third = gather_near(out_far)
    in_low = place_blocks([in_far, in_second, in_third, in_both], stacked).reshape(D, -1)
    proj_half = in_low[:, wide_half : wide_half + HALF_PAD]
    proj_other = swap_cores(proj_half)
    core_place = core.astype(jnp.int32).reshape(1)
    rows_wide = jax.ShapeDtypeStruct((rows, D), wide)
    rows_low = jax.ShapeDtypeStruct((rows, D), low)
    rows_heads = jax.ShapeDtypeStruct((rows, HALF_PAD), low)
    mod_shape = jax.ShapeDtypeStruct((images, 8, D), wide)
    patch_shape = jax.ShapeDtypeStruct((PDIM, D), wide)
    branch_one, hidden1, mlp_in = image_call(
        merge_kernel,
        "merge_heads",
        [heads_one, heads_two, proj_half, proj_other, flat(hidden0), modulation],
        [rows_low, rows_wide, rows_low],
        images,
        core=core_place,
    )
    mlp_in, out_second = tie(mlp_in, out_second)
    mlp_in_two = swap_cores(mlp_in)
    act, slope = feed_in(mlp_in, in_low, wide_half)
    act, mlp_in_two, out_third = tie(act, mlp_in_two, out_third)
    out_both = gather_last(out_second)
    act_two, slope_two = feed_in(mlp_in_two, in_low, wide_half)
    act_two, out_both = tie(act_two, out_both)
    out_low = place_blocks([out_far, out_second, out_third, out_both], stacked).reshape(D, -1)
    branch_theirs = out_of(act_two, out_low, low)
    branch_theirs = swap_cores(branch_theirs)
    branch_mine = out_of(act, out_low, wide)
    d_hidden2, d_branch_two, d_mod, g_head, loss_tile = image_call(
        functools.partial(ends_kernel, count),
        "ends",
        [
            branch_mine,
            branch_theirs,
            hidden1,
            noise.reshape(rows, -1),
            head,
            modulation,
        ],
        [rows_wide, rows_low, mod_shape],
        images,
        sums=[patch_shape, jax.ShapeDtypeStruct((8, 128), wide)],
    )
    loss_here = loss_tile[0, 0]
    d_branch_two_two = swap_cores(d_branch_two)
    d_pre = feed_back(d_branch_two, out_low, slope)
    d_pre, d_branch_two_two = tie(d_pre, d_branch_two_two)
    d_pre_two = feed_back(d_branch_two_two, out_low, slope_two)
    out_own, out_second, out_third, out_both = weight_grad(
        (d_branch_two, d_branch_two_two), (act, act_two), stacked
    )
    out_back = send(out_both, plane_peers((2, 1)))
    d_pre, out_third = tie(d_pre, out_third)
    d_mlp_theirs = swap_cores(out_of(d_pre_two, in_low, low))
    d_mlp_mine = out_of(d_pre, in_low, wide)
    d_pre, d_mlp_mine, out_back = tie(d_pre, d_mlp_mine, out_back)
    out_second = send(add_low(out_second, out_back), plane_peers((1, 2)))
    out_third = send(out_third, plane_peers((2, 1)))
    in_own, in_second, in_third, in_both = weight_grad(
        (mlp_in, mlp_in_two), (d_pre, d_pre_two), stacked
    )
    in_both, d_mlp_theirs, d_mlp_mine = tie(in_both, d_mlp_theirs, d_mlp_mine)
    d_hidden1, d_branch_one, d_mine, d_theirs, d_mod = image_call(
        merge_back_kernel,
        "merge_heads_back",
        [
            d_mlp_mine,
            d_mlp_theirs,
            hidden1,
            branch_one,
            d_hidden2,
            proj_half,
            proj_other,
            modulation,
            d_mod,
        ],
        [rows_wide, rows_low, rows_heads, rows_heads, mod_shape],
        images,
        core=core_place,
    )
    d_branch_one, d_mine, out_second, out_third, in_both = tie(
        d_branch_one, d_mine, out_second, out_third, in_both
    )
    in_back = send(in_both, plane_peers((2, 1)))
    g_out = far_share(add_low(add_low(out_own, out_third), out_second))
    d_theirs = swap_cores(d_theirs)
    d_qkv, d_spread = attention_back(qkv, d_mine, logs, bias_rows)
    d_qkv, d_branch_one, d_theirs, in_back, in_third = tie(
        d_qkv, d_branch_one, d_theirs, in_back, in_third
    )
    in_second = send(add_low(in_second, in_back), plane_peers((1, 2)))
    in_third = send(in_third, plane_peers((2, 1)))
    g_proj = both_cores(
        outer_sum(heads_one, d_branch_one)[:half],
        outer_sum(heads_two, d_branch_one)[:half],
        core,
        0,
    )
    spare = ((0, 0), (0, HALF_PAD - half))
    g_low_half, g_high_half = (jnp.pad(g_proj[:, :half], spare), jnp.pad(g_proj[:, half:], spare))
    g_proj_mine = jnp.where(core == 0, g_low_half, g_high_half)
    g_proj_theirs = jnp.where(core == 0, g_high_half, g_low_half).astype(low)
    g_proj = (g_proj_mine + swap_cores(g_proj_theirs).astype(wide)).astype(low)
    proj_own, proj_second, proj_third, proj_both = pick_blocks(
        g_proj.reshape(spread, -1, HALF_PAD), stacked
    )
    proj_both, d_theirs = tie(proj_both, d_theirs)
    proj_back = send(proj_both, plane_peers((2, 1)))
    d_qkv_two, d_spread_two = attention_back(qkv_two, d_theirs, logs_two, bias_rows)
    d_qkv_two, in_second, in_third, proj_back, proj_third, g_out = tie(
        d_qkv_two, in_second, in_third, proj_back, proj_third, g_out
    )
    g_in = far_share(add_low(add_low(in_own, in_third), in_second))
    d_spread = d_spread + d_spread_two
    proj_second = send(add_low(proj_second, proj_back), plane_peers((1, 2)))
    proj_third = send(proj_third, plane_peers((2, 1)))
    rel_half = gather_bias(d_spread)
    packed = jnp.concatenate([rel_half.reshape(-1), (loss_here * jnp.ones(1, wide))])
    bits = [1 << pos for pos in range(2, spread.bit_length() - 1)] + [1, 2]
    for bit in bits[:-3]:
        packed = packed + send(packed, dp_peers(bit))
    attn_own, attn_second, attn_third, attn_both = weight_grad(
        (attn_in, attn_in_two), (d_qkv, d_qkv_two), stacked
    )
    attn_both, proj_second, proj_third, packed = tie(attn_both, proj_second, proj_third, packed)
    packed = packed + send(packed, dp_peers(bits[-3]))
    g_proj = far_share(add_low(add_low(proj_own, proj_third), proj_second))
    attn_back = send(attn_both, plane_peers((2, 1)))
    d_qkv_two, attn_both, attn_third = tie(d_qkv_two, attn_both, attn_third)
    d_attn_theirs = out_of(d_qkv_two, qkv_low, low)
    d_qkv, d_attn_theirs, attn_back, packed = tie(d_qkv, d_attn_theirs, attn_back, packed)
    packed = packed + send(packed, dp_peers(bits[-2]))
    d_attn_theirs = swap_cores(d_attn_theirs)
    attn_second = send(add_low(attn_second, attn_back), plane_peers((1, 2)))
    attn_third = send(attn_third, plane_peers((2, 1)))
    d_attn_mine = out_of(d_qkv, qkv_low, wide)
    d_attn_mine, g_in, packed = tie(d_attn_mine, g_in, packed)
    packed = packed + send(packed, dp_peers(bits[-1]))
    d_mod, g_patch = image_call(
        start_back_kernel,
        "start_back",
        [
            d_attn_mine,
            d_attn_theirs,
            flat(hidden0),
            d_hidden1,
            flat(mixed),
            modulation,
            d_mod,
        ],
        [mod_shape],
        images,
        sums=[patch_shape],
    )

    d_modulation = d_mod.reshape(images, 8 * D).astype(low)
    mod_half = 4 * D
    d_keep = jnp.where(core == 0, d_modulation[:, :mod_half], d_modulation[:, mod_half:])
    d_give = jnp.where(core == 0, d_modulation[:, mod_half:], d_modulation[:, :mod_half])
    d_pair = both_cores(d_keep, swap_cores(d_give), core, 0)
    d_pair, attn_second, attn_third, packed = tie(d_pair, attn_second, attn_third, packed)
    d_far = gather_far(d_pair)
    attn_own, d_far = tie(attn_own, d_far)
    g_qkv = far_share(add_low(add_low(attn_own, attn_third), attn_second))
    d_second, d_third = gather_near(d_far)
    d_parts = [d_far, d_second, d_third, gather_last(d_second)]
    d_all = jnp.concatenate(d_parts, 0).reshape(spread * 2 * images, mod_half)
    mod_grad = outer_sum(scaled, d_all)
    d_scaled = dense_trans(d_all, mod_low)
    theirs = jnp.split(swap_cores(d_scaled), 4)
    d_scaled = d_scaled + jnp.concatenate([theirs[0], theirs[2], theirs[1], theirs[3]], 0)
    d_cond = sort_images(d_scaled * silu_slope(cond))
    g_table = first_contract(sorted_onehot.astype(wide), d_cond)
    g_time_out = first_contract(sorted_act, d_cond)
    d_time = lax.dot_general(
        d_cond, time_out, (((1,), (1,)), ((), ())), precision=HIGH, preferred_element_type=wide
    )
    g_ends = jnp.concatenate([g_patch, g_head], 0)
    g_ends = g_ends + swap_cores(g_ends)
    tail = jnp.concatenate([d_time, g_ends], 0)
    tail = tail.reshape(-1, spread, share).transpose(1, 0, 2)
    tail = scatter_parts(*pick_blocks(tail, relative))
    tail, g_qkv, g_proj = tie(tail, g_qkv, g_proj)
    d_time_here, g_ends = (tail[: -2 * PDIM], tail[-2 * PDIM :])
    g_time_in = first_contract(sorted_sinus, d_time_here * sorted_slope)
    embed_grad = jnp.concatenate([g_table, g_time_in, g_time_out, g_ends], 0)

    g_here = jnp.concatenate([g_qkv, g_in, g_proj, g_out], 1)
    g_there = swap_cores(g_here)
    g_mine = g_here.astype(wide)
    g_squares = segment_sums(
        jnp.sum(g_mine * g_mine, 0), [QKV_PAD, QKV_PAD + wide_half, QKV_PAD + wide_half + HALF_PAD], 0
    )
    g_squares = g_squares[jnp.array([0, 2, 1, 3] + list(range(4, 11)))]
    block_grad = both_columns(g_here, g_there, core_place)

    packed_other = swap_cores(packed)
    rel_grad = both_cores(
        packed[:-1].reshape(heads, -1), packed_other[:-1].reshape(heads, -1), core, 0
    )
    loss_sum = packed[-1] + packed_other[-1]

    first_core = (core == 0).astype(wide)

    def replica_squares(block, mod, embed):
        return first_core * (block + embed_squares(embed)) + mod_squares(mod, core)

    squares = jnp.concatenate(
        [
            g_squares + mod_squares(mod_grad, core) + first_core * embed_squares(embed_grad),
            replica_squares(block_weight_squares, mod_weights, embed_weights),
        ]
    )
    squares, block_grad, rel_grad = all_sum(squares, (block_grad, rel_grad))
    block_grad = block_grad.astype(wide)
    grad_parts, weight_parts = jnp.split(squares, 2)
    grad_sq = jnp.concatenate([grad_parts, jnp.sum(rel_grad * rel_grad)[None]])
    weight_sq = jnp.concatenate([weight_parts, jnp.sum(rel_bias * rel_bias)[None]])
    grad_norm = jnp.sqrt(jnp.sum(grad_sq))
    clip = jnp.minimum(1.0, CLIP_NORM / grad_norm)
    block_m, block_s, block_step = adam_update(
        block_grad, block_first, block_second, block_weights, clip
    )
    mod_m, mod_s, mod_step = adam_update(mod_grad, mod_first, mod_second, mod_weights, clip)
    embed_m, embed_s, embed_step = adam_update(
        embed_grad, embed_first, embed_second, embed_weights, clip
    )
    rel_m, rel_s, rel_step = adam_update(rel_grad, rel_first, rel_second, rel_bias, clip)
    update_parts = all_sum(replica_squares(block_squares(block_step), mod_step, embed_step))
    update_sq = jnp.concatenate([update_parts, jnp.sum(rel_step * rel_step)[None]])
    weight_norm = jnp.sqrt(weight_sq)
    update_norm = jnp.sqrt(update_sq)
    ratio = weight_norm / update_norm
    def spread_ratio(length, bounds, first, shift=0):
        place = shift + jnp.arange(length, dtype=jnp.int32)
        chosen = ratio[first]
        for step, bound in enumerate(bounds):
            chosen = jnp.where(place >= bound, ratio[first + step + 1], chosen)
        return chosen

    block_ratio = spread_ratio(block_weights.shape[1], [3 * D, 4 * D, 4 * D + MLPW], 0)
    mod_columns = mod_weights.shape[1]
    mod_ratio = spread_ratio(mod_columns, [6 * D], 4, core * mod_columns)
    ends = start + FREQ + D
    embed_bounds = [start, start + FREQ, ends, ends + PDIM]
    embed_ratio = spread_ratio(embed_weights.shape[0], embed_bounds, 6)
    block_new = block_weights - LEARN_RATE * block_ratio[None, :] * block_step
    mod_new = mod_weights - LEARN_RATE * mod_ratio[None, :] * mod_step
    embed_new = embed_weights - LEARN_RATE * embed_ratio[:, None] * embed_step
    rel_new = rel_bias - LEARN_RATE * ratio[11] * rel_step
    matrix_norms = jnp.stack([weight_norm, update_norm])
    return (
        loss_sum,
        grad_norm,
        matrix_norms,
        block_new,
        block_m,
        block_s,
        block_new.astype(jnp.bfloat16),
        mod_new,
        mod_m,
        mod_s,
        mod_new.astype(jnp.bfloat16),
        embed_new,
        embed_m,
        embed_s,
        embed_new.astype(jnp.bfloat16),
        rel_new,
        rel_m,
        rel_s,
        rel_new.astype(jnp.bfloat16),
        rel_grad * clip,
    )


def solution(mesh):
    spread, pair = mesh.devices.shape
    grid = jax.sharding.Mesh(mesh.devices.reshape(spread // 4, 4, pair), DP + ("mod",))
    placed = (
        P(DP + ("mod",), None, None),
        P(DP + ("mod",), None, None),
        P(DP + ("mod",)),
        P(DP + ("mod",)),
        P(DP + ("mod",)),
        P(DP, None),
        P(DP, None),
        P(DP, None),
        P(DP, "mod"),
        P(DP, "mod"),
        P(DP, "mod"),
        P(None, DP),
        P(None, DP),
        P(None, DP),
        P(),
        P(),
        P(),
    )
    return jax.shard_map(
        on_device,
        mesh=grid,
        in_specs=placed,
        out_specs=(
            P(),
            P(),
            P(),
            P(DP, None),
            P(DP, None),
            P(DP, None),
            P(DP, None),
            P(DP, "mod"),
            P(DP, "mod"),
            P(DP, "mod"),
            P(DP, "mod"),
            P(None, DP),
            P(None, DP),
            P(None, DP),
            P(None, DP),
            P(),
            P(),
            P(),
            P(),
            P(),
        ),
        check_vma=False,
    )
```

```python
import functools
import math

import jax
import jax.numpy as jnp
from jax import lax
from jax.experimental import pallas as pl
from jax.experimental.pallas import tpu as pltpu
from jax.sharding import PartitionSpec as P

D = 1152
HEADS = 16
HD = 72
MLPW = 4608
NCLASS = 1000
FREQ = 256
GRID = 16
PDIM = 16
NSTEPS = 1000
STEP = 10
SIDE = 2 * GRID - 1
QKV_HALF = 3 * D // 2
QKV_PAD = -(-QKV_HALF // 128) * 128
SPREAD = 2 * GRID * GRID
DP = ("far", "near")
VMEM = 60 << 20
LOG2E = math.log2(math.e)
HALF_PAD = -(-D // 256) * 128


FIRST_DECAY = 0.9
SECOND_DECAY = 0.999
ADAM_EPSILON = 1e-08
WEIGHT_DECAY = 0.01
LEARN_RATE = 0.25
CLIP_NORM = 0.05
HIGH = lax.Precision.HIGHEST


def dense(left, right):
    return jnp.dot(left, right, preferred_element_type=jnp.float32)


def dense_trans(left, right):
    return lax.dot_general(
        left, right, (((left.ndim - 1,), (1,)), ((), ())), preferred_element_type=jnp.float32
    )


def outer_sum(left, right):
    flat_left = left.reshape(-1, left.shape[-1])
    flat_right = right.reshape(-1, right.shape[-1])
    return lax.dot_general(
        flat_left, flat_right, (((0,), (0,)), ((), ())), preferred_element_type=jnp.float32
    )


def first_contract(left, right):
    return lax.dot_general(
        left, right, (((0,), (0,)), ((), ())), precision=HIGH, preferred_element_type=jnp.float32
    )


def layer_norm(values):
    center = values - jnp.mean(values, -1, keepdims=True)
    inverse = lax.rsqrt(jnp.mean(center * center, -1, keepdims=True) + 1e-06)
    return (center * inverse, inverse)


def norm_back(upstream, normed, inverse):
    return inverse * (
        upstream
        - jnp.mean(upstream, -1, keepdims=True)
        - normed * jnp.mean(upstream * normed, -1, keepdims=True)
    )


def silu_slope(values):
    sigma = jax.nn.sigmoid(values)
    return sigma * (1.0 + values * (1.0 - sigma))


def plan_table():
    betas = jnp.linspace(0.0001, 0.02, NSTEPS, dtype=jnp.float32)
    return jnp.exp(jnp.cumsum(jnp.log(1.0 - betas)))


def sinusoid(steps):
    half_width = FREQ // 2
    freqs = jnp.exp(-math.log(10000.0) * jnp.arange(half_width, dtype=jnp.float32) / half_width)
    angles = steps.astype(jnp.float32)[:, None] * freqs[None, :]
    return jnp.concatenate([jnp.cos(angles), jnp.sin(angles)], 1)


def dp_peers(mask):
    spread, pair = lax.axis_size(DP), lax.axis_size("mod")
    return [(i * pair + c, (i ^ mask) * pair + c) for i in range(spread) for c in range(pair)]


def plane_peers(masks):
    spread, pair = lax.axis_size(DP), lax.axis_size("mod")
    return [(i * pair + c, (i ^ masks[c]) * pair + c) for i in range(spread) for c in range(pair)]


def send(values, peers):
    return lax.ppermute(values, DP + ("mod",), peers)


def swap_cores(values):
    return lax.ppermute(values, "mod", [(0, 1), (1, 0)])


def far_groups():
    spread = lax.axis_size(DP)
    bits = [1 << k for k in range(2, spread.bit_length() - 1)]
    if len(bits) == 2:
        return [[bits[0], bits[1], bits[0] | bits[1]]]
    return [[bit] for bit in bits]


def far_masks():
    masks = [0]
    for group in far_groups():
        masks = masks + [mask | have for mask in group for have in masks]
    return masks


def block_places(far):
    me, core = lax.axis_index(DP), lax.axis_index("mod")
    second = jnp.where(core == 0, 1, 2)
    third = jnp.where(core == 0, 2, 1)
    near = jnp.stack([jnp.zeros_like(second), second, third, second | third])
    return ((me ^ near)[:, None] ^ far[None, :]).reshape(-1).astype(jnp.int32)


def relative_places():
    return block_places(jnp.array(far_masks(), jnp.int32))


def stacked_places():
    far = jnp.arange(lax.axis_size("far"), dtype=jnp.int32)
    return block_places(4 * (far ^ lax.axis_index("far")))


def move_kernel(slots, sources, targets, hold, in_sems, out_sems):
    total = len(sources)
    for first in range(0, total, slots):
        wave = range(first, min(first + slots, total))
        arriving = [
            pltpu.make_async_copy(sources[at], hold.at[at - first], in_sems.at[at]) for at in wave
        ]
        for copy in arriving:
            copy.start()
        leaving = []
        for at, copy in zip(wave, arriving):
            copy.wait()
            leaving.append(
                pltpu.make_async_copy(hold.at[at - first], targets[at], out_sems.at[at])
            )
            leaving[-1].start()
        for copy in leaving:
            copy.wait()


def place_kernel(counts, slots, places, *refs):
    ins, out = (refs[: len(counts)], refs[len(counts)])
    sources = [ins[part].at[row] for part, count in enumerate(counts) for row in range(count)]
    targets = [out.at[places[at]] for at in range(len(sources))]
    move_kernel(slots, sources, targets, *refs[len(counts) + 1 :])


def pick_kernel(counts, slots, places, source, *refs):
    outs = refs[: len(counts)]
    targets = [outs[part].at[row] for part, count in enumerate(counts) for row in range(count)]
    sources = [source.at[places[at]] for at in range(len(targets))]
    move_kernel(slots, sources, targets, *refs[len(counts) :])


def plane_slots(total, plane, kind):
    rows, columns = plane
    padded = -(-rows // 16) * 16 * -(-columns // 128) * 128 * jnp.dtype(kind).itemsize
    return max(1, min(total, (24 << 20) // padded))


def move_call(kernel, counts, places, operands, out_shape, out_count, plane, kind):
    total = sum(counts)
    slots = plane_slots(total, plane, kind)
    any_space = pl.BlockSpec(memory_space=pl.ANY)
    return pl.pallas_call(
        functools.partial(kernel, counts, slots),
        grid_spec=pltpu.PrefetchScalarGridSpec(
            num_scalar_prefetch=1,
            grid=(1,),
            in_specs=[any_space] * len(operands),
            out_specs=any_space if out_count is None else [any_space] * out_count,
            scratch_shapes=[
                pltpu.VMEM((slots,) + plane, kind),
                pltpu.SemaphoreType.DMA((total,)),
                pltpu.SemaphoreType.DMA((total,)),
            ],
        ),
        out_shape=out_shape,
        compiler_params=pltpu.CompilerParams(vmem_limit_bytes=VMEM),
        cost_estimate=pl.CostEstimate(
            flops=0,
            bytes_accessed=2 * total * plane[0] * plane[1] * jnp.dtype(kind).itemsize,
            transcendentals=0,
        ),
        name="move_blocks",
    )(places, *operands)


def place_blocks(parts, places):
    counts = [part.shape[0] for part in parts]
    plane, kind = (parts[0].shape[1:], parts[0].dtype)
    shape = jax.ShapeDtypeStruct((sum(counts),) + plane, kind)
    return move_call(place_kernel, counts, places, parts, shape, None, plane, kind)


def pick_blocks(values, places):
    counts = [values.shape[0] // 4] * 4
    plane, kind = (values.shape[1:], values.dtype)
    shape = [jax.ShapeDtypeStruct((count,) + plane, kind) for count in counts]
    return move_call(pick_kernel, counts, places, [values], shape, 4, plane, kind)


def tie(*values):
    return lax.optimization_barrier(values)


def gather_far(block):
    stack = block[None]
    for group in far_groups():
        stack = jnp.concatenate([stack] + [send(stack, dp_peers(mask)) for mask in group], 0)
    return stack


def gather_near(stack):
    return send(stack, plane_peers((1, 2))), send(stack, plane_peers((2, 1)))


def gather_last(second):
    return send(second, plane_peers((2, 1)))


def gather_parts(block):
    stack = gather_far(block)
    second, third = gather_near(stack)
    return [stack, second, third, gather_last(second)]


def far_stack(block):
    return lax.all_gather(block, "far", axis=0)


def far_share(stack):
    return lax.psum_scatter(stack, "far", scatter_dimension=0)


def add_low(left, right):
    return (left.astype(jnp.float32) + right.astype(jnp.float32)).astype(left.dtype)


def scatter_far(own):
    wide = jnp.float32
    for group in reversed(far_groups()):
        count = own.shape[0] // (len(group) + 1)
        total = own[:count].astype(wide)
        for pos, mask in enumerate(group):
            total = total + send(
                own[(pos + 1) * count : (pos + 2) * count], dp_peers(mask)
            ).astype(wide)
        own = total if count == 1 else total.astype(own.dtype)
    return own[0].astype(wide)


def scatter_parts(own, second, third, both, meanwhile=()):
    second = add_low(second, send(both, plane_peers((2, 1))))
    second, *meanwhile = tie(second, *meanwhile)
    from_third = send(third, plane_peers((2, 1)))
    from_second = send(second, plane_peers((1, 2)))
    share = scatter_far(add_low(add_low(own, from_third), from_second))
    return (share, *meanwhile) if meanwhile else share


def all_sum(values, meanwhile=()):
    return dp_sum(values + swap_cores(values), meanwhile)


def dp_sum(values, meanwhile=()):
    for pos in range(lax.axis_size(DP).bit_length() - 1):
        values = values + send(values, dp_peers(1 << pos))
        if pos == 1:
            values, *meanwhile = tie(values, *meanwhile)
    return (values, *meanwhile) if meanwhile else values


def product(left, right, dims):
    return lax.dot_general(left, right, (dims, ((), ())), preferred_element_type=jnp.float32)


def fill_bias(spread_ref, bias):
    tokens = GRID * GRID
    for head in range(bias.shape[0]):
        spread = spread_ref[head] * LOG2E
        for row in range(GRID):
            off = (GRID - 1 - row) * GRID
            moved = spread if off == 0 else pltpu.roll(spread, SPREAD - off, 1)
            bias[head, row * GRID : (row + 1) * GRID, :] = moved[:, :tokens]


def head_slices(values, head, heads):
    width = heads * HD
    return [
        values[:, part * width + head * HD : part * width + (head + 1) * HD] for part in range(3)
    ]


def attention_kernel(heads, qkv_ref, spread_ref, out_ref, log_ref, bias):
    @pl.when(pl.program_id(0) == 0)
    def _():
        fill_bias(spread_ref, bias)

    values = qkv_ref[...]
    outs, logs = ([], [])
    for head in range(heads):
        query, key, value = head_slices(values, head, heads)
        scores = product(query, key, ((1,), (1,))) * (HD ** (-0.5) * LOG2E) + bias[head]
        top = jnp.max(scores, -1, keepdims=True)
        powers = jnp.exp2(scores - top)
        total = jnp.sum(powers, -1, keepdims=True)
        summed = product(powers.astype(jnp.bfloat16), value, ((1,), (0,)))
        outs.append((summed * (1.0 / total)).astype(jnp.bfloat16))
        logs.append(top + jnp.log2(total))
    spare = out_ref.shape[1] - heads * HD
    if spare:
        outs.append(jnp.zeros((values.shape[0], spare), jnp.bfloat16))
    out_ref[...] = jnp.concatenate(outs, 1)
    log_ref[...] = jnp.concatenate(logs, 1)


def attention(qkv, spread):
    rows, columns = qkv.shape
    heads = spread.shape[0]
    tokens = GRID * GRID
    return pl.pallas_call(
        functools.partial(attention_kernel, heads),
        grid=(rows // tokens,),
        in_specs=[
            pl.BlockSpec((tokens, columns), lambda step: (step, 0)),
            pl.BlockSpec(spread.shape, lambda step: (0, 0, 0)),
        ],
        out_specs=[
            pl.BlockSpec((tokens, HALF_PAD), lambda step: (step, 0)),
            pl.BlockSpec((tokens, heads), lambda step: (step, 0)),
        ],
        out_shape=[
            jax.ShapeDtypeStruct((rows, HALF_PAD), jnp.bfloat16),
            jax.ShapeDtypeStruct((rows, heads), jnp.float32),
        ],
        scratch_shapes=[pltpu.VMEM((heads, tokens, tokens), jnp.float32)],
        compiler_params=pltpu.CompilerParams(vmem_limit_bytes=VMEM),
        cost_estimate=pl.CostEstimate(
            flops=4 * rows * tokens * heads * 256,
            bytes_accessed=rows * columns * 4,
            transcendentals=rows * tokens * heads,
        ),
        name="attention",
    )(qkv, spread)


def attention_back_kernel(
    heads, qkv_ref, upstream_ref, log_ref, spread_ref, d_qkv_ref, d_spread_ref, bias, d_bias
):
    tokens = GRID * GRID

    @pl.when(pl.program_id(0) == 0)
    def _():
        fill_bias(spread_ref, bias)
        d_bias[...] = jnp.zeros_like(d_bias)

    values, upstream, logs = (qkv_ref[...], upstream_ref[...], log_ref[...])
    d_query, d_key, d_value = ([], [], [])
    for head in range(heads):
        query, key, value = head_slices(values, head, heads)
        d_out = upstream[:, head * HD : (head + 1) * HD]
        scores = product(query, key, ((1,), (1,))) * (HD ** (-0.5) * LOG2E) + bias[head]
        probs = jnp.exp2(scores - logs[:, head : head + 1])
        d_probs = product(d_out, value, ((1,), (1,)))
        d_scores = probs * (d_probs - jnp.sum(probs * d_probs, -1, keepdims=True))
        d_bias[head] += d_scores
        d_scores = d_scores.astype(jnp.bfloat16)
        d_query.append((product(d_scores, key, ((1,), (0,))) * HD ** (-0.5)).astype(jnp.bfloat16))
        d_key.append((product(d_scores, query, ((0,), (0,))) * HD ** (-0.5)).astype(jnp.bfloat16))
        d_value.append(
            product(probs.astype(jnp.bfloat16), d_out, ((0,), (0,))).astype(jnp.bfloat16)
        )
    pieces = d_query + d_key + d_value
    spare = d_qkv_ref.shape[1] - 3 * heads * HD
    if spare:
        pieces = pieces + [jnp.zeros((tokens, spare), jnp.bfloat16)]
    d_qkv_ref[...] = jnp.concatenate(pieces, 1)

    @pl.when(pl.program_id(0) == pl.num_programs(0) - 1)
    def _():
        for head in range(heads):
            total = jnp.zeros((GRID, SPREAD), jnp.float32)
            for row in range(GRID):
                off = (GRID - 1 - row) * GRID
                rows = d_bias[head, row * GRID : (row + 1) * GRID, :]
                wide = jnp.concatenate([rows, jnp.zeros((GRID, SPREAD - tokens), jnp.float32)], 1)
                total += wide if off == 0 else pltpu.roll(wide, off, 1)
            d_spread_ref[head] = total


def attention_back(qkv, upstream, logs, spread):
    rows, columns = qkv.shape
    heads = spread.shape[0]
    tokens = GRID * GRID
    return pl.pallas_call(
        functools.partial(attention_back_kernel, heads),
        grid=(rows // tokens,),
        in_specs=[
            pl.BlockSpec((tokens, columns), lambda step: (step, 0)),
            pl.BlockSpec((tokens, upstream.shape[1]), lambda step: (step, 0)),
            pl.BlockSpec((tokens, heads), lambda step: (step, 0)),
            pl.BlockSpec(spread.shape, lambda step: (0, 0, 0)),
        ],
        out_specs=[
            pl.BlockSpec((tokens, columns), lambda step: (step, 0)),
            pl.BlockSpec(spread.shape, lambda step: (0, 0, 0)),
        ],
        out_shape=[
            jax.ShapeDtypeStruct((rows, columns), jnp.bfloat16),
            jax.ShapeDtypeStruct(spread.shape, jnp.float32),
        ],
        scratch_shapes=[pltpu.VMEM((heads, tokens, tokens), jnp.float32)] * 2,
        compiler_params=pltpu.CompilerParams(vmem_limit_bytes=VMEM),
        cost_estimate=pl.CostEstimate(
            flops=10 * rows * tokens * heads * 256,
            bytes_accessed=rows * columns * 6,
            transcendentals=rows * tokens * heads,
        ),
        name="attention_back",
    )(qkv, upstream, logs, spread)


def whole_block(shape):
    return pl.BlockSpec(shape, lambda step: (0,) * len(shape), pipeline_mode=pl.Buffered(1))


def column_tile(columns, choices=(768, 896, 256)):
    return next((tile for tile in choices if columns % tile == 0), 128)


def feed_in_kernel(values_ref, weights_ref, act_ref, slope_ref):
    weights = weights_ref[...]
    rate = math.sqrt(2.0 / math.pi)
    cubic = 0.044715 * rate
    for row in range(0, values_ref.shape[0], 256):
        pre = product(values_ref[row : row + 256, :], weights, ((1,), (0,)))
        square = pre * pre
        gate = 0.5 + 0.5 * jnp.tanh(pre * (rate + cubic * square))
        act = pre * gate
        slope = gate + (act - act * gate) * (2.0 * rate + 6.0 * cubic * square)
        act_ref[row : row + 256, :] = act.astype(jnp.bfloat16)
        slope_ref[row : row + 256, :] = slope.astype(jnp.bfloat16)


def feed_in(values, weights, columns):
    rows, depth = values.shape
    tile = column_tile(columns)
    return pl.pallas_call(
        feed_in_kernel,
        grid=(columns // tile,),
        in_specs=[whole_block((rows, depth)), pl.BlockSpec((depth, tile), lambda step: (0, step))],
        out_specs=[pl.BlockSpec((rows, tile), lambda step: (0, step))] * 2,
        out_shape=[jax.ShapeDtypeStruct((rows, columns), jnp.bfloat16)] * 2,
        compiler_params=pltpu.CompilerParams(vmem_limit_bytes=VMEM),
        cost_estimate=pl.CostEstimate(
            flops=2 * rows * depth * columns,
            bytes_accessed=4 * rows * columns,
            transcendentals=rows * columns,
        ),
        name="feed_in",
    )(values, weights)


def feed_back_kernel(values_ref, weights_ref, slope_ref, out_ref):
    weights = weights_ref[...]
    for row in range(0, values_ref.shape[0], 256):
        d_act = product(values_ref[row : row + 256, :], weights, ((1,), (0,)))
        d_pre = d_act * slope_ref[row : row + 256, :].astype(jnp.float32)
        out_ref[row : row + 256, :] = d_pre.astype(jnp.bfloat16)


def feed_back(values, weights, slope):
    rows, depth = values.shape
    columns = weights.shape[1]
    tile = column_tile(columns)
    return pl.pallas_call(
        feed_back_kernel,
        grid=(columns // tile,),
        in_specs=[
            whole_block((rows, depth)),
            pl.BlockSpec((depth, tile), lambda step: (0, step)),
            pl.BlockSpec((rows, tile), lambda step: (0, step)),
        ],
        out_specs=pl.BlockSpec((rows, tile), lambda step: (0, step)),
        out_shape=jax.ShapeDtypeStruct((rows, columns), jnp.bfloat16),
        compiler_params=pltpu.CompilerParams(vmem_limit_bytes=VMEM),
        cost_estimate=pl.CostEstimate(
            flops=2 * rows * depth * columns,
            bytes_accessed=4 * rows * columns,
            transcendentals=0,
        ),
        name="feed_back",
    )(values, weights, slope)


def into_heads_kernel(values_ref, weights_ref, out_ref):
    weights = weights_ref[...]
    for row in range(0, values_ref.shape[0], 256):
        out_ref[row : row + 256, :] = product(
            values_ref[row : row + 256, :], weights, ((1,), (0,))
        ).astype(jnp.bfloat16)


def into_heads(values, weights):
    rows, depth = values.shape
    columns = weights.shape[1]
    tile = column_tile(columns)
    return pl.pallas_call(
        into_heads_kernel,
        grid=(columns // tile,),
        in_specs=[whole_block((rows, depth)), pl.BlockSpec((depth, tile), lambda step: (0, step))],
        out_specs=pl.BlockSpec((rows, tile), lambda step: (0, step)),
        out_shape=jax.ShapeDtypeStruct((rows, columns), jnp.bfloat16),
        compiler_params=pltpu.CompilerParams(vmem_limit_bytes=VMEM),
        cost_estimate=pl.CostEstimate(
            flops=2 * rows * depth * columns, bytes_accessed=2 * rows * columns, transcendentals=0
        ),
        name="into_heads",
    )(values, weights)


def out_of_kernel(values_ref, weights_ref, out_ref):
    out_ref[...] = product(values_ref[...], weights_ref[...], ((1,), (1,))).astype(out_ref.dtype)


def out_of(values, weights, kind):
    rows, depth = values.shape
    columns = weights.shape[0]
    tile = min(rows, 256)
    return pl.pallas_call(
        out_of_kernel,
        grid=(rows // tile,),
        in_specs=[pl.BlockSpec((tile, depth), lambda step: (step, 0)), whole_block((columns, depth))],
        out_specs=pl.BlockSpec((tile, columns), lambda step: (step, 0)),
        out_shape=jax.ShapeDtypeStruct((rows, columns), kind),
        compiler_params=pltpu.CompilerParams(vmem_limit_bytes=VMEM),
        cost_estimate=pl.CostEstimate(
            flops=2 * rows * depth * columns, bytes_accessed=4 * rows * columns, transcendentals=0
        ),
        name="out_of",
    )(values, weights)


def weight_grad_kernel(places, left_one, left_two, right_one, right_two, *refs):
    outs, total = (refs[:4], refs[4])
    total[...] = product(left_one[...], right_one[...], ((0,), (0,))) + product(
        left_two[...], right_two[...], ((0,), (0,))
    )
    count, rows = outs[0].shape[:2]
    for part in range(4):
        for row in range(count):
            first = pl.multiple_of(places[part * count + row] * rows, 8)
            outs[part][row] = total[pl.ds(first, rows), :].astype(jnp.bfloat16)


def weight_grad(left, right, places):
    rows, depth = left[0].shape
    columns = right[0].shape[1]
    total = places.shape[0]
    block = depth // total
    if block % 8:
        whole = outer_sum(left[0], right[0]) + outer_sum(left[1], right[1])
        return pick_blocks(whole.astype(jnp.bfloat16).reshape(total, block, columns), places)
    tile = column_tile(columns, (256,))

    def whole_left(shape):
        return pl.BlockSpec(shape, lambda step, _: (0, 0), pipeline_mode=pl.Buffered(1))

    return pl.pallas_call(
        weight_grad_kernel,
        grid_spec=pltpu.PrefetchScalarGridSpec(
            num_scalar_prefetch=1,
            grid=(columns // tile,),
            in_specs=[whole_left((rows, depth))] * 2
            + [pl.BlockSpec((rows, tile), lambda step, _: (0, step))] * 2,
            out_specs=[pl.BlockSpec((total // 4, block, tile), lambda step, _: (0, 0, step))] * 4,
            scratch_shapes=[pltpu.VMEM((depth, tile), jnp.float32)],
        ),
        out_shape=[jax.ShapeDtypeStruct((total // 4, block, columns), jnp.bfloat16)] * 4,
        compiler_params=pltpu.CompilerParams(vmem_limit_bytes=VMEM),
        cost_estimate=pl.CostEstimate(
            flops=4 * rows * depth * columns, bytes_accessed=4 * depth * columns, transcendentals=0
        ),
        name="weight_grad",
    )(places, *left, *right)


def norm_rows(values):
    center = values - jnp.mean(values, -1, keepdims=True)
    inverse = lax.rsqrt(jnp.mean(center * center, -1, keepdims=True) + 1e-06)
    return center * inverse, inverse


def row_sum(values):
    return jnp.sum(values, 0, keepdims=True)


def image_call(kernel, name, operands, outs, images, sums=(), core=None):
    tokens = GRID * GRID
    lead = () if core is None else (core,)

    def spec(shape, whole):
        if whole:
            return pl.BlockSpec(
                shape, lambda step, *_: (0,) * len(shape), pipeline_mode=pl.Buffered(1)
            )
        if len(shape) == 3:
            return pl.BlockSpec((1,) + shape[1:], lambda step, *_: (step, 0, 0))
        return pl.BlockSpec((tokens, shape[1]), lambda step, *_: (step, 0))

    rows = images * tokens

    def is_whole(shape):
        return len(shape) == 2 and shape[0] != rows

    summed = [pl.BlockSpec(item.shape, lambda step, *_: (0, 0)) for item in sums]
    return pl.pallas_call(
        kernel,
        grid_spec=pltpu.PrefetchScalarGridSpec(
            num_scalar_prefetch=len(lead),
            grid=(images,),
            in_specs=[spec(item.shape, is_whole(item.shape)) for item in operands],
            out_specs=[spec(item.shape, False) for item in outs] + summed,
        ),
        out_shape=list(outs) + list(sums),
        compiler_params=pltpu.CompilerParams(vmem_limit_bytes=VMEM),
        cost_estimate=pl.CostEstimate(
            flops=4 * rows * D * D if lead else 64 * rows * D,
            bytes_accessed=16 * rows * D,
            transcendentals=0,
        ),
        name=name,
    )(*lead, *operands)


def core_rows(ref, core, mine):
    half = D // 2
    first = core * half if mine else (1 - core) * half
    return ref[pl.ds(pl.multiple_of(first, 16), half), :]


def merge_kernel(
    core_ref, one_ref, two_ref, mine_ref, other_ref, hidden_ref, mod_ref, branch_ref, out_ref, in_ref
):
    core = core_ref[0]
    half = D // 2
    one, two, mod = (one_ref[...][:, :half], two_ref[...][:, :half], mod_ref[0])

    def columns(ref):
        total = product(one, core_rows(ref, core, True), ((1,), (0,))) + product(
            two, core_rows(ref, core, False), ((1,), (0,))
        )
        return total[:, :half]

    mine, other = (columns(mine_ref), columns(other_ref))
    first = jnp.where(core == 0, mine, other)
    branch = jnp.concatenate([first, jnp.where(core == 0, other, mine)], 1)
    hidden = hidden_ref[...] + mod[2:3] * branch
    normed, _ = norm_rows(hidden)
    branch_ref[...] = branch.astype(jnp.bfloat16)
    out_ref[...] = hidden
    in_ref[...] = (normed * (1.0 + mod[4:5]) + mod[3:4]).astype(jnp.bfloat16)


def ends_kernel(
    count, mine_ref, theirs_ref, hidden_ref, noise_ref, head_ref, mod_ref, *refs
):
    d_hidden_ref, d_branch_ref, d_mod_ref, g_head_ref, loss_ref = refs
    wide, low = (jnp.float32, jnp.bfloat16)

    @pl.when(pl.program_id(0) == 0)
    def _():
        g_head_ref[...] = jnp.zeros_like(g_head_ref)
        loss_ref[...] = jnp.zeros_like(loss_ref)

    mod, head = (mod_ref[0], head_ref[...])
    branch = mine_ref[...] + theirs_ref[...].astype(wide)
    normed, inverse = norm_rows(hidden_ref[...] + mod[5:6] * branch)
    final_in = (normed * (1.0 + mod[7:8]) + mod[6:7]).astype(low)
    error = product(final_in, head, ((1,), (1,))) - noise_ref[...]
    loss_ref[...] += jnp.sum(error * error)
    d_predicted = (error * (2.0 / count)).astype(low)
    d_final = product(d_predicted, head, ((1,), (0,)))
    g_head_ref[...] += product(d_predicted, final_in, ((0,), (0,)))
    d_hidden = norm_back(d_final * (1.0 + mod[7:8]), normed, inverse)
    d_hidden_ref[...] = d_hidden
    d_branch_ref[...] = (mod[5:6] * d_hidden).astype(low)
    blank = jnp.zeros((5, D), wide)
    gate, shift, scale = (row_sum(d_hidden * branch), row_sum(d_final), row_sum(d_final * normed))
    d_mod_ref[0] = jnp.concatenate([blank, gate, shift, scale], 0)


def merge_back_kernel(
    core_ref, mine_ref, theirs_ref, hidden_ref, branch_ref, d_hidden_ref, p_mine, p_other, mod_ref,
    d_mod_ref, *refs
):
    d_out_ref, d_branch_ref, d_one_ref, d_two_ref, d_mod_out_ref = refs
    core = core_ref[0]
    wide, low = (jnp.float32, jnp.bfloat16)
    mod, half = (mod_ref[0], D // 2)
    d_in = mine_ref[...] + theirs_ref[...].astype(wide)
    normed, inverse = norm_rows(hidden_ref[...])
    d_hidden = d_hidden_ref[...] + norm_back(d_in * (1.0 + mod[4:5]), normed, inverse)
    d_out_ref[...] = d_hidden
    gate = row_sum(d_hidden * branch_ref[...].astype(wide))
    d_branch = mod[2:3] * d_hidden
    d_branch_ref[...] = d_branch.astype(low)
    low_half, high_half = (d_branch[:, :half], d_branch[:, half:])
    d_mine = jnp.where(core == 0, low_half, high_half).astype(low)
    d_other = jnp.where(core == 0, high_half, low_half).astype(low)

    def heads(mine):
        total = product(d_mine, core_rows(p_mine, core, mine)[:, :half], ((1,), (1,))) + product(
            d_other, core_rows(p_other, core, mine)[:, :half], ((1,), (1,))
        )
        spare = jnp.zeros((total.shape[0], HALF_PAD - half), low)
        return jnp.concatenate([total.astype(low), spare], 1)

    d_one_ref[...] = heads(True)
    d_two_ref[...] = heads(False)
    blank = jnp.zeros((2, D), wide)
    sums = [blank, gate, row_sum(d_in), row_sum(d_in * normed), d_mod_ref[0][5:8]]
    d_mod_out_ref[0] = jnp.concatenate(sums, 0)


def start_back_kernel(
    mine_ref, theirs_ref, hidden_ref, d_hidden_ref, mixed_ref, mod_ref, d_mod_ref, *refs
):
    d_mod_out_ref, g_patch_ref = refs
    wide = jnp.float32

    @pl.when(pl.program_id(0) == 0)
    def _():
        g_patch_ref[...] = jnp.zeros_like(g_patch_ref)

    mod = mod_ref[0]
    d_in = mine_ref[...] + theirs_ref[...].astype(wide)
    normed, inverse = norm_rows(hidden_ref[...])
    d_hidden = d_hidden_ref[...] + norm_back(d_in * (1.0 + mod[1:2]), normed, inverse)
    g_patch_ref[...] += product(mixed_ref[...], d_hidden.astype(jnp.bfloat16), ((0,), (0,)))
    d_mod_out_ref[0] = jnp.concatenate(
        [row_sum(d_in), row_sum(d_in * normed), d_mod_ref[0][2:8]], 0
    )


def shifts():
    offset = jnp.arange(SIDE, dtype=jnp.int32)[:, None, None]
    column = jnp.arange(GRID, dtype=jnp.int32)
    return (offset == GRID - 1 - column[:, None] + column[None, :]).astype(jnp.float32)


def spread_bias(relative):
    turned = relative.reshape(-1, SIDE, SIDE)[:, ::-1, ::-1]
    spread = jnp.einsum("hed,dxy->hxey", turned, shifts(), precision=HIGH)
    spread = spread.reshape(-1, GRID, SIDE * GRID)
    return jnp.pad(spread, ((0, 0), (0, 0), (0, SPREAD - SIDE * GRID)))


def gather_bias(d_spread):
    parts = d_spread[:, :, : SIDE * GRID].reshape(-1, GRID, SIDE, GRID)
    total = jnp.einsum("hxey,dxy->hed", parts, shifts(), precision=HIGH)
    return total[:, ::-1, ::-1].reshape(-1, SIDE * SIDE)


def both_columns_kernel(core_ref, *refs):
    here_refs, there_refs, out_ref = (refs[:4], refs[4:8], refs[8])
    half, wide_half = (D // 2, MLPW // 2)
    spans = [(0, part * half, half) for part in range(3)] + [(2, 0, half)]
    spans = spans + [(1, 0, wide_half), (3, 0, wide_half)]
    place = 0
    for piece, start, width in spans:
        here = here_refs[piece][:, start : start + width]
        there = there_refs[piece][:, start : start + width]
        first = jnp.where(core_ref[0] == 0, here, there)
        second = jnp.where(core_ref[0] == 0, there, here)
        out_ref[:, place : place + 2 * width] = jnp.concatenate([first, second], 1)
        place += 2 * width


def both_columns(here, there, core):
    rows = here[0].shape[0]
    columns = 4 * D + 2 * MLPW
    return pl.pallas_call(
        both_columns_kernel,
        grid_spec=pltpu.PrefetchScalarGridSpec(
            num_scalar_prefetch=1,
            grid=(1,),
            in_specs=[pl.BlockSpec(item.shape, lambda step, _: (0, 0)) for item in here + there],
            out_specs=pl.BlockSpec((rows, columns), lambda step, _: (0, 0)),
        ),
        out_shape=jax.ShapeDtypeStruct((rows, columns), here[0].dtype),
        compiler_params=pltpu.CompilerParams(vmem_limit_bytes=VMEM),
        name="both_columns",
    )(core, *here, *there)


def core_half(values, core, starts, width):
    return [
        jnp.where(
            core == 0,
            values[:, start : start + width],
            values[:, start + width : start + 2 * width],
        )
        for start in starts
    ]


def both_cores(mine, other, core, axis):
    return jnp.where(
        core == 0,
        jnp.concatenate([mine, other], axis),
        jnp.concatenate([other, mine], axis),
    )


def segment_sums(values, bounds, first):
    place = jnp.arange(values.shape[0], dtype=jnp.int32)
    segment = first + sum((place >= bound).astype(jnp.int32) for bound in bounds)
    wanted = segment[None, :] == jnp.arange(11, dtype=jnp.int32)[:, None]
    return jnp.sum(jnp.where(wanted, values[None, :], 0.0), 1)


def mod_squares(values, core):
    columns = jnp.sum(values * values, 0)
    bound = 6 * D - core * values.shape[1]
    return segment_sums(columns, [bound], 4)


def embed_squares(values):
    bounds = [NCLASS + 1, NCLASS + 1 + FREQ, NCLASS + 1 + FREQ + D, NCLASS + 1 + FREQ + D + PDIM]
    return segment_sums(jnp.sum(values * values, 1), bounds, 6)


def block_squares(values):
    return segment_sums(jnp.sum(values * values, 0), [3 * D, 4 * D, 4 * D + MLPW], 0)


def adam_update(grad, first, second, weight, clip):
    first_new = FIRST_DECAY * first + (1.0 - FIRST_DECAY) * (grad * clip)
    second_new = SECOND_DECAY * second + (1.0 - SECOND_DECAY) * (grad * clip) ** 2
    update = (
        first_new
        / (1.0 - FIRST_DECAY**STEP)
        / (jnp.sqrt(second_new / (1.0 - SECOND_DECAY**STEP)) + ADAM_EPSILON)
        + WEIGHT_DECAY * weight
    )
    return (first_new, second_new, update)


def on_device(
    latents,
    noise,
    timesteps,
    labels,
    drops,
    block_weights,
    block_first,
    block_second,
    mod_weights,
    mod_first,
    mod_second,
    embed_weights,
    embed_first,
    embed_second,
    rel_bias,
    rel_first,
    rel_second,
):
    low = jnp.bfloat16
    wide = jnp.float32
    core = lax.axis_index("mod")
    spread = lax.axis_size(DP)
    images = latents.shape[0]
    length = latents.shape[1]
    rows = images * length
    share = embed_weights.shape[1]
    count = float(images * spread * lax.axis_size("mod") * length * latents.shape[2])
    relative, stacked = (relative_places(), stacked_places())

    start = NCLASS + 1
    chosen = jnp.where(drops == 1, NCLASS, labels)
    codes = jnp.stack([timesteps // 32, timesteps % 32, chosen // 32, chosen % 32], 1)
    codes = codes.astype(low)
    codes = both_cores(codes, swap_cores(codes), core, 0)
    code_rows = -(-codes.size // share)
    codes = jnp.pad(codes.reshape(-1), (0, code_rows * share - codes.size))
    small = jnp.concatenate(
        [
            embed_weights[start : start + FREQ].astype(low),
            embed_weights[start + FREQ + D :].astype(low),
            codes.reshape(code_rows, share),
        ],
        0,
    )
    half = D // 2
    wide_half = MLPW // 2
    small_far = gather_far(small)
    now_weights, small_far = tie(block_weights, small_far)
    block_low = now_weights.astype(low)
    q_part, k_part, v_part, p_part = core_half(
        block_low, core, [0, D, 2 * D, 3 * D], half
    )
    in_part, out_part = core_half(block_low, core, [4 * D, 4 * D + MLPW], wide_half)
    pad_part = jnp.zeros((block_low.shape[0], QKV_PAD - QKV_HALF), low)
    attn_part = jnp.concatenate([q_part, k_part, v_part, pad_part], 1)
    proj_spare = jnp.zeros((block_low.shape[0], HALF_PAD - half), low)
    in_part = jnp.concatenate([in_part, p_part, proj_spare], 1)
    attn_far = gather_far(attn_part)
    small_second, small_third = gather_near(small_far)
    small = [small_far, small_second, small_third, gather_last(small_second)]
    later_weights, later_bias, later_embed, later_mod, small[0] = tie(
        block_weights, rel_bias, embed_weights, mod_weights, small[0]
    )
    table = later_embed[:start].astype(low)
    time_out = later_embed[start + FREQ : start + FREQ + D].astype(low).astype(wide)
    everyone = jnp.concatenate([part[:, FREQ + 2 * PDIM :] for part in small], 0)
    everyone = everyone.reshape(spread, -1)[:, : 2 * images * 4]
    everyone = everyone.reshape(spread * 2 * images, 4).astype(wide)
    all_steps = 32.0 * everyone[:, 0] + everyone[:, 1]
    all_chosen = (32.0 * everyone[:, 2] + everyone[:, 3]).astype(jnp.int32)
    small = place_blocks(small, relative)[:, : FREQ + 2 * PDIM]
    small = small.transpose(1, 0, 2).reshape(FREQ + 2 * PDIM, D)
    time_in = small[:FREQ].astype(wide)
    patch = small[FREQ : FREQ + PDIM]
    head = small[FREQ + PDIM :]

    attn_second, attn_third = gather_near(attn_far)
    in_part, attn_far = tie(in_part, attn_far)
    in_far = far_stack(in_part)

    sinus = sinusoid(all_steps)
    pre_time = jnp.dot(sinus, time_in, precision=HIGH, preferred_element_type=wide)
    time_act = jax.nn.silu(pre_time)
    image_of = relative[:, None] * 2 * images + jnp.arange(2 * images, dtype=jnp.int32)[None, :]
    sorting = image_of.reshape(1, -1) == jnp.arange(image_of.size, dtype=jnp.int32)[:, None]

    def sort_images(values):
        return jnp.dot(sorting.astype(wide), values, precision=HIGH, preferred_element_type=wide)

    sorted_sinus = sort_images(sinus)
    sorted_act = sort_images(time_act)
    classes = jnp.arange(start, dtype=jnp.int32)[None, :]
    sorted_class = sort_images(all_chosen[:, None].astype(wide)).astype(jnp.int32)
    first_column = lax.axis_index(DP) * share
    sorted_slope = sort_images(
        silu_slope(lax.dynamic_slice_in_dim(pre_time, first_column, share, 1))
    )
    onehot = all_chosen[:, None] == classes
    cond = jnp.dot(time_act, time_out, precision=HIGH, preferred_element_type=wide) + dense(
        onehot.astype(low), table
    )
    scaled = jax.nn.silu(cond).astype(low)
    scaled, attn_second, attn_third = tie(scaled, attn_second, attn_third)
    attn_both = gather_last(attn_second)
    mod_low = mod_weights.astype(low)
    mod_partial = dense(scaled, mod_low).astype(low)
    mod_parts = jnp.split(mod_partial.reshape(spread, 2 * images, -1), 4)
    heads = HEADS // 2
    bias_rows = spread_bias(jnp.where(core == 0, later_bias[:heads], later_bias[heads:]))
    first_core = (core == 0).astype(wide)
    weight_squares = first_core * (block_squares(later_weights) + embed_squares(later_embed))
    weight_squares = weight_squares + mod_squares(later_mod, core)
    (
        half_mod,
        in_far,
        attn_both,
        bias_rows,
        weight_squares,
        sorted_act,
        sorted_sinus,
        sorted_slope,
        sorted_class,
    ) = scatter_parts(
        *mod_parts,
        meanwhile=(
            in_far,
            attn_both,
            bias_rows,
            weight_squares,
            sorted_act,
            sorted_sinus,
            sorted_slope,
            sorted_class,
        ),
    )
    qkv_low = place_blocks([attn_far, attn_second, attn_third, attn_both], relative).reshape(D, -1)
    in_second, in_third = gather_near(in_far)
    out_part, in_far = tie(out_part, in_far)
    out_far = far_stack(out_part)
    mine = jnp.where(core == 0, half_mod[:images], half_mod[images:])
    theirs = jnp.where(core == 0, half_mod[images:], half_mod[:images])
    modulation = both_cores(mine, swap_cores(theirs), core, 1).reshape(images, 8, D)

    def moved(normed, shift):
        return (
            normed * (1.0 + modulation[:, shift + 1 : shift + 2]) + modulation[:, shift : shift + 1]
        ).astype(low)

    def flat(values):
        return values.reshape(rows, -1)

    def sum_cores(mine, theirs):
        return (mine + swap_cores(theirs).astype(wide)).reshape(images, length, -1)

    alpha_bar = jnp.sum(
        jnp.where(
            timesteps[:, None] == jnp.arange(NSTEPS, dtype=jnp.int32)[None, :],
            plan_table()[None, :],
            0.0,
        ),
        1,
    )
    mixed = (
        jnp.sqrt(alpha_bar)[:, None, None] * latents
        + jnp.sqrt(1.0 - alpha_bar)[:, None, None] * noise
    ).astype(low)
    hidden0 = dense(mixed, patch)
    normed1, inverse1 = layer_norm(hidden0)
    attn_in = flat(moved(normed1, 0))
    attn_in_two = swap_cores(attn_in)
    qkv = into_heads(attn_in, qkv_low)
    qkv_two = into_heads(attn_in_two, qkv_low)
    heads_two, logs_two = attention(qkv_two, bias_rows)
    qkv, logs_two, in_second, in_third, out_far = tie(qkv, logs_two, in_second, in_third, out_far)
    heads_two = swap_cores(heads_two)
    in_both = gather_last(in_second)
    heads_one, logs = attention(qkv, bias_rows)
    heads_one, heads_two, in_both, out_far = tie(heads_one, heads_two, in_both, out_far)
    out_second, out_third = gather_near(out_far)
    in_low = place_blocks([in_far, in_second, in_third, in_both], stacked).reshape(D, -1)
    proj_half = in_low[:, wide_half : wide_half + HALF_PAD]
    proj_other = swap_cores(proj_half)
    core_place = core.astype(jnp.int32).reshape(1)
    rows_wide = jax.ShapeDtypeStruct((rows, D), wide)
    rows_low = jax.ShapeDtypeStruct((rows, D), low)
    rows_heads = jax.ShapeDtypeStruct((rows, HALF_PAD), low)
    mod_shape = jax.ShapeDtypeStruct((images, 8, D), wide)
    patch_shape = jax.ShapeDtypeStruct((PDIM, D), wide)
    branch_one, hidden1, mlp_in = image_call(
        merge_kernel,
        "merge_heads",
        [heads_one, heads_two, proj_half, proj_other, flat(hidden0), modulation],
        [rows_low, rows_wide, rows_low],
        images,
        core=core_place,
    )
    mlp_in, out_second = tie(mlp_in, out_second)
    mlp_in_two = swap_cores(mlp_in)
    act, slope = feed_in(mlp_in, in_low, wide_half)
    act, mlp_in_two, out_third = tie(act, mlp_in_two, out_third)
    out_both = gather_last(out_second)
    act_two, slope_two = feed_in(mlp_in_two, in_low, wide_half)
    act_two, out_both = tie(act_two, out_both)
    out_low = place_blocks([out_far, out_second, out_third, out_both], stacked).reshape(D, -1)
    branch_theirs = out_of(act_two, out_low, low)
    branch_theirs = swap_cores(branch_theirs)
    branch_mine = out_of(act, out_low, wide)
    d_hidden2, d_branch_two, d_mod, g_head, loss_tile = image_call(
        functools.partial(ends_kernel, count),
        "ends",
        [
            branch_mine,
            branch_theirs,
            hidden1,
            noise.reshape(rows, -1),
            head,
            modulation,
        ],
        [rows_wide, rows_low, mod_shape],
        images,
        sums=[patch_shape, jax.ShapeDtypeStruct((8, 128), wide)],
    )
    loss_here = loss_tile[0, 0]
    d_branch_two_two = swap_cores(d_branch_two)
    d_pre = feed_back(d_branch_two, out_low, slope)
    d_pre, d_branch_two_two = tie(d_pre, d_branch_two_two)
    d_pre_two = feed_back(d_branch_two_two, out_low, slope_two)
    out_own, out_second, out_third, out_both = weight_grad(
        (d_branch_two, d_branch_two_two), (act, act_two), stacked
    )
    out_back = send(out_both, plane_peers((2, 1)))
    d_pre, out_third = tie(d_pre, out_third)
    d_mlp_theirs = swap_cores(out_of(d_pre_two, in_low, low))
    d_mlp_mine = out_of(d_pre, in_low, wide)
    d_pre, d_mlp_mine, out_back = tie(d_pre, d_mlp_mine, out_back)
    out_second = send(add_low(out_second, out_back), plane_peers((1, 2)))
    out_third = send(out_third, plane_peers((2, 1)))
    in_own, in_second, in_third, in_both = weight_grad(
        (mlp_in, mlp_in_two), (d_pre, d_pre_two), stacked
    )
    in_both, d_mlp_theirs, d_mlp_mine = tie(in_both, d_mlp_theirs, d_mlp_mine)
    d_hidden1, d_branch_one, d_mine, d_theirs, d_mod = image_call(
        merge_back_kernel,
        "merge_heads_back",
        [
            d_mlp_mine,
            d_mlp_theirs,
            hidden1,
            branch_one,
            d_hidden2,
            proj_half,
            proj_other,
            modulation,
            d_mod,
        ],
        [rows_wide, rows_low, rows_heads, rows_heads, mod_shape],
        images,
        core=core_place,
    )
    d_branch_one, d_mine, out_second, out_third, in_both = tie(
        d_branch_one, d_mine, out_second, out_third, in_both
    )
    in_back = send(in_both, plane_peers((2, 1)))
    g_out = far_share(add_low(add_low(out_own, out_third), out_second))
    d_theirs = swap_cores(d_theirs)
    d_qkv, d_spread = attention_back(qkv, d_mine, logs, bias_rows)
    d_qkv, d_branch_one, d_theirs, in_back, in_third = tie(
        d_qkv, d_branch_one, d_theirs, in_back, in_third
    )
    in_second = send(add_low(in_second, in_back), plane_peers((1, 2)))
    in_third = send(in_third, plane_peers((2, 1)))
    g_proj = both_cores(
        outer_sum(heads_one, d_branch_one)[:half],
        outer_sum(heads_two, d_branch_one)[:half],
        core,
        0,
    )
    spare = ((0, 0), (0, HALF_PAD - half))
    g_low_half, g_high_half = (jnp.pad(g_proj[:, :half], spare), jnp.pad(g_proj[:, half:], spare))
    g_proj_mine = jnp.where(core == 0, g_low_half, g_high_half)
    g_proj_theirs = jnp.where(core == 0, g_high_half, g_low_half).astype(low)
    g_proj = (g_proj_mine + swap_cores(g_proj_theirs).astype(wide)).astype(low)
    proj_own, proj_second, proj_third, proj_both = pick_blocks(
        g_proj.reshape(spread, -1, HALF_PAD), stacked
    )
    proj_both, d_theirs = tie(proj_both, d_theirs)
    proj_back = send(proj_both, plane_peers((2, 1)))
    d_qkv_two, d_spread_two = attention_back(qkv_two, d_theirs, logs_two, bias_rows)
    d_qkv_two, in_second, in_third, proj_back, proj_third, g_out = tie(
        d_qkv_two, in_second, in_third, proj_back, proj_third, g_out
    )
    g_in = far_share(add_low(add_low(in_own, in_third), in_second))
    d_spread = d_spread + d_spread_two
    proj_second = send(add_low(proj_second, proj_back), plane_peers((1, 2)))
    proj_third = send(proj_third, plane_peers((2, 1)))
    rel_half = gather_bias(d_spread)
    packed = jnp.concatenate([rel_half.reshape(-1), (loss_here * jnp.ones(1, wide))])
    bits = [1 << pos for pos in range(2, spread.bit_length() - 1)] + [1, 2]
    for bit in bits[:-3]:
        packed = packed + send(packed, dp_peers(bit))
    attn_own, attn_second, attn_third, attn_both = weight_grad(
        (attn_in, attn_in_two), (d_qkv, d_qkv_two), stacked
    )
    attn_both, proj_second, proj_third, packed = tie(attn_both, proj_second, proj_third, packed)
    packed = packed + send(packed, dp_peers(bits[-3]))
    g_proj = far_share(add_low(add_low(proj_own, proj_third), proj_second))
    attn_back = send(attn_both, plane_peers((2, 1)))
    d_qkv_two, attn_both, attn_third = tie(d_qkv_two, attn_both, attn_third)
    d_attn_theirs = out_of(d_qkv_two, qkv_low, low)
    d_qkv, d_attn_theirs, attn_back, packed = tie(d_qkv, d_attn_theirs, attn_back, packed)
    packed = packed + send(packed, dp_peers(bits[-2]))
    d_attn_theirs = swap_cores(d_attn_theirs)
    attn_second = send(add_low(attn_second, attn_back), plane_peers((1, 2)))
    attn_third = send(attn_third, plane_peers((2, 1)))
    d_attn_mine = out_of(d_qkv, qkv_low, wide)
    d_attn_mine, g_in, packed = tie(d_attn_mine, g_in, packed)
    packed = packed + send(packed, dp_peers(bits[-1]))
    d_mod, g_patch = image_call(
        start_back_kernel,
        "start_back",
        [
            d_attn_mine,
            d_attn_theirs,
            flat(hidden0),
            d_hidden1,
            flat(mixed),
            modulation,
            d_mod,
        ],
        [mod_shape],
        images,
        sums=[patch_shape],
    )

    d_modulation = d_mod.reshape(images, 8 * D).astype(low)
    mod_half = 4 * D
    d_keep = jnp.where(core == 0, d_modulation[:, :mod_half], d_modulation[:, mod_half:])
    d_give = jnp.where(core == 0, d_modulation[:, mod_half:], d_modulation[:, :mod_half])
    d_pair = both_cores(d_keep, swap_cores(d_give), core, 0)
    d_pair, attn_second, attn_third, packed = tie(d_pair, attn_second, attn_third, packed)
    d_far = gather_far(d_pair)
    attn_own, d_far = tie(attn_own, d_far)
    g_qkv = far_share(add_low(add_low(attn_own, attn_third), attn_second))
    d_second, d_third = gather_near(d_far)
    d_parts = [d_far, d_second, d_third, gather_last(d_second)]
    d_all = jnp.concatenate(d_parts, 0).reshape(spread * 2 * images, mod_half)
    mod_grad = outer_sum(scaled, d_all)
    d_scaled = dense_trans(d_all, mod_low)
    theirs = jnp.split(swap_cores(d_scaled), 4)
    d_scaled = d_scaled + jnp.concatenate([theirs[0], theirs[2], theirs[1], theirs[3]], 0)
    d_cond = sort_images(d_scaled * silu_slope(cond))
    g_table = first_contract((sorted_class == classes).astype(wide), d_cond)
    g_time_out = first_contract(sorted_act, d_cond)
    d_time = lax.dot_general(
        d_cond, time_out, (((1,), (1,)), ((), ())), precision=HIGH, preferred_element_type=wide
    )
    g_ends = jnp.concatenate([g_patch, g_head], 0)
    g_ends = g_ends + swap_cores(g_ends)
    tail = jnp.concatenate([d_time, g_ends], 0)
    tail = tail.reshape(-1, spread, share).transpose(1, 0, 2)
    tail = scatter_parts(*pick_blocks(tail, relative))
    tail, g_qkv, g_proj = tie(tail, g_qkv, g_proj)
    d_time_here, g_ends = (tail[: -2 * PDIM], tail[-2 * PDIM :])
    g_time_in = first_contract(sorted_sinus, d_time_here * sorted_slope)
    embed_grad = jnp.concatenate([g_table, g_time_in, g_time_out, g_ends], 0)

    g_here = [g_qkv, g_in, g_proj, g_out]
    g_there = [swap_cores(piece) for piece in g_here]
    g_squares = sum(
        jnp.where(jnp.arange(11) == matrix, jnp.sum(piece.astype(wide) ** 2), 0.0)
        for matrix, piece in zip((0, 2, 1, 3), g_here)
    )
    block_grad = both_columns(g_here, g_there, core_place)

    packed_other = swap_cores(packed)
    rel_grad = both_cores(
        packed[:-1].reshape(heads, -1), packed_other[:-1].reshape(heads, -1), core, 0
    )
    loss_sum = packed[-1] + packed_other[-1]

    first_core = (core == 0).astype(wide)

    def replica_squares(block, mod, embed):
        return first_core * (block + embed_squares(embed)) + mod_squares(mod, core)

    squares = jnp.concatenate(
        [
            g_squares + mod_squares(mod_grad, core) + first_core * embed_squares(embed_grad),
            weight_squares,
        ]
    )
    squares, block_grad, rel_grad = all_sum(squares, (block_grad, rel_grad))
    block_grad = block_grad.astype(wide)
    grad_parts, weight_parts = jnp.split(squares, 2)
    grad_sq = jnp.concatenate([grad_parts, jnp.sum(rel_grad * rel_grad)[None]])
    weight_sq = jnp.concatenate([weight_parts, jnp.sum(rel_bias * rel_bias)[None]])
    grad_norm = jnp.sqrt(jnp.sum(grad_sq))
    clip = jnp.minimum(1.0, CLIP_NORM / grad_norm)
    block_m, block_s, block_step = adam_update(
        block_grad, block_first, block_second, block_weights, clip
    )
    mod_m, mod_s, mod_step = adam_update(mod_grad, mod_first, mod_second, mod_weights, clip)
    embed_m, embed_s, embed_step = adam_update(
        embed_grad, embed_first, embed_second, embed_weights, clip
    )
    rel_m, rel_s, rel_step = adam_update(rel_grad, rel_first, rel_second, rel_bias, clip)
    update_parts = all_sum(replica_squares(block_squares(block_step), mod_step, embed_step))
    update_sq = jnp.concatenate([update_parts, jnp.sum(rel_step * rel_step)[None]])
    weight_norm = jnp.sqrt(weight_sq)
    update_norm = jnp.sqrt(update_sq)
    ratio = weight_norm / update_norm
    def spread_ratio(length, bounds, first, shift=0):
        place = shift + jnp.arange(length, dtype=jnp.int32)
        chosen = ratio[first]
        for step, bound in enumerate(bounds):
            chosen = jnp.where(place >= bound, ratio[first + step + 1], chosen)
        return chosen

    block_ratio = spread_ratio(block_weights.shape[1], [3 * D, 4 * D, 4 * D + MLPW], 0)
    mod_columns = mod_weights.shape[1]
    mod_ratio = spread_ratio(mod_columns, [6 * D], 4, core * mod_columns)
    ends = start + FREQ + D
    embed_bounds = [start, start + FREQ, ends, ends + PDIM]
    embed_ratio = spread_ratio(embed_weights.shape[0], embed_bounds, 6)
    block_new = block_weights - LEARN_RATE * block_ratio[None, :] * block_step
    mod_new = mod_weights - LEARN_RATE * mod_ratio[None, :] * mod_step
    embed_new = embed_weights - LEARN_RATE * embed_ratio[:, None] * embed_step
    rel_new = rel_bias - LEARN_RATE * ratio[11] * rel_step
    matrix_norms = jnp.stack([weight_norm, update_norm])
    return (
        loss_sum,
        grad_norm,
        matrix_norms,
        block_new,
        block_m,
        block_s,
        block_new.astype(jnp.bfloat16),
        mod_new,
        mod_m,
        mod_s,
        mod_new.astype(jnp.bfloat16),
        embed_new,
        embed_m,
        embed_s,
        embed_new.astype(jnp.bfloat16),
        rel_new,
        rel_m,
        rel_s,
        rel_new.astype(jnp.bfloat16),
        rel_grad * clip,
    )


def solution(mesh):
    spread, pair = mesh.devices.shape
    grid = jax.sharding.Mesh(mesh.devices.reshape(spread // 4, 4, pair), DP + ("mod",))
    placed = (
        P(DP + ("mod",), None, None),
        P(DP + ("mod",), None, None),
        P(DP + ("mod",)),
        P(DP + ("mod",)),
        P(DP + ("mod",)),
        P(DP, None),
        P(DP, None),
        P(DP, None),
        P(DP, "mod"),
        P(DP, "mod"),
        P(DP, "mod"),
        P(None, DP),
        P(None, DP),
        P(None, DP),
        P(),
        P(),
        P(),
    )
    return jax.shard_map(
        on_device,
        mesh=grid,
        in_specs=placed,
        out_specs=(
            P(),
            P(),
            P(),
            P(DP, None),
            P(DP, None),
            P(DP, None),
            P(DP, None),
            P(DP, "mod"),
            P(DP, "mod"),
            P(DP, "mod"),
            P(DP, "mod"),
            P(None, DP),
            P(None, DP),
            P(None, DP),
            P(None, DP),
            P(),
            P(),
            P(),
            P(),
            P(),
        ),
        check_vma=False,
    )
```

```python
import functools
import math

import jax
import jax.numpy as jnp
from jax import lax
from jax.experimental import pallas as pl
from jax.experimental.pallas import tpu as pltpu
from jax.sharding import PartitionSpec as P

D = 1152
HEADS = 16
HD = 72
MLPW = 4608
NCLASS = 1000
FREQ = 256
GRID = 16
PDIM = 16
NSTEPS = 1000
STEP = 10
SIDE = 2 * GRID - 1
QKV_HALF = 3 * D // 2
QKV_PAD = -(-QKV_HALF // 128) * 128
SPREAD = 2 * GRID * GRID
DP = ("far", "near")
VMEM = 60 << 20
LOG2E = math.log2(math.e)
HALF_PAD = -(-D // 256) * 128


FIRST_DECAY = 0.9
SECOND_DECAY = 0.999
ADAM_EPSILON = 1e-08
WEIGHT_DECAY = 0.01
LEARN_RATE = 0.25
CLIP_NORM = 0.05
HIGH = lax.Precision.HIGHEST


def dense(left, right):
    return jnp.dot(left, right, preferred_element_type=jnp.float32)


def dense_trans(left, right):
    return lax.dot_general(
        left, right, (((left.ndim - 1,), (1,)), ((), ())), preferred_element_type=jnp.float32
    )


def outer_sum(left, right):
    flat_left = left.reshape(-1, left.shape[-1])
    flat_right = right.reshape(-1, right.shape[-1])
    return lax.dot_general(
        flat_left, flat_right, (((0,), (0,)), ((), ())), preferred_element_type=jnp.float32
    )


def first_contract(left, right):
    return lax.dot_general(
        left, right, (((0,), (0,)), ((), ())), precision=HIGH, preferred_element_type=jnp.float32
    )


def layer_norm(values):
    center = values - jnp.mean(values, -1, keepdims=True)
    inverse = lax.rsqrt(jnp.mean(center * center, -1, keepdims=True) + 1e-06)
    return (center * inverse, inverse)


def norm_back(upstream, normed, inverse):
    return inverse * (
        upstream
        - jnp.mean(upstream, -1, keepdims=True)
        - normed * jnp.mean(upstream * normed, -1, keepdims=True)
    )


def silu_slope(values):
    sigma = jax.nn.sigmoid(values)
    return sigma * (1.0 + values * (1.0 - sigma))


def plan_table():
    betas = jnp.linspace(0.0001, 0.02, NSTEPS, dtype=jnp.float32)
    return jnp.exp(jnp.cumsum(jnp.log(1.0 - betas)))


def sinusoid(steps):
    half_width = FREQ // 2
    freqs = jnp.exp(-math.log(10000.0) * jnp.arange(half_width, dtype=jnp.float32) / half_width)
    angles = steps.astype(jnp.float32)[:, None] * freqs[None, :]
    return jnp.concatenate([jnp.cos(angles), jnp.sin(angles)], 1)


def dp_peers(mask):
    spread, pair = lax.axis_size(DP), lax.axis_size("mod")
    return [(i * pair + c, (i ^ mask) * pair + c) for i in range(spread) for c in range(pair)]


def plane_peers(masks):
    spread, pair = lax.axis_size(DP), lax.axis_size("mod")
    return [(i * pair + c, (i ^ masks[c]) * pair + c) for i in range(spread) for c in range(pair)]


def send(values, peers):
    return lax.ppermute(values, DP + ("mod",), peers)


def swap_cores(values):
    return lax.ppermute(values, "mod", [(0, 1), (1, 0)])


def far_groups():
    spread = lax.axis_size(DP)
    bits = [1 << k for k in range(2, spread.bit_length() - 1)]
    if len(bits) == 2:
        return [[bits[0], bits[1], bits[0] | bits[1]]]
    return [[bit] for bit in bits]


def far_masks():
    masks = [0]
    for group in far_groups():
        masks = masks + [mask | have for mask in group for have in masks]
    return masks


def block_places(far):
    me, core = lax.axis_index(DP), lax.axis_index("mod")
    second = jnp.where(core == 0, 1, 2)
    third = jnp.where(core == 0, 2, 1)
    near = jnp.stack([jnp.zeros_like(second), second, third, second | third])
    return ((me ^ near)[:, None] ^ far[None, :]).reshape(-1).astype(jnp.int32)


def relative_places():
    return block_places(jnp.array(far_masks(), jnp.int32))


def stacked_places():
    far = jnp.arange(lax.axis_size("far"), dtype=jnp.int32)
    return block_places(4 * (far ^ lax.axis_index("far")))


def move_kernel(slots, sources, targets, hold, in_sems, out_sems):
    total = len(sources)
    for first in range(0, total, slots):
        wave = range(first, min(first + slots, total))
        arriving = [
            pltpu.make_async_copy(sources[at], hold.at[at - first], in_sems.at[at]) for at in wave
        ]
        for copy in arriving:
            copy.start()
        leaving = []
        for at, copy in zip(wave, arriving):
            copy.wait()
            leaving.append(
                pltpu.make_async_copy(hold.at[at - first], targets[at], out_sems.at[at])
            )
            leaving[-1].start()
        for copy in leaving:
            copy.wait()


def place_kernel(counts, slots, places, *refs):
    ins, out = (refs[: len(counts)], refs[len(counts)])
    sources = [ins[part].at[row] for part, count in enumerate(counts) for row in range(count)]
    targets = [out.at[places[at]] for at in range(len(sources))]
    move_kernel(slots, sources, targets, *refs[len(counts) + 1 :])


def pick_kernel(counts, slots, places, source, *refs):
    outs = refs[: len(counts)]
    targets = [outs[part].at[row] for part, count in enumerate(counts) for row in range(count)]
    sources = [source.at[places[at]] for at in range(len(targets))]
    move_kernel(slots, sources, targets, *refs[len(counts) :])


def plane_slots(total, plane, kind):
    rows, columns = plane
    padded = -(-rows // 16) * 16 * -(-columns // 128) * 128 * jnp.dtype(kind).itemsize
    return max(1, min(total, (24 << 20) // padded))


def move_call(kernel, counts, places, operands, out_shape, out_count, plane, kind):
    total = sum(counts)
    slots = plane_slots(total, plane, kind)
    any_space = pl.BlockSpec(memory_space=pl.ANY)
    return pl.pallas_call(
        functools.partial(kernel, counts, slots),
        grid_spec=pltpu.PrefetchScalarGridSpec(
            num_scalar_prefetch=1,
            grid=(1,),
            in_specs=[any_space] * len(operands),
            out_specs=any_space if out_count is None else [any_space] * out_count,
            scratch_shapes=[
                pltpu.VMEM((slots,) + plane, kind),
                pltpu.SemaphoreType.DMA((total,)),
                pltpu.SemaphoreType.DMA((total,)),
            ],
        ),
        out_shape=out_shape,
        compiler_params=pltpu.CompilerParams(vmem_limit_bytes=VMEM),
        cost_estimate=pl.CostEstimate(
            flops=0,
            bytes_accessed=2 * total * plane[0] * plane[1] * jnp.dtype(kind).itemsize,
            transcendentals=0,
        ),
        name="move_blocks",
    )(places, *operands)


def place_blocks(parts, places):
    counts = [part.shape[0] for part in parts]
    plane, kind = (parts[0].shape[1:], parts[0].dtype)
    shape = jax.ShapeDtypeStruct((sum(counts),) + plane, kind)
    return move_call(place_kernel, counts, places, parts, shape, None, plane, kind)


def pick_blocks(values, places):
    counts = [values.shape[0] // 4] * 4
    plane, kind = (values.shape[1:], values.dtype)
    shape = [jax.ShapeDtypeStruct((count,) + plane, kind) for count in counts]
    return move_call(pick_kernel, counts, places, [values], shape, 4, plane, kind)


def tie(*values):
    return lax.optimization_barrier(values)


def gather_far(block):
    stack = block[None]
    for group in far_groups():
        stack = jnp.concatenate([stack] + [send(stack, dp_peers(mask)) for mask in group], 0)
    return stack


def gather_near(stack):
    return send(stack, plane_peers((1, 2))), send(stack, plane_peers((2, 1)))


def gather_last(second):
    return send(second, plane_peers((2, 1)))


def gather_parts(block):
    stack = gather_far(block)
    second, third = gather_near(stack)
    return [stack, second, third, gather_last(second)]


def far_stack(block):
    return lax.all_gather(block, "far", axis=0)


def far_share(stack):
    return lax.psum_scatter(stack, "far", scatter_dimension=0)


def add_low(left, right):
    return (left.astype(jnp.float32) + right.astype(jnp.float32)).astype(left.dtype)


def scatter_far(own):
    wide = jnp.float32
    for group in reversed(far_groups()):
        count = own.shape[0] // (len(group) + 1)
        total = own[:count].astype(wide)
        for pos, mask in enumerate(group):
            total = total + send(
                own[(pos + 1) * count : (pos + 2) * count], dp_peers(mask)
            ).astype(wide)
        own = total if count == 1 else total.astype(own.dtype)
    return own[0].astype(wide)


def scatter_parts(own, second, third, both, meanwhile=()):
    second = add_low(second, send(both, plane_peers((2, 1))))
    second, *meanwhile = tie(second, *meanwhile)
    from_third = send(third, plane_peers((2, 1)))
    from_second = send(second, plane_peers((1, 2)))
    share = scatter_far(add_low(add_low(own, from_third), from_second))
    return (share, *meanwhile) if meanwhile else share


def all_sum(values, meanwhile=()):
    return dp_sum(values + swap_cores(values), meanwhile)


def dp_sum(values, meanwhile=()):
    for pos in range(lax.axis_size(DP).bit_length() - 1):
        values = values + send(values, dp_peers(1 << pos))
        if pos == 1:
            values, *meanwhile = tie(values, *meanwhile)
    return (values, *meanwhile) if meanwhile else values


def product(left, right, dims):
    return lax.dot_general(left, right, (dims, ((), ())), preferred_element_type=jnp.float32)


def fill_bias(spread_ref, bias):
    tokens = GRID * GRID
    for head in range(bias.shape[0]):
        spread = spread_ref[head] * LOG2E
        for row in range(GRID):
            off = (GRID - 1 - row) * GRID
            moved = spread if off == 0 else pltpu.roll(spread, SPREAD - off, 1)
            bias[head, row * GRID : (row + 1) * GRID, :] = moved[:, :tokens]


def head_slices(values, head, heads):
    width = heads * HD
    return [
        values[:, part * width + head * HD : part * width + (head + 1) * HD] for part in range(3)
    ]


def attention_kernel(heads, qkv_ref, spread_ref, out_ref, log_ref, bias):
    @pl.when(pl.program_id(0) == 0)
    def _():
        fill_bias(spread_ref, bias)

    values = qkv_ref[...]
    outs, logs = ([], [])
    for head in range(heads):
        query, key, value = head_slices(values, head, heads)
        scores = product(query, key, ((1,), (1,))) * (HD ** (-0.5) * LOG2E) + bias[head]
        top = jnp.max(scores, -1, keepdims=True)
        powers = jnp.exp2(scores - top)
        total = jnp.sum(powers, -1, keepdims=True)
        summed = product(powers.astype(jnp.bfloat16), value, ((1,), (0,)))
        outs.append((summed * (1.0 / total)).astype(jnp.bfloat16))
        logs.append(top + jnp.log2(total))
    spare = out_ref.shape[1] - heads * HD
    if spare:
        outs.append(jnp.zeros((values.shape[0], spare), jnp.bfloat16))
    out_ref[...] = jnp.concatenate(outs, 1)
    log_ref[...] = jnp.concatenate(logs, 1)


def attention(qkv, spread):
    rows, columns = qkv.shape
    heads = spread.shape[0]
    tokens = GRID * GRID
    return pl.pallas_call(
        functools.partial(attention_kernel, heads),
        grid=(rows // tokens,),
        in_specs=[
            pl.BlockSpec((tokens, columns), lambda step: (step, 0)),
            pl.BlockSpec(spread.shape, lambda step: (0, 0, 0)),
        ],
        out_specs=[
            pl.BlockSpec((tokens, HALF_PAD), lambda step: (step, 0)),
            pl.BlockSpec((tokens, heads), lambda step: (step, 0)),
        ],
        out_shape=[
            jax.ShapeDtypeStruct((rows, HALF_PAD), jnp.bfloat16),
            jax.ShapeDtypeStruct((rows, heads), jnp.float32),
        ],
        scratch_shapes=[pltpu.VMEM((heads, tokens, tokens), jnp.float32)],
        compiler_params=pltpu.CompilerParams(vmem_limit_bytes=VMEM),
        cost_estimate=pl.CostEstimate(
            flops=4 * rows * tokens * heads * 256,
            bytes_accessed=rows * columns * 4,
            transcendentals=rows * tokens * heads,
        ),
        name="attention",
    )(qkv, spread)


def attention_back_kernel(
    heads, qkv_ref, upstream_ref, log_ref, spread_ref, d_qkv_ref, d_spread_ref, bias, d_bias
):
    tokens = GRID * GRID

    @pl.when(pl.program_id(0) == 0)
    def _():
        fill_bias(spread_ref, bias)
        d_bias[...] = jnp.zeros_like(d_bias)

    values, upstream, logs = (qkv_ref[...], upstream_ref[...], log_ref[...])
    d_query, d_key, d_value = ([], [], [])
    for head in range(heads):
        query, key, value = head_slices(values, head, heads)
        d_out = upstream[:, head * HD : (head + 1) * HD]
        scores = product(query, key, ((1,), (1,))) * (HD ** (-0.5) * LOG2E) + bias[head]
        probs = jnp.exp2(scores - logs[:, head : head + 1])
        d_probs = product(d_out, value, ((1,), (1,)))
        d_scores = probs * (d_probs - jnp.sum(probs * d_probs, -1, keepdims=True))
        d_bias[head] += d_scores
        d_scores = d_scores.astype(jnp.bfloat16)
        d_query.append((product(d_scores, key, ((1,), (0,))) * HD ** (-0.5)).astype(jnp.bfloat16))
        d_key.append((product(d_scores, query, ((0,), (0,))) * HD ** (-0.5)).astype(jnp.bfloat16))
        d_value.append(
            product(probs.astype(jnp.bfloat16), d_out, ((0,), (0,))).astype(jnp.bfloat16)
        )
    pieces = d_query + d_key + d_value
    spare = d_qkv_ref.shape[1] - 3 * heads * HD
    if spare:
        pieces = pieces + [jnp.zeros((tokens, spare), jnp.bfloat16)]
    d_qkv_ref[...] = jnp.concatenate(pieces, 1)

    @pl.when(pl.program_id(0) == pl.num_programs(0) - 1)
    def _():
        for head in range(heads):
            total = jnp.zeros((GRID, SPREAD), jnp.float32)
            for row in range(GRID):
                off = (GRID - 1 - row) * GRID
                rows = d_bias[head, row * GRID : (row + 1) * GRID, :]
                wide = jnp.concatenate([rows, jnp.zeros((GRID, SPREAD - tokens), jnp.float32)], 1)
                total += wide if off == 0 else pltpu.roll(wide, off, 1)
            d_spread_ref[head] = total


def attention_back(qkv, upstream, logs, spread):
    rows, columns = qkv.shape
    heads = spread.shape[0]
    tokens = GRID * GRID
    return pl.pallas_call(
        functools.partial(attention_back_kernel, heads),
        grid=(rows // tokens,),
        in_specs=[
            pl.BlockSpec((tokens, columns), lambda step: (step, 0)),
            pl.BlockSpec((tokens, upstream.shape[1]), lambda step: (step, 0)),
            pl.BlockSpec((tokens, heads), lambda step: (step, 0)),
            pl.BlockSpec(spread.shape, lambda step: (0, 0, 0)),
        ],
        out_specs=[
            pl.BlockSpec((tokens, columns), lambda step: (step, 0)),
            pl.BlockSpec(spread.shape, lambda step: (0, 0, 0)),
        ],
        out_shape=[
            jax.ShapeDtypeStruct((rows, columns), jnp.bfloat16),
            jax.ShapeDtypeStruct(spread.shape, jnp.float32),
        ],
        scratch_shapes=[pltpu.VMEM((heads, tokens, tokens), jnp.float32)] * 2,
        compiler_params=pltpu.CompilerParams(vmem_limit_bytes=VMEM),
        cost_estimate=pl.CostEstimate(
            flops=10 * rows * tokens * heads * 256,
            bytes_accessed=rows * columns * 6,
            transcendentals=rows * tokens * heads,
        ),
        name="attention_back",
    )(qkv, upstream, logs, spread)


def whole_block(shape):
    return pl.BlockSpec(shape, lambda step: (0,) * len(shape), pipeline_mode=pl.Buffered(1))


def column_tile(columns, choices=(768, 896, 256)):
    return next((tile for tile in choices if columns % tile == 0), 128)


def feed_in_kernel(values_ref, weights_ref, act_ref, slope_ref):
    weights = weights_ref[...]
    rate = math.sqrt(2.0 / math.pi)
    cubic = 0.044715 * rate
    for row in range(0, values_ref.shape[0], 256):
        pre = product(values_ref[row : row + 256, :], weights, ((1,), (0,)))
        square = pre * pre
        gate = 0.5 + 0.5 * jnp.tanh(pre * (rate + cubic * square))
        act = pre * gate
        slope = gate + (act - act * gate) * (2.0 * rate + 6.0 * cubic * square)
        act_ref[row : row + 256, :] = act.astype(jnp.bfloat16)
        slope_ref[row : row + 256, :] = slope.astype(jnp.bfloat16)


def feed_in(values, weights, columns):
    rows, depth = values.shape
    tile = column_tile(columns)
    return pl.pallas_call(
        feed_in_kernel,
        grid=(columns // tile,),
        in_specs=[whole_block((rows, depth)), pl.BlockSpec((depth, tile), lambda step: (0, step))],
        out_specs=[pl.BlockSpec((rows, tile), lambda step: (0, step))] * 2,
        out_shape=[jax.ShapeDtypeStruct((rows, columns), jnp.bfloat16)] * 2,
        compiler_params=pltpu.CompilerParams(vmem_limit_bytes=VMEM),
        cost_estimate=pl.CostEstimate(
            flops=2 * rows * depth * columns,
            bytes_accessed=4 * rows * columns,
            transcendentals=rows * columns,
        ),
        name="feed_in",
    )(values, weights)


def feed_back_kernel(values_ref, weights_ref, slope_ref, out_ref):
    weights = weights_ref[...]
    for row in range(0, values_ref.shape[0], 256):
        d_act = product(values_ref[row : row + 256, :], weights, ((1,), (0,)))
        d_pre = d_act * slope_ref[row : row + 256, :].astype(jnp.float32)
        out_ref[row : row + 256, :] = d_pre.astype(jnp.bfloat16)


def feed_back(values, weights, slope):
    rows, depth = values.shape
    columns = weights.shape[1]
    tile = column_tile(columns)
    return pl.pallas_call(
        feed_back_kernel,
        grid=(columns // tile,),
        in_specs=[
            whole_block((rows, depth)),
            pl.BlockSpec((depth, tile), lambda step: (0, step)),
            pl.BlockSpec((rows, tile), lambda step: (0, step)),
        ],
        out_specs=pl.BlockSpec((rows, tile), lambda step: (0, step)),
        out_shape=jax.ShapeDtypeStruct((rows, columns), jnp.bfloat16),
        compiler_params=pltpu.CompilerParams(vmem_limit_bytes=VMEM),
        cost_estimate=pl.CostEstimate(
            flops=2 * rows * depth * columns,
            bytes_accessed=4 * rows * columns,
            transcendentals=0,
        ),
        name="feed_back",
    )(values, weights, slope)


def into_heads_kernel(values_ref, weights_ref, out_ref):
    weights = weights_ref[...]
    for row in range(0, values_ref.shape[0], 256):
        out_ref[row : row + 256, :] = product(
            values_ref[row : row + 256, :], weights, ((1,), (0,))
        ).astype(jnp.bfloat16)


def into_heads(values, weights):
    rows, depth = values.shape
    columns = weights.shape[1]
    tile = column_tile(columns)
    return pl.pallas_call(
        into_heads_kernel,
        grid=(columns // tile,),
        in_specs=[whole_block((rows, depth)), pl.BlockSpec((depth, tile), lambda step: (0, step))],
        out_specs=pl.BlockSpec((rows, tile), lambda step: (0, step)),
        out_shape=jax.ShapeDtypeStruct((rows, columns), jnp.bfloat16),
        compiler_params=pltpu.CompilerParams(vmem_limit_bytes=VMEM),
        cost_estimate=pl.CostEstimate(
            flops=2 * rows * depth * columns, bytes_accessed=2 * rows * columns, transcendentals=0
        ),
        name="into_heads",
    )(values, weights)


def out_of_kernel(values_ref, weights_ref, out_ref):
    out_ref[...] = product(values_ref[...], weights_ref[...], ((1,), (1,))).astype(out_ref.dtype)


def out_of(values, weights, kind):
    rows, depth = values.shape
    columns = weights.shape[0]
    tile = min(rows, 256)
    return pl.pallas_call(
        out_of_kernel,
        grid=(rows // tile,),
        in_specs=[pl.BlockSpec((tile, depth), lambda step: (step, 0)), whole_block((columns, depth))],
        out_specs=pl.BlockSpec((tile, columns), lambda step: (step, 0)),
        out_shape=jax.ShapeDtypeStruct((rows, columns), kind),
        compiler_params=pltpu.CompilerParams(vmem_limit_bytes=VMEM),
        cost_estimate=pl.CostEstimate(
            flops=2 * rows * depth * columns, bytes_accessed=4 * rows * columns, transcendentals=0
        ),
        name="out_of",
    )(values, weights)


def weight_grad_kernel(places, left_one, left_two, right_one, right_two, *refs):
    outs, total = (refs[:4], refs[4])
    total[...] = product(left_one[...], right_one[...], ((0,), (0,))) + product(
        left_two[...], right_two[...], ((0,), (0,))
    )
    count, rows = outs[0].shape[:2]
    for part in range(4):
        for row in range(count):
            first = pl.multiple_of(places[part * count + row] * rows, 8)
            outs[part][row] = total[pl.ds(first, rows), :].astype(jnp.bfloat16)


def weight_grad(left, right, places):
    rows, depth = left[0].shape
    columns = right[0].shape[1]
    total = places.shape[0]
    block = depth // total
    if block % 8:
        whole = outer_sum(left[0], right[0]) + outer_sum(left[1], right[1])
        return pick_blocks(whole.astype(jnp.bfloat16).reshape(total, block, columns), places)
    tile = column_tile(columns, (256,))

    def whole_left(shape):
        return pl.BlockSpec(shape, lambda step, _: (0, 0), pipeline_mode=pl.Buffered(1))

    return pl.pallas_call(
        weight_grad_kernel,
        grid_spec=pltpu.PrefetchScalarGridSpec(
            num_scalar_prefetch=1,
            grid=(columns // tile,),
            in_specs=[whole_left((rows, depth))] * 2
            + [pl.BlockSpec((rows, tile), lambda step, _: (0, step))] * 2,
            out_specs=[pl.BlockSpec((total // 4, block, tile), lambda step, _: (0, 0, step))] * 4,
            scratch_shapes=[pltpu.VMEM((depth, tile), jnp.float32)],
        ),
        out_shape=[jax.ShapeDtypeStruct((total // 4, block, columns), jnp.bfloat16)] * 4,
        compiler_params=pltpu.CompilerParams(vmem_limit_bytes=VMEM),
        cost_estimate=pl.CostEstimate(
            flops=4 * rows * depth * columns, bytes_accessed=4 * depth * columns, transcendentals=0
        ),
        name="weight_grad",
    )(places, *left, *right)


def norm_rows(values):
    center = values - jnp.mean(values, -1, keepdims=True)
    inverse = lax.rsqrt(jnp.mean(center * center, -1, keepdims=True) + 1e-06)
    return center * inverse, inverse


def row_sum(values):
    return jnp.sum(values, 0, keepdims=True)


def image_call(kernel, name, operands, outs, images, sums=(), core=None):
    tokens = GRID * GRID
    lead = () if core is None else (core,)

    def spec(shape, whole):
        if whole:
            return pl.BlockSpec(
                shape, lambda step, *_: (0,) * len(shape), pipeline_mode=pl.Buffered(1)
            )
        if len(shape) == 3:
            return pl.BlockSpec((1,) + shape[1:], lambda step, *_: (step, 0, 0))
        return pl.BlockSpec((tokens, shape[1]), lambda step, *_: (step, 0))

    rows = images * tokens

    def is_whole(shape):
        return len(shape) == 2 and shape[0] != rows

    summed = [pl.BlockSpec(item.shape, lambda step, *_: (0, 0)) for item in sums]
    return pl.pallas_call(
        kernel,
        grid_spec=pltpu.PrefetchScalarGridSpec(
            num_scalar_prefetch=len(lead),
            grid=(images,),
            in_specs=[spec(item.shape, is_whole(item.shape)) for item in operands],
            out_specs=[spec(item.shape, False) for item in outs] + summed,
        ),
        out_shape=list(outs) + list(sums),
        compiler_params=pltpu.CompilerParams(vmem_limit_bytes=VMEM),
        cost_estimate=pl.CostEstimate(
            flops=4 * rows * D * D if lead else 64 * rows * D,
            bytes_accessed=16 * rows * D,
            transcendentals=0,
        ),
        name=name,
    )(*lead, *operands)


def core_rows(ref, core, mine):
    half = D // 2
    first = core * half if mine else (1 - core) * half
    return ref[pl.ds(pl.multiple_of(first, 16), half), :]


def merge_kernel(
    core_ref, one_ref, two_ref, mine_ref, other_ref, hidden_ref, mod_ref, branch_ref, out_ref, in_ref
):
    core = core_ref[0]
    half = D // 2
    one, two, mod = (one_ref[...][:, :half], two_ref[...][:, :half], mod_ref[0])

    def columns(ref):
        total = product(one, core_rows(ref, core, True), ((1,), (0,))) + product(
            two, core_rows(ref, core, False), ((1,), (0,))
        )
        return total[:, :half]

    mine, other = (columns(mine_ref), columns(other_ref))
    first = jnp.where(core == 0, mine, other)
    branch = jnp.concatenate([first, jnp.where(core == 0, other, mine)], 1)
    hidden = hidden_ref[...] + mod[2:3] * branch
    normed, _ = norm_rows(hidden)
    branch_ref[...] = branch.astype(jnp.bfloat16)
    out_ref[...] = hidden
    in_ref[...] = (normed * (1.0 + mod[4:5]) + mod[3:4]).astype(jnp.bfloat16)


def ends_kernel(
    count, mine_ref, theirs_ref, hidden_ref, noise_ref, head_ref, mod_ref, *refs
):
    d_hidden_ref, d_branch_ref, d_mod_ref, g_head_ref, loss_ref = refs
    wide, low = (jnp.float32, jnp.bfloat16)

    @pl.when(pl.program_id(0) == 0)
    def _():
        g_head_ref[...] = jnp.zeros_like(g_head_ref)
        loss_ref[...] = jnp.zeros_like(loss_ref)

    mod, head = (mod_ref[0], head_ref[...])
    branch = mine_ref[...] + theirs_ref[...].astype(wide)
    normed, inverse = norm_rows(hidden_ref[...] + mod[5:6] * branch)
    final_in = (normed * (1.0 + mod[7:8]) + mod[6:7]).astype(low)
    error = product(final_in, head, ((1,), (1,))) - noise_ref[...]
    loss_ref[...] += jnp.sum(error * error)
    d_predicted = (error * (2.0 / count)).astype(low)
    d_final = product(d_predicted, head, ((1,), (0,)))
    g_head_ref[...] += product(d_predicted, final_in, ((0,), (0,)))
    d_hidden = norm_back(d_final * (1.0 + mod[7:8]), normed, inverse)
    d_hidden_ref[...] = d_hidden
    d_branch_ref[...] = (mod[5:6] * d_hidden).astype(low)
    blank = jnp.zeros((5, D), wide)
    gate, shift, scale = (row_sum(d_hidden * branch), row_sum(d_final), row_sum(d_final * normed))
    d_mod_ref[0] = jnp.concatenate([blank, gate, shift, scale], 0)


def merge_back_kernel(
    core_ref, mine_ref, theirs_ref, hidden_ref, branch_ref, d_hidden_ref, p_mine, p_other, mod_ref,
    d_mod_ref, *refs
):
    d_out_ref, d_branch_ref, d_one_ref, d_two_ref, d_mod_out_ref = refs
    core = core_ref[0]
    wide, low = (jnp.float32, jnp.bfloat16)
    mod, half = (mod_ref[0], D // 2)
    d_in = mine_ref[...] + theirs_ref[...].astype(wide)
    normed, inverse = norm_rows(hidden_ref[...])
    d_hidden = d_hidden_ref[...] + norm_back(d_in * (1.0 + mod[4:5]), normed, inverse)
    d_out_ref[...] = d_hidden
    gate = row_sum(d_hidden * branch_ref[...].astype(wide))
    d_branch = mod[2:3] * d_hidden
    d_branch_ref[...] = d_branch.astype(low)
    low_half, high_half = (d_branch[:, :half], d_branch[:, half:])
    d_mine = jnp.where(core == 0, low_half, high_half).astype(low)
    d_other = jnp.where(core == 0, high_half, low_half).astype(low)

    def heads(mine):
        total = product(d_mine, core_rows(p_mine, core, mine)[:, :half], ((1,), (1,))) + product(
            d_other, core_rows(p_other, core, mine)[:, :half], ((1,), (1,))
        )
        spare = jnp.zeros((total.shape[0], HALF_PAD - half), low)
        return jnp.concatenate([total.astype(low), spare], 1)

    d_one_ref[...] = heads(True)
    d_two_ref[...] = heads(False)
    blank = jnp.zeros((2, D), wide)
    sums = [blank, gate, row_sum(d_in), row_sum(d_in * normed), d_mod_ref[0][5:8]]
    d_mod_out_ref[0] = jnp.concatenate(sums, 0)


def start_back_kernel(
    mine_ref, theirs_ref, hidden_ref, d_hidden_ref, mixed_ref, mod_ref, d_mod_ref, *refs
):
    d_mod_out_ref, g_patch_ref = refs
    wide = jnp.float32

    @pl.when(pl.program_id(0) == 0)
    def _():
        g_patch_ref[...] = jnp.zeros_like(g_patch_ref)

    mod = mod_ref[0]
    d_in = mine_ref[...] + theirs_ref[...].astype(wide)
    normed, inverse = norm_rows(hidden_ref[...])
    d_hidden = d_hidden_ref[...] + norm_back(d_in * (1.0 + mod[1:2]), normed, inverse)
    g_patch_ref[...] += product(mixed_ref[...], d_hidden.astype(jnp.bfloat16), ((0,), (0,)))
    d_mod_out_ref[0] = jnp.concatenate(
        [row_sum(d_in), row_sum(d_in * normed), d_mod_ref[0][2:8]], 0
    )


def shifts():
    offset = jnp.arange(SIDE, dtype=jnp.int32)[:, None, None]
    column = jnp.arange(GRID, dtype=jnp.int32)
    return (offset == GRID - 1 - column[:, None] + column[None, :]).astype(jnp.float32)


def spread_bias(relative):
    turned = relative.reshape(-1, SIDE, SIDE)[:, ::-1, ::-1]
    spread = jnp.einsum("hed,dxy->hxey", turned, shifts(), precision=HIGH)
    spread = spread.reshape(-1, GRID, SIDE * GRID)
    return jnp.pad(spread, ((0, 0), (0, 0), (0, SPREAD - SIDE * GRID)))


def gather_bias(d_spread):
    parts = d_spread[:, :, : SIDE * GRID].reshape(-1, GRID, SIDE, GRID)
    total = jnp.einsum("hxey,dxy->hed", parts, shifts(), precision=HIGH)
    return total[:, ::-1, ::-1].reshape(-1, SIDE * SIDE)


def both_columns_kernel(core_ref, *refs):
    here_refs, there_refs, out_ref = (refs[:4], refs[4:8], refs[8])
    half, wide_half = (D // 2, MLPW // 2)
    spans = [(0, part * half, half) for part in range(3)] + [(2, 0, half)]
    spans = spans + [(1, 0, wide_half), (3, 0, wide_half)]
    place = 0
    for piece, start, width in spans:
        here = here_refs[piece][:, start : start + width]
        there = there_refs[piece][:, start : start + width]
        first = jnp.where(core_ref[0] == 0, here, there)
        second = jnp.where(core_ref[0] == 0, there, here)
        out_ref[:, place : place + 2 * width] = jnp.concatenate([first, second], 1)
        place += 2 * width


def both_columns(here, there, core):
    rows = here[0].shape[0]
    columns = 4 * D + 2 * MLPW
    return pl.pallas_call(
        both_columns_kernel,
        grid_spec=pltpu.PrefetchScalarGridSpec(
            num_scalar_prefetch=1,
            grid=(1,),
            in_specs=[pl.BlockSpec(item.shape, lambda step, _: (0, 0)) for item in here + there],
            out_specs=pl.BlockSpec((rows, columns), lambda step, _: (0, 0)),
        ),
        out_shape=jax.ShapeDtypeStruct((rows, columns), here[0].dtype),
        compiler_params=pltpu.CompilerParams(vmem_limit_bytes=VMEM),
        name="both_columns",
    )(core, *here, *there)


def core_half(values, core, starts, width):
    return [
        jnp.where(
            core == 0,
            values[:, start : start + width],
            values[:, start + width : start + 2 * width],
        )
        for start in starts
    ]


def both_cores(mine, other, core, axis):
    return jnp.where(
        core == 0,
        jnp.concatenate([mine, other], axis),
        jnp.concatenate([other, mine], axis),
    )


def segment_sums(values, bounds, first):
    place = jnp.arange(values.shape[0], dtype=jnp.int32)
    segment = first + sum((place >= bound).astype(jnp.int32) for bound in bounds)
    wanted = segment[None, :] == jnp.arange(11, dtype=jnp.int32)[:, None]
    return jnp.sum(jnp.where(wanted, values[None, :], 0.0), 1)


def mod_squares(values, core):
    columns = jnp.sum(values * values, 0)
    bound = 6 * D - core * values.shape[1]
    return segment_sums(columns, [bound], 4)


def embed_squares(values):
    bounds = [NCLASS + 1, NCLASS + 1 + FREQ, NCLASS + 1 + FREQ + D, NCLASS + 1 + FREQ + D + PDIM]
    return segment_sums(jnp.sum(values * values, 1), bounds, 6)


def block_squares(values):
    return segment_sums(jnp.sum(values * values, 0), [3 * D, 4 * D, 4 * D + MLPW], 0)


def adam_update(grad, first, second, weight, clip):
    first_new = FIRST_DECAY * first + (1.0 - FIRST_DECAY) * (grad * clip)
    second_new = SECOND_DECAY * second + (1.0 - SECOND_DECAY) * (grad * clip) ** 2
    update = (
        first_new
        / (1.0 - FIRST_DECAY**STEP)
        / (jnp.sqrt(second_new / (1.0 - SECOND_DECAY**STEP)) + ADAM_EPSILON)
        + WEIGHT_DECAY * weight
    )
    return (first_new, second_new, update)


def on_device(
    latents,
    noise,
    timesteps,
    labels,
    drops,
    block_weights,
    block_first,
    block_second,
    mod_weights,
    mod_first,
    mod_second,
    embed_weights,
    embed_first,
    embed_second,
    rel_bias,
    rel_first,
    rel_second,
):
    low = jnp.bfloat16
    wide = jnp.float32
    core = lax.axis_index("mod")
    spread = lax.axis_size(DP)
    images = latents.shape[0]
    length = latents.shape[1]
    rows = images * length
    share = embed_weights.shape[1]
    count = float(images * spread * lax.axis_size("mod") * length * latents.shape[2])
    relative, stacked = (relative_places(), stacked_places())

    start = NCLASS + 1
    chosen = jnp.where(drops == 1, NCLASS, labels)
    codes = jnp.stack([timesteps // 32, timesteps % 32, chosen // 32, chosen % 32], 1)
    codes = codes.astype(low)
    codes = both_cores(codes, swap_cores(codes), core, 0)
    code_rows = -(-codes.size // share)
    codes = jnp.pad(codes.reshape(-1), (0, code_rows * share - codes.size))
    small = jnp.concatenate(
        [
            embed_weights[start : start + FREQ].astype(low),
            embed_weights[start + FREQ + D :].astype(low),
            codes.reshape(code_rows, share),
        ],
        0,
    )
    half = D // 2
    wide_half = MLPW // 2
    small_far = gather_far(small)
    now_weights, small_far = tie(block_weights, small_far)
    block_low = now_weights.astype(low)
    q_part, k_part, v_part, p_part = core_half(
        block_low, core, [0, D, 2 * D, 3 * D], half
    )
    in_part, out_part = core_half(block_low, core, [4 * D, 4 * D + MLPW], wide_half)
    pad_part = jnp.zeros((block_low.shape[0], QKV_PAD - QKV_HALF), low)
    attn_part = jnp.concatenate([q_part, k_part, v_part, pad_part], 1)
    proj_spare = jnp.zeros((block_low.shape[0], HALF_PAD - half), low)
    in_part = jnp.concatenate([in_part, p_part, proj_spare], 1)
    attn_far = gather_far(attn_part)
    small_second, small_third = gather_near(small_far)
    small = [small_far, small_second, small_third, gather_last(small_second)]
    later_weights, later_bias, later_embed, later_mod, small[0] = tie(
        block_weights, rel_bias, embed_weights, mod_weights, small[0]
    )
    table = later_embed[:start].astype(low)
    time_out = later_embed[start + FREQ : start + FREQ + D].astype(low).astype(wide)
    everyone = jnp.concatenate([part[:, FREQ + 2 * PDIM :] for part in small], 0)
    everyone = everyone.reshape(spread, -1)[:, : 2 * images * 4]
    everyone = everyone.reshape(spread * 2 * images, 4).astype(wide)
    all_steps = 32.0 * everyone[:, 0] + everyone[:, 1]
    all_chosen = (32.0 * everyone[:, 2] + everyone[:, 3]).astype(jnp.int32)
    small = place_blocks(small, relative)[:, : FREQ + 2 * PDIM]
    small = small.transpose(1, 0, 2).reshape(FREQ + 2 * PDIM, D)
    time_in = small[:FREQ].astype(wide)
    patch = small[FREQ : FREQ + PDIM]
    head = small[FREQ + PDIM :]

    attn_second, attn_third = gather_near(attn_far)
    in_part, attn_far = tie(in_part, attn_far)
    in_far = far_stack(in_part)

    sinus = sinusoid(all_steps)
    pre_time = jnp.dot(sinus, time_in, precision=HIGH, preferred_element_type=wide)
    time_act = jax.nn.silu(pre_time)
    image_of = relative[:, None] * 2 * images + jnp.arange(2 * images, dtype=jnp.int32)[None, :]
    sorting = image_of.reshape(1, -1) == jnp.arange(image_of.size, dtype=jnp.int32)[:, None]

    def sort_images(values):
        return jnp.dot(sorting.astype(wide), values, precision=HIGH, preferred_element_type=wide)

    sorted_sinus = sort_images(sinus)
    sorted_act = sort_images(time_act)
    classes = jnp.arange(start, dtype=jnp.int32)[None, :]
    sorted_class = sort_images(all_chosen[:, None].astype(wide)).astype(jnp.int32)
    first_column = lax.axis_index(DP) * share
    sorted_slope = sort_images(
        silu_slope(lax.dynamic_slice_in_dim(pre_time, first_column, share, 1))
    )
    onehot = all_chosen[:, None] == classes
    cond = jnp.dot(time_act, time_out, precision=HIGH, preferred_element_type=wide) + dense(
        onehot.astype(low), table
    )
    scaled = jax.nn.silu(cond).astype(low)
    scaled, attn_second, attn_third = tie(scaled, attn_second, attn_third)
    attn_both = gather_last(attn_second)
    mod_low = mod_weights.astype(low)
    mod_partial = dense(scaled, mod_low).astype(low)
    mod_parts = jnp.split(mod_partial.reshape(spread, 2 * images, -1), 4)
    heads = HEADS // 2
    bias_rows = spread_bias(jnp.where(core == 0, later_bias[:heads], later_bias[heads:]))
    first_core = (core == 0).astype(wide)
    weight_squares = first_core * (block_squares(later_weights) + embed_squares(later_embed))
    weight_squares = weight_squares + mod_squares(later_mod, core)
    (
        half_mod,
        in_far,
        attn_both,
        bias_rows,
        weight_squares,
        sorted_act,
        sorted_sinus,
        sorted_slope,
        sorted_class,
    ) = scatter_parts(
        *mod_parts,
        meanwhile=(
            in_far,
            attn_both,
            bias_rows,
            weight_squares,
            sorted_act,
            sorted_sinus,
            sorted_slope,
            sorted_class,
        ),
    )
    qkv_low = place_blocks([attn_far, attn_second, attn_third, attn_both], relative).reshape(D, -1)
    in_second, in_third = gather_near(in_far)
    out_part, in_far = tie(out_part, in_far)
    out_far = far_stack(out_part)
    mine = jnp.where(core == 0, half_mod[:images], half_mod[images:])
    theirs = jnp.where(core == 0, half_mod[images:], half_mod[:images])
    modulation = both_cores(mine, swap_cores(theirs), core, 1).reshape(images, 8, D)

    def moved(normed, shift):
        return (
            normed * (1.0 + modulation[:, shift + 1 : shift + 2]) + modulation[:, shift : shift + 1]
        ).astype(low)

    def flat(values):
        return values.reshape(rows, -1)

    def sum_cores(mine, theirs):
        return (mine + swap_cores(theirs).astype(wide)).reshape(images, length, -1)

    alpha_bar = jnp.sum(
        jnp.where(
            timesteps[:, None] == jnp.arange(NSTEPS, dtype=jnp.int32)[None, :],
            plan_table()[None, :],
            0.0,
        ),
        1,
    )
    mixed = (
        jnp.sqrt(alpha_bar)[:, None, None] * latents
        + jnp.sqrt(1.0 - alpha_bar)[:, None, None] * noise
    ).astype(low)
    hidden0 = dense(mixed, patch)
    normed1, inverse1 = layer_norm(hidden0)
    attn_in = flat(moved(normed1, 0))
    attn_in_two = swap_cores(attn_in)
    qkv = into_heads(attn_in, qkv_low)
    qkv_two = into_heads(attn_in_two, qkv_low)
    heads_two, logs_two = attention(qkv_two, bias_rows)
    qkv, logs_two, in_second, in_third, out_far = tie(qkv, logs_two, in_second, in_third, out_far)
    heads_two = swap_cores(heads_two)
    in_both = gather_last(in_second)
    heads_one, logs = attention(qkv, bias_rows)
    heads_one, heads_two, in_both, out_far = tie(heads_one, heads_two, in_both, out_far)
    out_second, out_third = gather_near(out_far)
    in_low = place_blocks([in_far, in_second, in_third, in_both], stacked).reshape(D, -1)
    proj_half = in_low[:, wide_half : wide_half + HALF_PAD]
    proj_other = swap_cores(proj_half)
    core_place = core.astype(jnp.int32).reshape(1)
    rows_wide = jax.ShapeDtypeStruct((rows, D), wide)
    rows_low = jax.ShapeDtypeStruct((rows, D), low)
    rows_heads = jax.ShapeDtypeStruct((rows, HALF_PAD), low)
    mod_shape = jax.ShapeDtypeStruct((images, 8, D), wide)
    patch_shape = jax.ShapeDtypeStruct((PDIM, D), wide)
    branch_one, hidden1, mlp_in = image_call(
        merge_kernel,
        "merge_heads",
        [heads_one, heads_two, proj_half, proj_other, flat(hidden0), modulation],
        [rows_low, rows_wide, rows_low],
        images,
        core=core_place,
    )
    mlp_in, out_second = tie(mlp_in, out_second)
    mlp_in_two = swap_cores(mlp_in)
    act, slope = feed_in(mlp_in, in_low, wide_half)
    act, mlp_in_two, out_third = tie(act, mlp_in_two, out_third)
    out_both = gather_last(out_second)
    act_two, slope_two = feed_in(mlp_in_two, in_low, wide_half)
    act_two, out_both = tie(act_two, out_both)
    out_low = place_blocks([out_far, out_second, out_third, out_both], stacked).reshape(D, -1)
    branch_theirs = out_of(act_two, out_low, low)
    branch_theirs = swap_cores(branch_theirs)
    branch_mine = out_of(act, out_low, wide)
    d_hidden2, d_branch_two, d_mod, g_head, loss_tile = image_call(
        functools.partial(ends_kernel, count),
        "ends",
        [
            branch_mine,
            branch_theirs,
            hidden1,
            noise.reshape(rows, -1),
            head,
            modulation,
        ],
        [rows_wide, rows_low, mod_shape],
        images,
        sums=[patch_shape, jax.ShapeDtypeStruct((8, 128), wide)],
    )
    loss_here = loss_tile[0, 0]
    d_branch_two_two = swap_cores(d_branch_two)
    d_pre = feed_back(d_branch_two, out_low, slope)
    d_pre, d_branch_two_two = tie(d_pre, d_branch_two_two)
    d_pre_two = feed_back(d_branch_two_two, out_low, slope_two)
    out_own, out_second, out_third, out_both = weight_grad(
        (d_branch_two, d_branch_two_two), (act, act_two), stacked
    )
    out_back = send(out_both, plane_peers((2, 1)))
    d_pre, out_third = tie(d_pre, out_third)
    d_mlp_theirs = swap_cores(out_of(d_pre_two, in_low, low))
    d_mlp_mine = out_of(d_pre, in_low, wide)
    d_pre, d_mlp_mine, out_back = tie(d_pre, d_mlp_mine, out_back)
    out_second = send(add_low(out_second, out_back), plane_peers((1, 2)))
    out_third = send(out_third, plane_peers((2, 1)))
    in_own, in_second, in_third, in_both = weight_grad(
        (mlp_in, mlp_in_two), (d_pre, d_pre_two), stacked
    )
    in_both, d_mlp_theirs, d_mlp_mine = tie(in_both, d_mlp_theirs, d_mlp_mine)
    d_hidden1, d_branch_one, d_mine, d_theirs, d_mod = image_call(
        merge_back_kernel,
        "merge_heads_back",
        [
            d_mlp_mine,
            d_mlp_theirs,
            hidden1,
            branch_one,
            d_hidden2,
            proj_half,
            proj_other,
            modulation,
            d_mod,
        ],
        [rows_wide, rows_low, rows_heads, rows_heads, mod_shape],
        images,
        core=core_place,
    )
    d_branch_one, d_mine, out_second, out_third, in_both = tie(
        d_branch_one, d_mine, out_second, out_third, in_both
    )
    in_back = send(in_both, plane_peers((2, 1)))
    g_out = far_share(add_low(add_low(out_own, out_third), out_second))
    d_theirs = swap_cores(d_theirs)
    d_qkv, d_spread = attention_back(qkv, d_mine, logs, bias_rows)
    d_qkv, d_branch_one, d_theirs, in_back, in_third = tie(
        d_qkv, d_branch_one, d_theirs, in_back, in_third
    )
    in_second = send(add_low(in_second, in_back), plane_peers((1, 2)))
    in_third = send(in_third, plane_peers((2, 1)))
    g_proj = both_cores(
        outer_sum(heads_one, d_branch_one)[:half],
        outer_sum(heads_two, d_branch_one)[:half],
        core,
        0,
    )
    spare = ((0, 0), (0, HALF_PAD - half))
    g_low_half, g_high_half = (jnp.pad(g_proj[:, :half], spare), jnp.pad(g_proj[:, half:], spare))
    g_proj_mine = jnp.where(core == 0, g_low_half, g_high_half)
    g_proj_theirs = jnp.where(core == 0, g_high_half, g_low_half).astype(low)
    g_proj = (g_proj_mine + swap_cores(g_proj_theirs).astype(wide)).astype(low)
    proj_own, proj_second, proj_third, proj_both = pick_blocks(
        g_proj.reshape(spread, -1, HALF_PAD), stacked
    )
    proj_both, d_theirs = tie(proj_both, d_theirs)
    proj_back = send(proj_both, plane_peers((2, 1)))
    d_qkv_two, d_spread_two = attention_back(qkv_two, d_theirs, logs_two, bias_rows)
    d_qkv_two, in_second, in_third, proj_back, proj_third, g_out = tie(
        d_qkv_two, in_second, in_third, proj_back, proj_third, g_out
    )
    g_in = far_share(add_low(add_low(in_own, in_third), in_second))
    d_spread = d_spread + d_spread_two
    proj_second = send(add_low(proj_second, proj_back), plane_peers((1, 2)))
    proj_third = send(proj_third, plane_peers((2, 1)))
    rel_half = gather_bias(d_spread)
    packed = jnp.concatenate([rel_half.reshape(-1), (loss_here * jnp.ones(1, wide))])
    bits = [1 << pos for pos in range(2, spread.bit_length() - 1)] + [1, 2]
    for bit in bits[:-3]:
        packed = packed + send(packed, dp_peers(bit))
    attn_own, attn_second, attn_third, attn_both = weight_grad(
        (attn_in, attn_in_two), (d_qkv, d_qkv_two), stacked
    )
    attn_both, proj_second, proj_third, packed = tie(attn_both, proj_second, proj_third, packed)
    packed = packed + send(packed, dp_peers(bits[-3]))
    g_proj = far_share(add_low(add_low(proj_own, proj_third), proj_second))
    attn_back = send(attn_both, plane_peers((2, 1)))
    d_qkv_two, attn_both, attn_third = tie(d_qkv_two, attn_both, attn_third)
    d_attn_theirs = out_of(d_qkv_two, qkv_low, low)
    d_qkv, d_attn_theirs, attn_back, packed = tie(d_qkv, d_attn_theirs, attn_back, packed)
    packed = packed + send(packed, dp_peers(bits[-2]))
    d_attn_theirs = swap_cores(d_attn_theirs)
    attn_second = send(add_low(attn_second, attn_back), plane_peers((1, 2)))
    attn_third = send(attn_third, plane_peers((2, 1)))
    d_attn_mine = out_of(d_qkv, qkv_low, wide)
    d_attn_mine, packed = tie(d_attn_mine, packed)
    packed = packed + send(packed, dp_peers(bits[-1]))
    d_mod, g_patch = image_call(
        start_back_kernel,
        "start_back",
        [
            d_attn_mine,
            d_attn_theirs,
            flat(hidden0),
            d_hidden1,
            flat(mixed),
            modulation,
            d_mod,
        ],
        [mod_shape],
        images,
        sums=[patch_shape],
    )

    d_modulation = d_mod.reshape(images, 8 * D).astype(low)
    mod_half = 4 * D
    d_keep = jnp.where(core == 0, d_modulation[:, :mod_half], d_modulation[:, mod_half:])
    d_give = jnp.where(core == 0, d_modulation[:, mod_half:], d_modulation[:, :mod_half])
    d_pair = both_cores(d_keep, swap_cores(d_give), core, 0)
    d_pair, attn_second, attn_third, packed, g_in = tie(
        d_pair, attn_second, attn_third, packed, g_in
    )
    d_far = gather_far(d_pair)
    attn_own, d_far = tie(attn_own, d_far)
    g_qkv = far_share(add_low(add_low(attn_own, attn_third), attn_second))
    d_second, d_third = gather_near(d_far)
    d_parts = [d_far, d_second, d_third, gather_last(d_second)]
    d_all = jnp.concatenate(d_parts, 0).reshape(spread * 2 * images, mod_half)
    mod_grad = outer_sum(scaled, d_all)
    d_scaled = dense_trans(d_all, mod_low)
    theirs = jnp.split(swap_cores(d_scaled), 4)
    d_scaled = d_scaled + jnp.concatenate([theirs[0], theirs[2], theirs[1], theirs[3]], 0)
    d_cond = sort_images(d_scaled * silu_slope(cond))
    g_table = first_contract((sorted_class == classes).astype(wide), d_cond)
    g_time_out = first_contract(sorted_act, d_cond)
    d_time = lax.dot_general(
        d_cond, time_out, (((1,), (1,)), ((), ())), precision=HIGH, preferred_element_type=wide
    )
    g_ends = jnp.concatenate([g_patch, g_head], 0)
    g_ends = g_ends + swap_cores(g_ends)
    tail = jnp.concatenate([d_time, g_ends], 0)
    tail = tail.reshape(-1, spread, share).transpose(1, 0, 2)
    tail = scatter_parts(*pick_blocks(tail, relative))
    tail, g_qkv, g_proj = tie(tail, g_qkv, g_proj)
    d_time_here, g_ends = (tail[: -2 * PDIM], tail[-2 * PDIM :])
    g_time_in = first_contract(sorted_sinus, d_time_here * sorted_slope)
    embed_grad = jnp.concatenate([g_table, g_time_in, g_time_out, g_ends], 0)

    g_here = [g_qkv, g_in, g_proj, g_out]
    g_there = [swap_cores(piece) for piece in g_here]
    g_squares = sum(
        jnp.where(jnp.arange(11) == matrix, jnp.sum(piece.astype(wide) ** 2), 0.0)
        for matrix, piece in zip((0, 2, 1, 3), g_here)
    )
    block_grad = both_columns(g_here, g_there, core_place)

    packed_other = swap_cores(packed)
    rel_grad = both_cores(
        packed[:-1].reshape(heads, -1), packed_other[:-1].reshape(heads, -1), core, 0
    )
    loss_sum = packed[-1] + packed_other[-1]

    first_core = (core == 0).astype(wide)

    def replica_squares(block, mod, embed):
        return first_core * (block + embed_squares(embed)) + mod_squares(mod, core)

    squares = jnp.concatenate(
        [
            g_squares + mod_squares(mod_grad, core) + first_core * embed_squares(embed_grad),
            weight_squares,
        ]
    )
    squares, block_grad, rel_grad = all_sum(squares, (block_grad, rel_grad))
    block_grad = block_grad.astype(wide)
    grad_parts, weight_parts = jnp.split(squares, 2)
    grad_sq = jnp.concatenate([grad_parts, jnp.sum(rel_grad * rel_grad)[None]])
    weight_sq = jnp.concatenate([weight_parts, jnp.sum(rel_bias * rel_bias)[None]])
    grad_norm = jnp.sqrt(jnp.sum(grad_sq))
    clip = jnp.minimum(1.0, CLIP_NORM / grad_norm)
    block_m, block_s, block_step = adam_update(
        block_grad, block_first, block_second, block_weights, clip
    )
    mod_m, mod_s, mod_step = adam_update(mod_grad, mod_first, mod_second, mod_weights, clip)
    embed_m, embed_s, embed_step = adam_update(
        embed_grad, embed_first, embed_second, embed_weights, clip
    )
    rel_m, rel_s, rel_step = adam_update(rel_grad, rel_first, rel_second, rel_bias, clip)
    update_parts = all_sum(replica_squares(block_squares(block_step), mod_step, embed_step))
    update_sq = jnp.concatenate([update_parts, jnp.sum(rel_step * rel_step)[None]])
    weight_norm = jnp.sqrt(weight_sq)
    update_norm = jnp.sqrt(update_sq)
    ratio = weight_norm / update_norm
    def spread_ratio(length, bounds, first, shift=0):
        place = shift + jnp.arange(length, dtype=jnp.int32)
        chosen = ratio[first]
        for step, bound in enumerate(bounds):
            chosen = jnp.where(place >= bound, ratio[first + step + 1], chosen)
        return chosen

    block_ratio = spread_ratio(block_weights.shape[1], [3 * D, 4 * D, 4 * D + MLPW], 0)
    mod_columns = mod_weights.shape[1]
    mod_ratio = spread_ratio(mod_columns, [6 * D], 4, core * mod_columns)
    ends = start + FREQ + D
    embed_bounds = [start, start + FREQ, ends, ends + PDIM]
    embed_ratio = spread_ratio(embed_weights.shape[0], embed_bounds, 6)
    block_new = block_weights - LEARN_RATE * block_ratio[None, :] * block_step
    mod_new = mod_weights - LEARN_RATE * mod_ratio[None, :] * mod_step
    embed_new = embed_weights - LEARN_RATE * embed_ratio[:, None] * embed_step
    rel_new = rel_bias - LEARN_RATE * ratio[11] * rel_step
    matrix_norms = jnp.stack([weight_norm, update_norm])
    return (
        loss_sum,
        grad_norm,
        matrix_norms,
        block_new,
        block_m,
        block_s,
        block_new.astype(jnp.bfloat16),
        mod_new,
        mod_m,
        mod_s,
        mod_new.astype(jnp.bfloat16),
        embed_new,
        embed_m,
        embed_s,
        embed_new.astype(jnp.bfloat16),
        rel_new,
        rel_m,
        rel_s,
        rel_new.astype(jnp.bfloat16),
        rel_grad * clip,
    )


def solution(mesh):
    spread, pair = mesh.devices.shape
    grid = jax.sharding.Mesh(mesh.devices.reshape(spread // 4, 4, pair), DP + ("mod",))
    placed = (
        P(DP + ("mod",), None, None),
        P(DP + ("mod",), None, None),
        P(DP + ("mod",)),
        P(DP + ("mod",)),
        P(DP + ("mod",)),
        P(DP, None),
        P(DP, None),
        P(DP, None),
        P(DP, "mod"),
        P(DP, "mod"),
        P(DP, "mod"),
        P(None, DP),
        P(None, DP),
        P(None, DP),
        P(),
        P(),
        P(),
    )
    return jax.shard_map(
        on_device,
        mesh=grid,
        in_specs=placed,
        out_specs=(
            P(),
            P(),
            P(),
            P(DP, None),
            P(DP, None),
            P(DP, None),
            P(DP, None),
            P(DP, "mod"),
            P(DP, "mod"),
            P(DP, "mod"),
            P(DP, "mod"),
            P(None, DP),
            P(None, DP),
            P(None, DP),
            P(None, DP),
            P(),
            P(),
            P(),
            P(),
            P(),
        ),
        check_vma=False,
    )
```
